32 devices in a mesh: dp: 4 (over y, core), expert: 8 (over z, x).
Axes of the slice: x: 2, y: 2, z: 4, core: 2. Of those that a mesh axis runs over, the one named last changes fastest.
Arguments:
- tokens: bfloat16 [4096, 768], P(('dp', 'expert')), may hold values from -6 to 6
- seg_ids: int32 [32, 128], P(('dp', 'expert')), may hold values from 0 to 3, never falling along the last dimension, each value on 1 to 96 neighbouring positions
- routes: int32 [4096, 1], P(('dp', 'expert')), may hold values from 0 to 15
- attn_gain: bfloat16 [768], replicated, may hold values from 0.099609375 to 1.8984375
- w_query: bfloat16 [768, 768], P('dp', 'expert'), may hold values from -0.21875 to 0.21875
- w_key: bfloat16 [768, 768], P('dp', 'expert'), may hold values from -0.21875 to 0.21875
- w_value: bfloat16 [768, 768], P('dp', 'expert'), may hold values from -0.21875 to 0.21875
- w_output: bfloat16 [768, 768], P('dp', 'expert'), may hold values from -1.25 to 1.25
- rel_bias: bfloat16 [32, 12], replicated, may hold values from -4 to 4
- ffn_gain: bfloat16 [768], replicated, may hold values from 0.099609375 to 1.8984375
- w_router: bfloat16 [768, 16], replicated, may hold values from -0.1796875 to 0.1796875
- w_in: bfloat16 [16, 768, 3072], P('expert', None, 'dp'), may hold values from -0.21875 to 0.21875
- w_out: bfloat16 [16, 3072, 768], P('expert', 'dp'), may hold values from -2.5 to 2.5
- d_out: bfloat16 [4096, 768], P(('dp', 'expert')), may hold values from -6 to 6
Outputs:
- output: bfloat16 [4096, 768], P(('dp', 'expert'))
- d_input: float32 [4096, 768], P(('dp', 'expert'))
- g_attn_gain: float32 [768], replicated
- g_query: float32 [768, 768], P('dp', 'expert')
- g_key: float32 [768, 768], P('dp', 'expert')
- g_value: float32 [768, 768], P('dp', 'expert')
- g_output: float32 [768, 768], P('dp', 'expert')
- g_rel_bias: float32 [32, 12], replicated
- g_ffn_gain: float32 [768], replicated
- g_router: float32 [768, 16], replicated
- g_in: float32 [16, 768, 3072], P('expert', None, 'dp')
- g_out: float32 [16, 3072, 768], P('expert', 'dp')
The draws below stay inside these ranges and needn't reach their ends.
Inputs may be any that keep to these rules, and one draw needn't show every extreme that they name: `seg_ids`: document numbers of one packed sequence, never falling, each document at most 96 tokens, and one document of every block exactly that long.
All inputs are finite; a program needn't handle non-finite values.
Results may differ from the reference program's by a relative error of at most 0.02.
Values may be sent and summed in bfloat16 or wider, within the bound.
No kernel may reach another device: no remote copies, remote signals or barrier semaphores. Data moves between devices by JAX's collectives and lax.ppermute only.
A program may use at most 128 MiB of HBM per device.

```python
import math
import jax
import jax.numpy as jnp
import numpy as np
from jax import lax

D = 768
H = 12
HEAD = 64
FF = 3072
BUCKETS = 32
TOK_DEV = 128
EXPERTS = 16
INNER = 768
GROUPS = 32
TOKENS = 4096


def shard_levels(stream_key, dims, shards, least, high):
    loudness, own = 1.0, jax.random.fold_in(stream_key, 6)
    for position, shards_of in shards:
        draws = jnp.exp(jax.random.uniform(jax.random.fold_in(own, position), (shards_of,), jnp.float32, least / len(shards), high / len(shards)))
        loudness = loudness * jnp.repeat(draws, dims[position] // shards_of).reshape([-1 if axis == position else 1 for axis in range(len(dims))])
    return loudness


def picks_of(own_key, rows, count, top, lift):
    sequence = jax.random.permutation(jax.random.fold_in(own_key, 1), count)
    pull = sequence
    for power in range(3):
        pull = pull * pull // count
    pull = pull * lift // count
    tickets = jax.random.randint(jax.random.fold_in(own_key, 2), (rows, count), 0, 4096) + pull
    fixed_rows = jax.random.permutation(jax.random.fold_in(own_key, 3), rows)[jnp.arange(count) % rows]
    tickets = jnp.where(jnp.arange(rows)[:, None] == fixed_rows[None, :], 1 << 14, tickets)
    merit = tickets * count + jnp.arange(count)
    return lax.top_k(merit.astype(jnp.int32), top)[1].astype(jnp.int32)


def split_up(count, total, reach, slope):
    portions = [(1 << 20) // math.isqrt(grade ** slope) + 1 for grade in range(2, count + 1)]
    rest, counts = total - reach - (count - 1), [1] * (count - 1)
    while rest > 0:
        movable = [i for i in range(count - 1) if counts[i] < reach]
        mass, remaining = sum([portions[i] for i in movable]), rest
        for i in movable:
            more = min(reach - counts[i], max(1, remaining * portions[i] // mass), rest)
            counts[i] = counts[i] + more
            rest = rest - more
    return np.array([reach] + counts)


def ragged(key, amount, total, limit, slope):
    if amount == 2:
        one = jax.random.randint(key, (), max(1, total - limit), min(limit, total - 1) + 1)
        return jnp.stack([one, total - one])
    sizes = jnp.asarray(split_up(amount, total, limit, slope), jnp.int32)
    twos = (amount - 1) // 2
    source_of, sink = sizes[1:1 + 2 * twos:2], sizes[2:2 + 2 * twos:2]
    slack = jnp.minimum(source_of - 1, limit - sink)
    moved = jax.random.randint(jax.random.fold_in(key, 1), (twos,), 0, 1 << 20) % (slack + 1)
    sizes = sizes.at[1:1 + 2 * twos:2].set(source_of - moved).at[2:2 + 2 * twos:2].set(sink + moved)
    return sizes[jax.random.permutation(jax.random.fold_in(key, 2), amount)]


def normal_values(key, shape, spread, most, split=(), held_as=jnp.bfloat16):
    drawn = jax.random.normal(key, shape, jnp.float32) * spread
    if len(split) > 0:
        drawn = shard_levels(key, shape, split, -0.22, 0.18) * drawn
    return jnp.clip(drawn, min=-most, max=most).astype(held_as)


def setup_inputs(seed: int = 0) -> dict:
    splits = jax.random.split(jax.random.key(seed), 15)
    return {
        "tokens": normal_values(splits[0], (TOKENS, D), 1.0, 6.0, ((0, 32),)),
        "seg_ids": jax.vmap(lambda own: jnp.searchsorted(jnp.cumsum(ragged(own, 4, TOK_DEV, (3 * TOK_DEV) // 4, 2)), jnp.arange(TOK_DEV), side="right"))(jax.random.split(splits[1], GROUPS)).reshape((GROUPS, TOK_DEV)).astype(jnp.int32),
        "routes": picks_of(splits[2], TOKENS, EXPERTS, 1, 512),
        "attn_gain": jnp.clip(1.0 + 0.18 * jax.random.normal(splits[3], (D,), jnp.float32), 0.099609375, 1.8984375).astype(jnp.bfloat16),
        "w_query": normal_values(splits[4], (D, INNER), D ** -0.5, 0.21875, ((0, 4), (1, 8))),
        "w_key": normal_values(splits[5], (D, INNER), D ** -0.5, 0.21875, ((0, 4), (1, 8))),
        "w_value": normal_values(splits[6], (D, INNER), D ** -0.5, 0.21875, ((0, 4), (1, 8))),
        "w_output": normal_values(splits[7], (INNER, D), (INNER // 32) ** -0.5, 1.25, ((0, 4), (1, 8))),
        "rel_bias": normal_values(splits[8], (BUCKETS, H), 1.0, 4.0),
        "ffn_gain": jnp.clip(1.0 + 0.18 * jax.random.normal(splits[9], (D,), jnp.float32), 0.099609375, 1.8984375).astype(jnp.bfloat16),
        "w_router": normal_values(splits[10], (D, EXPERTS), 0.03, 0.1796875),
        "w_in": normal_values(splits[11], (EXPERTS, D, FF), D ** -0.5, 0.21875, ((0, 8), (2, 4))),
        "w_out": normal_values(splits[12], (EXPERTS, FF, D), (EXPERTS / 35), 2.5, ((0, 8), (1, 4))),
        "d_out": normal_values(splits[13], (TOKENS, D), 1.0, 6.0, ((0, 32),)),
    }


EPSILON = 1e-06
LIMITS = (12, 16, 23, 32, 46, 64, 91)
MASKED = -1000000000.0
HIGHEST = lax.Precision.HIGHEST

@jax.custom_vjp
def low(v):
    return lax.optimization_barrier(v.astype(jnp.bfloat16)).astype(jnp.float32)

@jax.custom_vjp
def low_back(v):
    return v

def low_keep(v):
    return (low(v), None)

def low_pass(kept, grad):
    return (grad,)

def back_keep(v):
    return (v, None)

def back_low(kept, grad):
    return (low(grad),)
low.defvjp(low_keep, low_pass)
low_back.defvjp(back_keep, back_low)

def rounded_both(values):
    return low(low_back(values))

def matmul(left, right):
    return jnp.dot(left, right, precision=HIGHEST)

def bucket_table(length):
    spots = jnp.arange(length, dtype=jnp.int32)
    delta = spots[None, :] - spots[:, None]
    magnitude = jnp.abs(delta)
    distant = jnp.full_like(magnitude, 8)
    for threshold in LIMITS:
        distant = distant + (magnitude >= threshold).astype(jnp.int32)
    return jnp.where(delta > 0, 16, 0).astype(jnp.int32) + jnp.where(magnitude < 8, magnitude, distant)

def rms_scale(matrix):
    return lax.rsqrt(lax.optimization_barrier(jnp.mean(matrix * matrix, axis=-1, keepdims=True)) + EPSILON)

def reference(tokens, seg_ids, routes, attn_gain, w_query, w_key, w_value, w_output, rel_bias, ffn_gain, w_router, w_in, w_out, d_out):
    groups = tokens.shape[0] // TOK_DEV
    slots_each = TOK_DEV * 5 // (4 * EXPERTS)
    route_block = routes[:, 0].reshape(groups, TOK_DEV)
    expert_ids = jnp.arange(EXPERTS, dtype=jnp.int32)
    route_hits = (route_block[:, :, None] == expert_ids[None, None, :]).astype(jnp.int32)
    placed = lax.optimization_barrier(jnp.sum(jnp.cumsum(route_hits, axis=1) * route_hits, axis=2)) - 1
    kept = placed < slots_each
    slot_index = jnp.where(kept, route_block * slots_each + placed, EXPERTS * slots_each).astype(jnp.int32)
    token_ids = jnp.broadcast_to(jnp.arange(TOK_DEV, dtype=jnp.int32)[None, :], (groups, TOK_DEV))
    owners = jnp.full((groups, EXPERTS * slots_each + 1), TOK_DEV, dtype=jnp.int32)
    owners = owners.at[jnp.arange(groups, dtype=jnp.int32)[:, None], slot_index].set(token_ids)[:, :EXPERTS * slots_each]
    reader = jnp.minimum(slot_index, EXPERTS * slots_each - 1)
    hits_float = route_hits.astype(jnp.float32)
    kept_float = kept.astype(jnp.float32)
    bucket_ids = bucket_table(TOK_DEV)
    onehot_buckets = (bucket_ids[:, :, None] == jnp.arange(BUCKETS, dtype=jnp.int32)[None, None, :]).astype(jnp.float32)
    factor = HEAD ** (-0.5)

    def forward(inputs, gain_one, query_w, key_w, value_w, output_w, bias_table, gain_two, router_w, first_w, second_w):
        scale_one = rms_scale(inputs)
        normed_one = low(inputs * scale_one * gain_one)
        query_rows = rounded_both(matmul(normed_one, query_w)).reshape(groups, TOK_DEV, H, HEAD)
        key_rows = rounded_both(matmul(normed_one, key_w)).reshape(groups, TOK_DEV, H, HEAD)
        value_rows = rounded_both(matmul(normed_one, value_w)).reshape(groups, TOK_DEV, H, HEAD)
        bias_full = jnp.einsum('ijb,bh->hij', onehot_buckets, bias_table, precision=HIGHEST)

        def attend_block(operands):
            query_block, key_block, value_block, segment_block = operands
            scores = jnp.einsum('ihd,jhd->hij', query_block, key_block, precision=HIGHEST) * factor + bias_full
            scores = low_back(scores)
            same_doc = segment_block[:, None] == segment_block[None, :]
            scores = jnp.where(same_doc[None, :, :], scores, MASKED)
            probs = low(jax.nn.softmax(scores, axis=-1))
            return jnp.einsum('hij,jhd->ihd', probs, value_block, precision=HIGHEST).reshape(TOK_DEV, INNER)
        attended = lax.map(jax.checkpoint(attend_block), (query_rows, key_rows, value_rows, seg_ids))
        attended = rounded_both(attended.reshape(groups * TOK_DEV, INNER))
        hidden = inputs + low_back(matmul(attended, output_w))
        scale_two = rms_scale(hidden)
        normed_two = hidden * scale_two * gain_two
        chance = jax.nn.softmax(matmul(normed_two, router_w), axis=-1)
        gate_value = lax.optimization_barrier(jnp.sum(chance.reshape(groups, TOK_DEV, EXPERTS) * hits_float, axis=2))
        sent = rounded_both(normed_two).reshape(groups, TOK_DEV, D)
        padded = jnp.concatenate([sent, jnp.zeros((groups, 1, D), jnp.float32)], axis=1)
        buffer = jnp.take_along_axis(padded, owners[:, :, None], axis=1)
        buffer = buffer.reshape(groups, EXPERTS, slots_each, D).transpose(1, 0, 2, 3).reshape(EXPERTS, groups * slots_each, D)

        def expert_block(operands):
            slot_rows, first_one, second_one = operands
            pre_act = low_back(matmul(slot_rows, first_one))
            activated = low(jax.nn.gelu(pre_act, approximate=True))
            return rounded_both(matmul(activated, second_one))
        returned = lax.map(jax.checkpoint(expert_block), (buffer, first_w, second_w))
        returned = returned.reshape(EXPERTS, groups, slots_each, D).transpose(1, 0, 2, 3).reshape(groups, EXPERTS * slots_each, D)
        fetched = jnp.take_along_axis(returned, reader[:, :, None], axis=1)
        mixture = fetched * (gate_value * kept_float)[:, :, None]
        return hidden + mixture.reshape(groups * TOK_DEV, D)
    result, pullback = jax.vjp(forward, tokens.astype(jnp.float32), attn_gain.astype(jnp.float32), w_query.astype(jnp.float32), w_key.astype(jnp.float32), w_value.astype(jnp.float32), w_output.astype(jnp.float32), rel_bias.astype(jnp.float32), ffn_gain.astype(jnp.float32), w_router.astype(jnp.float32), w_in.astype(jnp.float32), w_out.astype(jnp.float32))
    grads = pullback(d_out.astype(jnp.float32))
    return (result.astype(jnp.bfloat16), grads[0], grads[1], grads[2], grads[3], grads[4], grads[5], grads[6], grads[7], grads[8], grads[9], grads[10])
```

```python
import jax
import jax.numpy as jnp
from jax import lax
from jax.sharding import PartitionSpec as P

EPSILON = 1e-06
LIMITS = (12, 16, 23, 32, 46, 64, 91)
MASKED = -1000000000.0
HIGHEST = lax.Precision.HIGHEST
LOW = jnp.bfloat16
FULL = jnp.float32


def bucket_table(length):
    spots = jnp.arange(length, dtype=jnp.int32)
    delta = spots[None, :] - spots[:, None]
    magnitude = jnp.abs(delta)
    distant = jnp.full_like(magnitude, 8)
    for threshold in LIMITS:
        distant = distant + (magnitude >= threshold).astype(jnp.int32)
    return jnp.where(delta > 0, 16, 0).astype(jnp.int32) + jnp.where(
        magnitude < 8, magnitude, distant
    )


def normalize(matrix, gain_vec):
    scale = lax.rsqrt(jnp.mean(matrix * matrix, axis=-1, keepdims=True) + EPSILON)
    return (matrix * scale * gain_vec, scale)


def norm_back(matrix, scale, gain_vec, incoming):
    weighted = incoming * gain_vec
    average = jnp.mean(matrix * weighted, axis=-1, keepdims=True)
    return (
        scale * weighted - matrix * (scale * scale * scale) * average,
        jnp.sum(incoming * matrix * scale, axis=0),
    )


def contract_rows(left, right, precision=None):
    return lax.dot_general(
        left, right, (((0,), (0,)), ((), ())), precision=precision, preferred_element_type=FULL
    )


def contract_cols(left, right, precision=None):
    return lax.dot_general(
        left, right, (((1,), (1,)), ((), ())), precision=precision, preferred_element_type=FULL
    )


def smooth(values):
    return jax.nn.gelu(values, approximate=True)


def swap(value, axis, mask):
    count = lax.axis_size(axis)
    return lax.ppermute(value, axis, [(i, i ^ mask) for i in range(count)])


def gather_bits(value, axis, masks):
    return jnp.concatenate([value] + [swap(value, axis, mask) for mask in masks], axis=0)


def absolute(stacked, position):
    count = stacked.shape[0]
    return jnp.concatenate(
        [lax.dynamic_index_in_dim(stacked, position ^ j, 0, keepdims=True) for j in range(count)],
        axis=0,
    )


def scatter_sum(stacked, axis):
    bit = 1
    while stacked.shape[0] > 1:
        pairs = stacked.reshape((stacked.shape[0] // 2, 2) + stacked.shape[1:])
        taken = swap(pairs[:, 1], axis, bit)
        stacked = (pairs[:, 0].astype(FULL) + taken.astype(FULL)).astype(stacked.dtype)
        bit = bit * 2
    return stacked[0]


def gather_rel(value, axis):
    count = lax.axis_size(axis)
    stacked = value[None]
    bit = count // 2
    parts = []
    while bit >= 1:
        other = swap(stacked, axis, bit)
        stacked = jnp.concatenate([stacked, other], axis=0)
        parts.append(bit)
        bit = bit // 2
    bits = len(parts)
    stacked = stacked.reshape((2,) * bits + value.shape)
    stacked = stacked.transpose(tuple(reversed(range(bits))) + tuple(range(bits, stacked.ndim)))
    return stacked.reshape((count,) + value.shape)


def gather_weights(payload):
    ranks, dps = lax.axis_size("expert"), lax.axis_size("dp")
    half = payload.shape[0] // 2
    low_masks = list(range(2, ranks, 2))
    high_dp = list(range(2, dps, 2))
    halves = []
    for part, order in ((payload[:half], "xy"), (payload[half:], "yx")):
        value = part[None]
        value = gather_bits(value, "expert", low_masks)
        for letter in order:
            if letter == "x":
                value = gather_bits(value[None], "expert", [1])
            else:
                value = gather_bits(value[None], "dp", high_dp)
        value = gather_bits(value[None], "dp", [1])
        if order == "xy":
            value = value.transpose(3, 2, 1, 0, 4, 5)
        else:
            value = value.transpose(3, 1, 2, 0, 4, 5)
        halves.append(value.reshape((ranks, dps) + part.shape))
    stacked = jnp.concatenate(halves, axis=2)
    stacked = absolute(stacked, lax.axis_index("expert"))
    stacked = absolute(jnp.swapaxes(stacked, 0, 1), lax.axis_index("dp"))
    return jnp.swapaxes(stacked, 0, 1)


def per_device(
    tokens,
    seg_ids,
    routes,
    attn_gain,
    w_query,
    w_key,
    w_value,
    w_output,
    rel_bias,
    ffn_gain,
    w_router,
    w_in,
    w_out,
    d_out,
):
    inputs = tokens.astype(FULL)
    length, model_width = inputs.shape
    bucket_count, head_count = rel_bias.shape
    experts_total = w_router.shape[1]
    local_experts = w_in.shape[0]
    ranks, dps = lax.axis_size("expert"), lax.axis_size("dp")
    capacity = length * 5 // (4 * experts_total)
    slot_total = experts_total * capacity
    rank_slots = local_experts * capacity
    blocks = ranks * dps

    route_hits = (routes == jnp.arange(experts_total, dtype=jnp.int32)[None, :]).astype(jnp.int32)
    placed = jnp.sum(jnp.cumsum(route_hits, axis=0) * route_hits, axis=1) - 1
    slot_index = jnp.where(placed < capacity, routes[:, 0] * capacity + placed, slot_total)
    slot_mask = (slot_index[:, None] == jnp.arange(slot_total, dtype=jnp.int32)[None, :]).astype(
        LOW
    )
    hits_float = route_hits.astype(FULL)

    payload = jnp.concatenate([w_query, w_key, w_value, w_output], axis=1)
    rows_here, columns_here = w_query.shape
    weights_all = gather_weights(payload)
    weights_all = weights_all.reshape(ranks, dps * rows_here, 4, columns_here)
    full_w = weights_all.transpose(2, 1, 0, 3).reshape(4, dps * rows_here, ranks * columns_here)
    query_w, key_w, value_w, output_w = full_w[0], full_w[1], full_w[2], full_w[3]

    upstream = d_out.astype(FULL)
    up_out = contract_rows(slot_mask, d_out).astype(LOW).reshape(ranks, rank_slots, model_width)
    up_arrived = lax.all_to_all(up_out, "expert", split_axis=0, concat_axis=0, tiled=True)
    up_rows = gather_rel(up_arrived, "dp").reshape(blocks, local_experts, capacity, model_width)
    up_act = jnp.einsum("secd,efd->secf", up_rows, w_out, preferred_element_type=FULL)

    inner_width = query_w.shape[1]
    head_size = inner_width // head_count
    factor = head_size ** (-0.5)
    gain_one = attn_gain.astype(FULL)
    normed_one, scale_one = normalize(inputs, gain_one)
    normed_low = normed_one.astype(LOW)
    normed_all = lax.all_gather(normed_low, "expert", axis=0, tiled=True)
    query_rows = jnp.dot(normed_low, query_w, preferred_element_type=FULL).astype(LOW)
    key_rows = jnp.dot(normed_low, key_w, preferred_element_type=FULL).astype(LOW)
    value_rows = jnp.dot(normed_low, value_w, preferred_element_type=FULL).astype(LOW)
    query_heads = query_rows.reshape(length, head_count, head_size)
    key_heads = key_rows.reshape(length, head_count, head_size)
    value_heads = value_rows.reshape(length, head_count, head_size)
    bucket_ids = bucket_table(length)
    onehot_buckets = (
        bucket_ids[:, :, None] == jnp.arange(bucket_count, dtype=jnp.int32)[None, None, :]
    ).astype(LOW)
    bias_full = jnp.einsum("ijb,bh->hij", onehot_buckets, rel_bias, preferred_element_type=FULL)
    segment_row = seg_ids[0]
    same_doc = (segment_row[:, None] == segment_row[None, :])[None, :, :]
    scores = (
        jnp.einsum("ihd,jhd->hij", query_heads, key_heads, preferred_element_type=FULL) * factor
        + bias_full
    )
    weights = jax.nn.softmax(jnp.where(same_doc, scores, MASKED), axis=-1)
    weights_low = weights.astype(LOW)
    attended = jnp.einsum("hij,jhd->ihd", weights_low, value_heads, preferred_element_type=FULL)
    attended = attended.reshape(length, inner_width).astype(LOW)
    attended_all = lax.all_gather(attended, "expert", axis=0, tiled=True)
    hidden = inputs + jnp.dot(attended, output_w, preferred_element_type=FULL)
    gain_two = ffn_gain.astype(FULL)
    normed_two, scale_two = normalize(hidden, gain_two)
    router_w = w_router.astype(FULL)
    chance = jax.nn.softmax(jnp.dot(normed_two, router_w, precision=HIGHEST), axis=-1)
    gate_value = jnp.sum(chance * hits_float, axis=1)

    outgoing = contract_rows(slot_mask, normed_two.astype(LOW)).astype(LOW)
    gate_slots = jnp.sum(slot_mask.astype(FULL) * gate_value[:, None], axis=0)
    gate_slots = gate_slots.reshape(ranks, 1, rank_slots)
    gate_high = gate_slots.astype(LOW)
    gate_low = (gate_slots - gate_high.astype(FULL)).astype(LOW)
    gate_row = jnp.concatenate(
        [gate_high, gate_low, jnp.zeros((ranks, 1, model_width - 2 * rank_slots), LOW)], axis=2
    )
    outgoing = jnp.concatenate(
        [outgoing.reshape(ranks, rank_slots, model_width), gate_row], axis=1
    )
    arrived = lax.all_to_all(outgoing, "expert", split_axis=0, concat_axis=0, tiled=True)
    gathered = gather_rel(arrived, "dp").reshape(blocks, rank_slots + 1, model_width)
    slot_rows = gathered[:, :rank_slots].reshape(blocks, local_experts, capacity, model_width)
    gate_rows = gathered[:, rank_slots, :rank_slots].astype(FULL) + gathered[
        :, rank_slots, rank_slots : 2 * rank_slots
    ].astype(FULL)
    gate_rows = gate_rows.reshape(blocks, local_experts, capacity, 1)

    pre_act = jnp.einsum("secd,edf->secf", slot_rows, w_in, preferred_element_type=FULL)
    activated_f, gelu_back = jax.vjp(smooth, pre_act)
    activated = activated_f.astype(LOW)
    gate_part = jnp.sum(activated.astype(FULL) * up_act, axis=3)
    pre_grad = gelu_back(up_act * gate_rows)[0].astype(LOW)
    input_part = jnp.einsum("secf,edf->secd", pre_grad, w_in, preferred_element_type=FULL)
    gate_part = gate_part.reshape(blocks, 1, rank_slots).astype(LOW)
    gate_part = jnp.pad(gate_part, ((0, 0), (0, 0), (0, model_width - rank_slots)))
    back = jnp.concatenate(
        [input_part.astype(LOW).reshape(blocks, rank_slots, model_width), gate_part], axis=1
    )
    back = scatter_sum(back.reshape(dps, ranks, rank_slots + 1, model_width), "dp")
    dispatch_back = lax.all_to_all(back, "expert", split_axis=0, concat_axis=0, tiled=True)

    partial_out = jnp.einsum("secf,efd->secd", activated, w_out, preferred_element_type=FULL)
    returned = scatter_sum(
        partial_out.astype(LOW).reshape(dps, ranks, rank_slots, model_width), "dp"
    )
    back_rows = lax.all_to_all(returned, "expert", split_axis=0, concat_axis=0, tiled=True)
    first_grad = jnp.einsum("secd,secf->edf", slot_rows, pre_grad, preferred_element_type=FULL)
    grad_rows = (up_rows.astype(FULL) * gate_rows).astype(LOW)
    second_grad = jnp.einsum("secf,secd->efd", activated, grad_rows, preferred_element_type=FULL)

    fetched = jnp.dot(
        slot_mask, back_rows.reshape(slot_total, model_width), preferred_element_type=FULL
    )
    output = (hidden + gate_value[:, None] * fetched).astype(LOW)

    gate_slots_grad = dispatch_back[:, rank_slots, :rank_slots].astype(FULL).reshape(1, slot_total)
    gate_grad = jnp.sum(slot_mask.astype(FULL) * gate_slots_grad, axis=1)
    logit_grad = chance * (hits_float - gate_value[:, None]) * gate_grad[:, None]
    router_grad = contract_rows(normed_two, logit_grad, HIGHEST)
    normed_two_grad = contract_cols(logit_grad, router_w, HIGHEST)
    normed_two_grad = normed_two_grad + jnp.dot(
        slot_mask,
        dispatch_back[:, :rank_slots].reshape(slot_total, model_width),
        preferred_element_type=FULL,
    )
    hidden_part, ffn_gain_grad = norm_back(hidden, scale_two, gain_two, normed_two_grad)
    g_ffn_gain, g_router = lax.psum((ffn_gain_grad, router_grad), ("dp", "expert"))
    hidden_grad = upstream + hidden_part
    branch_grad = hidden_grad.astype(LOW)
    attended_grad = (
        contract_cols(branch_grad, output_w).astype(LOW).reshape(length, head_count, head_size)
    )
    value_grad = jnp.einsum("hij,ihd->jhd", weights_low, attended_grad, preferred_element_type=FULL)
    value_grad = value_grad.reshape(length, inner_width).astype(LOW)
    prob_grad = jnp.einsum("ihd,jhd->hij", attended_grad, value_heads, preferred_element_type=FULL)
    score_grad = (
        weights * (prob_grad - jnp.sum(prob_grad * weights, axis=-1, keepdims=True))
    ).astype(LOW)
    query_grad = (
        jnp.einsum("hij,jhd->ihd", score_grad, key_heads, preferred_element_type=FULL) * factor
    )
    query_grad = query_grad.reshape(length, inner_width).astype(LOW)
    key_grad = (
        jnp.einsum("hij,ihd->jhd", score_grad, query_heads, preferred_element_type=FULL) * factor
    )
    key_grad = key_grad.reshape(length, inner_width).astype(LOW)
    bias_grad = jnp.einsum("hij,ijb->bh", score_grad, onehot_buckets, preferred_element_type=FULL)

    factors = jnp.concatenate(
        [
            item.reshape(length, ranks, columns_here).transpose(1, 2, 0)
            for item in (query_grad, key_grad, value_grad, branch_grad)
        ],
        axis=1,
    )
    factors = lax.all_to_all(factors, "expert", split_axis=0, concat_axis=0, tiled=True)
    factors = factors.transpose(0, 2, 1).reshape(ranks * length, 4 * columns_here)
    grads_qkv = contract_rows(normed_all, factors[:, : 3 * columns_here])
    grads_out = contract_rows(attended_all, factors[:, 3 * columns_here :])
    grads = jnp.concatenate([grads_qkv, grads_out], axis=1).astype(LOW)
    grads = grads.reshape(dps, rows_here, 4 * columns_here)
    grads = scatter_sum(absolute(grads, lax.axis_index("dp")), "dp").astype(FULL)
    g_query, g_key, g_value, g_output = (
        grads[:, i * columns_here : (i + 1) * columns_here] for i in range(4)
    )

    normed_one_grad = (
        contract_cols(query_grad, query_w)
        + contract_cols(key_grad, key_w)
        + contract_cols(value_grad, value_w)
    )
    input_norm_grad, attn_gain_grad = norm_back(inputs, scale_one, gain_one, normed_one_grad)
    d_input = hidden_grad + input_norm_grad
    g_attn_gain, g_rel_bias = lax.psum((attn_gain_grad, bias_grad), ("dp", "expert"))
    return (
        output,
        d_input,
        g_attn_gain,
        g_query,
        g_key,
        g_value,
        g_output,
        g_rel_bias,
        g_ffn_gain,
        g_router,
        first_grad,
        second_grad,
    )


def solution(mesh):
    return jax.shard_map(
        per_device,
        mesh=mesh,
        in_specs=(
            P(("dp", "expert"), None),
            P(("dp", "expert"), None),
            P(("dp", "expert"), None),
            P(),
            P("dp", "expert"),
            P("dp", "expert"),
            P("dp", "expert"),
            P("dp", "expert"),
            P(),
            P(),
            P(),
            P("expert", None, "dp"),
            P("expert", "dp", None),
            P(("dp", "expert"), None),
        ),
        out_specs=(
            P(("dp", "expert"), None),
            P(("dp", "expert"), None),
            P(),
            P("dp", "expert"),
            P("dp", "expert"),
            P("dp", "expert"),
            P("dp", "expert"),
            P(),
            P(),
            P(),
            P("expert", None, "dp"),
            P("expert", "dp", None),
        ),
        check_vma=False,
    )
```

```python
import functools

import jax
import jax.numpy as jnp
from jax import lax
from jax.experimental import pallas as pl
from jax.experimental.pallas import tpu as pltpu
from jax.sharding import PartitionSpec as P

EPSILON = 1e-06
LIMITS = (12, 16, 23, 32, 46, 64, 91)
MASKED = -1000000000.0
HIGHEST = lax.Precision.HIGHEST
LOW = jnp.bfloat16
FULL = jnp.float32


def bucket_table(length):
    spots = jnp.arange(length, dtype=jnp.int32)
    delta = spots[None, :] - spots[:, None]
    magnitude = jnp.abs(delta)
    distant = jnp.full_like(magnitude, 8)
    for threshold in LIMITS:
        distant = distant + (magnitude >= threshold).astype(jnp.int32)
    return jnp.where(delta > 0, 16, 0).astype(jnp.int32) + jnp.where(
        magnitude < 8, magnitude, distant
    )


def normalize(matrix, gain_vec):
    scale = lax.rsqrt(jnp.mean(matrix * matrix, axis=-1, keepdims=True) + EPSILON)
    return (matrix * scale * gain_vec, scale)


def norm_back(matrix, scale, gain_vec, incoming):
    weighted = incoming * gain_vec
    average = jnp.mean(matrix * weighted, axis=-1, keepdims=True)
    return (
        scale * weighted - matrix * (scale * scale * scale) * average,
        jnp.sum(incoming * matrix * scale, axis=0),
    )


def contract_rows(left, right, precision=None):
    return lax.dot_general(
        left, right, (((0,), (0,)), ((), ())), precision=precision, preferred_element_type=FULL
    )


def contract_cols(left, right, precision=None):
    return lax.dot_general(
        left, right, (((1,), (1,)), ((), ())), precision=precision, preferred_element_type=FULL
    )


def smooth(values):
    return jax.nn.gelu(values, approximate=True)


def swap(value, axis, mask):
    count = lax.axis_size(axis)
    return lax.ppermute(value, axis, [(i, i ^ mask) for i in range(count)])


def gather_bits(value, axis, masks):
    return jnp.concatenate([value] + [swap(value, axis, mask) for mask in masks], axis=0)


def absolute(stacked, position):
    count = stacked.shape[0]
    return jnp.concatenate(
        [lax.dynamic_index_in_dim(stacked, position ^ j, 0, keepdims=True) for j in range(count)],
        axis=0,
    )


def scatter_sum(stacked, axis):
    bit = 1
    while stacked.shape[0] > 1:
        pairs = stacked.reshape((stacked.shape[0] // 2, 2) + stacked.shape[1:])
        taken = swap(pairs[:, 1], axis, bit)
        stacked = (pairs[:, 0].astype(FULL) + taken.astype(FULL)).astype(stacked.dtype)
        bit = bit * 2
    return stacked[0]


def gather_rel(value, axis):
    count = lax.axis_size(axis)
    stacked = value[None]
    bit = count // 2
    parts = []
    while bit >= 1:
        other = swap(stacked, axis, bit)
        stacked = jnp.concatenate([stacked, other], axis=0)
        parts.append(bit)
        bit = bit // 2
    bits = len(parts)
    stacked = stacked.reshape((2,) * bits + value.shape)
    stacked = stacked.transpose(tuple(reversed(range(bits))) + tuple(range(bits, stacked.ndim)))
    return stacked.reshape((count,) + value.shape)


def all_sum(value):
    for axis in ("dp", "expert"):
        bit = 1
        while bit < lax.axis_size(axis):
            value = value + swap(value, axis, bit)
            bit = bit * 2
    return value


def gather_pieces(payload):
    ranks, dps = lax.axis_size("expert"), lax.axis_size("dp")
    half = payload.shape[0] // 2
    far = list(range(0, ranks, 2))
    sides = {"x": ("expert", [0, 1]), "y": ("dp", list(range(0, dps, 2)))}
    pieces, places = [], []
    for index, order in enumerate(("xy", "yx")):
        value = payload[index * half : (index + 1) * half][None]
        value = gather_bits(value, "expert", far[1:])
        axis, masks = sides[order[0]]
        value = gather_bits(value[None], axis, masks[1:])
        other_axis, other_masks = sides[order[1]]
        found = [(value, 0)] + [(swap(value, other_axis, m), m) for m in other_masks[1:]]
        found = [(v, m, 0) for v, m in found] + [(swap(v, "dp", 1), m, 1) for v, m in found]
        for piece, mask, core in found:
            offsets = []
            for first in masks:
                for low in far:
                    x_mask, y_mask = (first, mask) if order == "xy" else (mask, first)
                    offsets.append((low ^ x_mask, y_mask ^ core))
            pieces.append(piece)
            places.append((index, offsets))
    return pieces, places


def place_weights(places, piece_refs, w_ref, sem):
    my_expert, my_dp = lax.axis_index("expert"), lax.axis_index("dp")
    copies = []
    for ref, (half, offsets) in zip(piece_refs, places):
        low_count, rows = ref.shape[1], ref.shape[2]
        for index, (e_mask, d_mask) in enumerate(offsets):
            start = (my_dp ^ d_mask) * (2 * rows) + half * rows
            copies.append(
                pltpu.make_async_copy(
                    ref.at[index // low_count, index % low_count],
                    w_ref.at[my_expert ^ e_mask, pl.ds(pl.multiple_of(start, 16), rows), :],
                    sem,
                )
            )
    for copy in copies:
        copy.start()
    return copies


def dot(left, right, dims=((1,), (0,)), precision=None):
    return lax.dot_general(
        left, right, (dims, ((), ())), precision=precision, preferred_element_type=FULL
    )


NT = ((1,), (1,))
TN = ((0,), (0,))


def forward_kernel(
    places, slab, rank_slots, tokens_ref, normed_ref, seg_col_ref, seg_row_ref, bias_ref, gain_ref,
    router_ref, hits_ref, mask_t_ref, *rest
):
    count = len(places)
    piece_refs, rest = rest[:count], rest[count:]
    (heads_ref, weights_ref, attended_ref, hidden_ref, chance_ref, slabs_ref,
     w_ref, qkv_ref, att_t_ref, sem) = rest
    copies = place_weights(places, piece_refs, w_ref, sem)
    ranks, width, columns = w_ref.shape
    cols = columns // 4
    head_count = weights_ref.shape[0]
    head = width // head_count
    same_doc = seg_col_ref[...] == seg_row_ref[...]
    normed = normed_ref[...]
    for copy in copies:
        copy.wait()
    for e in range(ranks):
        turned = dot(normed, w_ref[e]).T
        for m in range(3):
            qkv_ref[m, e * cols : (e + 1) * cols, :] = turned[m * cols : (m + 1) * cols]
    heads_ref[...] = qkv_ref[...].astype(LOW)
    for h in range(head_count):
        rows = slice(h * head, (h + 1) * head)
        scores = dot(heads_ref[0, rows, :], heads_ref[1, rows, :], TN) * head ** (-0.5)
        scores = jnp.where(same_doc, scores + bias_ref[h], MASKED)
        grown = jnp.exp(scores - jnp.max(scores, axis=1, keepdims=True))
        weights = grown / jnp.sum(grown, axis=1, keepdims=True)
        weights_ref[h] = weights
        att_t_ref[rows, :] = dot(heads_ref[2, rows, :], weights.astype(LOW), NT)
    attended = att_t_ref[...].T.astype(LOW)
    attended_ref[...] = attended
    low_lane = 3 * cols // 128 * 128
    for e in range(ranks):
        turned = dot(attended, w_ref[e, :, low_lane:]).T
        att_t_ref[e * cols : (e + 1) * cols, :] = turned[3 * cols - low_lane :]
    hidden = tokens_ref[...].astype(FULL) + att_t_ref[...].T
    hidden_ref[...] = hidden
    normed_two, _ = normalize(hidden, gain_ref[...].astype(FULL))
    logits = dot(normed_two, router_ref[...].astype(FULL), precision=HIGHEST)
    grown = jnp.exp(logits - jnp.max(logits, axis=1, keepdims=True))
    chance = grown / jnp.sum(grown, axis=1, keepdims=True)
    chance_ref[...] = chance
    gate = jnp.sum(chance * hits_ref[...], axis=1, keepdims=True)
    mask_t = mask_t_ref[...]
    slots = dot(mask_t, normed_two.astype(LOW))
    gates = dot(mask_t.astype(FULL), jnp.broadcast_to(gate, (gate.shape[0], 128)), precision=HIGHEST)
    sub = lax.broadcasted_iota(jnp.int32, (slab, 128), 0)
    lane = lax.broadcasted_iota(jnp.int32, (slab, 128), 1)
    for r in range(ranks):
        mine = gates[r * slab : (r + 1) * slab]
        high = mine.astype(LOW).astype(FULL)
        spread = jnp.where(lane == sub, high, 0.0) + jnp.where(lane == sub + 64, mine - high, 0.0)
        row = jnp.sum(spread, axis=0, keepdims=True)
        rows = slots[r * slab : (r + 1) * slab]
        start = rows[:, :128] + jnp.where(sub == rank_slots, row, 0.0)
        slabs_ref[r, :, :128] = start.astype(LOW)
        slabs_ref[r, :, 128:] = rows[:, 128:].astype(LOW)


def backward_kernel(
    places, rank_slots, tokens_ref, gain_one_ref, gain_two_ref, router_t_ref, hits_ref, mask_ref,
    back_ref, up_ref, hidden_ref, chance_ref, heads_ref, weights_ref, *rest
):
    count = len(places)
    piece_refs, rest = rest[:count], rest[count:]
    (d_input_ref, factors_ref, score_grad_ref, router_grad_ref, gains_ref,
     w_ref, turned_ref, grads_ref, sem) = rest
    copies = place_weights(places, piece_refs, w_ref, sem)
    ranks, width, columns = w_ref.shape
    cols = columns // 4
    head_count = weights_ref.shape[0]
    head = width // head_count
    factor = head ** (-0.5)
    slab = back_ref.shape[1]
    hidden = hidden_ref[...]
    gain_two = gain_two_ref[...].astype(FULL)
    normed_two, scale_two = normalize(hidden, gain_two)
    mask = mask_ref[...]
    chance, hits = chance_ref[...], hits_ref[...]
    gate = jnp.sum(chance * hits, axis=1, keepdims=True)
    back = back_ref[...].reshape(ranks * slab, width)
    sub = lax.broadcasted_iota(jnp.int32, (slab, 128), 0)
    lane = lax.broadcasted_iota(jnp.int32, (slab, 128), 1)
    spread = []
    for r in range(ranks):
        row = back_ref[r, :, :128].astype(FULL)[rank_slots : rank_slots + 1]
        column = jnp.sum(jnp.where(lane == sub, row, 0.0), axis=1, keepdims=True)
        spread.append(jnp.broadcast_to(column, (slab, 128)))
    spread = jnp.concatenate(spread, axis=0).astype(LOW)
    gate_grad = dot(mask, spread)[:, :1]
    logit_grad = chance * (hits - gate) * gate_grad
    router_grad_ref[...] = dot(logit_grad, normed_two, TN, HIGHEST)
    router_t = router_t_ref[...].astype(FULL)
    normed_two_grad = dot(logit_grad, router_t, precision=HIGHEST) + dot(mask, back)
    hidden_part, ffn_gain_grad = norm_back(hidden, scale_two, gain_two, normed_two_grad)
    hidden_grad = up_ref[...].astype(FULL) + hidden_part
    turned_ref[...] = hidden_grad.astype(LOW).astype(FULL).T
    for copy in copies:
        copy.wait()
    low_lane = 3 * cols // 128 * 128
    att_grad = None
    for e in range(ranks):
        own = turned_ref[e * cols : (e + 1) * cols, :]
        if 3 * cols > low_lane:
            own = jnp.concatenate([jnp.zeros((3 * cols - low_lane, 128), FULL), own], axis=0)
        part = dot(w_ref[e, :, low_lane:], own.astype(LOW))
        att_grad = part if att_grad is None else att_grad + part
    att_grad = att_grad.astype(LOW)
    for h in range(head_count):
        rows = slice(h * head, (h + 1) * head)
        own = att_grad[rows]
        weights = weights_ref[h]
        grads_ref[2, rows, :] = dot(own, weights.astype(LOW))
        prob_grad = dot(own, heads_ref[2, rows, :], TN)
        score_grad = weights * (prob_grad - jnp.sum(prob_grad * weights, axis=1, keepdims=True))
        score_grad = score_grad.astype(LOW)
        score_grad_ref[h] = score_grad
        grads_ref[0, rows, :] = dot(heads_ref[1, rows, :], score_grad, NT) * factor
        grads_ref[1, rows, :] = dot(heads_ref[0, rows, :], score_grad) * factor
    total = None
    for e in range(ranks):
        span = slice(e * cols, (e + 1) * cols)
        own = [grads_ref[m, span, :] for m in range(3)]
        factors_ref[e] = jnp.concatenate(own + [turned_ref[span, :]], axis=0).astype(LOW)
        held = jnp.concatenate(own + [jnp.zeros((cols, 128), FULL)], axis=0).astype(LOW)
        part = dot(w_ref[e], held)
        total = part if total is None else total + part
    inputs = tokens_ref[...].astype(FULL)
    gain_one = gain_one_ref[...].astype(FULL)
    _, scale_one = normalize(inputs, gain_one)
    norm_part, attn_gain_grad = norm_back(inputs, scale_one, gain_one, total.T)
    d_input_ref[...] = hidden_grad + norm_part
    gains_ref[0:1, :] = ffn_gain_grad.reshape(1, width)
    gains_ref[1:2, :] = attn_gain_grad.reshape(1, width)


VMEM = pl.BlockSpec(memory_space=pltpu.VMEM)
ANY = pl.BlockSpec(memory_space=pl.ANY)
LIMIT = 40 * 1024 * 1024


def shaped(dtype, *shape):
    return jax.ShapeDtypeStruct(shape, dtype)


def per_device(
    tokens,
    seg_ids,
    routes,
    attn_gain,
    w_query,
    w_key,
    w_value,
    w_output,
    rel_bias,
    ffn_gain,
    w_router,
    w_in,
    w_out,
    d_out,
):
    inputs = tokens.astype(FULL)
    length, model_width = inputs.shape
    bucket_count, head_count = rel_bias.shape
    experts_total = w_router.shape[1]
    local_experts = w_in.shape[0]
    ranks, dps = lax.axis_size("expert"), lax.axis_size("dp")
    capacity = length * 5 // (4 * experts_total)
    slot_total = experts_total * capacity
    rank_slots = local_experts * capacity
    blocks = ranks * dps

    slab = -(-(rank_slots + 1) // 8) * 8

    payload = jnp.concatenate([w_query, w_key, w_value, w_output], axis=1)
    rows_here, columns_here = w_query.shape
    pieces, places = gather_pieces(payload)

    route_hits = (routes == jnp.arange(experts_total, dtype=jnp.int32)[None, :]).astype(jnp.int32)
    placed = jnp.sum(jnp.cumsum(route_hits, axis=0) * route_hits, axis=1) - 1
    slot_index = jnp.where(placed < capacity, routes[:, 0] * capacity + placed, slot_total)
    slot_mask = (slot_index[:, None] == jnp.arange(slot_total, dtype=jnp.int32)[None, :]).astype(
        LOW
    )
    hits_float = route_hits.astype(FULL)
    slab_mask = jnp.pad(
        slot_mask.reshape(length, ranks, rank_slots), ((0, 0), (0, 0), (0, slab - rank_slots))
    ).reshape(length, ranks * slab)

    upstream = d_out.astype(FULL)
    up_out = contract_rows(slot_mask, d_out).astype(LOW).reshape(ranks, rank_slots, model_width)
    up_arrived = lax.all_to_all(up_out, "expert", split_axis=0, concat_axis=0, tiled=True)
    up_rows = gather_rel(up_arrived, "dp").reshape(blocks, local_experts, capacity, model_width)
    up_act = jnp.einsum("secd,efd->secf", up_rows, w_out, preferred_element_type=FULL)

    inner_width = dps * rows_here
    gain_one = attn_gain.astype(FULL)
    normed_low = normalize(inputs, gain_one)[0].astype(LOW)
    normed_all = lax.all_gather(normed_low, "expert", axis=0, tiled=True)
    bucket_ids = bucket_table(length)
    onehot_buckets = (
        bucket_ids[:, :, None] == jnp.arange(bucket_count, dtype=jnp.int32)[None, None, :]
    ).astype(LOW)
    bias_full = jnp.einsum("ijb,bh->hij", onehot_buckets, rel_bias, preferred_element_type=FULL)
    w_shape = (ranks, inner_width, 4 * columns_here)
    heads, weights, attended, hidden, chance, outgoing = pl.pallas_call(
        functools.partial(forward_kernel, places, slab, rank_slots),
        out_shape=(
            shaped(LOW, 3, inner_width, length),
            shaped(FULL, head_count, length, length),
            shaped(LOW, length, inner_width),
            shaped(FULL, length, model_width),
            shaped(FULL, length, experts_total),
            shaped(LOW, ranks, slab, model_width),
        ),
        in_specs=[VMEM] * 9 + [ANY] * len(pieces),
        out_specs=(VMEM,) * 6,
        scratch_shapes=[
            pltpu.VMEM(w_shape, LOW),
            pltpu.VMEM((3, inner_width, length), FULL),
            pltpu.VMEM((inner_width, length), FULL),
            pltpu.SemaphoreType.DMA,
        ],
        compiler_params=pltpu.CompilerParams(vmem_limit_bytes=LIMIT),
        name="attention_forward",
    )(
        tokens,
        normed_low,
        seg_ids.reshape(length, 1),
        seg_ids,
        bias_full,
        ffn_gain.reshape(1, model_width),
        w_router,
        hits_float,
        slab_mask.T,
        *pieces,
    )
    attended_all = lax.all_gather(attended, "expert", axis=0, tiled=True)
    gate_value = jnp.sum(chance * hits_float, axis=1)

    arrived = lax.all_to_all(outgoing, "expert", split_axis=0, concat_axis=0, tiled=True)
    gathered = gather_rel(arrived, "dp").reshape(blocks, slab, model_width)
    slot_rows = gathered[:, :rank_slots].reshape(blocks, local_experts, capacity, model_width)
    gate_rows = gathered[:, rank_slots, :rank_slots].astype(FULL) + gathered[
        :, rank_slots, 64 : 64 + rank_slots
    ].astype(FULL)
    gate_rows = gate_rows.reshape(blocks, local_experts, capacity, 1)

    pre_act = jnp.einsum("secd,edf->secf", slot_rows, w_in, preferred_element_type=FULL)
    activated_f, gelu_back = jax.vjp(smooth, pre_act)
    activated = activated_f.astype(LOW)
    gate_part = jnp.sum(activated.astype(FULL) * up_act, axis=3)
    pre_grad = gelu_back(up_act * gate_rows)[0].astype(LOW)
    input_part = jnp.einsum("secf,edf->secd", pre_grad, w_in, preferred_element_type=FULL)
    gate_part = gate_part.reshape(blocks, 1, rank_slots).astype(LOW)
    gate_part = jnp.pad(
        gate_part, ((0, 0), (0, slab - rank_slots - 1), (0, model_width - rank_slots))
    )
    back = jnp.concatenate(
        [input_part.astype(LOW).reshape(blocks, rank_slots, model_width), gate_part], axis=1
    )
    back = scatter_sum(back.reshape(dps, ranks, slab, model_width), "dp")
    dispatch_back = lax.all_to_all(back, "expert", split_axis=0, concat_axis=0, tiled=True)

    partial_out = jnp.einsum("secf,efd->secd", activated, w_out, preferred_element_type=FULL)
    returned = scatter_sum(
        partial_out.astype(LOW).reshape(dps, ranks, rank_slots, model_width), "dp"
    )
    back_rows = lax.all_to_all(returned, "expert", split_axis=0, concat_axis=0, tiled=True)
    first_grad = jnp.einsum("secd,secf->edf", slot_rows, pre_grad, preferred_element_type=FULL)
    grad_rows = (up_rows.astype(FULL) * gate_rows).astype(LOW)
    second_grad = jnp.einsum("secf,secd->efd", activated, grad_rows, preferred_element_type=FULL)

    fetched = jnp.dot(
        slot_mask, back_rows.reshape(slot_total, model_width), preferred_element_type=FULL
    )
    output = (hidden + gate_value[:, None] * fetched).astype(LOW)

    d_input, factors, score_grad, router_grad, gain_grads = pl.pallas_call(
        functools.partial(backward_kernel, places, rank_slots),
        out_shape=(
            shaped(FULL, length, model_width),
            shaped(LOW, ranks, 4 * columns_here, length),
            shaped(LOW, head_count, length, length),
            shaped(FULL, experts_total, model_width),
            shaped(FULL, 2, model_width),
        ),
        in_specs=[VMEM] * 12 + [ANY] * len(pieces),
        out_specs=(VMEM,) * 5,
        scratch_shapes=[
            pltpu.VMEM(w_shape, LOW),
            pltpu.VMEM((inner_width, length), FULL),
            pltpu.VMEM((3, inner_width, length), FULL),
            pltpu.SemaphoreType.DMA,
        ],
        compiler_params=pltpu.CompilerParams(vmem_limit_bytes=LIMIT),
        name="attention_backward",
    )(
        tokens,
        attn_gain.reshape(1, model_width),
        ffn_gain.reshape(1, model_width),
        w_router.T,
        hits_float,
        slab_mask,
        dispatch_back,
        d_out,
        hidden,
        chance,
        heads,
        weights,
        *pieces,
    )
    bias_grad = jnp.einsum("hij,ijb->bh", score_grad, onehot_buckets, preferred_element_type=FULL)

    factors = lax.all_to_all(factors, "expert", split_axis=0, concat_axis=0, tiled=True)
    factors = factors.transpose(0, 2, 1).reshape(ranks * length, 4 * columns_here)
    grads_qkv = contract_rows(normed_all, factors[:, : 3 * columns_here])
    grads_out = contract_rows(attended_all, factors[:, 3 * columns_here :])
    grads = jnp.concatenate([grads_qkv, grads_out], axis=1).astype(LOW)
    grads = grads.reshape(dps, rows_here, 4 * columns_here)
    grads = scatter_sum(absolute(grads, lax.axis_index("dp")), "dp").astype(FULL)
    g_query, g_key, g_value, g_output = (
        grads[:, i * columns_here : (i + 1) * columns_here] for i in range(4)
    )

    bias_row = jnp.pad(bias_grad.reshape(1, -1), ((0, 0), (0, model_width - bias_grad.size)))
    small = all_sum(jnp.concatenate([router_grad, gain_grads, bias_row], axis=0))
    g_router = small[:experts_total].T
    g_ffn_gain, g_attn_gain = small[experts_total], small[experts_total + 1]
    g_rel_bias = small[experts_total + 2, : bias_grad.size].reshape(bias_grad.shape)
    return (
        output,
        d_input,
        g_attn_gain,
        g_query,
        g_key,
        g_value,
        g_output,
        g_rel_bias,
        g_ffn_gain,
        g_router,
        first_grad,
        second_grad,
    )


def solution(mesh):
    return jax.shard_map(
        per_device,
        mesh=mesh,
        in_specs=(
            P(("dp", "expert"), None),
            P(("dp", "expert"), None),
            P(("dp", "expert"), None),
            P(),
            P("dp", "expert"),
            P("dp", "expert"),
            P("dp", "expert"),
            P("dp", "expert"),
            P(),
            P(),
            P(),
            P("expert", None, "dp"),
            P("expert", "dp", None),
            P(("dp", "expert"), None),
        ),
        out_specs=(
            P(("dp", "expert"), None),
            P(("dp", "expert"), None),
            P(),
            P("dp", "expert"),
            P("dp", "expert"),
            P("dp", "expert"),
            P("dp", "expert"),
            P(),
            P(),
            P(),
            P("expert", None, "dp"),
            P("expert", "dp", None),
        ),
        check_vma=False,
    )
```

```python
import functools

import jax
import jax.numpy as jnp
import numpy as np
from jax import lax
from jax.experimental import pallas as pl
from jax.experimental.pallas import tpu as pltpu
from jax.sharding import PartitionSpec as P

EPSILON = 1e-06
LIMITS = (12, 16, 23, 32, 46, 64, 91)
MASKED = -1000000000.0
HIGHEST = lax.Precision.HIGHEST
LOW = jnp.bfloat16
FULL = jnp.float32


def bucket_onehot(buckets, length):
    delta = np.arange(2 * length) - length
    magnitude = np.abs(delta)
    distant = 8 + sum((magnitude >= threshold).astype(np.int32) for threshold in LIMITS)
    ids = np.where(delta > 0, 16, 0) + np.where(magnitude < 8, magnitude, distant)
    return (ids[None, :] == np.arange(buckets)[:, None]).astype(np.float32)


def packing(local_experts, ranks, capacity, slab):
    table = np.zeros((local_experts, ranks, capacity, ranks, slab), np.float32)
    for e in range(local_experts):
        for r in range(ranks):
            for c in range(capacity):
                table[e, r, c, r, e * capacity + c] = 1.0
    return table.reshape(local_experts * ranks * capacity, ranks * slab)


def normalize(matrix, gain_vec):
    scale = lax.rsqrt(jnp.mean(matrix * matrix, axis=-1, keepdims=True) + EPSILON)
    return (matrix * scale * gain_vec, scale)


def norm_back(matrix, scale, gain_vec, incoming):
    weighted = incoming * gain_vec
    average = jnp.mean(matrix * weighted, axis=-1, keepdims=True)
    return (
        scale * weighted - matrix * (scale * scale * scale) * average,
        jnp.sum(incoming * matrix * scale, axis=0, keepdims=True),
    )


def swap(value, axis, mask):
    count = lax.axis_size(axis)
    return lax.ppermute(value, axis, [(i, i ^ mask) for i in range(count)])


def gather_bits(value, axis, masks):
    return jnp.concatenate([value] + [swap(value, axis, mask) for mask in masks], axis=0)


def fan_out(slabs):
    return [slabs[0]] + [swap(slabs[j], "expert", j) for j in range(1, len(slabs))]


def gather_list(value):
    found = {0: value}
    bit = lax.axis_size("dp") // 2
    while bit >= 1:
        found.update({index ^ bit: swap(item, "dp", bit) for index, item in found.items()})
        bit = bit // 2
    return [found[index] for index in range(len(found))]


def scatter_list(items, last=True):
    bit = 1
    while len(items) > 1:
        taken = [swap(item, "dp", bit) for item in items[1::2]]
        if len(items) == 2 and not last:
            return items[0], taken[0]
        items = [
            (kept.astype(FULL) + got.astype(FULL)).astype(kept.dtype)
            for kept, got in zip(items[0::2], taken)
        ]
        bit = bit * 2
    return items[0]


def all_sum(value):
    for axis in ("dp", "expert"):
        bit = 1
        while bit < lax.axis_size(axis):
            value = value + swap(value, axis, bit)
            bit = bit * 2
    return value


def gather_pieces(payload, early):
    ranks, dps = lax.axis_size("expert"), lax.axis_size("dp")
    half = payload.shape[0] // 2
    far = list(range(0, ranks, 2))
    sides = {"x": ("expert", [0, 1]), "y": ("dp", list(range(0, dps, 2)))}
    values = [
        gather_bits(payload[index * half : (index + 1) * half][None], "expert", far[1:])
        for index in range(2)
    ]
    values, early = lax.optimization_barrier((values, early))
    pieces, places = [], []
    for index, order in enumerate(("xy", "yx")):
        axis, masks = sides[order[0]]
        value = gather_bits(values[index][None], axis, masks[1:])
        other_axis, other_masks = sides[order[1]]
        found = [(value, 0)] + [(swap(value, other_axis, m), m) for m in other_masks[1:]]
        found = [(v, m, 0) for v, m in found] + [(swap(v, "dp", 1), m, 1) for v, m in found]
        for piece, mask, core in found:
            offsets = []
            for first in masks:
                for low in far:
                    x_mask, y_mask = (first, mask) if order == "xy" else (mask, first)
                    offsets.append((low ^ x_mask, y_mask ^ core))
            pieces.append(piece)
            places.append((index, offsets))
    return pieces, places, early


def place_weights(places, piece_refs, w_ref, sem):
    my_expert, my_dp = lax.axis_index("expert"), lax.axis_index("dp")
    copies = []
    for ref, (half, offsets) in zip(piece_refs, places):
        low_count, rows = ref.shape[1], ref.shape[2]
        for index, (e_mask, d_mask) in enumerate(offsets):
            start = (my_dp ^ d_mask) * (2 * rows) + half * rows
            copies.append(
                pltpu.make_async_copy(
                    ref.at[index // low_count, index % low_count],
                    w_ref.at[my_expert ^ e_mask, pl.ds(pl.multiple_of(start, 16), rows), :],
                    sem,
                )
            )
    for copy in copies:
        copy.start()
    return copies


def dot(left, right, dims=((1,), (0,)), precision=None):
    return lax.dot_general(
        left, right, (dims, ((), ())), precision=precision, preferred_element_type=FULL
    )


NT = ((1,), (1,))
TN = ((0,), (0,))


def grid_of(rows):
    sub = lax.broadcasted_iota(jnp.int32, (rows, 128), 0)
    lane = lax.broadcasted_iota(jnp.int32, (rows, 128), 1)
    return sub, lane


def row_to_column(row, rows, shift=0):
    sub, lane = grid_of(rows)
    column = jnp.sum(jnp.where(lane == sub + shift, row, 0.0), axis=1, keepdims=True)
    return jnp.broadcast_to(column, (rows, 128))


def column_to_row(column, shift=0):
    sub, lane = grid_of(column.shape[0])
    return jnp.sum(jnp.where(lane == sub + shift, column, 0.0), axis=0, keepdims=True)


def turn(value, shift):
    return pltpu.roll(value, shift % value.shape[1], 1)


def slide(value, direction):
    sub = lax.broadcasted_iota(jnp.int32, value.shape, 0)
    for bit in (1, 2, 4):
        value = jnp.where((sub & bit) != 0, turn(value, direction * bit), value)
    return value


def slid_rows(row, count):
    value = slide(jnp.broadcast_to(row, (8, row.shape[1])), 1)
    while value.shape[0] < count:
        value = jnp.concatenate([value, turn(value, value.shape[0])], axis=0)
    return value


def slid_sum(value):
    while value.shape[0] > 8:
        half = value.shape[0] // 2
        value = value[:half] + turn(value[half:], -half)
    return jnp.sum(slide(value, -1), axis=0, keepdims=True)


def early_kernel(
    ranks, local_experts, capacity, slab, tokens_ref, routes_ref, gain_ref, d_out_ref, table_ref,
    onehot_ref, normed_ref, hits_ref, mask_ref, mask_t_ref, bias_ref, *up_refs
):
    length = tokens_ref.shape[0]
    normed, _ = normalize(tokens_ref[...].astype(FULL), gain_ref[...].astype(FULL))
    normed_ref[...] = normed.astype(LOW)
    experts = hits_ref.shape[1]
    routes = jnp.broadcast_to(routes_ref[...].astype(FULL), (length, length)).T
    route = routes[:, :1].astype(jnp.int32)
    lanes = lax.broadcasted_iota(jnp.int32, (length, experts), 1)
    hits = (lanes == route).astype(FULL)
    hits_ref[...] = hits
    row = lax.broadcasted_iota(jnp.int32, (length, length), 0)
    col = lax.broadcasted_iota(jnp.int32, (length, length), 1)
    before = dot((col < row).astype(FULL).astype(LOW), hits.astype(LOW))
    placed = jnp.sum(before * hits, axis=1, keepdims=True).astype(jnp.int32)
    rank = jnp.zeros_like(route)
    for r in range(1, ranks):
        rank = rank + (route >= r * local_experts).astype(jnp.int32)
    spot = (rank ^ lax.axis_index("expert")) * slab
    spot = spot + (route - rank * local_experts) * capacity + placed
    spot = jnp.where(placed < capacity, spot, -1)
    places = lax.broadcasted_iota(jnp.int32, (length, ranks * slab), 1)
    mask = (places == spot).astype(FULL)
    mask_ref[...] = mask.astype(LOW)
    mask_t = mask.T.astype(LOW)
    mask_t_ref[...] = mask_t
    slabs = dot(mask_t, d_out_ref[...])
    for r in range(ranks):
        up_refs[r][...] = slabs[r * slab : (r + 1) * slab].astype(LOW)
    values = dot(table_ref[...], onehot_ref[...])
    for h in range(bias_ref.shape[0]):
        bias_ref[h] = slid_rows(values[h : h + 1], length)[:, length:]


def forward_kernel(
    places, slab, rank_slots, tokens_ref, normed_ref, seg_ref, bias_ref, gain_ref,
    router_t_ref, hits_ref, mask_t_ref, *rest
):
    count = len(places)
    piece_refs, rest = rest[:count], rest[count:]
    heads_ref, weights_ref, attended_ref, hidden_ref, chance_ref = rest[:5]
    slab_refs = rest[5:-4]
    w_ref, qkv_ref, att_t_ref, sem = rest[-4:]
    copies = place_weights(places, piece_refs, w_ref, sem)
    ranks, width, columns = w_ref.shape
    cols = columns // 4
    head_count = weights_ref.shape[0]
    head = width // head_count
    length = tokens_ref.shape[0]
    segments = jnp.broadcast_to(seg_ref[...].astype(FULL), (length, length))
    same_doc = segments == segments.T
    normed = normed_ref[...]
    for copy in copies:
        copy.wait()
    for e in range(ranks):
        turned = dot(normed, w_ref[e]).T
        for m in range(3):
            qkv_ref[m, e * cols : (e + 1) * cols, :] = turned[m * cols : (m + 1) * cols]
    heads_ref[...] = qkv_ref[...].astype(LOW)
    for h in range(head_count):
        rows = slice(h * head, (h + 1) * head)
        scores = dot(heads_ref[0, rows, :], heads_ref[1, rows, :], TN) * head ** (-0.5)
        scores = jnp.where(same_doc, scores + bias_ref[h], MASKED)
        grown = jnp.exp(scores - jnp.max(scores, axis=1, keepdims=True))
        weights = grown / jnp.sum(grown, axis=1, keepdims=True)
        weights_ref[h] = weights
        att_t_ref[rows, :] = dot(heads_ref[2, rows, :], weights.astype(LOW), NT)
    attended = att_t_ref[...].T.astype(LOW)
    attended_ref[...] = attended
    low_lane = 3 * cols // 128 * 128
    for e in range(ranks):
        turned = dot(attended, w_ref[e, :, low_lane:]).T
        att_t_ref[e * cols : (e + 1) * cols, :] = turned[3 * cols - low_lane :]
    hidden = tokens_ref[...].astype(FULL) + att_t_ref[...].T
    hidden_ref[...] = hidden
    normed_two, _ = normalize(hidden, gain_ref[...].astype(FULL))
    logits = dot(normed_two, router_t_ref[...].astype(FULL), NT, HIGHEST)
    grown = jnp.exp(logits - jnp.max(logits, axis=1, keepdims=True))
    chance = grown / jnp.sum(grown, axis=1, keepdims=True)
    chance_ref[...] = chance
    gate = jnp.sum(chance * hits_ref[...], axis=1, keepdims=True)
    mask_t = mask_t_ref[...]
    slots = dot(mask_t, normed_two.astype(LOW))
    gates = dot(mask_t.astype(FULL), jnp.broadcast_to(gate, (length, 128)), precision=HIGHEST)
    sub, _ = grid_of(slab)
    for r in range(ranks):
        mine = gates[r * slab : (r + 1) * slab]
        high = mine.astype(LOW).astype(FULL)
        row = column_to_row(high) + column_to_row(mine - high, 64)
        rows = slots[r * slab : (r + 1) * slab]
        start = rows[:, :128] + jnp.where(sub == rank_slots, row, 0.0)
        slab_refs[r][:, :128] = start.astype(LOW)
        slab_refs[r][:, 128:] = rows[:, 128:].astype(LOW)


def upstream_kernel(pack_ref, w_out_ref, *rest):
    piece_refs, (rows_ref, act_ref) = rest[:-2], rest[-2:]
    local_experts = w_out_ref.shape[0]
    chunk = pack_ref.shape[0] // local_experts
    for p, piece in enumerate(piece_refs):
        packed = dot(pack_ref[...], piece[...]).astype(LOW)
        for e in range(local_experts):
            rows_ref[e, p * chunk : (p + 1) * chunk, :] = packed[e * chunk : (e + 1) * chunk]
    for e in range(local_experts):
        act_ref[e] = dot(rows_ref[e], w_out_ref[e], NT)


def unpack(pack_t, rows_ref, p, chunk):
    rows = [rows_ref[e, p * chunk : (p + 1) * chunk, :] for e in range(rows_ref.shape[0])]
    return dot(pack_t, jnp.concatenate(rows, axis=0))


def expert_kernel(
    count, slab, rank_slots, pack_ref, pack_t_ref, w_in_ref, up_act_ref, *rest
):
    piece_refs, rest = rest[:count], rest[count:]
    back_refs, rest = rest[:count], rest[count:]
    rows_ref, act_ref, pre_grad_ref, gates_ref, pre_ref, back_ref, part_ref = rest
    local_experts = w_in_ref.shape[0]
    chunk = pack_ref.shape[0] // local_experts
    ranks = pack_ref.shape[1] // slab
    pack, pack_t = pack_ref[...], pack_t_ref[...]
    for p, piece in enumerate(piece_refs):
        packed = dot(pack, piece[...]).astype(LOW)
        tile = piece[:, :128].astype(FULL)
        spread = []
        for shift in (0, 64):
            columns = [
                row_to_column(tile[r * slab + rank_slots : r * slab + rank_slots + 1], slab, shift)
                for r in range(ranks)
            ]
            spread.append(dot(pack, jnp.concatenate(columns, axis=0).astype(LOW)))
        gates = spread[0] + spread[1]
        for e in range(local_experts):
            rows_ref[e, p * chunk : (p + 1) * chunk, :] = packed[e * chunk : (e + 1) * chunk]
            gates_ref[e, p * chunk : (p + 1) * chunk, :] = gates[e * chunk : (e + 1) * chunk]
    root = np.float32(np.sqrt(2.0 / np.pi))
    step = 16
    for e in range(local_experts):
        pre_ref[...] = dot(rows_ref[e], w_in_ref[e])

        def body(index, carry):
            span = pl.ds(pl.multiple_of(index * step, step), step)
            pre = pre_ref[span, :]
            up = up_act_ref[e, span, :]
            square = pre * pre
            curve = jnp.tanh(root * pre * (1.0 + 0.044715 * square))
            rise = 0.5 + 0.5 * curve
            act = (pre * rise).astype(LOW)
            act_ref[e, span, :] = act
            slope = rise + pre * (rise * (1.0 - curve)) * (root + 3 * 0.044715 * root * square)
            gate = gates_ref[e, span, :][:, :1]
            pre_grad_ref[e, span, :] = (slope * (up * gate)).astype(LOW)
            part = jnp.sum(act.astype(FULL) * up, axis=1, keepdims=True)
            part_ref[e, span, :] = jnp.broadcast_to(part, (step, 128)).astype(LOW)
            return carry

        lax.fori_loop(0, pre_ref.shape[0] // step, body, 0, unroll=2)
        back_ref[e] = dot(pre_grad_ref[e], w_in_ref[e], NT).astype(LOW)
    sub, _ = grid_of(slab)
    for p in range(count):
        rows = unpack(pack_t, back_ref, p, chunk)
        parts = unpack(pack_t, part_ref, p, chunk)
        pieces = []
        for r in range(ranks):
            span = slice(r * slab, (r + 1) * slab)
            row = column_to_row(parts[span])
            pieces.append(rows[span, :128] + jnp.where(sub == rank_slots, row, 0.0))
        back_refs[p][:, :128] = jnp.concatenate(pieces, axis=0).astype(LOW)
        back_refs[p][:, 128:] = rows[:, 128:].astype(LOW)


def expert_grad_kernel(
    count, pack_t_ref, w_out_ref, rows_ref, act_ref, pre_grad_ref, gates_ref, up_rows_ref, *rest
):
    out_refs, (g_in_ref, g_out_ref, returned_ref) = rest[:count], rest[count:]
    local_experts = w_out_ref.shape[0]
    chunk = rows_ref.shape[1] // count
    pack_t = pack_t_ref[...]
    for e in range(local_experts):
        returned_ref[e] = dot(act_ref[e], w_out_ref[e]).astype(LOW)
    for p in range(count):
        out_refs[p][...] = unpack(pack_t, returned_ref, p, chunk).astype(LOW)
    for e in range(local_experts):
        g_in_ref[e] = dot(rows_ref[e], pre_grad_ref[e], TN)
        slot_grad = (up_rows_ref[e].astype(FULL) * gates_ref[e][:, :1]).astype(LOW)
        g_out_ref[e] = dot(act_ref[e], slot_grad, TN)


def split_kernel(first_ref, second_ref, *out_refs):
    slab = out_refs[0].shape[0]
    total = first_ref[...].astype(FULL) + second_ref[...].astype(FULL)
    for r, ref in enumerate(out_refs):
        ref[...] = total[r * slab : (r + 1) * slab].astype(LOW)


def joined(refs):
    return jnp.concatenate([ref[...].astype(FULL) for ref in refs], axis=0).astype(LOW)


def backward_kernel(
    places, rank_slots, tokens_ref, gain_one_ref, gain_two_ref, router_t_ref, hits_ref, mask_ref,
    up_ref, hidden_ref, chance_ref, heads_ref, weights_ref, onehot_ref, *rest
):
    count = len(places)
    piece_refs, rest = rest[:count], rest[count:]
    w_ref, turned_ref, grads_ref, bias_ref, sent_ref, sem = rest[-6:]
    ranks, width, columns = w_ref.shape
    back_refs, rest = rest[:ranks], rest[ranks:-6]
    d_input_ref, small_ref = rest[:2]
    factor_refs = rest[2:]
    copies = place_weights(places, piece_refs, w_ref, sem)
    cols = columns // 4
    head_count = weights_ref.shape[0]
    head = width // head_count
    factor = head ** (-0.5)
    length = tokens_ref.shape[0]
    slab = back_refs[0].shape[0]
    hidden = hidden_ref[...]
    gain_two = gain_two_ref[...].astype(FULL)
    normed_two, scale_two = normalize(hidden, gain_two)
    mask = mask_ref[...]
    chance, hits = chance_ref[...], hits_ref[...]
    gate = jnp.sum(chance * hits, axis=1, keepdims=True)
    spread = [
        row_to_column(ref[:, :128].astype(FULL)[rank_slots : rank_slots + 1], slab)
        for ref in back_refs
    ]
    gate_grad = dot(mask, jnp.concatenate(spread, axis=0).astype(LOW))[:, :1]
    logit_grad = chance * (hits - gate) * gate_grad
    experts = hits.shape[1]
    small_ref[:experts, :] = dot(logit_grad, normed_two, TN, HIGHEST)
    router_t = router_t_ref[...].astype(FULL)
    normed_two_grad = dot(logit_grad, router_t, precision=HIGHEST) + dot(mask, joined(back_refs))
    hidden_part, ffn_gain_grad = norm_back(hidden, scale_two, gain_two, normed_two_grad)
    hidden_grad = up_ref[...].astype(FULL) + hidden_part
    turned_ref[...] = hidden_grad.astype(LOW).astype(FULL).T
    for copy in copies:
        copy.wait()
    low_lane = 3 * cols // 128 * 128
    att_grad = None
    for e in range(ranks):
        own = turned_ref[e * cols : (e + 1) * cols, :]
        if 3 * cols > low_lane:
            own = jnp.concatenate([jnp.zeros((3 * cols - low_lane, 128), FULL), own], axis=0)
        part = dot(w_ref[e, :, low_lane:], own.astype(LOW))
        att_grad = part if att_grad is None else att_grad + part
    att_grad = att_grad.astype(LOW)
    for h in range(head_count):
        rows = slice(h * head, (h + 1) * head)
        own = att_grad[rows]
        weights = weights_ref[h]
        grads_ref[2, rows, :] = dot(own, weights.astype(LOW))
        prob_grad = dot(own, heads_ref[2, rows, :], TN)
        score_grad = weights * (prob_grad - jnp.sum(prob_grad * weights, axis=1, keepdims=True))
        score_grad = score_grad.astype(LOW)
        grads_ref[0, rows, :] = dot(heads_ref[1, rows, :], score_grad, NT) * factor
        grads_ref[1, rows, :] = dot(heads_ref[0, rows, :], score_grad) * factor
        wide = [jnp.zeros((length, length), FULL), score_grad.astype(FULL)]
        bias_ref[h : h + 1, :] = slid_sum(jnp.concatenate(wide, axis=1))
    total = None
    for e in range(ranks):
        span = slice(e * cols, (e + 1) * cols)
        held = [grads_ref[m, span, :] for m in range(3)] + [jnp.zeros((cols, 128), FULL)]
        part = dot(w_ref[e], jnp.concatenate(held, axis=0).astype(LOW))
        total = part if total is None else total + part
        sent = [grads_ref[m, span, :] for m in range(3)] + [turned_ref[span, :]]
        sent_ref[e] = jnp.concatenate(sent, axis=0)
    for e in range(ranks):
        factor_refs[e][...] = sent_ref[lax.axis_index("expert") ^ e].astype(LOW)
    inputs = tokens_ref[...].astype(FULL)
    gain_one = gain_one_ref[...].astype(FULL)
    _, scale_one = normalize(inputs, gain_one)
    norm_part, attn_gain_grad = norm_back(inputs, scale_one, gain_one, total.T)
    d_input_ref[...] = hidden_grad + norm_part
    sums = dot(bias_ref[...], onehot_ref[...], NT, HIGHEST)
    small_ref[experts : experts + 1, :] = ffn_gain_grad
    small_ref[experts + 1 : experts + 2, :] = attn_gain_grad
    small_ref[experts + 2 :, :] = jnp.zeros((small_ref.shape[0] - experts - 2, width), FULL)
    small_ref[experts + 2 : experts + 2 + head_count, : sums.shape[1]] = sums


def product_kernel(
    ranks, dps, rank_slots, normed_ref, attended_ref, hidden_ref, chance_ref, hits_ref, mask_ref, *rest
):
    factor_refs, rest = rest[:ranks], rest[ranks:]
    returned_refs, rest = rest[:ranks], rest[ranks:]
    output_ref, total_ref = rest[0], rest[-1]
    piece_refs = rest[1:-1]
    length = hidden_ref.shape[0]
    cols = factor_refs[0].shape[0] // 4
    first, second = None, None
    for j, ref in enumerate(factor_refs):
        span = lax.axis_index("expert") ^ j
        held = ref[...].astype(FULL)
        part = dot(held[: 3 * cols].astype(LOW), normed_ref[span])
        first = part if first is None else first + part
        part = dot(held[3 * cols :].astype(LOW), attended_ref[span])
        second = part if second is None else second + part
    total = jnp.concatenate([first, second], axis=0).T
    rows = piece_refs[0].shape[0]
    for j in range(dps):
        total_ref[j] = total[j * rows : (j + 1) * rows]
    for j, ref in enumerate(piece_refs):
        ref[...] = total_ref[lax.axis_index("dp") ^ j].astype(LOW)
    gate = jnp.sum(chance_ref[...] * hits_ref[...], axis=1, keepdims=True)
    fetched = dot(mask_ref[...], joined(returned_refs))
    output_ref[...] = (hidden_ref[...] + gate * fetched).astype(LOW)


VMEM = pl.BlockSpec(memory_space=pltpu.VMEM)
ANY = pl.BlockSpec(memory_space=pl.ANY)
LIMIT = 60 * 1024 * 1024


def shaped(dtype, *shape):
    return jax.ShapeDtypeStruct(shape, dtype)


def call(kernel, name, out_shape, args, pieces=(), scratch=(), more=()):
    return pl.pallas_call(
        kernel,
        out_shape=tuple(out_shape),
        in_specs=[VMEM] * len(args) + [ANY] * len(pieces) + [VMEM] * len(more),
        out_specs=(VMEM,) * len(out_shape),
        scratch_shapes=list(scratch),
        compiler_params=pltpu.CompilerParams(vmem_limit_bytes=LIMIT),
        name=name,
    )(*args, *pieces, *more)


def per_device(
    tokens,
    seg_ids,
    routes,
    attn_gain,
    w_query,
    w_key,
    w_value,
    w_output,
    rel_bias,
    ffn_gain,
    w_router,
    w_in,
    w_out,
    d_out,
):
    length, model_width = tokens.shape
    bucket_count, head_count = rel_bias.shape
    experts_total = w_router.shape[1]
    local_experts, _, hidden_here = w_in.shape
    ranks, dps = lax.axis_size("expert"), lax.axis_size("dp")
    capacity = length * 5 // (4 * experts_total)
    rank_slots = local_experts * capacity
    slab = -(-(rank_slots + 1) // 8) * 8
    rows_here, columns_here = w_query.shape
    inner_width = dps * rows_here
    packed_rows = dps * ranks * capacity
    gain_one = attn_gain.reshape(1, model_width)
    gain_two = ffn_gain.reshape(1, model_width)
    router_t = w_router.T
    pack = packing(local_experts, ranks, capacity, slab)
    pack, pack_t = jnp.asarray(pack, LOW), jnp.asarray(pack.T, LOW)

    normed_low, hits, mask, mask_t, bias_full, *up_slabs = call(
        functools.partial(early_kernel, ranks, local_experts, capacity, slab),
        "early",
        [
            shaped(LOW, length, model_width),
            shaped(FULL, length, experts_total),
            shaped(LOW, length, ranks * slab),
            shaped(LOW, ranks * slab, length),
            shaped(FULL, head_count, length, length),
        ]
        + [shaped(LOW, slab, model_width)] * ranks,
        [
            tokens,
            routes.reshape(1, length),
            gain_one,
            d_out,
            rel_bias.T,
            jnp.asarray(bucket_onehot(bucket_count, length), LOW),
        ],
    )

    payload = jnp.concatenate([w_query, w_key, w_value, w_output], axis=1)
    pieces, places, (normed_low, hits, mask, mask_t, bias_full, up_slabs) = gather_pieces(
        payload, (normed_low, hits, mask, mask_t, bias_full, up_slabs)
    )
    pieces, normed_later, up_slabs = lax.optimization_barrier((pieces, normed_low, up_slabs))
    normed_all = lax.all_gather(normed_later, "expert", axis=0)

    w_shape = (ranks, inner_width, 4 * columns_here)
    heads, weights, attended, hidden, chance, *slabs = call(
        functools.partial(forward_kernel, places, slab, rank_slots),
        "attention_forward",
        [
            shaped(LOW, 3, inner_width, length),
            shaped(FULL, head_count, length, length),
            shaped(LOW, length, inner_width),
            shaped(FULL, length, model_width),
            shaped(FULL, length, experts_total),
        ]
        + [shaped(LOW, slab, model_width)] * ranks,
        [tokens, normed_low, seg_ids, bias_full, gain_two, router_t, hits, mask_t],
        pieces,
        [
            pltpu.VMEM(w_shape, LOW),
            pltpu.VMEM((3, inner_width, length), FULL),
            pltpu.VMEM((inner_width, length), FULL),
            pltpu.SemaphoreType.DMA,
        ],
    )

    up_pieces = gather_list(jnp.concatenate(fan_out(up_slabs), axis=0))
    row_pieces = gather_list(jnp.concatenate(fan_out(slabs), axis=0))
    attended_all = lax.all_gather(attended, "expert", axis=0)
    by_expert = (local_experts, packed_rows)
    up_rows, up_act = call(
        upstream_kernel,
        "upstream_rows",
        [shaped(LOW, *by_expert, model_width), shaped(FULL, *by_expert, hidden_here)],
        [pack, w_out, *up_pieces],
    )

    *back, slot_rows, activated, pre_grad, gates = call(
        functools.partial(expert_kernel, dps, slab, rank_slots),
        "experts",
        [shaped(LOW, ranks * slab, model_width)] * dps
        + [
            shaped(LOW, *by_expert, model_width),
            shaped(LOW, *by_expert, hidden_here),
            shaped(LOW, *by_expert, hidden_here),
            shaped(FULL, *by_expert, 128),
        ],
        [pack, pack_t, w_in, up_act, *row_pieces],
        scratch=[
            pltpu.VMEM((packed_rows, hidden_here), FULL),
            pltpu.VMEM((*by_expert, model_width), LOW),
            pltpu.VMEM((*by_expert, 128), LOW),
        ],
    )
    slab_shapes = [shaped(LOW, slab, model_width)] * ranks
    back = fan_out(call(split_kernel, "back_slabs", slab_shapes, scatter_list(back, last=False)))
    *returned, first_grad, second_grad = call(
        functools.partial(expert_grad_kernel, dps),
        "expert_gradients",
        [shaped(LOW, ranks * slab, model_width)] * dps
        + [shaped(FULL, *w_in.shape), shaped(FULL, *w_out.shape)],
        [pack_t, w_out, slot_rows, activated, pre_grad, gates, up_rows],
        scratch=[pltpu.VMEM((*by_expert, model_width), LOW)],
    )
    returned = fan_out(
        call(split_kernel, "returned_slabs", slab_shapes, scatter_list(returned, last=False))
    )

    small_rows = -(-(experts_total + 2 + head_count) // 8) * 8
    d_input, small, *factors = call(
        functools.partial(backward_kernel, places, rank_slots),
        "attention_backward",
        [
            shaped(FULL, length, model_width),
            shaped(FULL, small_rows, model_width),
        ]
        + [shaped(LOW, 4 * columns_here, length)] * ranks,
        [
            tokens,
            gain_one,
            gain_two,
            router_t,
            hits,
            mask,
            d_out,
            hidden,
            chance,
            heads,
            weights,
            jnp.asarray(bucket_onehot(bucket_count, length), FULL),
        ],
        pieces,
        [
            pltpu.VMEM(w_shape, LOW),
            pltpu.VMEM((inner_width, length), FULL),
            pltpu.VMEM((3, inner_width, length), FULL),
            pltpu.VMEM((head_count, 2 * length), FULL),
            pltpu.VMEM((ranks, 4 * columns_here, length), FULL),
            pltpu.SemaphoreType.DMA,
        ],
        back,
    )

    factors = fan_out(factors)
    small = all_sum(small)
    output, *grads = call(
        functools.partial(product_kernel, ranks, dps, rank_slots),
        "weight_gradients",
        [shaped(LOW, length, model_width)] + [shaped(LOW, rows_here, 4 * columns_here)] * dps,
        [normed_all, attended_all, hidden, chance, hits, mask, *factors, *returned],
        scratch=[pltpu.VMEM((dps, rows_here, 4 * columns_here), FULL)],
    )
    kept, got = scatter_list(grads, last=False)
    grads = kept.astype(FULL) + got.astype(FULL)
    g_query, g_key, g_value, g_output = (
        grads[:, i * columns_here : (i + 1) * columns_here] for i in range(4)
    )
    g_router = small[:experts_total].T
    g_ffn_gain, g_attn_gain = small[experts_total], small[experts_total + 1]
    g_rel_bias = small[experts_total + 2 : experts_total + 2 + head_count, :bucket_count].T
    return (
        output,
        d_input,
        g_attn_gain,
        g_query,
        g_key,
        g_value,
        g_output,
        g_rel_bias,
        g_ffn_gain,
        g_router,
        first_grad,
        second_grad,
    )


def solution(mesh):
    return jax.shard_map(
        per_device,
        mesh=mesh,
        in_specs=(
            P(("dp", "expert"), None),
            P(("dp", "expert"), None),
            P(("dp", "expert"), None),
            P(),
            P("dp", "expert"),
            P("dp", "expert"),
            P("dp", "expert"),
            P("dp", "expert"),
            P(),
            P(),
            P(),
            P("expert", None, "dp"),
            P("expert", "dp", None),
            P(("dp", "expert"), None),
        ),
        out_specs=(
            P(("dp", "expert"), None),
            P(("dp", "expert"), None),
            P(),
            P("dp", "expert"),
            P("dp", "expert"),
            P("dp", "expert"),
            P("dp", "expert"),
            P(),
            P(),
            P(),
            P("expert", None, "dp"),
            P("expert", "dp", None),
        ),
        check_vma=False,
    )
```

```python
import functools

import jax
import jax.numpy as jnp
import numpy as np
from jax import lax
from jax.experimental import pallas as pl
from jax.experimental.pallas import tpu as pltpu
from jax.sharding import PartitionSpec as P

EPSILON = 1e-06
LIMITS = (12, 16, 23, 32, 46, 64, 91)
MASKED = -1000000000.0
HIGHEST = lax.Precision.HIGHEST
LOW = jnp.bfloat16
FULL = jnp.float32


def bucket_onehot(buckets, length):
    delta = np.arange(2 * length) - length
    magnitude = np.abs(delta)
    distant = 8 + sum((magnitude >= threshold).astype(np.int32) for threshold in LIMITS)
    ids = np.where(delta > 0, 16, 0) + np.where(magnitude < 8, magnitude, distant)
    return (ids[None, :] == np.arange(buckets)[:, None]).astype(np.float32)


def packing(local_experts, ranks, capacity, slab):
    table = np.zeros((local_experts, ranks, capacity, ranks, slab), np.float32)
    for e in range(local_experts):
        for r in range(ranks):
            for c in range(capacity):
                table[e, r, c, r, e * capacity + c] = 1.0
    return table.reshape(local_experts * ranks * capacity, ranks * slab)


def normalize(matrix, gain_vec):
    scale = lax.rsqrt(jnp.mean(matrix * matrix, axis=-1, keepdims=True) + EPSILON)
    return (matrix * scale * gain_vec, scale)


def norm_back(matrix, scale, gain_vec, incoming):
    weighted = incoming * gain_vec
    average = jnp.mean(matrix * weighted, axis=-1, keepdims=True)
    return (
        scale * weighted - matrix * (scale * scale * scale) * average,
        jnp.sum(incoming * matrix * scale, axis=0, keepdims=True),
    )


def swap(value, axis, mask):
    count = lax.axis_size(axis)
    return lax.ppermute(value, axis, [(i, i ^ mask) for i in range(count)])


def gather_bits(value, axis, masks):
    return jnp.concatenate([value] + [swap(value, axis, mask) for mask in masks], axis=0)


def exchange(value):
    return lax.all_to_all(value, "expert", split_axis=0, concat_axis=0, tiled=True)


def gather_list(value):
    found = {0: value}
    bit = lax.axis_size("dp") // 2
    while bit >= 1:
        found.update({index ^ bit: swap(item, "dp", bit) for index, item in found.items()})
        bit = bit // 2
    return [found[index] for index in range(len(found))]


def scatter_list(items, dtype=LOW):
    bit = 1
    while len(items) > 1:
        taken = [swap(item, "dp", bit) for item in items[1::2]]
        kind = dtype if len(items) == 2 else LOW
        items = [
            (kept.astype(FULL) + got.astype(FULL)).astype(kind)
            for kept, got in zip(items[0::2], taken)
        ]
        bit = bit * 2
    return items[0]


def all_sum(value):
    for axis in ("dp", "expert"):
        bit = 1
        while bit < lax.axis_size(axis):
            value = value + swap(value, axis, bit)
            bit = bit * 2
    return value


def gather_pieces(payload, early):
    ranks, dps = lax.axis_size("expert"), lax.axis_size("dp")
    half = payload.shape[0] // 2
    far = list(range(0, ranks, 2))
    sides = {"x": ("expert", [0, 1]), "y": ("dp", list(range(0, dps, 2)))}
    values = [
        gather_bits(payload[index * half : (index + 1) * half][None], "expert", far[1:])
        for index in range(2)
    ]
    values, early = lax.optimization_barrier((values, early))
    pieces, places = [], []
    for index, order in enumerate(("xy", "yx")):
        axis, masks = sides[order[0]]
        value = gather_bits(values[index][None], axis, masks[1:])
        other_axis, other_masks = sides[order[1]]
        found = [(value, 0)] + [(swap(value, other_axis, m), m) for m in other_masks[1:]]
        found = [(v, m, 0) for v, m in found] + [(swap(v, "dp", 1), m, 1) for v, m in found]
        for piece, mask, core in found:
            offsets = []
            for first in masks:
                for low in far:
                    x_mask, y_mask = (first, mask) if order == "xy" else (mask, first)
                    offsets.append((low ^ x_mask, y_mask ^ core))
            pieces.append(piece)
            places.append((index, offsets))
    return pieces, places, early


def place_weights(places, piece_refs, w_ref, sem):
    my_expert, my_dp = lax.axis_index("expert"), lax.axis_index("dp")
    copies = []
    for ref, (half, offsets) in zip(piece_refs, places):
        low_count, rows = ref.shape[1], ref.shape[2]
        for index, (e_mask, d_mask) in enumerate(offsets):
            start = (my_dp ^ d_mask) * (2 * rows) + half * rows
            copies.append(
                pltpu.make_async_copy(
                    ref.at[index // low_count, index % low_count],
                    w_ref.at[my_expert ^ e_mask, pl.ds(pl.multiple_of(start, 16), rows), :],
                    sem,
                )
            )
    for copy in copies:
        copy.start()
    return copies


def dot(left, right, dims=((1,), (0,)), precision=None):
    return lax.dot_general(
        left, right, (dims, ((), ())), precision=precision, preferred_element_type=FULL
    )


NT = ((1,), (1,))
TN = ((0,), (0,))


def grid_of(rows):
    sub = lax.broadcasted_iota(jnp.int32, (rows, 128), 0)
    lane = lax.broadcasted_iota(jnp.int32, (rows, 128), 1)
    return sub, lane


def row_to_column(row, rows, shift=0):
    sub, lane = grid_of(rows)
    column = jnp.sum(jnp.where(lane == sub + shift, row, 0.0), axis=1, keepdims=True)
    return jnp.broadcast_to(column, (rows, 128))


def column_to_row(column, shift=0):
    sub, lane = grid_of(column.shape[0])
    return jnp.sum(jnp.where(lane == sub + shift, column, 0.0), axis=0, keepdims=True)


def turn(value, shift):
    return pltpu.roll(value, shift % value.shape[1], 1)


def slide(value, direction):
    sub = lax.broadcasted_iota(jnp.int32, value.shape, 0)
    for bit in (1, 2, 4):
        value = jnp.where((sub & bit) != 0, turn(value, direction * bit), value)
    return value


def slid_rows(row, count):
    value = slide(jnp.broadcast_to(row, (8, row.shape[1])), 1)
    while value.shape[0] < count:
        value = jnp.concatenate([value, turn(value, value.shape[0])], axis=0)
    return value


def slid_sum(value):
    while value.shape[0] > 8:
        half = value.shape[0] // 2
        value = value[:half] + turn(value[half:], -half)
    return jnp.sum(slide(value, -1), axis=0, keepdims=True)


def early_kernel(
    ranks, local_experts, capacity, slab, tokens_ref, routes_ref, gain_ref, d_out_ref, table_ref,
    onehot_ref, normed_ref, hits_ref, mask_ref, mask_t_ref, bias_ref, up_ref
):
    length = tokens_ref.shape[0]
    normed, _ = normalize(tokens_ref[...].astype(FULL), gain_ref[0:1, :])
    normed_ref[...] = normed.astype(LOW)
    experts = hits_ref.shape[1]
    routes = jnp.broadcast_to(routes_ref[...].astype(FULL), (length, length)).T
    route = routes[:, :1].astype(jnp.int32)
    lanes = lax.broadcasted_iota(jnp.int32, (length, experts), 1)
    hits = (lanes == route).astype(FULL)
    hits_ref[...] = hits
    row = lax.broadcasted_iota(jnp.int32, (length, length), 0)
    col = lax.broadcasted_iota(jnp.int32, (length, length), 1)
    before = dot((col < row).astype(FULL).astype(LOW), hits.astype(LOW))
    placed = jnp.sum(before * hits, axis=1, keepdims=True).astype(jnp.int32)
    rank = jnp.zeros_like(route)
    for r in range(1, ranks):
        rank = rank + (route >= r * local_experts).astype(jnp.int32)
    spot = rank * slab + (route - rank * local_experts) * capacity + placed
    spot = jnp.where(placed < capacity, spot, -1)
    places = lax.broadcasted_iota(jnp.int32, (length, ranks * slab), 1)
    mask = (places == spot).astype(FULL)
    mask_ref[...] = mask.astype(LOW)
    mask_t = mask.T.astype(LOW)
    mask_t_ref[...] = mask_t
    slabs = dot(mask_t, d_out_ref[...])
    for r in range(ranks):
        up_ref[r] = slabs[r * slab : (r + 1) * slab].astype(LOW)
    values = dot(table_ref[...], onehot_ref[...])
    for h in range(bias_ref.shape[0]):
        bias_ref[h] = slid_rows(values[h : h + 1], length)[:, length:]


def forward_kernel(
    places, slab, rank_slots, tokens_ref, normed_ref, seg_ref, bias_ref, gain_ref,
    router_t_ref, hits_ref, mask_t_ref, *rest
):
    count = len(places)
    piece_refs, rest = rest[:count], rest[count:]
    heads_ref, weights_ref, attended_ref, hidden_ref, chance_ref = rest[:5]
    slabs_ref = rest[5]
    w_ref, qkv_ref, att_t_ref, sem = rest[-4:]
    copies = place_weights(places, piece_refs, w_ref, sem)
    ranks, width, columns = w_ref.shape
    cols = columns // 4
    head_count = weights_ref.shape[0]
    head = width // head_count
    length = tokens_ref.shape[0]
    segments = jnp.broadcast_to(seg_ref[...].astype(FULL), (length, length))
    same_doc = segments == segments.T
    normed = normed_ref[...]
    for copy in copies:
        copy.wait()
    for e in range(ranks):
        turned = dot(normed, w_ref[e]).T
        for m in range(3):
            qkv_ref[m, e * cols : (e + 1) * cols, :] = turned[m * cols : (m + 1) * cols]
    heads_ref[...] = qkv_ref[...].astype(LOW)
    for h in range(head_count):
        rows = slice(h * head, (h + 1) * head)
        scores = dot(heads_ref[0, rows, :], heads_ref[1, rows, :], TN) * head ** (-0.5)
        scores = jnp.where(same_doc, scores + bias_ref[h], MASKED)
        grown = jnp.exp(scores - jnp.max(scores, axis=1, keepdims=True))
        weights = grown / jnp.sum(grown, axis=1, keepdims=True)
        weights_ref[h] = weights
        att_t_ref[rows, :] = dot(heads_ref[2, rows, :], weights.astype(LOW), NT)
    attended = att_t_ref[...].T.astype(LOW)
    attended_ref[...] = attended
    low_lane = 3 * cols // 128 * 128
    for e in range(ranks):
        turned = dot(attended, w_ref[e, :, low_lane:]).T
        att_t_ref[e * cols : (e + 1) * cols, :] = turned[3 * cols - low_lane :]
    hidden = tokens_ref[...].astype(FULL) + att_t_ref[...].T
    hidden_ref[...] = hidden
    normed_two, _ = normalize(hidden, gain_ref[1:2, :])
    logits = dot(normed_two, router_t_ref[...].astype(FULL), NT, HIGHEST)
    grown = jnp.exp(logits - jnp.max(logits, axis=1, keepdims=True))
    chance = grown / jnp.sum(grown, axis=1, keepdims=True)
    chance_ref[...] = chance
    gate = jnp.sum(chance * hits_ref[...], axis=1, keepdims=True)
    mask_t = mask_t_ref[...]
    slots = dot(mask_t, normed_two.astype(LOW))
    gates = dot(mask_t.astype(FULL), jnp.broadcast_to(gate, (length, 128)), precision=HIGHEST)
    sub, _ = grid_of(slab)
    for r in range(ranks):
        mine = gates[r * slab : (r + 1) * slab]
        high = mine.astype(LOW).astype(FULL)
        row = column_to_row(high) + column_to_row(mine - high, 64)
        rows = slots[r * slab : (r + 1) * slab]
        start = rows[:, :128] + jnp.where(sub == rank_slots, row, 0.0)
        slabs_ref[r, :, :128] = start.astype(LOW)
        slabs_ref[r, :, 128:] = rows[:, 128:].astype(LOW)


def upstream_kernel(pack_ref, w_out_ref, *rest):
    piece_refs, (rows_ref, act_ref) = rest[:-2], rest[-2:]
    local_experts = w_out_ref.shape[0]
    chunk = pack_ref.shape[0] // local_experts
    for p, piece in enumerate(piece_refs):
        packed = dot(pack_ref[...], piece[...]).astype(LOW)
        for e in range(local_experts):
            rows_ref[e, p * chunk : (p + 1) * chunk, :] = packed[e * chunk : (e + 1) * chunk]
    for e in range(local_experts):
        act_ref[e] = dot(rows_ref[e], w_out_ref[e], NT)


def unpack(pack_t, rows_ref, p, chunk):
    rows = [rows_ref[e, p * chunk : (p + 1) * chunk, :] for e in range(rows_ref.shape[0])]
    return dot(pack_t, jnp.concatenate(rows, axis=0))


def expert_kernel(
    count, slab, rank_slots, pack_ref, pack_t_ref, w_in_ref, up_act_ref, *rest
):
    piece_refs, rest = rest[:count], rest[count:]
    back_refs, rest = rest[:count], rest[count:]
    rows_ref, act_ref, pre_grad_ref, gates_ref, pre_ref, back_ref, part_ref = rest
    local_experts = w_in_ref.shape[0]
    chunk = pack_ref.shape[0] // local_experts
    ranks = pack_ref.shape[1] // slab
    pack, pack_t = pack_ref[...], pack_t_ref[...]
    for p, piece in enumerate(piece_refs):
        packed = dot(pack, piece[...]).astype(LOW)
        tile = piece[:, :128].astype(FULL)
        spread = []
        for shift in (0, 64):
            columns = [
                row_to_column(tile[r * slab + rank_slots : r * slab + rank_slots + 1], slab, shift)
                for r in range(ranks)
            ]
            spread.append(dot(pack, jnp.concatenate(columns, axis=0).astype(LOW)))
        gates = spread[0] + spread[1]
        for e in range(local_experts):
            rows_ref[e, p * chunk : (p + 1) * chunk, :] = packed[e * chunk : (e + 1) * chunk]
            gates_ref[e, p * chunk : (p + 1) * chunk, :] = gates[e * chunk : (e + 1) * chunk]
    root = np.float32(np.sqrt(2.0 / np.pi))
    step = 16
    for e in range(local_experts):
        pre_ref[...] = dot(rows_ref[e], w_in_ref[e])

        def body(index, carry):
            span = pl.ds(pl.multiple_of(index * step, step), step)
            pre = pre_ref[span, :]
            up = up_act_ref[e, span, :]
            square = pre * pre
            curve = jnp.tanh(root * pre * (1.0 + 0.044715 * square))
            rise = 0.5 + 0.5 * curve
            act = (pre * rise).astype(LOW)
            act_ref[e, span, :] = act
            slope = rise + pre * (rise * (1.0 - curve)) * (root + 3 * 0.044715 * root * square)
            gate = gates_ref[e, span, :][:, :1]
            pre_grad_ref[e, span, :] = (slope * (up * gate)).astype(LOW)
            part = jnp.sum(act.astype(FULL) * up, axis=1, keepdims=True)
            part_ref[e, span, :] = jnp.broadcast_to(part, (step, 128)).astype(LOW)
            return carry

        lax.fori_loop(0, pre_ref.shape[0] // step, body, 0, unroll=2)
        back_ref[e] = dot(pre_grad_ref[e], w_in_ref[e], NT).astype(LOW)
    sub, _ = grid_of(slab)
    for p in range(count):
        rows = unpack(pack_t, back_ref, p, chunk)
        parts = unpack(pack_t, part_ref, p, chunk)
        pieces = []
        for r in range(ranks):
            span = slice(r * slab, (r + 1) * slab)
            row = column_to_row(parts[span])
            pieces.append(rows[span, :128] + jnp.where(sub == rank_slots, row, 0.0))
        back_refs[p][:, :128] = jnp.concatenate(pieces, axis=0).astype(LOW)
        back_refs[p][:, 128:] = rows[:, 128:].astype(LOW)


def expert_grad_kernel(
    count, pack_t_ref, w_out_ref, rows_ref, act_ref, pre_grad_ref, gates_ref, up_rows_ref, *rest
):
    out_refs, (g_in_ref, g_out_ref, returned_ref) = rest[:count], rest[count:]
    local_experts = w_out_ref.shape[0]
    chunk = rows_ref.shape[1] // count
    pack_t = pack_t_ref[...]
    for e in range(local_experts):
        returned_ref[e] = dot(act_ref[e], w_out_ref[e]).astype(LOW)
    for p in range(count):
        out_refs[p][...] = unpack(pack_t, returned_ref, p, chunk).astype(LOW)
    for e in range(local_experts):
        g_in_ref[e] = dot(rows_ref[e], pre_grad_ref[e], TN)
        slot_grad = (up_rows_ref[e].astype(FULL) * gates_ref[e][:, :1]).astype(LOW)
        g_out_ref[e] = dot(act_ref[e], slot_grad, TN)


def joined(ref):
    ranks, slab, width = ref.shape
    return ref[...].astype(FULL).reshape(ranks * slab, width).astype(LOW)


def backward_kernel(
    places, rank_slots, tokens_ref, gain_ref, router_t_ref, hits_ref, mask_ref,
    up_ref, hidden_ref, chance_ref, heads_ref, weights_ref, onehot_ref, *rest
):
    count = len(places)
    piece_refs, rest = rest[:count], rest[count:]
    (back_ref, d_input_ref, small_ref, factors_ref,
     w_ref, turned_ref, grads_ref, bias_ref, sem) = rest
    ranks, width, columns = w_ref.shape
    copies = place_weights(places, piece_refs, w_ref, sem)
    cols = columns // 4
    head_count = weights_ref.shape[0]
    head = width // head_count
    factor = head ** (-0.5)
    length = tokens_ref.shape[0]
    slab = back_ref.shape[1]
    hidden = hidden_ref[...]
    gain_two = gain_ref[1:2, :]
    normed_two, scale_two = normalize(hidden, gain_two)
    mask = mask_ref[...]
    chance, hits = chance_ref[...], hits_ref[...]
    gate = jnp.sum(chance * hits, axis=1, keepdims=True)
    spread = [
        row_to_column(back_ref[r, :, :128].astype(FULL)[rank_slots : rank_slots + 1], slab)
        for r in range(ranks)
    ]
    gate_grad = dot(mask, jnp.concatenate(spread, axis=0).astype(LOW))[:, :1]
    logit_grad = chance * (hits - gate) * gate_grad
    experts = hits.shape[1]
    small_ref[:experts, :] = dot(logit_grad, normed_two, TN, HIGHEST)
    router_t = router_t_ref[...].astype(FULL)
    normed_two_grad = dot(logit_grad, router_t, precision=HIGHEST) + dot(mask, joined(back_ref))
    hidden_part, ffn_gain_grad = norm_back(hidden, scale_two, gain_two, normed_two_grad)
    hidden_grad = up_ref[...].astype(FULL) + hidden_part
    turned_ref[...] = hidden_grad.astype(LOW).astype(FULL).T
    for copy in copies:
        copy.wait()
    low_lane = 3 * cols // 128 * 128
    att_grad = None
    for e in range(ranks):
        own = turned_ref[e * cols : (e + 1) * cols, :]
        if 3 * cols > low_lane:
            own = jnp.concatenate([jnp.zeros((3 * cols - low_lane, 128), FULL), own], axis=0)
        part = dot(w_ref[e, :, low_lane:], own.astype(LOW))
        att_grad = part if att_grad is None else att_grad + part
    att_grad = att_grad.astype(LOW)
    for h in range(head_count):
        rows = slice(h * head, (h + 1) * head)
        own = att_grad[rows]
        weights = weights_ref[h]
        grads_ref[2, rows, :] = dot(own, weights.astype(LOW))
        prob_grad = dot(own, heads_ref[2, rows, :], TN)
        score_grad = weights * (prob_grad - jnp.sum(prob_grad * weights, axis=1, keepdims=True))
        score_grad = score_grad.astype(LOW)
        grads_ref[0, rows, :] = dot(heads_ref[1, rows, :], score_grad, NT) * factor
        grads_ref[1, rows, :] = dot(heads_ref[0, rows, :], score_grad) * factor
        wide = [jnp.zeros((length, length), FULL), score_grad.astype(FULL)]
        bias_ref[h : h + 1, :] = slid_sum(jnp.concatenate(wide, axis=1))
    total = None
    for e in range(ranks):
        span = slice(e * cols, (e + 1) * cols)
        held = [grads_ref[m, span, :] for m in range(3)] + [jnp.zeros((cols, 128), FULL)]
        part = dot(w_ref[e], jnp.concatenate(held, axis=0).astype(LOW))
        total = part if total is None else total + part
        sent = [grads_ref[m, span, :] for m in range(3)] + [turned_ref[span, :]]
        factors_ref[e] = jnp.concatenate(sent, axis=0).astype(LOW)
    inputs = tokens_ref[...].astype(FULL)
    gain_one = gain_ref[0:1, :]
    _, scale_one = normalize(inputs, gain_one)
    norm_part, attn_gain_grad = norm_back(inputs, scale_one, gain_one, total.T)
    d_input_ref[...] = hidden_grad + norm_part
    sums = dot(bias_ref[...], onehot_ref[...], NT, HIGHEST)
    small_ref[experts : experts + 1, :] = ffn_gain_grad
    small_ref[experts + 1 : experts + 2, :] = attn_gain_grad
    small_ref[experts + 2 :, :] = jnp.zeros((small_ref.shape[0] - experts - 2, width), FULL)
    small_ref[experts + 2 : experts + 2 + head_count, : sums.shape[1]] = sums


def product_kernel(
    dps, normed_ref, attended_ref, hidden_ref, chance_ref, hits_ref, mask_ref, factors_ref,
    returned_ref, output_ref, *rest
):
    piece_refs, total_ref = rest[:-1], rest[-1]
    ranks, columns, length = factors_ref.shape
    cols = columns // 4
    first, second = None, None
    for e in range(ranks):
        held = factors_ref[e].astype(FULL)
        part = dot(held[: 3 * cols].astype(LOW), normed_ref[e])
        first = part if first is None else first + part
        part = dot(held[3 * cols :].astype(LOW), attended_ref[e])
        second = part if second is None else second + part
    total = jnp.concatenate([first, second], axis=0).T
    rows = piece_refs[0].shape[0]
    for j in range(dps):
        total_ref[j] = total[j * rows : (j + 1) * rows]
    for j, ref in enumerate(piece_refs):
        ref[...] = total_ref[lax.axis_index("dp") ^ j].astype(LOW)
    gate = jnp.sum(chance_ref[...] * hits_ref[...], axis=1, keepdims=True)
    fetched = dot(mask_ref[...], joined(returned_ref))
    output_ref[...] = (hidden_ref[...] + gate * fetched).astype(LOW)


VMEM = pl.BlockSpec(memory_space=pltpu.VMEM)
ANY = pl.BlockSpec(memory_space=pl.ANY)
LIMIT = 60 * 1024 * 1024


def shaped(dtype, *shape):
    return jax.ShapeDtypeStruct(shape, dtype)


def call(kernel, name, out_shape, args, pieces=(), scratch=(), more=()):
    return pl.pallas_call(
        kernel,
        out_shape=tuple(out_shape),
        in_specs=[VMEM] * len(args) + [ANY] * len(pieces) + [VMEM] * len(more),
        out_specs=(VMEM,) * len(out_shape),
        scratch_shapes=list(scratch),
        compiler_params=pltpu.CompilerParams(vmem_limit_bytes=LIMIT),
        name=name,
    )(*args, *pieces, *more)


def per_device(
    tokens,
    seg_ids,
    routes,
    attn_gain,
    w_query,
    w_key,
    w_value,
    w_output,
    rel_bias,
    ffn_gain,
    w_router,
    w_in,
    w_out,
    d_out,
):
    length, model_width = tokens.shape
    bucket_count, head_count = rel_bias.shape
    experts_total = w_router.shape[1]
    local_experts, _, hidden_here = w_in.shape
    ranks, dps = lax.axis_size("expert"), lax.axis_size("dp")
    capacity = length * 5 // (4 * experts_total)
    rank_slots = local_experts * capacity
    slab = -(-(rank_slots + 1) // 8) * 8
    rows_here, columns_here = w_query.shape
    inner_width = dps * rows_here
    packed_rows = dps * ranks * capacity
    gains = jnp.stack([attn_gain, ffn_gain]).astype(FULL)
    slabs_shape = shaped(LOW, ranks, slab, model_width)
    router_t = w_router.T
    pack = packing(local_experts, ranks, capacity, slab)
    pack, pack_t = jnp.asarray(pack, LOW), jnp.asarray(pack.T, LOW)

    normed_low, hits, mask, mask_t, bias_full, up_slabs = call(
        functools.partial(early_kernel, ranks, local_experts, capacity, slab),
        "early",
        [
            shaped(LOW, length, model_width),
            shaped(FULL, length, experts_total),
            shaped(LOW, length, ranks * slab),
            shaped(LOW, ranks * slab, length),
            shaped(FULL, head_count, length, length),
            slabs_shape,
        ],
        [
            tokens,
            routes.reshape(1, length),
            gains,
            d_out,
            rel_bias.T,
            jnp.asarray(bucket_onehot(bucket_count, length), LOW),
        ],
    )

    payload = jnp.concatenate([w_query, w_key, w_value, w_output], axis=1)
    pieces, places, (normed_low, hits, mask, mask_t, bias_full, up_slabs) = gather_pieces(
        payload, (normed_low, hits, mask, mask_t, bias_full, up_slabs)
    )
    up_arrived = exchange(up_slabs).reshape(ranks * slab, model_width)
    pieces, normed_later, up_arrived = lax.optimization_barrier((pieces, normed_low, up_arrived))
    normed_all = lax.all_gather(normed_later, "expert", axis=0)

    w_shape = (ranks, inner_width, 4 * columns_here)
    heads, weights, attended, hidden, chance, slabs = call(
        functools.partial(forward_kernel, places, slab, rank_slots),
        "attention_forward",
        [
            shaped(LOW, 3, inner_width, length),
            shaped(FULL, head_count, length, length),
            shaped(LOW, length, inner_width),
            shaped(FULL, length, model_width),
            shaped(FULL, length, experts_total),
            slabs_shape,
        ],
        [tokens, normed_low, seg_ids, bias_full, gains, router_t, hits, mask_t],
        pieces,
        [
            pltpu.VMEM(w_shape, LOW),
            pltpu.VMEM((3, inner_width, length), FULL),
            pltpu.VMEM((inner_width, length), FULL),
            pltpu.SemaphoreType.DMA,
        ],
    )

    up_pieces = gather_list(up_arrived)
    row_pieces = gather_list(exchange(slabs).reshape(ranks * slab, model_width))
    attended_all = lax.all_gather(attended, "expert", axis=0)
    by_expert = (local_experts, packed_rows)
    up_rows, up_act = call(
        upstream_kernel,
        "upstream_rows",
        [shaped(LOW, *by_expert, model_width), shaped(FULL, *by_expert, hidden_here)],
        [pack, w_out, *up_pieces],
    )

    *back, slot_rows, activated, pre_grad, gates = call(
        functools.partial(expert_kernel, dps, slab, rank_slots),
        "experts",
        [shaped(LOW, ranks * slab, model_width)] * dps
        + [
            shaped(LOW, *by_expert, model_width),
            shaped(LOW, *by_expert, hidden_here),
            shaped(LOW, *by_expert, hidden_here),
            shaped(FULL, *by_expert, 128),
        ],
        [pack, pack_t, w_in, up_act, *row_pieces],
        scratch=[
            pltpu.VMEM((packed_rows, hidden_here), FULL),
            pltpu.VMEM((*by_expert, model_width), LOW),
            pltpu.VMEM((*by_expert, 128), LOW),
        ],
    )
    back = scatter_list(back).reshape(ranks, slab, model_width)
    back, activated = lax.optimization_barrier((back, activated))
    back = exchange(back)
    *returned, first_grad, second_grad = call(
        functools.partial(expert_grad_kernel, dps),
        "expert_gradients",
        [shaped(LOW, ranks * slab, model_width)] * dps
        + [shaped(FULL, *w_in.shape), shaped(FULL, *w_out.shape)],
        [pack_t, w_out, slot_rows, activated, pre_grad, gates, up_rows],
        scratch=[pltpu.VMEM((*by_expert, model_width), LOW)],
    )
    returned = scatter_list(returned).reshape(ranks, slab, model_width)

    small_rows = -(-(experts_total + 2 + head_count) // 8) * 8
    d_input, small, factors = call(
        functools.partial(backward_kernel, places, rank_slots),
        "attention_backward",
        [
            shaped(FULL, length, model_width),
            shaped(FULL, small_rows, model_width),
            shaped(LOW, ranks, 4 * columns_here, length),
        ],
        [
            tokens,
            gains,
            router_t,
            hits,
            mask,
            d_out,
            hidden,
            chance,
            heads,
            weights,
            jnp.asarray(bucket_onehot(bucket_count, length), FULL),
        ],
        pieces,
        [
            pltpu.VMEM(w_shape, LOW),
            pltpu.VMEM((inner_width, length), FULL),
            pltpu.VMEM((3, inner_width, length), FULL),
            pltpu.VMEM((head_count, 2 * length), FULL),
            pltpu.SemaphoreType.DMA,
        ],
        [back],
    )

    factors, returned = lax.optimization_barrier((factors, returned))
    factors = exchange(factors)
    returned = exchange(returned)
    small = all_sum(small)
    output, *grads = call(
        functools.partial(product_kernel, dps),
        "weight_gradients",
        [shaped(LOW, length, model_width)] + [shaped(LOW, rows_here, 4 * columns_here)] * dps,
        [normed_all, attended_all, hidden, chance, hits, mask, factors, returned],
        scratch=[pltpu.VMEM((dps, rows_here, 4 * columns_here), FULL)],
    )
    grads = scatter_list(grads, FULL)
    g_query, g_key, g_value, g_output = (
        grads[:, i * columns_here : (i + 1) * columns_here] for i in range(4)
    )
    g_router = small[:experts_total].T
    g_ffn_gain, g_attn_gain = small[experts_total], small[experts_total + 1]
    g_rel_bias = small[experts_total + 2 : experts_total + 2 + head_count, :bucket_count].T
    return (
        output,
        d_input,
        g_attn_gain,
        g_query,
        g_key,
        g_value,
        g_output,
        g_rel_bias,
        g_ffn_gain,
        g_router,
        first_grad,
        second_grad,
    )


def solution(mesh):
    return jax.shard_map(
        per_device,
        mesh=mesh,
        in_specs=(
            P(("dp", "expert"), None),
            P(("dp", "expert"), None),
            P(("dp", "expert"), None),
            P(),
            P("dp", "expert"),
            P("dp", "expert"),
            P("dp", "expert"),
            P("dp", "expert"),
            P(),
            P(),
            P(),
            P("expert", None, "dp"),
            P("expert", "dp", None),
            P(("dp", "expert"), None),
        ),
        out_specs=(
            P(("dp", "expert"), None),
            P(("dp", "expert"), None),
            P(),
            P("dp", "expert"),
            P("dp", "expert"),
            P("dp", "expert"),
            P("dp", "expert"),
            P(),
            P(),
            P(),
            P("expert", None, "dp"),
            P("expert", "dp", None),
        ),
        check_vma=False,
    )
```

```python
import functools

import jax
import jax.numpy as jnp
import numpy as np
from jax import lax
from jax.experimental import pallas as pl
from jax.experimental.pallas import tpu as pltpu
from jax.sharding import PartitionSpec as P

EPSILON = 1e-06
LIMITS = (12, 16, 23, 32, 46, 64, 91)
MASKED = -1000000000.0
HIGHEST = lax.Precision.HIGHEST
LOW = jnp.bfloat16
FULL = jnp.float32


def bucket_onehot(buckets, length):
    delta = np.arange(2 * length) - length
    magnitude = np.abs(delta)
    distant = 8 + sum((magnitude >= threshold).astype(np.int32) for threshold in LIMITS)
    ids = np.where(delta > 0, 16, 0) + np.where(magnitude < 8, magnitude, distant)
    return (ids[None, :] == np.arange(buckets)[:, None]).astype(np.float32)


def packing(local_experts, ranks, capacity, slab):
    table = np.zeros((local_experts, ranks, capacity, ranks, slab), np.float32)
    for e in range(local_experts):
        for r in range(ranks):
            for c in range(capacity):
                table[e, r, c, r, e * capacity + c] = 1.0
    return table.reshape(local_experts * ranks * capacity, ranks * slab)


def normalize(matrix, gain_vec):
    scale = lax.rsqrt(jnp.mean(matrix * matrix, axis=-1, keepdims=True) + EPSILON)
    return (matrix * scale * gain_vec, scale)


def norm_back(matrix, scale, gain_vec, incoming):
    weighted = incoming * gain_vec
    average = jnp.mean(matrix * weighted, axis=-1, keepdims=True)
    return (
        scale * weighted - matrix * (scale * scale * scale) * average,
        jnp.sum(incoming * matrix * scale, axis=0, keepdims=True),
    )


def swap(value, axis, mask):
    count = lax.axis_size(axis)
    return lax.ppermute(value, axis, [(i, i ^ mask) for i in range(count)])


def gather_bits(value, axis, masks):
    return jnp.concatenate([value] + [swap(value, axis, mask) for mask in masks], axis=0)


def exchange(value):
    return lax.all_to_all(value, "expert", split_axis=0, concat_axis=0, tiled=True)


def gather_far(value):
    found = {0: value}
    bit = lax.axis_size("dp") // 2
    while bit > 1:
        found.update({index ^ bit: swap(item, "dp", bit) for index, item in found.items()})
        bit = bit // 2
    return found


def gather_near(found):
    found = {**found, **{index ^ 1: swap(item, "dp", 1) for index, item in found.items()}}
    return [found[index] for index in range(len(found))]


def add(left, right, dtype=LOW):
    return (left.astype(FULL) + right.astype(FULL)).astype(dtype)


def scatter_terms(items):
    bit = 1
    while len(items) > 2:
        taken = [swap(item, "dp", bit) for item in items[1::2]]
        items = [add(kept, got) for kept, got in zip(items[0::2], taken)]
        bit = bit * 2
    return items[0], swap(items[1], "dp", bit)


def all_sum(value):
    for axis in ("dp", "expert"):
        bit = 1
        while bit < lax.axis_size(axis):
            value = value + swap(value, axis, bit)
            bit = bit * 2
    return value


def together(*values):
    return lax.optimization_barrier(values)


def gather_pieces(payload, early, up_slabs):
    ranks, dps = lax.axis_size("expert"), lax.axis_size("dp")
    half = payload.shape[0] // 2
    far = list(range(0, ranks, 2))
    sides = {"x": ("expert", [0, 1]), "y": ("dp", list(range(0, dps, 2)))}
    values = [
        gather_bits(payload[index * half : (index + 1) * half][None], "expert", far[1:])
        for index in range(2)
    ]
    values, early = together(values, early)
    firsts = []
    for value, letter in zip(values, "xy"):
        axis, masks = sides[letter]
        firsts.append(gather_bits(value[None], axis, masks[1:]))
    firsts, up_slabs = together(firsts, up_slabs)
    up_arrived = exchange(up_slabs)
    seconds = []
    for value, letter in zip(firsts, "yx"):
        axis, masks = sides[letter]
        seconds.append([swap(value, axis, mask) for mask in masks[1:]])
    others = [swap(value, "dp", 1) for value in firsts]
    seconds, others, up_arrived = together(seconds, others, up_arrived)
    pieces, places = [], []
    for index, order in enumerate(("xy", "yx")):
        masks, other_masks = sides[order[0]][1], sides[order[1]][1]
        found = [(firsts[index], 0, 0), (others[index], 0, 1)]
        for value, mask in zip(seconds[index], other_masks[1:]):
            found += [(value, mask, 0), (swap(value, "dp", 1), mask, 1)]
        for piece, mask, core in found:
            offsets = []
            for first in masks:
                for low in far:
                    x_mask, y_mask = (first, mask) if order == "xy" else (mask, first)
                    offsets.append((low ^ x_mask, y_mask ^ core))
            pieces.append(piece)
            places.append((index, offsets))
    return pieces, places, early, up_arrived


def place_weights(places, piece_refs, w_ref, sem):
    my_expert, my_dp = lax.axis_index("expert"), lax.axis_index("dp")
    copies = []
    for ref, (half, offsets) in zip(piece_refs, places):
        low_count, rows = ref.shape[1], ref.shape[2]
        for index, (e_mask, d_mask) in enumerate(offsets):
            start = (my_dp ^ d_mask) * (2 * rows) + half * rows
            copies.append(
                pltpu.make_async_copy(
                    ref.at[index // low_count, index % low_count],
                    w_ref.at[my_expert ^ e_mask, pl.ds(pl.multiple_of(start, 16), rows), :],
                    sem,
                )
            )
    for copy in copies:
        copy.start()
    return copies


def dot(left, right, dims=((1,), (0,)), precision=None):
    return lax.dot_general(
        left, right, (dims, ((), ())), precision=precision, preferred_element_type=FULL
    )


NT = ((1,), (1,))
TN = ((0,), (0,))


def grid_of(rows):
    sub = lax.broadcasted_iota(jnp.int32, (rows, 128), 0)
    lane = lax.broadcasted_iota(jnp.int32, (rows, 128), 1)
    return sub, lane


def row_to_column(row, rows, shift=0):
    sub, lane = grid_of(rows)
    column = jnp.sum(jnp.where(lane == sub + shift, row, 0.0), axis=1, keepdims=True)
    return jnp.broadcast_to(column, (rows, 128))


def column_to_row(column, shift=0):
    sub, lane = grid_of(column.shape[0])
    return jnp.sum(jnp.where(lane == sub + shift, column, 0.0), axis=0, keepdims=True)


def turn(value, shift):
    return pltpu.roll(value, shift % value.shape[1], 1)


def slide(value, direction):
    sub = lax.broadcasted_iota(jnp.int32, value.shape, 0)
    for bit in (1, 2, 4):
        value = jnp.where((sub & bit) != 0, turn(value, direction * bit), value)
    return value


def slid_rows(row, count):
    value = slide(jnp.broadcast_to(row, (8, row.shape[1])), 1)
    while value.shape[0] < count:
        value = jnp.concatenate([value, turn(value, value.shape[0])], axis=0)
    return value


def slid_sum(value):
    while value.shape[0] > 8:
        half = value.shape[0] // 2
        value = value[:half] + turn(value[half:], -half)
    return jnp.sum(slide(value, -1), axis=0, keepdims=True)


def early_kernel(
    ranks, local_experts, capacity, slab, tokens_ref, routes_ref, gain_ref, d_out_ref, table_ref,
    onehot_ref, normed_ref, hits_ref, mask_ref, mask_t_ref, bias_ref, up_ref
):
    length = tokens_ref.shape[0]
    normed, _ = normalize(tokens_ref[...].astype(FULL), gain_ref[0:1, :])
    normed_ref[...] = normed.astype(LOW)
    experts = hits_ref.shape[1]
    routes = jnp.broadcast_to(routes_ref[...].astype(FULL), (length, length)).T
    route = routes[:, :1].astype(jnp.int32)
    lanes = lax.broadcasted_iota(jnp.int32, (length, experts), 1)
    hits = (lanes == route).astype(FULL)
    hits_ref[...] = hits
    row = lax.broadcasted_iota(jnp.int32, (length, length), 0)
    col = lax.broadcasted_iota(jnp.int32, (length, length), 1)
    before = dot((col < row).astype(FULL).astype(LOW), hits.astype(LOW))
    placed = jnp.sum(before * hits, axis=1, keepdims=True).astype(jnp.int32)
    rank = jnp.zeros_like(route)
    for r in range(1, ranks):
        rank = rank + (route >= r * local_experts).astype(jnp.int32)
    spot = rank * slab + (route - rank * local_experts) * capacity + placed
    spot = jnp.where(placed < capacity, spot, -1)
    places = lax.broadcasted_iota(jnp.int32, (length, ranks * slab), 1)
    mask = (places == spot).astype(FULL)
    mask_ref[...] = mask.astype(LOW)
    mask_t = mask.T.astype(LOW)
    mask_t_ref[...] = mask_t
    slabs = dot(mask_t, d_out_ref[...])
    for r in range(ranks):
        up_ref[r] = slabs[r * slab : (r + 1) * slab].astype(LOW)
    values = dot(table_ref[...], onehot_ref[...])
    for h in range(bias_ref.shape[0]):
        bias_ref[h] = slid_rows(values[h : h + 1], length)[:, length:]


def forward_kernel(
    places, slab, rank_slots, tokens_ref, normed_ref, seg_ref, bias_ref, gain_ref,
    router_t_ref, hits_ref, mask_t_ref, *rest
):
    count = len(places)
    piece_refs, rest = rest[:count], rest[count:]
    heads_ref, weights_ref, attended_ref, hidden_ref, chance_ref = rest[:5]
    slabs_ref = rest[5]
    w_ref, qkv_ref, att_t_ref, sem = rest[-4:]
    copies = place_weights(places, piece_refs, w_ref, sem)
    ranks, width, columns = w_ref.shape
    cols = columns // 4
    head_count = weights_ref.shape[0]
    head = width // head_count
    length = tokens_ref.shape[0]
    segments = jnp.broadcast_to(seg_ref[...].astype(FULL), (length, length))
    same_doc = segments == segments.T
    normed = normed_ref[...]
    for copy in copies:
        copy.wait()
    for e in range(ranks):
        turned = dot(normed, w_ref[e]).T
        for m in range(3):
            qkv_ref[m, e * cols : (e + 1) * cols, :] = turned[m * cols : (m + 1) * cols]
    heads_ref[...] = qkv_ref[...].astype(LOW)
    for h in range(head_count):
        rows = slice(h * head, (h + 1) * head)
        scores = dot(heads_ref[0, rows, :], heads_ref[1, rows, :], TN) * head ** (-0.5)
        scores = jnp.where(same_doc, scores + bias_ref[h], MASKED)
        grown = jnp.exp(scores - jnp.max(scores, axis=1, keepdims=True))
        weights = grown / jnp.sum(grown, axis=1, keepdims=True)
        weights_ref[h] = weights
        att_t_ref[rows, :] = dot(heads_ref[2, rows, :], weights.astype(LOW), NT)
    attended = att_t_ref[...].T.astype(LOW)
    attended_ref[...] = attended
    low_lane = 3 * cols // 128 * 128
    for e in range(ranks):
        turned = dot(attended, w_ref[e, :, low_lane:]).T
        att_t_ref[e * cols : (e + 1) * cols, :] = turned[3 * cols - low_lane :]
    hidden = tokens_ref[...].astype(FULL) + att_t_ref[...].T
    hidden_ref[...] = hidden
    normed_two, _ = normalize(hidden, gain_ref[1:2, :])
    logits = dot(normed_two, router_t_ref[...].astype(FULL), NT, HIGHEST)
    grown = jnp.exp(logits - jnp.max(logits, axis=1, keepdims=True))
    chance = grown / jnp.sum(grown, axis=1, keepdims=True)
    chance_ref[...] = chance
    gate = jnp.sum(chance * hits_ref[...], axis=1, keepdims=True)
    mask_t = mask_t_ref[...]
    slots = dot(mask_t, normed_two.astype(LOW))
    gates = dot(mask_t.astype(FULL), jnp.broadcast_to(gate, (length, 128)), precision=HIGHEST)
    sub, _ = grid_of(slab)
    for r in range(ranks):
        mine = gates[r * slab : (r + 1) * slab]
        high = mine.astype(LOW).astype(FULL)
        row = column_to_row(high) + column_to_row(mine - high, 64)
        rows = slots[r * slab : (r + 1) * slab]
        start = rows[:, :128] + jnp.where(sub == rank_slots, row, 0.0)
        slabs_ref[r, :, :128] = start.astype(LOW)
        slabs_ref[r, :, 128:] = rows[:, 128:].astype(LOW)


def upstream_kernel(pack_ref, w_out_ref, *rest):
    piece_refs, (rows_ref, act_ref) = rest[:-2], rest[-2:]
    local_experts = w_out_ref.shape[0]
    chunk = pack_ref.shape[0] // local_experts
    for p, piece in enumerate(piece_refs):
        packed = dot(pack_ref[...], piece[...]).astype(LOW)
        for e in range(local_experts):
            rows_ref[e, p * chunk : (p + 1) * chunk, :] = packed[e * chunk : (e + 1) * chunk]
    for e in range(local_experts):
        act_ref[e] = dot(rows_ref[e], w_out_ref[e], NT)


def unpack(pack_t, rows_ref, p, chunk):
    rows = [rows_ref[e, p * chunk : (p + 1) * chunk, :] for e in range(rows_ref.shape[0])]
    return dot(pack_t, jnp.concatenate(rows, axis=0))


def expert_kernel(
    count, slab, rank_slots, pack_ref, pack_t_ref, w_in_ref, up_act_ref, *rest
):
    piece_refs, rest = rest[:count], rest[count:]
    back_refs, rest = rest[:count], rest[count:]
    rows_ref, act_ref, pre_grad_ref, gates_ref, pre_ref, back_ref, part_ref = rest
    local_experts = w_in_ref.shape[0]
    chunk = pack_ref.shape[0] // local_experts
    ranks = pack_ref.shape[1] // slab
    pack, pack_t = pack_ref[...], pack_t_ref[...]
    for p, piece in enumerate(piece_refs):
        packed = dot(pack, piece[...]).astype(LOW)
        tile = piece[:, :128].astype(FULL)
        spread = []
        for shift in (0, 64):
            columns = [
                row_to_column(tile[r * slab + rank_slots : r * slab + rank_slots + 1], slab, shift)
                for r in range(ranks)
            ]
            spread.append(dot(pack, jnp.concatenate(columns, axis=0).astype(LOW)))
        gates = spread[0] + spread[1]
        for e in range(local_experts):
            rows_ref[e, p * chunk : (p + 1) * chunk, :] = packed[e * chunk : (e + 1) * chunk]
            gates_ref[e, p * chunk : (p + 1) * chunk, :] = gates[e * chunk : (e + 1) * chunk]
    root = np.float32(np.sqrt(2.0 / np.pi))
    step = 16
    for e in range(local_experts):
        pre_ref[...] = dot(rows_ref[e], w_in_ref[e])

        def body(index, carry):
            span = pl.ds(pl.multiple_of(index * step, step), step)
            pre = pre_ref[span, :]
            up = up_act_ref[e, span, :]
            square = pre * pre
            curve = jnp.tanh(root * pre * (1.0 + 0.044715 * square))
            rise = 0.5 + 0.5 * curve
            act = (pre * rise).astype(LOW)
            act_ref[e, span, :] = act
            slope = rise + pre * (rise * (1.0 - curve)) * (root + 3 * 0.044715 * root * square)
            gate = gates_ref[e, span, :][:, :1]
            pre_grad_ref[e, span, :] = (slope * (up * gate)).astype(LOW)
            part = jnp.sum(act.astype(FULL) * up, axis=1, keepdims=True)
            part_ref[e, span, :] = jnp.broadcast_to(part, (step, 128)).astype(LOW)
            return carry

        lax.fori_loop(0, pre_ref.shape[0] // step, body, 0, unroll=2)
        back_ref[e] = dot(pre_grad_ref[e], w_in_ref[e], NT).astype(LOW)
    sub, _ = grid_of(slab)
    for p in range(count):
        rows = unpack(pack_t, back_ref, p, chunk)
        parts = unpack(pack_t, part_ref, p, chunk)
        pieces = []
        for r in range(ranks):
            span = slice(r * slab, (r + 1) * slab)
            row = column_to_row(parts[span])
            pieces.append(rows[span, :128] + jnp.where(sub == rank_slots, row, 0.0))
        back_refs[p][:, :128] = jnp.concatenate(pieces, axis=0).astype(LOW)
        back_refs[p][:, 128:] = rows[:, 128:].astype(LOW)


def expert_out_kernel(pack_t_ref, w_out_ref, act_ref, *rest):
    out_refs, returned_ref = rest[:-1], rest[-1]
    chunk = act_ref.shape[1] // len(out_refs)
    for e in range(w_out_ref.shape[0]):
        returned_ref[e] = dot(act_ref[e], w_out_ref[e]).astype(LOW)
    for p, ref in enumerate(out_refs):
        ref[...] = unpack(pack_t_ref[...], returned_ref, p, chunk).astype(LOW)


def expert_grad_kernel(
    rows_ref, act_ref, pre_grad_ref, gates_ref, up_rows_ref, g_in_ref, g_out_ref, token_ref
):
    for e in range(rows_ref.shape[0]):
        g_in_ref[e] = dot(rows_ref[e], pre_grad_ref[e], TN)
        slot_grad = (up_rows_ref[e].astype(FULL) * gates_ref[e][:, :1]).astype(LOW)
        g_out_ref[e] = dot(act_ref[e], slot_grad, TN)
    token_ref[...] = jnp.zeros(token_ref.shape, FULL)


def joined(ref):
    ranks, slab, width = ref.shape
    return ref[...].astype(FULL).reshape(ranks * slab, width).astype(LOW)


def backward_kernel(
    places, rank_slots, tokens_ref, gain_ref, router_t_ref, hits_ref, mask_ref,
    up_ref, hidden_ref, chance_ref, heads_ref, weights_ref, onehot_ref, token_ref, *rest
):
    count = len(places)
    piece_refs, rest = rest[:count], rest[count:]
    (back_ref, d_input_ref, small_ref, factors_ref,
     w_ref, turned_ref, grads_ref, bias_ref, sem) = rest
    ranks, width, columns = w_ref.shape
    copies = place_weights(places, piece_refs, w_ref, sem)
    cols = columns // 4
    head_count = weights_ref.shape[0]
    head = width // head_count
    factor = head ** (-0.5)
    length = tokens_ref.shape[0]
    slab = back_ref.shape[1]
    hidden = hidden_ref[...]
    gain_two = gain_ref[1:2, :]
    normed_two, scale_two = normalize(hidden, gain_two)
    mask = mask_ref[...]
    chance, hits = chance_ref[...], hits_ref[...]
    gate = jnp.sum(chance * hits, axis=1, keepdims=True)
    spread = [
        row_to_column(back_ref[r, :, :128].astype(FULL)[rank_slots : rank_slots + 1], slab)
        for r in range(ranks)
    ]
    gate_grad = dot(mask, jnp.concatenate(spread, axis=0).astype(LOW))[:, :1]
    logit_grad = chance * (hits - gate) * gate_grad
    experts = hits.shape[1]
    small_ref[:experts, :] = dot(logit_grad, normed_two, TN, HIGHEST)
    router_t = router_t_ref[...].astype(FULL)
    normed_two_grad = dot(logit_grad, router_t, precision=HIGHEST) + dot(mask, joined(back_ref))
    hidden_part, ffn_gain_grad = norm_back(hidden, scale_two, gain_two, normed_two_grad)
    hidden_grad = up_ref[...].astype(FULL) + hidden_part
    turned_ref[...] = hidden_grad.astype(LOW).astype(FULL).T
    for copy in copies:
        copy.wait()
    low_lane = 3 * cols // 128 * 128
    att_grad = None
    for e in range(ranks):
        own = turned_ref[e * cols : (e + 1) * cols, :]
        if 3 * cols > low_lane:
            own = jnp.concatenate([jnp.zeros((3 * cols - low_lane, 128), FULL), own], axis=0)
        part = dot(w_ref[e, :, low_lane:], own.astype(LOW))
        att_grad = part if att_grad is None else att_grad + part
    att_grad = att_grad.astype(LOW)
    for h in range(head_count):
        rows = slice(h * head, (h + 1) * head)
        own = att_grad[rows]
        weights = weights_ref[h]
        grads_ref[2, rows, :] = dot(own, weights.astype(LOW))
        prob_grad = dot(own, heads_ref[2, rows, :], TN)
        score_grad = weights * (prob_grad - jnp.sum(prob_grad * weights, axis=1, keepdims=True))
        score_grad = score_grad.astype(LOW)
        grads_ref[0, rows, :] = dot(heads_ref[1, rows, :], score_grad, NT) * factor
        grads_ref[1, rows, :] = dot(heads_ref[0, rows, :], score_grad) * factor
        wide = [jnp.zeros((length, length), FULL), score_grad.astype(FULL)]
        bias_ref[h : h + 1, :] = slid_sum(jnp.concatenate(wide, axis=1))
    total = None
    for e in range(ranks):
        span = slice(e * cols, (e + 1) * cols)
        held = [grads_ref[m, span, :] for m in range(3)] + [jnp.zeros((cols, 128), FULL)]
        part = dot(w_ref[e], jnp.concatenate(held, axis=0).astype(LOW))
        total = part if total is None else total + part
        sent = [grads_ref[m, span, :] for m in range(3)] + [turned_ref[span, :]]
        factors_ref[e] = jnp.concatenate(sent, axis=0).astype(LOW)
    inputs = tokens_ref[...].astype(FULL)
    gain_one = gain_ref[0:1, :]
    _, scale_one = normalize(inputs, gain_one)
    norm_part, attn_gain_grad = norm_back(inputs, scale_one, gain_one, total.T)
    d_input_ref[...] = hidden_grad + norm_part
    sums = dot(bias_ref[...], onehot_ref[...], NT, HIGHEST)
    small_ref[experts : experts + 1, :] = ffn_gain_grad
    small_ref[experts + 1 : experts + 2, :] = attn_gain_grad
    small_ref[experts + 2 :, :] = jnp.zeros((small_ref.shape[0] - experts - 2, width), FULL)
    for h in range(head_count):
        line, place = experts + 2 + h // 6, 128 * (h % 6)
        small_ref[line : line + 1, place : place + sums.shape[1]] = sums[h : h + 1]


def product_kernel(
    dps, normed_ref, attended_ref, hidden_ref, chance_ref, hits_ref, mask_ref, factors_ref,
    returned_ref, output_ref, *rest
):
    piece_refs, total_ref = rest[:-1], rest[-1]
    ranks, columns, length = factors_ref.shape
    cols = columns // 4
    first, second = None, None
    for e in range(ranks):
        held = factors_ref[e].astype(FULL)
        part = dot(held[: 3 * cols].astype(LOW), normed_ref[e])
        first = part if first is None else first + part
        part = dot(held[3 * cols :].astype(LOW), attended_ref[e])
        second = part if second is None else second + part
    total = jnp.concatenate([first, second], axis=0).T
    rows = piece_refs[0].shape[0]
    for j in range(dps):
        total_ref[j] = total[j * rows : (j + 1) * rows]
    for j, ref in enumerate(piece_refs):
        ref[...] = total_ref[lax.axis_index("dp") ^ j].astype(LOW)
    gate = jnp.sum(chance_ref[...] * hits_ref[...], axis=1, keepdims=True)
    fetched = dot(mask_ref[...], joined(returned_ref))
    output_ref[...] = (hidden_ref[...] + gate * fetched).astype(LOW)


VMEM = pl.BlockSpec(memory_space=pltpu.VMEM)
ANY = pl.BlockSpec(memory_space=pl.ANY)
LIMIT = 60 * 1024 * 1024


def shaped(dtype, *shape):
    return jax.ShapeDtypeStruct(shape, dtype)


def call(kernel, name, micros, out_shape, args, pieces=(), scratch=(), more=()):
    return pl.pallas_call(
        kernel,
        out_shape=tuple(out_shape),
        in_specs=[VMEM] * len(args) + [ANY] * len(pieces) + [VMEM] * len(more),
        out_specs=(VMEM,) * len(out_shape),
        scratch_shapes=list(scratch),
        compiler_params=pltpu.CompilerParams(vmem_limit_bytes=LIMIT),
        cost_estimate=pl.CostEstimate(
            flops=0, bytes_accessed=micros * 3_600_000, transcendentals=0
        ),
        name=name,
    )(*args, *pieces, *more)


def per_device(
    tokens,
    seg_ids,
    routes,
    attn_gain,
    w_query,
    w_key,
    w_value,
    w_output,
    rel_bias,
    ffn_gain,
    w_router,
    w_in,
    w_out,
    d_out,
):
    length, model_width = tokens.shape
    bucket_count, head_count = rel_bias.shape
    experts_total = w_router.shape[1]
    local_experts, _, hidden_here = w_in.shape
    ranks, dps = lax.axis_size("expert"), lax.axis_size("dp")
    capacity = length * 5 // (4 * experts_total)
    rank_slots = local_experts * capacity
    slab = -(-(rank_slots + 1) // 8) * 8
    rows_here, columns_here = w_query.shape
    inner_width = dps * rows_here
    packed_rows = dps * ranks * capacity
    gains = jnp.stack([attn_gain, ffn_gain]).astype(FULL)
    slabs_shape = shaped(LOW, ranks, slab, model_width)
    router_t = w_router.T
    pack = packing(local_experts, ranks, capacity, slab)
    pack, pack_t = jnp.asarray(pack, LOW), jnp.asarray(pack.T, LOW)

    normed_low, hits, mask, mask_t, bias_full, up_slabs = call(
        functools.partial(early_kernel, ranks, local_experts, capacity, slab),
        "early",
        3,
        [
            shaped(LOW, length, model_width),
            shaped(FULL, length, experts_total),
            shaped(LOW, length, ranks * slab),
            shaped(LOW, ranks * slab, length),
            shaped(FULL, head_count, length, length),
            slabs_shape,
        ],
        [
            tokens,
            routes.reshape(1, length),
            gains,
            d_out,
            rel_bias.T,
            jnp.asarray(bucket_onehot(bucket_count, length), LOW),
        ],
    )

    payload = jnp.concatenate([w_query, w_key, w_value, w_output], axis=1)
    early = (normed_low, hits, mask, mask_t, bias_full)
    pieces, places, early, up_arrived = gather_pieces(payload, early, up_slabs)
    normed_low, hits, mask, mask_t, bias_full = early
    pieces, normed_later = together(pieces, normed_low)
    normed_all = lax.all_gather(normed_later, "expert", axis=0)
    up_far = gather_far(up_arrived.reshape(ranks * slab, model_width))

    w_shape = (ranks, inner_width, 4 * columns_here)
    heads, weights, attended, hidden, chance, slabs = call(
        functools.partial(forward_kernel, places, slab, rank_slots),
        "attention_forward",
        10,
        [
            shaped(LOW, 3, inner_width, length),
            shaped(FULL, head_count, length, length),
            shaped(LOW, length, inner_width),
            shaped(FULL, length, model_width),
            shaped(FULL, length, experts_total),
            slabs_shape,
        ],
        [tokens, normed_low, seg_ids, bias_full, gains, router_t, hits, mask_t],
        pieces,
        [
            pltpu.VMEM(w_shape, LOW),
            pltpu.VMEM((3, inner_width, length), FULL),
            pltpu.VMEM((inner_width, length), FULL),
            pltpu.SemaphoreType.DMA,
        ],
    )

    slabs, up_far = together(slabs, up_far)
    arrived = exchange(slabs).reshape(ranks * slab, model_width)
    attended_all = lax.all_gather(attended, "expert", axis=0)
    up_pieces = gather_near(up_far)
    by_expert = (local_experts, packed_rows)
    up_rows, up_act = call(
        upstream_kernel,
        "upstream_rows",
        5,
        [shaped(LOW, *by_expert, model_width), shaped(FULL, *by_expert, hidden_here)],
        [pack, w_out, *up_pieces],
    )
    arrived, up_act = together(arrived, up_act)
    row_pieces = gather_near(gather_far(arrived))

    *back, slot_rows, activated, pre_grad, gates = call(
        functools.partial(expert_kernel, dps, slab, rank_slots),
        "experts",
        10,
        [shaped(LOW, ranks * slab, model_width)] * dps
        + [
            shaped(LOW, *by_expert, model_width),
            shaped(LOW, *by_expert, hidden_here),
            shaped(LOW, *by_expert, hidden_here),
            shaped(FULL, *by_expert, 128),
        ],
        [pack, pack_t, w_in, up_act, *row_pieces],
        scratch=[
            pltpu.VMEM((packed_rows, hidden_here), FULL),
            pltpu.VMEM((*by_expert, model_width), LOW),
            pltpu.VMEM((*by_expert, 128), LOW),
        ],
    )
    kept, got = scatter_terms(back)
    first_grad, second_grad, token = call(
        expert_grad_kernel,
        "expert_gradients",
        8,
        [shaped(FULL, *w_in.shape), shaped(FULL, *w_out.shape), shaped(FULL, 8, 128)],
        [slot_rows, activated, pre_grad, gates, up_rows],
    )
    got, token = together(got, token)
    back = add(kept, got).reshape(ranks, slab, model_width)
    back, activated = together(back, activated)
    back = exchange(back)
    returned = call(
        expert_out_kernel,
        "expert_outputs",
        3,
        [shaped(LOW, ranks * slab, model_width)] * dps,
        [pack_t, w_out, activated],
        scratch=[pltpu.VMEM((*by_expert, model_width), LOW)],
    )
    returned = add(*scatter_terms(returned)).reshape(ranks, slab, model_width)
    back, returned = together(back, returned)
    returned = exchange(returned)

    bias_rows = -(-head_count // 6)
    small_rows = -(-(experts_total + 2 + bias_rows) // 8) * 8
    d_input, small, factors = call(
        functools.partial(backward_kernel, places, rank_slots),
        "attention_backward",
        12,
        [
            shaped(FULL, length, model_width),
            shaped(FULL, small_rows, model_width),
            shaped(LOW, ranks, 4 * columns_here, length),
        ],
        [
            tokens,
            gains,
            router_t,
            hits,
            mask,
            d_out,
            hidden,
            chance,
            heads,
            weights,
            jnp.asarray(bucket_onehot(bucket_count, length), FULL),
            token,
        ],
        pieces,
        [
            pltpu.VMEM(w_shape, LOW),
            pltpu.VMEM((inner_width, length), FULL),
            pltpu.VMEM((3, inner_width, length), FULL),
            pltpu.VMEM((head_count, 2 * length), FULL),
            pltpu.SemaphoreType.DMA,
        ],
        [back],
    )

    factors, small, returned = together(factors, small, returned)
    factors = exchange(factors)
    factors, small = together(factors, all_sum(small))
    output, *grads = call(
        functools.partial(product_kernel, dps),
        "weight_gradients",
        5,
        [shaped(LOW, length, model_width)] + [shaped(LOW, rows_here, 4 * columns_here)] * dps,
        [normed_all, attended_all, hidden, chance, hits, mask, factors, returned],
        scratch=[pltpu.VMEM((dps, rows_here, 4 * columns_here), FULL)],
    )
    grads = add(*scatter_terms(grads), FULL)
    g_query, g_key, g_value, g_output = (
        grads[:, i * columns_here : (i + 1) * columns_here] for i in range(4)
    )
    g_router = small[:experts_total].T
    g_ffn_gain, g_attn_gain = small[experts_total], small[experts_total + 1]
    g_rel_bias = small[experts_total + 2 : experts_total + 2 + bias_rows].reshape(-1, 128)
    g_rel_bias = g_rel_bias[:head_count, :bucket_count].T
    return (
        output,
        d_input,
        g_attn_gain,
        g_query,
        g_key,
        g_value,
        g_output,
        g_rel_bias,
        g_ffn_gain,
        g_router,
        first_grad,
        second_grad,
    )


def solution(mesh):
    return jax.shard_map(
        per_device,
        mesh=mesh,
        in_specs=(
            P(("dp", "expert"), None),
            P(("dp", "expert"), None),
            P(("dp", "expert"), None),
            P(),
            P("dp", "expert"),
            P("dp", "expert"),
            P("dp", "expert"),
            P("dp", "expert"),
            P(),
            P(),
            P(),
            P("expert", None, "dp"),
            P("expert", "dp", None),
            P(("dp", "expert"), None),
        ),
        out_specs=(
            P(("dp", "expert"), None),
            P(("dp", "expert"), None),
            P(),
            P("dp", "expert"),
            P("dp", "expert"),
            P("dp", "expert"),
            P("dp", "expert"),
            P(),
            P(),
            P(),
            P("expert", None, "dp"),
            P("expert", "dp", None),
        ),
        check_vma=False,
    )
```

```python
import functools

import jax
import jax.numpy as jnp
import numpy as np
from jax import lax
from jax.experimental import pallas as pl
from jax.experimental.pallas import tpu as pltpu
from jax.sharding import PartitionSpec as P

EPSILON = 1e-06
LIMITS = (12, 16, 23, 32, 46, 64, 91)
MASKED = -1000000000.0
HIGHEST = lax.Precision.HIGHEST
LOW = jnp.bfloat16
FULL = jnp.float32


def bucket_onehot(buckets, length):
    delta = np.arange(2 * length) - length
    magnitude = np.abs(delta)
    distant = 8 + sum((magnitude >= threshold).astype(np.int32) for threshold in LIMITS)
    ids = np.where(delta > 0, 16, 0) + np.where(magnitude < 8, magnitude, distant)
    return (ids[None, :] == np.arange(buckets)[:, None]).astype(np.float32)


def packing(local_experts, ranks, capacity, slab):
    table = np.zeros((local_experts, ranks, capacity, ranks, slab), np.float32)
    for e in range(local_experts):
        for r in range(ranks):
            for c in range(capacity):
                table[e, r, c, r, e * capacity + c] = 1.0
    return table.reshape(local_experts * ranks * capacity, ranks * slab)


def normalize(matrix, gain_vec):
    scale = lax.rsqrt(jnp.mean(matrix * matrix, axis=-1, keepdims=True) + EPSILON)
    return (matrix * scale * gain_vec, scale)


def norm_back(matrix, scale, gain_vec, incoming):
    weighted = incoming * gain_vec
    average = jnp.mean(matrix * weighted, axis=-1, keepdims=True)
    return (
        scale * weighted - matrix * (scale * scale * scale) * average,
        jnp.sum(incoming * matrix * scale, axis=0, keepdims=True),
    )


def swap(value, axis, mask):
    count = lax.axis_size(axis)
    return lax.ppermute(value, axis, [(i, i ^ mask) for i in range(count)])


def gather_bits(value, axis, masks):
    return jnp.concatenate([value] + [swap(value, axis, mask) for mask in masks], axis=0)


def exchange(value):
    return lax.all_to_all(value, "expert", split_axis=0, concat_axis=0, tiled=True)


def gather_far(value):
    found = {0: value}
    bit = lax.axis_size("dp") // 2
    while bit > 1:
        found.update({index ^ bit: swap(item, "dp", bit) for index, item in found.items()})
        bit = bit // 2
    return found


def gather_near(found):
    found = {**found, **{index ^ 1: swap(item, "dp", 1) for index, item in found.items()}}
    return [found[index] for index in range(len(found))]


def add(left, right, dtype=LOW):
    return (left.astype(FULL) + right.astype(FULL)).astype(dtype)


def scatter_terms(items):
    bit = 1
    while len(items) > 2:
        taken = [swap(item, "dp", bit) for item in items[1::2]]
        items = [add(kept, got) for kept, got in zip(items[0::2], taken)]
        bit = bit * 2
    return items[0], swap(items[1], "dp", bit)


def sum_steps():
    steps = []
    for axis in ("dp", "expert"):
        bit = 1
        while bit < lax.axis_size(axis):
            steps.append((axis, bit))
            bit = bit * 2
    return steps


def together(*values):
    return lax.optimization_barrier(values)


def gather_pieces(payload, early):
    ranks, dps = lax.axis_size("expert"), lax.axis_size("dp")
    half = payload.shape[0] // 2
    far = list(range(0, ranks, 2))
    sides = {"x": ("expert", [0, 1]), "y": ("dp", list(range(0, dps, 2)))}
    value, early = together(gather_bits(payload[None], "expert", far[1:]), early)
    values = (value[:, :half], value[:, half:])
    firsts = []
    for value, letter in zip(values, "xy"):
        axis, masks = sides[letter]
        firsts.append(gather_bits(value[None], axis, masks[1:]))
    seconds = []
    for value, letter in zip(firsts, "yx"):
        axis, masks = sides[letter]
        seconds.append([swap(value, axis, mask) for mask in masks[1:]])
    others = [swap(value, "dp", 1) for value in firsts]
    pieces, places = [], []
    for index, order in enumerate(("xy", "yx")):
        masks, other_masks = sides[order[0]][1], sides[order[1]][1]
        found = [(firsts[index], 0, 0), (others[index], 0, 1)]
        for value, mask in zip(seconds[index], other_masks[1:]):
            found += [(value, mask, 0), (swap(value, "dp", 1), mask, 1)]
        for piece, mask, core in found:
            offsets = []
            for first in masks:
                for low in far:
                    x_mask, y_mask = (first, mask) if order == "xy" else (mask, first)
                    offsets.append((low ^ x_mask, y_mask ^ core))
            pieces.append(piece)
            places.append((index, offsets))
    return pieces, places, early


def place_weights(places, piece_refs, w_ref, sem):
    my_expert, my_dp = lax.axis_index("expert"), lax.axis_index("dp")
    copies = []
    for ref, (half, offsets) in zip(piece_refs, places):
        low_count, rows = ref.shape[1], ref.shape[2]
        for index, (e_mask, d_mask) in enumerate(offsets):
            start = (my_dp ^ d_mask) * (2 * rows) + half * rows
            copies.append(
                pltpu.make_async_copy(
                    ref.at[index // low_count, index % low_count],
                    w_ref.at[my_expert ^ e_mask, pl.ds(pl.multiple_of(start, 16), rows), :],
                    sem,
                )
            )
    for copy in copies:
        copy.start()
    return copies


def dot(left, right, dims=((1,), (0,)), precision=None):
    return lax.dot_general(
        left, right, (dims, ((), ())), precision=precision, preferred_element_type=FULL
    )


NT = ((1,), (1,))
TN = ((0,), (0,))


def grid_of(rows):
    sub = lax.broadcasted_iota(jnp.int32, (rows, 128), 0)
    lane = lax.broadcasted_iota(jnp.int32, (rows, 128), 1)
    return sub, lane


def row_to_column(row, rows, shift=0):
    sub, lane = grid_of(rows)
    column = jnp.sum(jnp.where(lane == sub + shift, row, 0.0), axis=1, keepdims=True)
    return jnp.broadcast_to(column, (rows, 128))


def column_to_row(column, shift=0):
    sub, lane = grid_of(column.shape[0])
    return jnp.sum(jnp.where(lane == sub + shift, column, 0.0), axis=0, keepdims=True)


def turn(value, shift):
    return pltpu.roll(value, shift % value.shape[1], 1)


def slide(value, direction):
    sub = lax.broadcasted_iota(jnp.int32, value.shape, 0)
    for bit in (1, 2, 4):
        value = jnp.where((sub & bit) != 0, turn(value, direction * bit), value)
    return value


def slid_rows(row, count):
    value = slide(jnp.broadcast_to(row, (8, row.shape[1])), 1)
    while value.shape[0] < count:
        value = jnp.concatenate([value, turn(value, value.shape[0])], axis=0)
    return value


def slid_sum(value):
    while value.shape[0] > 8:
        half = value.shape[0] // 2
        value = value[:half] + turn(value[half:], -half)
    return jnp.sum(slide(value, -1), axis=0, keepdims=True)


def early_kernel(
    ranks, local_experts, capacity, slab, tokens_ref, routes_ref, gain_ref, d_out_ref, table_ref,
    onehot_ref, normed_ref, hits_ref, mask_ref, mask_t_ref, bias_ref, up_ref
):
    length = tokens_ref.shape[0]
    normed, _ = normalize(tokens_ref[...].astype(FULL), gain_ref[0:1, :])
    normed_ref[...] = normed.astype(LOW)
    experts = hits_ref.shape[1]
    routes = jnp.broadcast_to(routes_ref[...].astype(FULL), (length, length)).T
    route = routes[:, :1].astype(jnp.int32)
    lanes = lax.broadcasted_iota(jnp.int32, (length, experts), 1)
    hits = (lanes == route).astype(FULL)
    hits_ref[...] = hits
    row = lax.broadcasted_iota(jnp.int32, (length, length), 0)
    col = lax.broadcasted_iota(jnp.int32, (length, length), 1)
    before = dot((col < row).astype(FULL).astype(LOW), hits.astype(LOW))
    placed = jnp.sum(before * hits, axis=1, keepdims=True).astype(jnp.int32)
    rank = jnp.zeros_like(route)
    for r in range(1, ranks):
        rank = rank + (route >= r * local_experts).astype(jnp.int32)
    spot = rank * slab + (route - rank * local_experts) * capacity + placed
    spot = jnp.where(placed < capacity, spot, -1)
    places = lax.broadcasted_iota(jnp.int32, (length, ranks * slab), 1)
    mask = (places == spot).astype(FULL)
    mask_ref[...] = mask.astype(LOW)
    mask_t = mask.T.astype(LOW)
    mask_t_ref[...] = mask_t
    slabs = dot(mask_t, d_out_ref[...])
    for r in range(ranks):
        up_ref[r] = slabs[r * slab : (r + 1) * slab].astype(LOW)
    values = dot(table_ref[...], onehot_ref[...])
    for h in range(bias_ref.shape[0]):
        bias_ref[h] = slid_rows(values[h : h + 1], length)[:, length:]


def forward_kernel(
    places, slab, rank_slots, tokens_ref, normed_ref, seg_ref, bias_ref, gain_ref,
    router_t_ref, hits_ref, mask_t_ref, *rest
):
    count = len(places)
    piece_refs, rest = rest[:count], rest[count:]
    heads_ref, weights_ref, attended_ref, hidden_ref, chance_ref = rest[:5]
    slabs_ref = rest[5]
    w_ref, qkv_ref, att_t_ref, sem = rest[-4:]
    copies = place_weights(places, piece_refs, w_ref, sem)
    ranks, width, columns = w_ref.shape
    cols = columns // 4
    head_count = weights_ref.shape[0]
    head = width // head_count
    length = tokens_ref.shape[0]
    segments = jnp.broadcast_to(seg_ref[...].astype(FULL), (length, length))
    same_doc = segments == segments.T
    normed = normed_ref[...]
    for copy in copies:
        copy.wait()
    for e in range(ranks):
        turned = dot(normed, w_ref[e]).T
        for m in range(3):
            qkv_ref[m, e * cols : (e + 1) * cols, :] = turned[m * cols : (m + 1) * cols]
    heads_ref[...] = qkv_ref[...].astype(LOW)
    for h in range(head_count):
        rows = slice(h * head, (h + 1) * head)
        scores = dot(heads_ref[0, rows, :], heads_ref[1, rows, :], TN) * head ** (-0.5)
        scores = jnp.where(same_doc, scores + bias_ref[h], MASKED)
        grown = jnp.exp(scores - jnp.max(scores, axis=1, keepdims=True))
        weights = grown / jnp.sum(grown, axis=1, keepdims=True)
        weights_ref[h] = weights
        att_t_ref[rows, :] = dot(heads_ref[2, rows, :], weights.astype(LOW), NT)
    attended = att_t_ref[...].T.astype(LOW)
    attended_ref[...] = attended
    low_lane = 3 * cols // 128 * 128
    for e in range(ranks):
        turned = dot(attended, w_ref[e, :, low_lane:]).T
        att_t_ref[e * cols : (e + 1) * cols, :] = turned[3 * cols - low_lane :]
    hidden = tokens_ref[...].astype(FULL) + att_t_ref[...].T
    hidden_ref[...] = hidden
    normed_two, _ = normalize(hidden, gain_ref[1:2, :])
    logits = dot(normed_two, router_t_ref[...].astype(FULL), NT, HIGHEST)
    grown = jnp.exp(logits - jnp.max(logits, axis=1, keepdims=True))
    chance = grown / jnp.sum(grown, axis=1, keepdims=True)
    chance_ref[...] = chance
    gate = jnp.sum(chance * hits_ref[...], axis=1, keepdims=True)
    mask_t = mask_t_ref[...]
    slots = dot(mask_t, normed_two.astype(LOW))
    gates = dot(mask_t.astype(FULL), jnp.broadcast_to(gate, (length, 128)), precision=HIGHEST)
    sub, _ = grid_of(slab)
    for r in range(ranks):
        mine = gates[r * slab : (r + 1) * slab]
        high = mine.astype(LOW).astype(FULL)
        row = column_to_row(high) + column_to_row(mine - high, 64)
        rows = slots[r * slab : (r + 1) * slab]
        start = rows[:, :128] + jnp.where(sub == rank_slots, row, 0.0)
        slabs_ref[r, :, :128] = start.astype(LOW)
        slabs_ref[r, :, 128:] = rows[:, 128:].astype(LOW)


def upstream_kernel(pack_ref, w_out_ref, *rest):
    piece_refs, (rows_ref, act_ref) = rest[:-2], rest[-2:]
    local_experts = w_out_ref.shape[0]
    chunk = pack_ref.shape[0] // local_experts
    for p, piece in enumerate(piece_refs):
        packed = dot(pack_ref[...], piece[...]).astype(LOW)
        for e in range(local_experts):
            rows_ref[e, p * chunk : (p + 1) * chunk, :] = packed[e * chunk : (e + 1) * chunk]
    for e in range(local_experts):
        act_ref[e] = dot(rows_ref[e], w_out_ref[e], NT)


def unpack(pack_t, rows_ref, p, chunk):
    rows = [rows_ref[e, p * chunk : (p + 1) * chunk, :] for e in range(rows_ref.shape[0])]
    return dot(pack_t, jnp.concatenate(rows, axis=0))


def expert_kernel(
    count, slab, rank_slots, pack_ref, pack_t_ref, w_in_ref, up_act_ref, *rest
):
    piece_refs, rest = rest[:count], rest[count:]
    back_refs, rest = rest[:count], rest[count:]
    rows_ref, act_ref, pre_grad_ref, gates_ref, pre_ref, back_ref, part_ref = rest
    local_experts = w_in_ref.shape[0]
    chunk = pack_ref.shape[0] // local_experts
    ranks = pack_ref.shape[1] // slab
    pack, pack_t = pack_ref[...], pack_t_ref[...]
    for p, piece in enumerate(piece_refs):
        packed = dot(pack, piece[...]).astype(LOW)
        tile = piece[:, :128].astype(FULL)
        spread = []
        for shift in (0, 64):
            columns = [
                row_to_column(tile[r * slab + rank_slots : r * slab + rank_slots + 1], slab, shift)
                for r in range(ranks)
            ]
            spread.append(dot(pack, jnp.concatenate(columns, axis=0).astype(LOW)))
        gates = spread[0] + spread[1]
        for e in range(local_experts):
            rows_ref[e, p * chunk : (p + 1) * chunk, :] = packed[e * chunk : (e + 1) * chunk]
            gates_ref[e, p * chunk : (p + 1) * chunk, :] = gates[e * chunk : (e + 1) * chunk]
    root = np.float32(np.sqrt(2.0 / np.pi))
    step = 16
    for e in range(local_experts):
        pre_ref[...] = dot(rows_ref[e], w_in_ref[e])

        def body(index, carry):
            span = pl.ds(pl.multiple_of(index * step, step), step)
            pre = pre_ref[span, :]
            up = up_act_ref[e, span, :]
            square = pre * pre
            curve = jnp.tanh(root * pre * (1.0 + 0.044715 * square))
            rise = 0.5 + 0.5 * curve
            act = (pre * rise).astype(LOW)
            act_ref[e, span, :] = act
            slope = rise + pre * (rise * (1.0 - curve)) * (root + 3 * 0.044715 * root * square)
            gate = gates_ref[e, span, :][:, :1]
            pre_grad_ref[e, span, :] = (slope * (up * gate)).astype(LOW)
            part = jnp.sum(act.astype(FULL) * up, axis=1, keepdims=True)
            part_ref[e, span, :] = jnp.broadcast_to(part, (step, 128)).astype(LOW)
            return carry

        lax.fori_loop(0, pre_ref.shape[0] // step, body, 0, unroll=2)
        back_ref[e] = dot(pre_grad_ref[e], w_in_ref[e], NT).astype(LOW)
    sub, _ = grid_of(slab)
    for p in range(count):
        rows = unpack(pack_t, back_ref, p, chunk)
        parts = unpack(pack_t, part_ref, p, chunk)
        pieces = []
        for r in range(ranks):
            span = slice(r * slab, (r + 1) * slab)
            row = column_to_row(parts[span])
            pieces.append(rows[span, :128] + jnp.where(sub == rank_slots, row, 0.0))
        back_refs[p][:, :128] = jnp.concatenate(pieces, axis=0).astype(LOW)
        back_refs[p][:, 128:] = rows[:, 128:].astype(LOW)


def expert_out_kernel(pack_t_ref, w_out_ref, act_ref, *rest):
    out_refs, returned_ref = rest[:-1], rest[-1]
    chunk = act_ref.shape[1] // len(out_refs)
    for e in range(w_out_ref.shape[0]):
        returned_ref[e] = dot(act_ref[e], w_out_ref[e]).astype(LOW)
    for p, ref in enumerate(out_refs):
        ref[...] = unpack(pack_t_ref[...], returned_ref, p, chunk).astype(LOW)


def expert_grad_kernel(
    rows_ref, act_ref, pre_grad_ref, gates_ref, up_rows_ref, g_in_ref, g_out_ref, token_ref
):
    for e in range(rows_ref.shape[0]):
        g_in_ref[e] = dot(rows_ref[e], pre_grad_ref[e], TN)
        slot_grad = (up_rows_ref[e].astype(FULL) * gates_ref[e][:, :1]).astype(LOW)
        g_out_ref[e] = dot(act_ref[e], slot_grad, TN)
    token_ref[...] = jnp.zeros(token_ref.shape, FULL)


def joined(ref):
    ranks, slab, width = ref.shape
    return ref[...].astype(FULL).reshape(ranks * slab, width).astype(LOW)


def backward_kernel(
    places, rank_slots, tokens_ref, gain_ref, router_t_ref, hits_ref, mask_ref,
    up_ref, hidden_ref, chance_ref, heads_ref, weights_ref, onehot_ref, token_ref, *rest
):
    count = len(places)
    piece_refs, rest = rest[:count], rest[count:]
    (back_ref, d_input_ref, small_ref, factors_ref,
     w_ref, turned_ref, grads_ref, bias_ref, sem) = rest
    ranks, width, columns = w_ref.shape
    copies = place_weights(places, piece_refs, w_ref, sem)
    cols = columns // 4
    head_count = weights_ref.shape[0]
    head = width // head_count
    factor = head ** (-0.5)
    length = tokens_ref.shape[0]
    slab = back_ref.shape[1]
    hidden = hidden_ref[...]
    gain_two = gain_ref[1:2, :]
    normed_two, scale_two = normalize(hidden, gain_two)
    mask = mask_ref[...]
    chance, hits = chance_ref[...], hits_ref[...]
    gate = jnp.sum(chance * hits, axis=1, keepdims=True)
    spread = [
        row_to_column(back_ref[r, :, :128].astype(FULL)[rank_slots : rank_slots + 1], slab)
        for r in range(ranks)
    ]
    gate_grad = dot(mask, jnp.concatenate(spread, axis=0).astype(LOW))[:, :1]
    logit_grad = chance * (hits - gate) * gate_grad
    experts = hits.shape[1]
    small_ref[:experts, :] = dot(logit_grad, normed_two, TN, HIGHEST)
    router_t = router_t_ref[...].astype(FULL)
    normed_two_grad = dot(logit_grad, router_t, precision=HIGHEST) + dot(mask, joined(back_ref))
    hidden_part, ffn_gain_grad = norm_back(hidden, scale_two, gain_two, normed_two_grad)
    hidden_grad = up_ref[...].astype(FULL) + hidden_part
    turned_ref[...] = hidden_grad.astype(LOW).astype(FULL).T
    for copy in copies:
        copy.wait()
    low_lane = 3 * cols // 128 * 128
    att_grad = None
    for e in range(ranks):
        own = turned_ref[e * cols : (e + 1) * cols, :]
        if 3 * cols > low_lane:
            own = jnp.concatenate([jnp.zeros((3 * cols - low_lane, 128), FULL), own], axis=0)
        part = dot(w_ref[e, :, low_lane:], own.astype(LOW))
        att_grad = part if att_grad is None else att_grad + part
    att_grad = att_grad.astype(LOW)
    for h in range(head_count):
        rows = slice(h * head, (h + 1) * head)
        own = att_grad[rows]
        weights = weights_ref[h]
        grads_ref[2, rows, :] = dot(own, weights.astype(LOW))
        prob_grad = dot(own, heads_ref[2, rows, :], TN)
        score_grad = weights * (prob_grad - jnp.sum(prob_grad * weights, axis=1, keepdims=True))
        score_grad = score_grad.astype(LOW)
        grads_ref[0, rows, :] = dot(heads_ref[1, rows, :], score_grad, NT) * factor
        grads_ref[1, rows, :] = dot(heads_ref[0, rows, :], score_grad) * factor
        wide = [jnp.zeros((length, length), FULL), score_grad.astype(FULL)]
        bias_ref[h : h + 1, :] = slid_sum(jnp.concatenate(wide, axis=1))
    total = None
    for e in range(ranks):
        span = slice(e * cols, (e + 1) * cols)
        held = [grads_ref[m, span, :] for m in range(3)] + [jnp.zeros((cols, 128), FULL)]
        part = dot(w_ref[e], jnp.concatenate(held, axis=0).astype(LOW))
        total = part if total is None else total + part
        sent = [grads_ref[m, span, :] for m in range(3)] + [turned_ref[span, :]]
        factors_ref[e] = jnp.concatenate(sent, axis=0).astype(LOW)
    inputs = tokens_ref[...].astype(FULL)
    gain_one = gain_ref[0:1, :]
    _, scale_one = normalize(inputs, gain_one)
    norm_part, attn_gain_grad = norm_back(inputs, scale_one, gain_one, total.T)
    d_input_ref[...] = hidden_grad + norm_part
    sums = dot(bias_ref[...], onehot_ref[...], NT, HIGHEST)
    small_ref[experts : experts + 1, :] = ffn_gain_grad
    small_ref[experts + 1 : experts + 2, :] = attn_gain_grad
    small_ref[experts + 2 :, :] = jnp.zeros((small_ref.shape[0] - experts - 2, width), FULL)
    for h in range(head_count):
        line, place = experts + 2 + h // 6, 128 * (h % 6)
        small_ref[line : line + 1, place : place + sums.shape[1]] = sums[h : h + 1]


def product_kernel(
    dps, normed_ref, attended_ref, hidden_ref, chance_ref, hits_ref, mask_ref, factors_ref,
    returned_ref, output_ref, *rest
):
    piece_refs, total_ref = rest[:-1], rest[-1]
    ranks, columns, length = factors_ref.shape
    cols = columns // 4
    first, second = None, None
    for e in range(ranks):
        held = factors_ref[e].astype(FULL)
        part = dot(held[: 3 * cols].astype(LOW), normed_ref[e])
        first = part if first is None else first + part
        part = dot(held[3 * cols :].astype(LOW), attended_ref[e])
        second = part if second is None else second + part
    total = jnp.concatenate([first, second], axis=0).T
    rows = piece_refs[0].shape[0]
    for j in range(dps):
        total_ref[j] = total[j * rows : (j + 1) * rows]
    for j, ref in enumerate(piece_refs):
        ref[...] = total_ref[lax.axis_index("dp") ^ j].astype(LOW)
    gate = jnp.sum(chance_ref[...] * hits_ref[...], axis=1, keepdims=True)
    fetched = dot(mask_ref[...], joined(returned_ref))
    output_ref[...] = (hidden_ref[...] + gate * fetched).astype(LOW)


VMEM = pl.BlockSpec(memory_space=pltpu.VMEM)
ANY = pl.BlockSpec(memory_space=pl.ANY)
LIMIT = 60 * 1024 * 1024


def shaped(dtype, *shape):
    return jax.ShapeDtypeStruct(shape, dtype)


def call(kernel, name, micros, out_shape, args, pieces=(), scratch=(), more=()):
    return pl.pallas_call(
        kernel,
        out_shape=tuple(out_shape),
        in_specs=[VMEM] * len(args) + [ANY] * len(pieces) + [VMEM] * len(more),
        out_specs=(VMEM,) * len(out_shape),
        scratch_shapes=list(scratch),
        compiler_params=pltpu.CompilerParams(vmem_limit_bytes=LIMIT),
        cost_estimate=pl.CostEstimate(
            flops=0, bytes_accessed=micros * 3_600_000, transcendentals=0
        ),
        name=name,
    )(*args, *pieces, *more)


def per_device(
    tokens,
    seg_ids,
    routes,
    attn_gain,
    w_query,
    w_key,
    w_value,
    w_output,
    rel_bias,
    ffn_gain,
    w_router,
    w_in,
    w_out,
    d_out,
):
    length, model_width = tokens.shape
    bucket_count, head_count = rel_bias.shape
    experts_total = w_router.shape[1]
    local_experts, _, hidden_here = w_in.shape
    ranks, dps = lax.axis_size("expert"), lax.axis_size("dp")
    capacity = length * 5 // (4 * experts_total)
    rank_slots = local_experts * capacity
    slab = -(-(rank_slots + 1) // 8) * 8
    rows_here, columns_here = w_query.shape
    inner_width = dps * rows_here
    packed_rows = dps * ranks * capacity
    gains = jnp.stack([attn_gain, ffn_gain]).astype(FULL)
    slabs_shape = shaped(LOW, ranks, slab, model_width)
    router_t = w_router.T
    pack = packing(local_experts, ranks, capacity, slab)
    pack, pack_t = jnp.asarray(pack, LOW), jnp.asarray(pack.T, LOW)

    normed_low, hits, mask, mask_t, bias_full, up_slabs = call(
        functools.partial(early_kernel, ranks, local_experts, capacity, slab),
        "early",
        3,
        [
            shaped(LOW, length, model_width),
            shaped(FULL, length, experts_total),
            shaped(LOW, length, ranks * slab),
            shaped(LOW, ranks * slab, length),
            shaped(FULL, head_count, length, length),
            slabs_shape,
        ],
        [
            tokens,
            routes.reshape(1, length),
            gains,
            d_out,
            rel_bias.T,
            jnp.asarray(bucket_onehot(bucket_count, length), LOW),
        ],
    )

    payload = jnp.concatenate([w_query, w_key, w_value, w_output], axis=1)
    early = (normed_low, hits, mask, mask_t, bias_full)
    pieces, places, early = gather_pieces(payload, early)
    normed_low, hits, mask, mask_t, bias_full = early
    pieces, normed_later, up_slabs = together(pieces, normed_low, up_slabs)
    normed_all = lax.all_gather(normed_later, "expert", axis=0)
    up_arrived = exchange(up_slabs).reshape(ranks * slab, model_width)

    w_shape = (ranks, inner_width, 4 * columns_here)
    heads, weights, attended, hidden, chance, slabs = call(
        functools.partial(forward_kernel, places, slab, rank_slots),
        "attention_forward",
        10,
        [
            shaped(LOW, 3, inner_width, length),
            shaped(FULL, head_count, length, length),
            shaped(LOW, length, inner_width),
            shaped(FULL, length, model_width),
            shaped(FULL, length, experts_total),
            slabs_shape,
        ],
        [tokens, normed_low, seg_ids, bias_full, gains, router_t, hits, mask_t],
        pieces,
        [
            pltpu.VMEM(w_shape, LOW),
            pltpu.VMEM((3, inner_width, length), FULL),
            pltpu.VMEM((inner_width, length), FULL),
            pltpu.SemaphoreType.DMA,
        ],
    )

    slabs, up_arrived = together(slabs, up_arrived)
    arrived = exchange(slabs).reshape(ranks * slab, model_width)
    attended_all = lax.all_gather(attended, "expert", axis=0)
    up_pieces = gather_near(gather_far(up_arrived))
    arrived, up_pieces = together(arrived, up_pieces)
    row_far = gather_far(arrived)
    by_expert = (local_experts, packed_rows)
    up_rows, up_act = call(
        upstream_kernel,
        "upstream_rows",
        5,
        [shaped(LOW, *by_expert, model_width), shaped(FULL, *by_expert, hidden_here)],
        [pack, w_out, *up_pieces],
    )
    row_far, up_act = together(row_far, up_act)
    row_pieces = gather_near(row_far)

    *back, slot_rows, activated, pre_grad, gates = call(
        functools.partial(expert_kernel, dps, slab, rank_slots),
        "experts",
        10,
        [shaped(LOW, ranks * slab, model_width)] * dps
        + [
            shaped(LOW, *by_expert, model_width),
            shaped(LOW, *by_expert, hidden_here),
            shaped(LOW, *by_expert, hidden_here),
            shaped(FULL, *by_expert, 128),
        ],
        [pack, pack_t, w_in, up_act, *row_pieces],
        scratch=[
            pltpu.VMEM((packed_rows, hidden_here), FULL),
            pltpu.VMEM((*by_expert, model_width), LOW),
            pltpu.VMEM((*by_expert, 128), LOW),
        ],
    )
    kept, got = scatter_terms(back)
    returned = call(
        expert_out_kernel,
        "expert_outputs",
        3,
        [shaped(LOW, ranks * slab, model_width)] * dps,
        [pack_t, w_out, activated],
        scratch=[pltpu.VMEM((*by_expert, model_width), LOW)],
    )
    got, returned = together(got, returned)
    back = add(kept, got).reshape(ranks, slab, model_width)
    back, activated, returned = together(back, activated, returned)
    back = exchange(back)
    first_grad, second_grad, token = call(
        expert_grad_kernel,
        "expert_gradients",
        8,
        [shaped(FULL, *w_in.shape), shaped(FULL, *w_out.shape), shaped(FULL, 8, 128)],
        [slot_rows, activated, pre_grad, gates, up_rows],
    )
    returned = add(*scatter_terms(returned)).reshape(ranks, slab, model_width)
    back, returned = together(back, returned)
    returned = exchange(returned)

    bias_rows = -(-head_count // 6)
    small_rows = -(-(experts_total + 2 + bias_rows) // 8) * 8
    d_input, small, factors = call(
        functools.partial(backward_kernel, places, rank_slots),
        "attention_backward",
        12,
        [
            shaped(FULL, length, model_width),
            shaped(FULL, small_rows, model_width),
            shaped(LOW, ranks, 4 * columns_here, length),
        ],
        [
            tokens,
            gains,
            router_t,
            hits,
            mask,
            d_out,
            hidden,
            chance,
            heads,
            weights,
            jnp.asarray(bucket_onehot(bucket_count, length), FULL),
            token,
        ],
        pieces,
        [
            pltpu.VMEM(w_shape, LOW),
            pltpu.VMEM((inner_width, length), FULL),
            pltpu.VMEM((3, inner_width, length), FULL),
            pltpu.VMEM((head_count, 2 * length), FULL),
            pltpu.SemaphoreType.DMA,
        ],
        [back],
    )

    factors, small, returned = together(factors, small, returned)
    factors = exchange(factors)
    *steps, one_but_last, last = sum_steps()
    for axis, bit in steps:
        small = small + swap(small, axis, bit)
    factors, small = together(factors, small)
    small = small + swap(small, *one_but_last)
    output, *grads = call(
        functools.partial(product_kernel, dps),
        "weight_gradients",
        5,
        [shaped(LOW, length, model_width)] + [shaped(LOW, rows_here, 4 * columns_here)] * dps,
        [normed_all, attended_all, hidden, chance, hits, mask, factors, returned],
        scratch=[pltpu.VMEM((dps, rows_here, 4 * columns_here), FULL)],
    )
    grads, small = together(grads, small)
    small = small + swap(small, *last)
    grads = add(*scatter_terms(grads), FULL)
    g_query, g_key, g_value, g_output = (
        grads[:, i * columns_here : (i + 1) * columns_here] for i in range(4)
    )
    g_router = small[:experts_total].T
    g_ffn_gain, g_attn_gain = small[experts_total], small[experts_total + 1]
    g_rel_bias = small[experts_total + 2 : experts_total + 2 + bias_rows].reshape(-1, 128)
    g_rel_bias = g_rel_bias[:head_count, :bucket_count].T
    return (
        output,
        d_input,
        g_attn_gain,
        g_query,
        g_key,
        g_value,
        g_output,
        g_rel_bias,
        g_ffn_gain,
        g_router,
        first_grad,
        second_grad,
    )


def solution(mesh):
    return jax.shard_map(
        per_device,
        mesh=mesh,
        in_specs=(
            P(("dp", "expert"), None),
            P(("dp", "expert"), None),
            P(("dp", "expert"), None),
            P(),
            P("dp", "expert"),
            P("dp", "expert"),
            P("dp", "expert"),
            P("dp", "expert"),
            P(),
            P(),
            P(),
            P("expert", None, "dp"),
            P("expert", "dp", None),
            P(("dp", "expert"), None),
        ),
        out_specs=(
            P(("dp", "expert"), None),
            P(("dp", "expert"), None),
            P(),
            P("dp", "expert"),
            P("dp", "expert"),
            P("dp", "expert"),
            P("dp", "expert"),
            P(),
            P(),
            P(),
            P("expert", None, "dp"),
            P("expert", "dp", None),
        ),
        check_vma=False,
    )
```

```python
import functools

import jax
import jax.numpy as jnp
import numpy as np
from jax import lax
from jax.experimental import pallas as pl
from jax.experimental.pallas import tpu as pltpu
from jax.sharding import PartitionSpec as P

EPSILON = 1e-06
LIMITS = (12, 16, 23, 32, 46, 64, 91)
MASKED = -1000000000.0
HIGHEST = lax.Precision.HIGHEST
LOW = jnp.bfloat16
FULL = jnp.float32


def bucket_onehot(buckets, length):
    delta = np.arange(2 * length) - length
    magnitude = np.abs(delta)
    distant = 8 + sum((magnitude >= threshold).astype(np.int32) for threshold in LIMITS)
    ids = np.where(delta > 0, 16, 0) + np.where(magnitude < 8, magnitude, distant)
    return (ids[None, :] == np.arange(buckets)[:, None]).astype(np.float32)


def packing(local_experts, ranks, capacity, slab):
    table = np.zeros((local_experts, ranks, capacity, ranks, slab), np.float32)
    for e in range(local_experts):
        for r in range(ranks):
            for c in range(capacity):
                table[e, r, c, r, e * capacity + c] = 1.0
    return table.reshape(local_experts * ranks * capacity, ranks * slab)


def normalize(matrix, gain_vec):
    scale = lax.rsqrt(jnp.mean(matrix * matrix, axis=-1, keepdims=True) + EPSILON)
    return (matrix * scale * gain_vec, scale)


def norm_back(matrix, scale, gain_vec, incoming):
    weighted = incoming * gain_vec
    average = jnp.mean(matrix * weighted, axis=-1, keepdims=True)
    return (
        scale * weighted - matrix * (scale * scale * scale) * average,
        jnp.sum(incoming * matrix * scale, axis=0, keepdims=True),
    )


def swap(value, axis, mask):
    count = lax.axis_size(axis)
    return lax.ppermute(value, axis, [(i, i ^ mask) for i in range(count)])


def gather_bits(value, axis, masks):
    return jnp.concatenate([value] + [swap(value, axis, mask) for mask in masks], axis=0)


def exchange(value):
    return lax.all_to_all(value, "expert", split_axis=0, concat_axis=0, tiled=True)


def gather_far(value):
    found = {0: value}
    bit = lax.axis_size("dp") // 2
    while bit > 1:
        found.update({index ^ bit: swap(item, "dp", bit) for index, item in found.items()})
        bit = bit // 2
    return found


def gather_near(found):
    found = {**found, **{index ^ 1: swap(item, "dp", 1) for index, item in found.items()}}
    return [found[index] for index in range(len(found))]


def add(left, right, dtype=LOW):
    return (left.astype(FULL) + right.astype(FULL)).astype(dtype)


def scatter_near(items):
    taken = [swap(item, "dp", 1) for item in items[1::2]]
    return [add(kept, got) for kept, got in zip(items[0::2], taken)]


def scatter_far(items):
    bit = 2
    while len(items) > 2:
        taken = [swap(item, "dp", bit) for item in items[1::2]]
        items = [add(kept, got) for kept, got in zip(items[0::2], taken)]
        bit = bit * 2
    return items[0], swap(items[1], "dp", bit)


def scatter_terms(items):
    return scatter_far(scatter_near(items))


def sum_steps():
    steps = []
    for axis in ("dp", "expert"):
        bit = 1
        while bit < lax.axis_size(axis):
            steps.append((axis, bit))
            bit = bit * 2
    return steps


def together(*values):
    return lax.optimization_barrier(values)


def gather_pieces(payload, early):
    ranks, dps = lax.axis_size("expert"), lax.axis_size("dp")
    half = payload.shape[0] // 2
    far = list(range(0, ranks, 2))
    sides = {"x": ("expert", [0, 1]), "y": ("dp", list(range(0, dps, 2)))}
    value, early = together(gather_bits(payload[None], "expert", far[1:]), early)
    values = (value[:, :half], value[:, half:])
    firsts = []
    for value, letter in zip(values, "xy"):
        axis, masks = sides[letter]
        firsts.append(gather_bits(value[None], axis, masks[1:]))
    seconds = []
    for value, letter in zip(firsts, "yx"):
        axis, masks = sides[letter]
        seconds.append([swap(value, axis, mask) for mask in masks[1:]])
    others = [swap(value, "dp", 1) for value in firsts]
    pieces, places = [], []
    for index, order in enumerate(("xy", "yx")):
        masks, other_masks = sides[order[0]][1], sides[order[1]][1]
        found = [(firsts[index], 0, 0), (others[index], 0, 1)]
        for value, mask in zip(seconds[index], other_masks[1:]):
            found += [(value, mask, 0), (swap(value, "dp", 1), mask, 1)]
        for piece, mask, core in found:
            offsets = []
            for first in masks:
                for low in far:
                    x_mask, y_mask = (first, mask) if order == "xy" else (mask, first)
                    offsets.append((low ^ x_mask, y_mask ^ core))
            pieces.append(piece)
            places.append((index, offsets))
    return pieces, places, early


def place_weights(places, piece_refs, w_ref, sem):
    my_expert, my_dp = lax.axis_index("expert"), lax.axis_index("dp")
    copies = []
    for ref, (half, offsets) in zip(piece_refs, places):
        low_count, rows = ref.shape[1], ref.shape[2]
        for index, (e_mask, d_mask) in enumerate(offsets):
            start = (my_dp ^ d_mask) * (2 * rows) + half * rows
            copies.append(
                pltpu.make_async_copy(
                    ref.at[index // low_count, index % low_count],
                    w_ref.at[my_expert ^ e_mask, pl.ds(pl.multiple_of(start, 16), rows), :],
                    sem,
                )
            )
    for copy in copies:
        copy.start()
    return copies


def dot(left, right, dims=((1,), (0,)), precision=None):
    return lax.dot_general(
        left, right, (dims, ((), ())), precision=precision, preferred_element_type=FULL
    )


NT = ((1,), (1,))
TN = ((0,), (0,))


def grid_of(rows):
    sub = lax.broadcasted_iota(jnp.int32, (rows, 128), 0)
    lane = lax.broadcasted_iota(jnp.int32, (rows, 128), 1)
    return sub, lane


def row_to_column(row, rows, shift=0):
    sub, lane = grid_of(rows)
    column = jnp.sum(jnp.where(lane == sub + shift, row, 0.0), axis=1, keepdims=True)
    return jnp.broadcast_to(column, (rows, 128))


def column_to_row(column, shift=0):
    sub, lane = grid_of(column.shape[0])
    return jnp.sum(jnp.where(lane == sub + shift, column, 0.0), axis=0, keepdims=True)


def turn(value, shift):
    return pltpu.roll(value, shift % value.shape[1], 1)


def slide(value, direction):
    sub = lax.broadcasted_iota(jnp.int32, value.shape, 0)
    for bit in (1, 2, 4):
        value = jnp.where((sub & bit) != 0, turn(value, direction * bit), value)
    return value


def slid_rows(row, count):
    value = slide(jnp.broadcast_to(row, (8, row.shape[1])), 1)
    while value.shape[0] < count:
        value = jnp.concatenate([value, turn(value, value.shape[0])], axis=0)
    return value


def slid_sum(value):
    while value.shape[0] > 8:
        half = value.shape[0] // 2
        value = value[:half] + turn(value[half:], -half)
    return jnp.sum(slide(value, -1), axis=0, keepdims=True)


def early_kernel(
    ranks, local_experts, capacity, slab, tokens_ref, routes_ref, gain_ref, d_out_ref, table_ref,
    onehot_ref, normed_ref, hits_ref, mask_ref, mask_t_ref, bias_ref, up_ref
):
    length = tokens_ref.shape[0]
    normed, _ = normalize(tokens_ref[...].astype(FULL), gain_ref[0:1, :])
    normed_ref[...] = normed.astype(LOW)
    experts = hits_ref.shape[1]
    routes = jnp.broadcast_to(routes_ref[...].astype(FULL), (length, length)).T
    route = routes[:, :1].astype(jnp.int32)
    lanes = lax.broadcasted_iota(jnp.int32, (length, experts), 1)
    hits = (lanes == route).astype(FULL)
    hits_ref[...] = hits
    row = lax.broadcasted_iota(jnp.int32, (length, length), 0)
    col = lax.broadcasted_iota(jnp.int32, (length, length), 1)
    before = dot((col < row).astype(FULL).astype(LOW), hits.astype(LOW))
    placed = jnp.sum(before * hits, axis=1, keepdims=True).astype(jnp.int32)
    rank = jnp.zeros_like(route)
    for r in range(1, ranks):
        rank = rank + (route >= r * local_experts).astype(jnp.int32)
    spot = rank * slab + (route - rank * local_experts) * capacity + placed
    spot = jnp.where(placed < capacity, spot, -1)
    places = lax.broadcasted_iota(jnp.int32, (length, ranks * slab), 1)
    mask = (places == spot).astype(FULL)
    mask_ref[...] = mask.astype(LOW)
    mask_t = mask.T.astype(LOW)
    mask_t_ref[...] = mask_t
    slabs = dot(mask_t, d_out_ref[...])
    for r in range(ranks):
        up_ref[r] = slabs[r * slab : (r + 1) * slab].astype(LOW)
    values = dot(table_ref[...], onehot_ref[...])
    for h in range(bias_ref.shape[0]):
        bias_ref[h] = slid_rows(values[h : h + 1], length)[:, length:]


def forward_kernel(
    places, slab, rank_slots, tokens_ref, normed_ref, seg_ref, bias_ref, gain_ref,
    router_t_ref, hits_ref, mask_t_ref, *rest
):
    count = len(places)
    piece_refs, rest = rest[:count], rest[count:]
    heads_ref, weights_ref, attended_ref, hidden_ref, chance_ref = rest[:5]
    slabs_ref = rest[5]
    w_ref, qkv_ref, att_t_ref, sem = rest[-4:]
    copies = place_weights(places, piece_refs, w_ref, sem)
    ranks, width, columns = w_ref.shape
    cols = columns // 4
    head_count = weights_ref.shape[0]
    head = width // head_count
    length = tokens_ref.shape[0]
    segments = jnp.broadcast_to(seg_ref[...].astype(FULL), (length, length))
    same_doc = segments == segments.T
    normed = normed_ref[...]
    for copy in copies:
        copy.wait()
    for e in range(ranks):
        turned = dot(normed, w_ref[e]).T
        for m in range(3):
            qkv_ref[m, e * cols : (e + 1) * cols, :] = turned[m * cols : (m + 1) * cols]
    heads_ref[...] = qkv_ref[...].astype(LOW)
    for h in range(head_count):
        rows = slice(h * head, (h + 1) * head)
        scores = dot(heads_ref[0, rows, :], heads_ref[1, rows, :], TN) * head ** (-0.5)
        scores = jnp.where(same_doc, scores + bias_ref[h], MASKED)
        grown = jnp.exp(scores - jnp.max(scores, axis=1, keepdims=True))
        weights = grown / jnp.sum(grown, axis=1, keepdims=True)
        weights_ref[h] = weights
        att_t_ref[rows, :] = dot(heads_ref[2, rows, :], weights.astype(LOW), NT)
    attended = att_t_ref[...].T.astype(LOW)
    attended_ref[...] = attended
    low_lane = 3 * cols // 128 * 128
    for e in range(ranks):
        turned = dot(attended, w_ref[e, :, low_lane:]).T
        att_t_ref[e * cols : (e + 1) * cols, :] = turned[3 * cols - low_lane :]
    hidden = tokens_ref[...].astype(FULL) + att_t_ref[...].T
    hidden_ref[...] = hidden
    normed_two, _ = normalize(hidden, gain_ref[1:2, :])
    logits = dot(normed_two, router_t_ref[...].astype(FULL), NT, HIGHEST)
    grown = jnp.exp(logits - jnp.max(logits, axis=1, keepdims=True))
    chance = grown / jnp.sum(grown, axis=1, keepdims=True)
    chance_ref[...] = chance
    gate = jnp.sum(chance * hits_ref[...], axis=1, keepdims=True)
    mask_t = mask_t_ref[...]
    slots = dot(mask_t, normed_two.astype(LOW))
    gates = dot(mask_t.astype(FULL), jnp.broadcast_to(gate, (length, 128)), precision=HIGHEST)
    sub, _ = grid_of(slab)
    for r in range(ranks):
        mine = gates[r * slab : (r + 1) * slab]
        high = mine.astype(LOW).astype(FULL)
        row = column_to_row(high) + column_to_row(mine - high, 64)
        rows = slots[r * slab : (r + 1) * slab]
        start = rows[:, :128] + jnp.where(sub == rank_slots, row, 0.0)
        slabs_ref[r, :, :128] = start.astype(LOW)
        slabs_ref[r, :, 128:] = rows[:, 128:].astype(LOW)


def upstream_kernel(pack_ref, w_out_ref, *rest):
    piece_refs, (rows_ref, act_ref) = rest[:-2], rest[-2:]
    local_experts = w_out_ref.shape[0]
    chunk = pack_ref.shape[0] // local_experts
    for p, piece in enumerate(piece_refs):
        packed = dot(pack_ref[...], piece[...]).astype(LOW)
        for e in range(local_experts):
            rows_ref[e, p * chunk : (p + 1) * chunk, :] = packed[e * chunk : (e + 1) * chunk]
    for e in range(local_experts):
        act_ref[e] = dot(rows_ref[e], w_out_ref[e], NT)


def unpack(pack_t, rows_ref, p, chunk):
    rows = [rows_ref[e, p * chunk : (p + 1) * chunk, :] for e in range(rows_ref.shape[0])]
    return dot(pack_t, jnp.concatenate(rows, axis=0))


def expert_kernel(
    count, slab, rank_slots, pack_ref, pack_t_ref, w_in_ref, up_act_ref, *rest
):
    piece_refs, rest = rest[:count], rest[count:]
    back_refs, rest = rest[:count], rest[count:]
    rows_ref, act_ref, pre_grad_ref, gates_ref, pre_ref, back_ref, part_ref = rest
    local_experts = w_in_ref.shape[0]
    chunk = pack_ref.shape[0] // local_experts
    ranks = pack_ref.shape[1] // slab
    pack, pack_t = pack_ref[...], pack_t_ref[...]
    for p, piece in enumerate(piece_refs):
        packed = dot(pack, piece[...]).astype(LOW)
        tile = piece[:, :128].astype(FULL)
        spread = []
        for shift in (0, 64):
            columns = [
                row_to_column(tile[r * slab + rank_slots : r * slab + rank_slots + 1], slab, shift)
                for r in range(ranks)
            ]
            spread.append(dot(pack, jnp.concatenate(columns, axis=0).astype(LOW)))
        gates = spread[0] + spread[1]
        for e in range(local_experts):
            rows_ref[e, p * chunk : (p + 1) * chunk, :] = packed[e * chunk : (e + 1) * chunk]
            gates_ref[e, p * chunk : (p + 1) * chunk, :] = gates[e * chunk : (e + 1) * chunk]
    root = np.float32(np.sqrt(2.0 / np.pi))
    step = 16
    for e in range(local_experts):
        pre_ref[...] = dot(rows_ref[e], w_in_ref[e])

        def body(index, carry):
            span = pl.ds(pl.multiple_of(index * step, step), step)
            pre = pre_ref[span, :]
            up = up_act_ref[e, span, :]
            square = pre * pre
            curve = jnp.tanh(root * pre * (1.0 + 0.044715 * square))
            rise = 0.5 + 0.5 * curve
            act = (pre * rise).astype(LOW)
            act_ref[e, span, :] = act
            slope = rise + pre * (rise * (1.0 - curve)) * (root + 3 * 0.044715 * root * square)
            gate = gates_ref[e, span, :][:, :1]
            pre_grad_ref[e, span, :] = (slope * (up * gate)).astype(LOW)
            part = jnp.sum(act.astype(FULL) * up, axis=1, keepdims=True)
            part_ref[e, span, :] = jnp.broadcast_to(part, (step, 128)).astype(LOW)
            return carry

        lax.fori_loop(0, pre_ref.shape[0] // step, body, 0, unroll=2)
        back_ref[e] = dot(pre_grad_ref[e], w_in_ref[e], NT).astype(LOW)
    sub, _ = grid_of(slab)
    for p in range(count):
        rows = unpack(pack_t, back_ref, p, chunk)
        parts = unpack(pack_t, part_ref, p, chunk)
        pieces = []
        for r in range(ranks):
            span = slice(r * slab, (r + 1) * slab)
            row = column_to_row(parts[span])
            pieces.append(rows[span, :128] + jnp.where(sub == rank_slots, row, 0.0))
        back_refs[p][:, :128] = jnp.concatenate(pieces, axis=0).astype(LOW)
        back_refs[p][:, 128:] = rows[:, 128:].astype(LOW)


def expert_out_kernel(pack_t_ref, w_out_ref, act_ref, *rest):
    out_refs, returned_ref = rest[:-1], rest[-1]
    chunk = act_ref.shape[1] // len(out_refs)
    for e in range(w_out_ref.shape[0]):
        returned_ref[e] = dot(act_ref[e], w_out_ref[e]).astype(LOW)
    for p, ref in enumerate(out_refs):
        ref[...] = unpack(pack_t_ref[...], returned_ref, p, chunk).astype(LOW)


def expert_grad_kernel(
    rows_ref, act_ref, pre_grad_ref, gates_ref, up_rows_ref, g_in_ref, g_out_ref, token_ref
):
    for e in range(rows_ref.shape[0]):
        g_in_ref[e] = dot(rows_ref[e], pre_grad_ref[e], TN)
        slot_grad = (up_rows_ref[e].astype(FULL) * gates_ref[e][:, :1]).astype(LOW)
        g_out_ref[e] = dot(act_ref[e], slot_grad, TN)
    token_ref[...] = jnp.zeros(token_ref.shape, FULL)


def joined(ref):
    ranks, slab, width = ref.shape
    return ref[...].astype(FULL).reshape(ranks * slab, width).astype(LOW)


def backward_kernel(
    places, rank_slots, tokens_ref, gain_ref, router_t_ref, hits_ref, mask_ref,
    up_ref, hidden_ref, chance_ref, heads_ref, weights_ref, onehot_ref, *rest
):
    count = len(places)
    piece_refs, rest = rest[:count], rest[count:]
    (back_ref, d_input_ref, small_ref, factors_ref,
     w_ref, turned_ref, grads_ref, bias_ref, sem) = rest
    ranks, width, columns = w_ref.shape
    copies = place_weights(places, piece_refs, w_ref, sem)
    cols = columns // 4
    head_count = weights_ref.shape[0]
    head = width // head_count
    factor = head ** (-0.5)
    length = tokens_ref.shape[0]
    slab = back_ref.shape[1]
    hidden = hidden_ref[...]
    gain_two = gain_ref[1:2, :]
    normed_two, scale_two = normalize(hidden, gain_two)
    mask = mask_ref[...]
    chance, hits = chance_ref[...], hits_ref[...]
    gate = jnp.sum(chance * hits, axis=1, keepdims=True)
    spread = [
        row_to_column(back_ref[r, :, :128].astype(FULL)[rank_slots : rank_slots + 1], slab)
        for r in range(ranks)
    ]
    gate_grad = dot(mask, jnp.concatenate(spread, axis=0).astype(LOW))[:, :1]
    logit_grad = chance * (hits - gate) * gate_grad
    experts = hits.shape[1]
    small_ref[:experts, :] = dot(logit_grad, normed_two, TN, HIGHEST)
    router_t = router_t_ref[...].astype(FULL)
    normed_two_grad = dot(logit_grad, router_t, precision=HIGHEST) + dot(mask, joined(back_ref))
    hidden_part, ffn_gain_grad = norm_back(hidden, scale_two, gain_two, normed_two_grad)
    hidden_grad = up_ref[...].astype(FULL) + hidden_part
    turned_ref[...] = hidden_grad.astype(LOW).astype(FULL).T
    for copy in copies:
        copy.wait()
    low_lane = 3 * cols // 128 * 128
    att_grad = None
    for e in range(ranks):
        own = turned_ref[e * cols : (e + 1) * cols, :]
        if 3 * cols > low_lane:
            own = jnp.concatenate([jnp.zeros((3 * cols - low_lane, 128), FULL), own], axis=0)
        part = dot(w_ref[e, :, low_lane:], own.astype(LOW))
        att_grad = part if att_grad is None else att_grad + part
    att_grad = att_grad.astype(LOW)
    for h in range(head_count):
        rows = slice(h * head, (h + 1) * head)
        own = att_grad[rows]
        weights = weights_ref[h]
        grads_ref[2, rows, :] = dot(own, weights.astype(LOW))
        prob_grad = dot(own, heads_ref[2, rows, :], TN)
        score_grad = weights * (prob_grad - jnp.sum(prob_grad * weights, axis=1, keepdims=True))
        score_grad = score_grad.astype(LOW)
        grads_ref[0, rows, :] = dot(heads_ref[1, rows, :], score_grad, NT) * factor
        grads_ref[1, rows, :] = dot(heads_ref[0, rows, :], score_grad) * factor
        wide = [jnp.zeros((length, length), FULL), score_grad.astype(FULL)]
        bias_ref[h : h + 1, :] = slid_sum(jnp.concatenate(wide, axis=1))
    total = None
    for e in range(ranks):
        span = slice(e * cols, (e + 1) * cols)
        held = [grads_ref[m, span, :] for m in range(3)] + [jnp.zeros((cols, 128), FULL)]
        part = dot(w_ref[e], jnp.concatenate(held, axis=0).astype(LOW))
        total = part if total is None else total + part
        sent = [grads_ref[m, span, :] for m in range(3)] + [turned_ref[span, :]]
        factors_ref[e] = jnp.concatenate(sent, axis=0).astype(LOW)
    inputs = tokens_ref[...].astype(FULL)
    gain_one = gain_ref[0:1, :]
    _, scale_one = normalize(inputs, gain_one)
    norm_part, attn_gain_grad = norm_back(inputs, scale_one, gain_one, total.T)
    d_input_ref[...] = hidden_grad + norm_part
    sums = dot(bias_ref[...], onehot_ref[...], NT, HIGHEST)
    small_ref[experts : experts + 1, :] = ffn_gain_grad
    small_ref[experts + 1 : experts + 2, :] = attn_gain_grad
    small_ref[experts + 2 :, :] = jnp.zeros((small_ref.shape[0] - experts - 2, width), FULL)
    for h in range(head_count):
        line, place = experts + 2 + h // 6, 128 * (h % 6)
        small_ref[line : line + 1, place : place + sums.shape[1]] = sums[h : h + 1]


def product_kernel(
    normed_far_ref, normed_near_ref, attended_far_ref, attended_near_ref, hidden_ref, chance_ref,
    hits_ref, mask_ref, factors_ref, returned_ref, token_ref, output_ref, *rest
):
    piece_refs, total_ref = rest[:-1], rest[-1]
    ranks, columns, length = factors_ref.shape
    cols = columns // 4
    first, second = None, None
    for j in range(ranks):
        held = factors_ref[lax.axis_index("expert") ^ j].astype(FULL)
        normed_ref, attended_ref = (
            (normed_near_ref, attended_near_ref) if j % 2 else (normed_far_ref, attended_far_ref)
        )
        part = dot(held[: 3 * cols].astype(LOW), normed_ref[j // 2])
        first = part if first is None else first + part
        part = dot(held[3 * cols :].astype(LOW), attended_ref[j // 2])
        second = part if second is None else second + part
    total = jnp.concatenate([first, second], axis=0).T
    rows = piece_refs[0].shape[0]
    for j in range(len(piece_refs)):
        total_ref[j] = total[j * rows : (j + 1) * rows]
    for j, ref in enumerate(piece_refs):
        ref[...] = total_ref[lax.axis_index("dp") ^ j].astype(LOW)
    gate = jnp.sum(chance_ref[...] * hits_ref[...], axis=1, keepdims=True)
    fetched = dot(mask_ref[...], joined(returned_ref))
    output_ref[...] = (hidden_ref[...] + gate * fetched).astype(LOW)


VMEM = pl.BlockSpec(memory_space=pltpu.VMEM)
ANY = pl.BlockSpec(memory_space=pl.ANY)
LIMIT = 60 * 1024 * 1024


def shaped(dtype, *shape):
    return jax.ShapeDtypeStruct(shape, dtype)


def call(kernel, name, micros, out_shape, args, pieces=(), scratch=(), more=()):
    return pl.pallas_call(
        kernel,
        out_shape=tuple(out_shape),
        in_specs=[VMEM] * len(args) + [ANY] * len(pieces) + [VMEM] * len(more),
        out_specs=(VMEM,) * len(out_shape),
        scratch_shapes=list(scratch),
        compiler_params=pltpu.CompilerParams(vmem_limit_bytes=LIMIT),
        cost_estimate=pl.CostEstimate(
            flops=0, bytes_accessed=micros * 3_600_000, transcendentals=0
        ),
        name=name,
    )(*args, *pieces, *more)


def per_device(
    tokens,
    seg_ids,
    routes,
    attn_gain,
    w_query,
    w_key,
    w_value,
    w_output,
    rel_bias,
    ffn_gain,
    w_router,
    w_in,
    w_out,
    d_out,
):
    length, model_width = tokens.shape
    bucket_count, head_count = rel_bias.shape
    experts_total = w_router.shape[1]
    local_experts, _, hidden_here = w_in.shape
    ranks, dps = lax.axis_size("expert"), lax.axis_size("dp")
    capacity = length * 5 // (4 * experts_total)
    rank_slots = local_experts * capacity
    slab = -(-(rank_slots + 1) // 8) * 8
    rows_here, columns_here = w_query.shape
    inner_width = dps * rows_here
    packed_rows = dps * ranks * capacity
    gains = jnp.stack([attn_gain, ffn_gain]).astype(FULL)
    slabs_shape = shaped(LOW, ranks, slab, model_width)
    router_t = w_router.T
    pack = packing(local_experts, ranks, capacity, slab)
    pack, pack_t = jnp.asarray(pack, LOW), jnp.asarray(pack.T, LOW)

    normed_low, hits, mask, mask_t, bias_full, up_slabs = call(
        functools.partial(early_kernel, ranks, local_experts, capacity, slab),
        "early",
        3,
        [
            shaped(LOW, length, model_width),
            shaped(FULL, length, experts_total),
            shaped(LOW, length, ranks * slab),
            shaped(LOW, ranks * slab, length),
            shaped(FULL, head_count, length, length),
            slabs_shape,
        ],
        [
            tokens,
            routes.reshape(1, length),
            gains,
            d_out,
            rel_bias.T,
            jnp.asarray(bucket_onehot(bucket_count, length), LOW),
        ],
    )

    payload = jnp.concatenate([w_query, w_key, w_value, w_output], axis=1)
    early = (normed_low, hits, mask, mask_t, bias_full)
    pieces, places, early = gather_pieces(payload, early)
    normed_low, hits, mask, mask_t, bias_full = early
    pieces, up_slabs = together(pieces, up_slabs)
    up_arrived = exchange(up_slabs).reshape(ranks * slab, model_width)

    w_shape = (ranks, inner_width, 4 * columns_here)
    heads, weights, attended, hidden, chance, slabs = call(
        functools.partial(forward_kernel, places, slab, rank_slots),
        "attention_forward",
        10,
        [
            shaped(LOW, 3, inner_width, length),
            shaped(FULL, head_count, length, length),
            shaped(LOW, length, inner_width),
            shaped(FULL, length, model_width),
            shaped(FULL, length, experts_total),
            slabs_shape,
        ],
        [tokens, normed_low, seg_ids, bias_full, gains, router_t, hits, mask_t],
        pieces,
        [
            pltpu.VMEM(w_shape, LOW),
            pltpu.VMEM((3, inner_width, length), FULL),
            pltpu.VMEM((inner_width, length), FULL),
            pltpu.SemaphoreType.DMA,
        ],
    )

    slabs, up_arrived = together(slabs, up_arrived)
    arrived = exchange(slabs).reshape(ranks * slab, model_width)
    up_pieces = gather_near(gather_far(up_arrived))
    arrived, up_pieces, normed_own = together(arrived, up_pieces, normed_low)
    row_far = gather_far(arrived)
    far = list(range(2, ranks, 2))
    normed_far = gather_bits(normed_own[None], "expert", far)
    by_expert = (local_experts, packed_rows)
    up_rows, up_act = call(
        upstream_kernel,
        "upstream_rows",
        5,
        [shaped(LOW, *by_expert, model_width), shaped(FULL, *by_expert, hidden_here)],
        [pack, w_out, *up_pieces],
    )
    row_far, up_act = together(row_far, up_act)
    row_pieces = gather_near(row_far)

    *back, slot_rows, activated, pre_grad, gates = call(
        functools.partial(expert_kernel, dps, slab, rank_slots),
        "experts",
        10,
        [shaped(LOW, ranks * slab, model_width)] * dps
        + [
            shaped(LOW, *by_expert, model_width),
            shaped(LOW, *by_expert, hidden_here),
            shaped(LOW, *by_expert, hidden_here),
            shaped(FULL, *by_expert, 128),
        ],
        [pack, pack_t, w_in, up_act, *row_pieces],
        scratch=[
            pltpu.VMEM((packed_rows, hidden_here), FULL),
            pltpu.VMEM((*by_expert, model_width), LOW),
            pltpu.VMEM((*by_expert, 128), LOW),
        ],
    )
    back, normed_far, attended_own = together(back, normed_far, attended)
    kept, got = scatter_terms(back)
    normed_near = swap(normed_far, "expert", 1)
    attended_far = gather_bits(attended_own[None], "expert", far)
    returned = call(
        expert_out_kernel,
        "expert_outputs",
        3,
        [shaped(LOW, ranks * slab, model_width)] * dps,
        [pack_t, w_out, activated],
        scratch=[pltpu.VMEM((*by_expert, model_width), LOW)],
    )
    returned = scatter_near(returned)
    got, returned = together(got, returned)
    back = add(kept, got).reshape(ranks, slab, model_width)
    back = exchange(back)
    returned, attended_far = together(returned, attended_far)
    attended_near = swap(attended_far, "expert", 1)
    returned = add(*scatter_far(returned)).reshape(ranks, slab, model_width)
    back, returned = together(back, returned)
    returned = exchange(returned)

    bias_rows = -(-head_count // 6)
    small_rows = -(-(experts_total + 2 + bias_rows) // 8) * 8
    d_input, small, factors = call(
        functools.partial(backward_kernel, places, rank_slots),
        "attention_backward",
        12,
        [
            shaped(FULL, length, model_width),
            shaped(FULL, small_rows, model_width),
            shaped(LOW, ranks, 4 * columns_here, length),
        ],
        [
            tokens,
            gains,
            router_t,
            hits,
            mask,
            d_out,
            hidden,
            chance,
            heads,
            weights,
            jnp.asarray(bucket_onehot(bucket_count, length), FULL),
        ],
        pieces,
        [
            pltpu.VMEM(w_shape, LOW),
            pltpu.VMEM((inner_width, length), FULL),
            pltpu.VMEM((3, inner_width, length), FULL),
            pltpu.VMEM((head_count, 2 * length), FULL),
            pltpu.SemaphoreType.DMA,
        ],
        [back],
    )

    factors, small, returned, activated = together(factors, small, returned, activated)
    factors = exchange(factors)
    first_grad, second_grad, token = call(
        expert_grad_kernel,
        "expert_gradients",
        8,
        [shaped(FULL, *w_in.shape), shaped(FULL, *w_out.shape), shaped(FULL, 8, 128)],
        [slot_rows, activated, pre_grad, gates, up_rows],
    )
    *steps, one_but_last, last = sum_steps()
    for axis, bit in steps:
        small = small + swap(small, axis, bit)
    factors, small, token = together(factors, small, token)
    small = small + swap(small, *one_but_last)
    output, *grads = call(
        product_kernel,
        "weight_gradients",
        5,
        [shaped(LOW, length, model_width)] + [shaped(LOW, rows_here, 4 * columns_here)] * dps,
        [
            normed_far,
            normed_near,
            attended_far,
            attended_near,
            hidden,
            chance,
            hits,
            mask,
            factors,
            returned,
            token,
        ],
        scratch=[pltpu.VMEM((dps, rows_here, 4 * columns_here), FULL)],
    )
    grads, small = together(scatter_near(grads), small)
    small = small + swap(small, *last)
    grads = add(*scatter_far(grads), FULL)
    g_query, g_key, g_value, g_output = (
        grads[:, i * columns_here : (i + 1) * columns_here] for i in range(4)
    )
    g_router = small[:experts_total].T
    g_ffn_gain, g_attn_gain = small[experts_total], small[experts_total + 1]
    g_rel_bias = small[experts_total + 2 : experts_total + 2 + bias_rows].reshape(-1, 128)
    g_rel_bias = g_rel_bias[:head_count, :bucket_count].T
    return (
        output,
        d_input,
        g_attn_gain,
        g_query,
        g_key,
        g_value,
        g_output,
        g_rel_bias,
        g_ffn_gain,
        g_router,
        first_grad,
        second_grad,
    )


def solution(mesh):
    return jax.shard_map(
        per_device,
        mesh=mesh,
        in_specs=(
            P(("dp", "expert"), None),
            P(("dp", "expert"), None),
            P(("dp", "expert"), None),
            P(),
            P("dp", "expert"),
            P("dp", "expert"),
            P("dp", "expert"),
            P("dp", "expert"),
            P(),
            P(),
            P(),
            P("expert", None, "dp"),
            P("expert", "dp", None),
            P(("dp", "expert"), None),
        ),
        out_specs=(
            P(("dp", "expert"), None),
            P(("dp", "expert"), None),
            P(),
            P("dp", "expert"),
            P("dp", "expert"),
            P("dp", "expert"),
            P("dp", "expert"),
            P(),
            P(),
            P(),
            P("expert", None, "dp"),
            P("expert", "dp", None),
        ),
        check_vma=False,
    )
```

```python
import functools

import jax
import jax.numpy as jnp
import numpy as np
from jax import lax
from jax.experimental import pallas as pl
from jax.experimental.pallas import tpu as pltpu
from jax.sharding import PartitionSpec as P

EPSILON = 1e-06
LIMITS = (12, 16, 23, 32, 46, 64, 91)
MASKED = -1000000000.0
HIGHEST = lax.Precision.HIGHEST
LOW = jnp.bfloat16
FULL = jnp.float32


def bucket_onehot(buckets, length):
    delta = np.arange(2 * length) - length
    magnitude = np.abs(delta)
    distant = 8 + sum((magnitude >= threshold).astype(np.int32) for threshold in LIMITS)
    ids = np.where(delta > 0, 16, 0) + np.where(magnitude < 8, magnitude, distant)
    return (ids[None, :] == np.arange(buckets)[:, None]).astype(np.float32)


def packing(local_experts, ranks, capacity, slab):
    table = np.zeros((local_experts, ranks, capacity, ranks, slab), np.float32)
    for e in range(local_experts):
        for r in range(ranks):
            for c in range(capacity):
                table[e, r, c, r, e * capacity + c] = 1.0
    return table.reshape(local_experts * ranks * capacity, ranks * slab)


def normalize(matrix, gain_vec):
    scale = lax.rsqrt(jnp.mean(matrix * matrix, axis=-1, keepdims=True) + EPSILON)
    return (matrix * scale * gain_vec, scale)


def norm_back(matrix, scale, gain_vec, incoming):
    weighted = incoming * gain_vec
    average = jnp.mean(matrix * weighted, axis=-1, keepdims=True)
    return (
        scale * weighted - matrix * (scale * scale * scale) * average,
        jnp.sum(incoming * matrix * scale, axis=0, keepdims=True),
    )


def swap(value, axis, mask):
    count = lax.axis_size(axis)
    return lax.ppermute(value, axis, [(i, i ^ mask) for i in range(count)])


def gather_bits(value, axis, masks):
    return jnp.concatenate([value] + [swap(value, axis, mask) for mask in masks], axis=0)


def exchange(value):
    return lax.all_to_all(value, "expert", split_axis=0, concat_axis=0, tiled=True)


def gather_far(value):
    found = {0: value}
    bit = lax.axis_size("dp") // 2
    while bit > 1:
        found.update({index ^ bit: swap(item, "dp", bit) for index, item in found.items()})
        bit = bit // 2
    return found


def gather_near(found):
    found = {**found, **{index ^ 1: swap(item, "dp", 1) for index, item in found.items()}}
    return [found[index] for index in range(len(found))]


def add(left, right, dtype=LOW):
    return (left.astype(FULL) + right.astype(FULL)).astype(dtype)


def scatter_near(items):
    taken = [swap(item, "dp", 1) for item in items[1::2]]
    return [add(kept, got) for kept, got in zip(items[0::2], taken)]


def scatter_far(items):
    bit = 2
    while len(items) > 2:
        taken = [swap(item, "dp", bit) for item in items[1::2]]
        items = [add(kept, got) for kept, got in zip(items[0::2], taken)]
        bit = bit * 2
    return items[0], swap(items[1], "dp", bit)


def scatter_terms(items):
    return scatter_far(scatter_near(items))


def sum_steps():
    steps = []
    for axis in ("dp", "expert"):
        bit = 1
        while bit < lax.axis_size(axis):
            steps.append((axis, bit))
            bit = bit * 2
    return steps


def together(*values):
    return lax.optimization_barrier(values)


def gather_pieces(payload, early):
    ranks, dps = lax.axis_size("expert"), lax.axis_size("dp")
    half = payload.shape[0] // 2
    far = list(range(0, ranks, 2))
    sides = {"x": ("expert", [0, 1]), "y": ("dp", list(range(0, dps, 2)))}
    value, early = together(gather_bits(payload[None], "expert", far[1:]), early)
    values = (value[:, :half], value[:, half:])
    firsts = []
    for value, letter in zip(values, "xy"):
        axis, masks = sides[letter]
        firsts.append(gather_bits(value[None], axis, masks[1:]))
    seconds = []
    for value, letter in zip(firsts, "yx"):
        axis, masks = sides[letter]
        seconds.append([swap(value, axis, mask) for mask in masks[1:]])
    others = [swap(value, "dp", 1) for value in firsts]
    pieces, places = [], []
    for index, order in enumerate(("xy", "yx")):
        masks, other_masks = sides[order[0]][1], sides[order[1]][1]
        found = [(firsts[index], 0, 0), (others[index], 0, 1)]
        for value, mask in zip(seconds[index], other_masks[1:]):
            found += [(value, mask, 0), (swap(value, "dp", 1), mask, 1)]
        for piece, mask, core in found:
            offsets = []
            for first in masks:
                for low in far:
                    x_mask, y_mask = (first, mask) if order == "xy" else (mask, first)
                    offsets.append((low ^ x_mask, y_mask ^ core))
            pieces.append(piece)
            places.append((index, offsets))
    return pieces, places, early


def place_weights(places, piece_refs, w_ref, sem):
    my_expert, my_dp = lax.axis_index("expert"), lax.axis_index("dp")
    copies = []
    for ref, (half, offsets) in zip(piece_refs, places):
        low_count, rows = ref.shape[1], ref.shape[2]
        for index, (e_mask, d_mask) in enumerate(offsets):
            start = (my_dp ^ d_mask) * (2 * rows) + half * rows
            copies.append(
                pltpu.make_async_copy(
                    ref.at[index // low_count, index % low_count],
                    w_ref.at[my_expert ^ e_mask, pl.ds(pl.multiple_of(start, 16), rows), :],
                    sem,
                )
            )
    for copy in copies:
        copy.start()
    return copies


def dot(left, right, dims=((1,), (0,)), precision=None):
    return lax.dot_general(
        left, right, (dims, ((), ())), precision=precision, preferred_element_type=FULL
    )


NT = ((1,), (1,))
TN = ((0,), (0,))


def grid_of(rows):
    sub = lax.broadcasted_iota(jnp.int32, (rows, 128), 0)
    lane = lax.broadcasted_iota(jnp.int32, (rows, 128), 1)
    return sub, lane


def row_to_column(row, rows, shift=0):
    sub, lane = grid_of(rows)
    column = jnp.sum(jnp.where(lane == sub + shift, row, 0.0), axis=1, keepdims=True)
    return jnp.broadcast_to(column, (rows, 128))


def column_to_row(column, shift=0):
    sub, lane = grid_of(column.shape[0])
    return jnp.sum(jnp.where(lane == sub + shift, column, 0.0), axis=0, keepdims=True)


def turn(value, shift):
    return pltpu.roll(value, shift % value.shape[1], 1)


def slide(value, direction):
    sub = lax.broadcasted_iota(jnp.int32, value.shape, 0)
    for bit in (1, 2, 4):
        value = jnp.where((sub & bit) != 0, turn(value, direction * bit), value)
    return value


def slid_rows(row, count):
    value = slide(jnp.broadcast_to(row, (8, row.shape[1])), 1)
    while value.shape[0] < count:
        value = jnp.concatenate([value, turn(value, value.shape[0])], axis=0)
    return value


def slid_sum(value):
    while value.shape[0] > 8:
        half = value.shape[0] // 2
        value = value[:half] + turn(value[half:], -half)
    return jnp.sum(slide(value, -1), axis=0, keepdims=True)


def early_kernel(
    ranks, local_experts, capacity, slab, tokens_ref, routes_ref, gain_ref, d_out_ref, table_ref,
    onehot_ref, normed_ref, hits_ref, mask_ref, mask_t_ref, bias_ref, up_ref
):
    length = tokens_ref.shape[0]
    normed, _ = normalize(tokens_ref[...].astype(FULL), gain_ref[0:1, :])
    normed_ref[...] = normed.astype(LOW)
    experts = hits_ref.shape[1]
    routes = jnp.broadcast_to(routes_ref[...].astype(FULL), (length, length)).T
    route = routes[:, :1].astype(jnp.int32)
    lanes = lax.broadcasted_iota(jnp.int32, (length, experts), 1)
    hits = (lanes == route).astype(FULL)
    hits_ref[...] = hits
    row = lax.broadcasted_iota(jnp.int32, (length, length), 0)
    col = lax.broadcasted_iota(jnp.int32, (length, length), 1)
    before = dot((col < row).astype(FULL).astype(LOW), hits.astype(LOW))
    placed = jnp.sum(before * hits, axis=1, keepdims=True).astype(jnp.int32)
    rank = jnp.zeros_like(route)
    for r in range(1, ranks):
        rank = rank + (route >= r * local_experts).astype(jnp.int32)
    spot = rank * slab + (route - rank * local_experts) * capacity + placed
    spot = jnp.where(placed < capacity, spot, -1)
    places = lax.broadcasted_iota(jnp.int32, (length, ranks * slab), 1)
    mask = (places == spot).astype(FULL)
    mask_ref[...] = mask.astype(LOW)
    mask_t = mask.T.astype(LOW)
    mask_t_ref[...] = mask_t
    slabs = dot(mask_t, d_out_ref[...])
    for r in range(ranks):
        up_ref[r] = slabs[r * slab : (r + 1) * slab].astype(LOW)
    values = dot(table_ref[...], onehot_ref[...])
    for h in range(bias_ref.shape[0]):
        bias_ref[h] = slid_rows(values[h : h + 1], length)[:, length:]


def forward_kernel(
    places, slab, rank_slots, tokens_ref, normed_ref, seg_ref, bias_ref, gain_ref,
    router_t_ref, hits_ref, mask_t_ref, *rest
):
    count = len(places)
    piece_refs, rest = rest[:count], rest[count:]
    heads_ref, weights_ref, attended_ref, hidden_ref, chance_ref = rest[:5]
    slabs_ref = rest[5]
    w_ref, qkv_ref, att_t_ref, sem = rest[-4:]
    copies = place_weights(places, piece_refs, w_ref, sem)
    ranks, width, columns = w_ref.shape
    cols = columns // 4
    head_count = weights_ref.shape[0]
    head = width // head_count
    length = tokens_ref.shape[0]
    segments = jnp.broadcast_to(seg_ref[...].astype(FULL), (length, length))
    same_doc = segments == segments.T
    normed = normed_ref[...]
    for copy in copies:
        copy.wait()
    for e in range(ranks):
        turned = dot(normed, w_ref[e]).T
        for m in range(3):
            qkv_ref[m, e * cols : (e + 1) * cols, :] = turned[m * cols : (m + 1) * cols]
    heads_ref[...] = qkv_ref[...].astype(LOW)
    for h in range(head_count):
        rows = slice(h * head, (h + 1) * head)
        scores = dot(heads_ref[0, rows, :], heads_ref[1, rows, :], TN) * head ** (-0.5)
        scores = jnp.where(same_doc, scores + bias_ref[h], MASKED)
        grown = jnp.exp(scores - jnp.max(scores, axis=1, keepdims=True))
        weights = grown / jnp.sum(grown, axis=1, keepdims=True)
        weights_ref[h] = weights
        att_t_ref[rows, :] = dot(heads_ref[2, rows, :], weights.astype(LOW), NT)
    attended = att_t_ref[...].T.astype(LOW)
    attended_ref[...] = attended
    low_lane = 3 * cols // 128 * 128
    for e in range(ranks):
        turned = dot(attended, w_ref[e, :, low_lane:]).T
        att_t_ref[e * cols : (e + 1) * cols, :] = turned[3 * cols - low_lane :]
    hidden = tokens_ref[...].astype(FULL) + att_t_ref[...].T
    hidden_ref[...] = hidden
    normed_two, _ = normalize(hidden, gain_ref[1:2, :])
    logits = dot(normed_two, router_t_ref[...].astype(FULL), NT, HIGHEST)
    grown = jnp.exp(logits - jnp.max(logits, axis=1, keepdims=True))
    chance = grown / jnp.sum(grown, axis=1, keepdims=True)
    chance_ref[...] = chance
    gate = jnp.sum(chance * hits_ref[...], axis=1, keepdims=True)
    mask_t = mask_t_ref[...]
    slots = dot(mask_t, normed_two.astype(LOW))
    gates = dot(mask_t.astype(FULL), jnp.broadcast_to(gate, (length, 128)), precision=HIGHEST)
    sub, _ = grid_of(slab)
    for r in range(ranks):
        mine = gates[r * slab : (r + 1) * slab]
        high = mine.astype(LOW).astype(FULL)
        row = column_to_row(high) + column_to_row(mine - high, 64)
        rows = slots[r * slab : (r + 1) * slab]
        start = rows[:, :128] + jnp.where(sub == rank_slots, row, 0.0)
        slabs_ref[r, :, :128] = start.astype(LOW)
        slabs_ref[r, :, 128:] = rows[:, 128:].astype(LOW)


def upstream_kernel(pack_ref, w_out_ref, *rest):
    piece_refs, (rows_ref, act_ref) = rest[:-2], rest[-2:]
    local_experts = w_out_ref.shape[0]
    chunk = pack_ref.shape[0] // local_experts
    for p, piece in enumerate(piece_refs):
        packed = dot(pack_ref[...], piece[...]).astype(LOW)
        for e in range(local_experts):
            rows_ref[e, p * chunk : (p + 1) * chunk, :] = packed[e * chunk : (e + 1) * chunk]
    for e in range(local_experts):
        act_ref[e] = dot(rows_ref[e], w_out_ref[e], NT)


def unpack(pack_t, rows_ref, p, chunk):
    rows = [rows_ref[e, p * chunk : (p + 1) * chunk, :] for e in range(rows_ref.shape[0])]
    return dot(pack_t, jnp.concatenate(rows, axis=0))


def expert_kernel(
    count, slab, rank_slots, pack_ref, pack_t_ref, w_in_ref, up_act_ref, *rest
):
    piece_refs, rest = rest[:count], rest[count:]
    back_refs, rest = rest[:count], rest[count:]
    rows_ref, act_ref, pre_grad_ref, gates_ref, pre_ref, back_ref, part_ref = rest
    local_experts = w_in_ref.shape[0]
    chunk = pack_ref.shape[0] // local_experts
    ranks = pack_ref.shape[1] // slab
    pack, pack_t = pack_ref[...], pack_t_ref[...]
    for p, piece in enumerate(piece_refs):
        packed = dot(pack, piece[...]).astype(LOW)
        tile = piece[:, :128].astype(FULL)
        spread = []
        for shift in (0, 64):
            columns = [
                row_to_column(tile[r * slab + rank_slots : r * slab + rank_slots + 1], slab, shift)
                for r in range(ranks)
            ]
            spread.append(dot(pack, jnp.concatenate(columns, axis=0).astype(LOW)))
        gates = spread[0] + spread[1]
        for e in range(local_experts):
            rows_ref[e, p * chunk : (p + 1) * chunk, :] = packed[e * chunk : (e + 1) * chunk]
            gates_ref[e, p * chunk : (p + 1) * chunk, :] = gates[e * chunk : (e + 1) * chunk]
    root = np.float32(np.sqrt(2.0 / np.pi))
    step = 16
    for e in range(local_experts):
        pre_ref[...] = dot(rows_ref[e], w_in_ref[e])

        def body(index, carry):
            span = pl.ds(pl.multiple_of(index * step, step), step)
            pre = pre_ref[span, :]
            up = up_act_ref[e, span, :]
            square = pre * pre
            curve = jnp.tanh(root * pre * (1.0 + 0.044715 * square))
            rise = 0.5 + 0.5 * curve
            act = (pre * rise).astype(LOW)
            act_ref[e, span, :] = act
            slope = rise + pre * (rise * (1.0 - curve)) * (root + 3 * 0.044715 * root * square)
            gate = gates_ref[e, span, :][:, :1]
            pre_grad_ref[e, span, :] = (slope * (up * gate)).astype(LOW)
            part = jnp.sum(act.astype(FULL) * up, axis=1, keepdims=True)
            part_ref[e, span, :] = jnp.broadcast_to(part, (step, 128)).astype(LOW)
            return carry

        lax.fori_loop(0, pre_ref.shape[0] // step, body, 0, unroll=2)
        back_ref[e] = dot(pre_grad_ref[e], w_in_ref[e], NT).astype(LOW)
    sub, _ = grid_of(slab)
    for p in range(count):
        rows = unpack(pack_t, back_ref, p, chunk)
        parts = unpack(pack_t, part_ref, p, chunk)
        pieces = []
        for r in range(ranks):
            span = slice(r * slab, (r + 1) * slab)
            row = column_to_row(parts[span])
            pieces.append(rows[span, :128] + jnp.where(sub == rank_slots, row, 0.0))
        back_refs[p][:, :128] = jnp.concatenate(pieces, axis=0).astype(LOW)
        back_refs[p][:, 128:] = rows[:, 128:].astype(LOW)


def expert_out_kernel(pack_t_ref, w_out_ref, act_ref, *rest):
    out_refs, returned_ref = rest[:-1], rest[-1]
    chunk = act_ref.shape[1] // len(out_refs)
    for e in range(w_out_ref.shape[0]):
        returned_ref[e] = dot(act_ref[e], w_out_ref[e]).astype(LOW)
    for p, ref in enumerate(out_refs):
        ref[...] = unpack(pack_t_ref[...], returned_ref, p, chunk).astype(LOW)


def expert_grad_kernel(
    rows_ref, act_ref, pre_grad_ref, gates_ref, up_rows_ref, g_in_ref, g_out_ref, token_ref
):
    for e in range(rows_ref.shape[0]):
        g_in_ref[e] = dot(rows_ref[e], pre_grad_ref[e], TN)
        slot_grad = (up_rows_ref[e].astype(FULL) * gates_ref[e][:, :1]).astype(LOW)
        g_out_ref[e] = dot(act_ref[e], slot_grad, TN)
    token_ref[...] = jnp.zeros(token_ref.shape, FULL)


def joined(ref):
    ranks, slab, width = ref.shape
    return ref[...].astype(FULL).reshape(ranks * slab, width).astype(LOW)


def backward_kernel(
    places, rank_slots, tokens_ref, gain_ref, router_t_ref, hits_ref, mask_ref,
    up_ref, hidden_ref, chance_ref, heads_ref, weights_ref, onehot_ref, *rest
):
    count = len(places)
    piece_refs, rest = rest[:count], rest[count:]
    (back_ref, d_input_ref, small_ref, factors_ref,
     w_ref, turned_ref, grads_ref, bias_ref, sem) = rest
    ranks, width, columns = w_ref.shape
    copies = place_weights(places, piece_refs, w_ref, sem)
    cols = columns // 4
    head_count = weights_ref.shape[0]
    head = width // head_count
    factor = head ** (-0.5)
    length = tokens_ref.shape[0]
    slab = back_ref.shape[1]
    hidden = hidden_ref[...]
    gain_two = gain_ref[1:2, :]
    normed_two, scale_two = normalize(hidden, gain_two)
    mask = mask_ref[...]
    chance, hits = chance_ref[...], hits_ref[...]
    gate = jnp.sum(chance * hits, axis=1, keepdims=True)
    spread = [
        row_to_column(back_ref[r, :, :128].astype(FULL)[rank_slots : rank_slots + 1], slab)
        for r in range(ranks)
    ]
    gate_grad = dot(mask, jnp.concatenate(spread, axis=0).astype(LOW))[:, :1]
    logit_grad = chance * (hits - gate) * gate_grad
    experts = hits.shape[1]
    small_ref[:experts, :] = dot(logit_grad, normed_two, TN, HIGHEST)
    router_t = router_t_ref[...].astype(FULL)
    normed_two_grad = dot(logit_grad, router_t, precision=HIGHEST) + dot(mask, joined(back_ref))
    hidden_part, ffn_gain_grad = norm_back(hidden, scale_two, gain_two, normed_two_grad)
    hidden_grad = up_ref[...].astype(FULL) + hidden_part
    turned_ref[...] = hidden_grad.astype(LOW).astype(FULL).T
    for copy in copies:
        copy.wait()
    low_lane = 3 * cols // 128 * 128
    att_grad = None
    for e in range(ranks):
        own = turned_ref[e * cols : (e + 1) * cols, :]
        if 3 * cols > low_lane:
            own = jnp.concatenate([jnp.zeros((3 * cols - low_lane, 128), FULL), own], axis=0)
        part = dot(w_ref[e, :, low_lane:], own.astype(LOW))
        att_grad = part if att_grad is None else att_grad + part
    att_grad = att_grad.astype(LOW)
    for h in range(head_count):
        rows = slice(h * head, (h + 1) * head)
        own = att_grad[rows]
        weights = weights_ref[h]
        grads_ref[2, rows, :] = dot(own, weights.astype(LOW))
        prob_grad = dot(own, heads_ref[2, rows, :], TN)
        score_grad = weights * (prob_grad - jnp.sum(prob_grad * weights, axis=1, keepdims=True))
        score_grad = score_grad.astype(LOW)
        grads_ref[0, rows, :] = dot(heads_ref[1, rows, :], score_grad, NT) * factor
        grads_ref[1, rows, :] = dot(heads_ref[0, rows, :], score_grad) * factor
        wide = [jnp.zeros((length, length), FULL), score_grad.astype(FULL)]
        bias_ref[h : h + 1, :] = slid_sum(jnp.concatenate(wide, axis=1))
    total = None
    for e in range(ranks):
        span = slice(e * cols, (e + 1) * cols)
        held = [grads_ref[m, span, :] for m in range(3)] + [jnp.zeros((cols, 128), FULL)]
        part = dot(w_ref[e], jnp.concatenate(held, axis=0).astype(LOW))
        total = part if total is None else total + part
        sent = [grads_ref[m, span, :] for m in range(3)] + [turned_ref[span, :]]
        factors_ref[e] = jnp.concatenate(sent, axis=0).astype(LOW)
    inputs = tokens_ref[...].astype(FULL)
    gain_one = gain_ref[0:1, :]
    _, scale_one = normalize(inputs, gain_one)
    norm_part, attn_gain_grad = norm_back(inputs, scale_one, gain_one, total.T)
    d_input_ref[...] = hidden_grad + norm_part
    sums = dot(bias_ref[...], onehot_ref[...], NT, HIGHEST)
    small_ref[experts : experts + 1, :] = ffn_gain_grad
    small_ref[experts + 1 : experts + 2, :] = attn_gain_grad
    small_ref[experts + 2 :, :] = jnp.zeros((small_ref.shape[0] - experts - 2, width), FULL)
    for h in range(head_count):
        line, place = experts + 2 + h // 6, 128 * (h % 6)
        small_ref[line : line + 1, place : place + sums.shape[1]] = sums[h : h + 1]


def product_kernel(
    normed_ref, attended_ref, hidden_ref, chance_ref, hits_ref, mask_ref, factors_ref,
    returned_ref, token_ref, output_ref, *rest
):
    piece_refs, total_ref = rest[:-1], rest[-1]
    ranks, columns, length = factors_ref.shape
    cols = columns // 4
    first, second = None, None
    for e in range(ranks):
        held = factors_ref[e].astype(FULL)
        part = dot(held[: 3 * cols].astype(LOW), normed_ref[e])
        first = part if first is None else first + part
        part = dot(held[3 * cols :].astype(LOW), attended_ref[e])
        second = part if second is None else second + part
    total = jnp.concatenate([first, second], axis=0).T
    rows = piece_refs[0].shape[0]
    for j in range(len(piece_refs)):
        total_ref[j] = total[j * rows : (j + 1) * rows]
    for j, ref in enumerate(piece_refs):
        ref[...] = total_ref[lax.axis_index("dp") ^ j].astype(LOW)
    gate = jnp.sum(chance_ref[...] * hits_ref[...], axis=1, keepdims=True)
    fetched = dot(mask_ref[...], joined(returned_ref))
    output_ref[...] = (hidden_ref[...] + gate * fetched).astype(LOW)


VMEM = pl.BlockSpec(memory_space=pltpu.VMEM)
ANY = pl.BlockSpec(memory_space=pl.ANY)
LIMIT = 60 * 1024 * 1024


def shaped(dtype, *shape):
    return jax.ShapeDtypeStruct(shape, dtype)


def call(kernel, name, micros, out_shape, args, pieces=(), scratch=(), more=()):
    return pl.pallas_call(
        kernel,
        out_shape=tuple(out_shape),
        in_specs=[VMEM] * len(args) + [ANY] * len(pieces) + [VMEM] * len(more),
        out_specs=(VMEM,) * len(out_shape),
        scratch_shapes=list(scratch),
        compiler_params=pltpu.CompilerParams(vmem_limit_bytes=LIMIT),
        cost_estimate=pl.CostEstimate(
            flops=0, bytes_accessed=micros * 3_600_000, transcendentals=0
        ),
        name=name,
    )(*args, *pieces, *more)


def per_device(
    tokens,
    seg_ids,
    routes,
    attn_gain,
    w_query,
    w_key,
    w_value,
    w_output,
    rel_bias,
    ffn_gain,
    w_router,
    w_in,
    w_out,
    d_out,
):
    length, model_width = tokens.shape
    bucket_count, head_count = rel_bias.shape
    experts_total = w_router.shape[1]
    local_experts, _, hidden_here = w_in.shape
    ranks, dps = lax.axis_size("expert"), lax.axis_size("dp")
    capacity = length * 5 // (4 * experts_total)
    rank_slots = local_experts * capacity
    slab = -(-(rank_slots + 1) // 8) * 8
    rows_here, columns_here = w_query.shape
    inner_width = dps * rows_here
    packed_rows = dps * ranks * capacity
    gains = jnp.stack([attn_gain, ffn_gain]).astype(FULL)
    slabs_shape = shaped(LOW, ranks, slab, model_width)
    router_t = w_router.T
    pack = packing(local_experts, ranks, capacity, slab)
    pack, pack_t = jnp.asarray(pack, LOW), jnp.asarray(pack.T, LOW)

    normed_low, hits, mask, mask_t, bias_full, up_slabs = call(
        functools.partial(early_kernel, ranks, local_experts, capacity, slab),
        "early",
        3,
        [
            shaped(LOW, length, model_width),
            shaped(FULL, length, experts_total),
            shaped(LOW, length, ranks * slab),
            shaped(LOW, ranks * slab, length),
            shaped(FULL, head_count, length, length),
            slabs_shape,
        ],
        [
            tokens,
            routes.reshape(1, length),
            gains,
            d_out,
            rel_bias.T,
            jnp.asarray(bucket_onehot(bucket_count, length), LOW),
        ],
    )

    payload = jnp.concatenate([w_query, w_key, w_value, w_output], axis=1)
    early = (normed_low, hits, mask, mask_t, bias_full)
    pieces, places, early = gather_pieces(payload, early)
    normed_low, hits, mask, mask_t, bias_full = early
    pieces, up_slabs = together(pieces, up_slabs)
    up_arrived = exchange(up_slabs).reshape(ranks * slab, model_width)

    w_shape = (ranks, inner_width, 4 * columns_here)
    heads, weights, attended, hidden, chance, slabs = call(
        functools.partial(forward_kernel, places, slab, rank_slots),
        "attention_forward",
        10,
        [
            shaped(LOW, 3, inner_width, length),
            shaped(FULL, head_count, length, length),
            shaped(LOW, length, inner_width),
            shaped(FULL, length, model_width),
            shaped(FULL, length, experts_total),
            slabs_shape,
        ],
        [tokens, normed_low, seg_ids, bias_full, gains, router_t, hits, mask_t],
        pieces,
        [
            pltpu.VMEM(w_shape, LOW),
            pltpu.VMEM((3, inner_width, length), FULL),
            pltpu.VMEM((inner_width, length), FULL),
            pltpu.SemaphoreType.DMA,
        ],
    )

    slabs, up_arrived = together(slabs, up_arrived)
    arrived = exchange(slabs).reshape(ranks * slab, model_width)
    up_pieces = gather_near(gather_far(up_arrived))
    arrived, up_pieces, normed_own, attended = together(
        arrived, up_pieces, normed_low, attended
    )
    row_far = gather_far(arrived)
    normed_all = lax.all_gather(normed_own, "expert", axis=0)
    attended_all = lax.all_gather(attended, "expert", axis=0)
    by_expert = (local_experts, packed_rows)
    up_rows, up_act = call(
        upstream_kernel,
        "upstream_rows",
        5,
        [shaped(LOW, *by_expert, model_width), shaped(FULL, *by_expert, hidden_here)],
        [pack, w_out, *up_pieces],
    )
    row_far, up_act = together(row_far, up_act)
    row_pieces = gather_near(row_far)

    *back, slot_rows, activated, pre_grad, gates = call(
        functools.partial(expert_kernel, dps, slab, rank_slots),
        "experts",
        10,
        [shaped(LOW, ranks * slab, model_width)] * dps
        + [
            shaped(LOW, *by_expert, model_width),
            shaped(LOW, *by_expert, hidden_here),
            shaped(LOW, *by_expert, hidden_here),
            shaped(FULL, *by_expert, 128),
        ],
        [pack, pack_t, w_in, up_act, *row_pieces],
        scratch=[
            pltpu.VMEM((packed_rows, hidden_here), FULL),
            pltpu.VMEM((*by_expert, model_width), LOW),
            pltpu.VMEM((*by_expert, 128), LOW),
        ],
    )
    kept, got = scatter_terms(back)
    returned = call(
        expert_out_kernel,
        "expert_outputs",
        3,
        [shaped(LOW, ranks * slab, model_width)] * dps,
        [pack_t, w_out, activated],
        scratch=[pltpu.VMEM((*by_expert, model_width), LOW)],
    )
    returned = scatter_near(returned)
    got, returned = together(got, returned)
    back = add(kept, got).reshape(ranks, slab, model_width)
    back = exchange(back)
    returned = add(*scatter_far(returned)).reshape(ranks, slab, model_width)
    back, returned = together(back, returned)
    returned = exchange(returned)

    bias_rows = -(-head_count // 6)
    small_rows = -(-(experts_total + 2 + bias_rows) // 8) * 8
    d_input, small, factors = call(
        functools.partial(backward_kernel, places, rank_slots),
        "attention_backward",
        12,
        [
            shaped(FULL, length, model_width),
            shaped(FULL, small_rows, model_width),
            shaped(LOW, ranks, 4 * columns_here, length),
        ],
        [
            tokens,
            gains,
            router_t,
            hits,
            mask,
            d_out,
            hidden,
            chance,
            heads,
            weights,
            jnp.asarray(bucket_onehot(bucket_count, length), FULL),
        ],
        pieces,
        [
            pltpu.VMEM(w_shape, LOW),
            pltpu.VMEM((inner_width, length), FULL),
            pltpu.VMEM((3, inner_width, length), FULL),
            pltpu.VMEM((head_count, 2 * length), FULL),
            pltpu.SemaphoreType.DMA,
        ],
        [back],
    )

    factors, small, returned, activated = together(factors, small, returned, activated)
    factors = exchange(factors)
    first_grad, second_grad, token = call(
        expert_grad_kernel,
        "expert_gradients",
        8,
        [shaped(FULL, *w_in.shape), shaped(FULL, *w_out.shape), shaped(FULL, 8, 128)],
        [slot_rows, activated, pre_grad, gates, up_rows],
    )
    *steps, one_but_last, last = sum_steps()
    for axis, bit in steps:
        small = small + swap(small, axis, bit)
    factors, small, token = together(factors, small, token)
    small = small + swap(small, *one_but_last)
    output, *grads = call(
        product_kernel,
        "weight_gradients",
        5,
        [shaped(LOW, length, model_width)] + [shaped(LOW, rows_here, 4 * columns_here)] * dps,
        [
            normed_all,
            attended_all,
            hidden,
            chance,
            hits,
            mask,
            factors,
            returned,
            token,
        ],
        scratch=[pltpu.VMEM((dps, rows_here, 4 * columns_here), FULL)],
    )
    grads, small = together(scatter_near(grads), small)
    small = small + swap(small, *last)
    grads = add(*scatter_far(grads), FULL)
    g_query, g_key, g_value, g_output = (
        grads[:, i * columns_here : (i + 1) * columns_here] for i in range(4)
    )
    g_router = small[:experts_total].T
    g_ffn_gain, g_attn_gain = small[experts_total], small[experts_total + 1]
    g_rel_bias = small[experts_total + 2 : experts_total + 2 + bias_rows].reshape(-1, 128)
    g_rel_bias = g_rel_bias[:head_count, :bucket_count].T
    return (
        output,
        d_input,
        g_attn_gain,
        g_query,
        g_key,
        g_value,
        g_output,
        g_rel_bias,
        g_ffn_gain,
        g_router,
        first_grad,
        second_grad,
    )


def solution(mesh):
    return jax.shard_map(
        per_device,
        mesh=mesh,
        in_specs=(
            P(("dp", "expert"), None),
            P(("dp", "expert"), None),
            P(("dp", "expert"), None),
            P(),
            P("dp", "expert"),
            P("dp", "expert"),
            P("dp", "expert"),
            P("dp", "expert"),
            P(),
            P(),
            P(),
            P("expert", None, "dp"),
            P("expert", "dp", None),
            P(("dp", "expert"), None),
        ),
        out_specs=(
            P(("dp", "expert"), None),
            P(("dp", "expert"), None),
            P(),
            P("dp", "expert"),
            P("dp", "expert"),
            P("dp", "expert"),
            P("dp", "expert"),
            P(),
            P(),
            P(),
            P("expert", None, "dp"),
            P("expert", "dp", None),
        ),
        check_vma=False,
    )
```

```python
import functools

import jax
import jax.numpy as jnp
import numpy as np
from jax import lax
from jax.experimental import pallas as pl
from jax.experimental.pallas import tpu as pltpu
from jax.sharding import PartitionSpec as P

EPSILON = 1e-06
LIMITS = (12, 16, 23, 32, 46, 64, 91)
MASKED = -1000000000.0
HIGHEST = lax.Precision.HIGHEST
LOW = jnp.bfloat16
FULL = jnp.float32


def bucket_onehot(buckets, length):
    delta = np.arange(2 * length) - length
    magnitude = np.abs(delta)
    distant = 8 + sum((magnitude >= threshold).astype(np.int32) for threshold in LIMITS)
    ids = np.where(delta > 0, 16, 0) + np.where(magnitude < 8, magnitude, distant)
    return (ids[None, :] == np.arange(buckets)[:, None]).astype(np.float32)


def packing(local_experts, ranks, capacity, slab):
    table = np.zeros((local_experts, ranks, capacity, ranks, slab), np.float32)
    for e in range(local_experts):
        for r in range(ranks):
            for c in range(capacity):
                table[e, r, c, r, e * capacity + c] = 1.0
    return table.reshape(local_experts * ranks * capacity, ranks * slab)


def normalize(matrix, gain_vec):
    scale = lax.rsqrt(jnp.mean(matrix * matrix, axis=-1, keepdims=True) + EPSILON)
    return (matrix * scale * gain_vec, scale)


def norm_back(matrix, scale, gain_vec, incoming):
    weighted = incoming * gain_vec
    average = jnp.mean(matrix * weighted, axis=-1, keepdims=True)
    return (
        scale * weighted - matrix * (scale * scale * scale) * average,
        jnp.sum(incoming * matrix * scale, axis=0, keepdims=True),
    )


def swap(value, axis, mask):
    count = lax.axis_size(axis)
    return lax.ppermute(value, axis, [(i, i ^ mask) for i in range(count)])


def gather_bits(value, axis, masks):
    return jnp.concatenate([value] + [swap(value, axis, mask) for mask in masks], axis=0)


def exchange(value):
    return lax.all_to_all(value, "expert", split_axis=0, concat_axis=0, tiled=True)


def halves():
    half = lax.axis_size("expert") // 2
    return [list(range(half)), list(range(half, 2 * half))]


def gather_far(value):
    found = {0: value}
    bit = lax.axis_size("dp") // 2
    while bit > 1:
        found.update({index ^ bit: swap(item, "dp", bit) for index, item in found.items()})
        bit = bit // 2
    return found


def gather_near(found):
    found = {**found, **{index ^ 1: swap(item, "dp", 1) for index, item in found.items()}}
    return [found[index] for index in range(len(found))]


def add(left, right, dtype=LOW):
    return (left.astype(FULL) + right.astype(FULL)).astype(dtype)


def scatter_near(items):
    taken = [swap(item, "dp", 1) for item in items[1::2]]
    return [add(kept, got) for kept, got in zip(items[0::2], taken)]


def scatter_far(items):
    bit = 2
    while len(items) > 2:
        taken = [swap(item, "dp", bit) for item in items[1::2]]
        items = [add(kept, got) for kept, got in zip(items[0::2], taken)]
        bit = bit * 2
    return items[0], swap(items[1], "dp", bit)


def scatter_terms(items):
    return scatter_far(scatter_near(items))


def sum_steps():
    steps = []
    for axis in ("dp", "expert"):
        bit = 1
        while bit < lax.axis_size(axis):
            steps.append((axis, bit))
            bit = bit * 2
    return steps


def together(*values):
    return lax.optimization_barrier(values)


def gather_pieces(payload, early):
    ranks, dps = lax.axis_size("expert"), lax.axis_size("dp")
    half = payload.shape[0] // 2
    far = list(range(0, ranks, 2))
    sides = {"x": ("expert", [0, 1]), "y": ("dp", list(range(0, dps, 2)))}
    value, early = together(gather_bits(payload[None], "expert", far[1:]), early)
    values = (value[:, :half], value[:, half:])
    firsts = []
    for value, letter in zip(values, "xy"):
        axis, masks = sides[letter]
        firsts.append(gather_bits(value[None], axis, masks[1:]))
    seconds = []
    for value, letter in zip(firsts, "yx"):
        axis, masks = sides[letter]
        seconds.append([swap(value, axis, mask) for mask in masks[1:]])
    others = [swap(value, "dp", 1) for value in firsts]
    pieces, places = [], []
    for index, order in enumerate(("xy", "yx")):
        masks, other_masks = sides[order[0]][1], sides[order[1]][1]
        found = [(firsts[index], 0, 0), (others[index], 0, 1)]
        for value, mask in zip(seconds[index], other_masks[1:]):
            found += [(value, mask, 0), (swap(value, "dp", 1), mask, 1)]
        for piece, mask, core in found:
            offsets = []
            for first in masks:
                for low in far:
                    x_mask, y_mask = (first, mask) if order == "xy" else (mask, first)
                    offsets.append((low ^ x_mask, y_mask ^ core))
            pieces.append(piece)
            places.append((index, offsets))
    return pieces, places, early


def place_weights(places, piece_refs, w_ref, sem):
    my_expert, my_dp = lax.axis_index("expert"), lax.axis_index("dp")
    copies = []
    for ref, (half, offsets) in zip(piece_refs, places):
        low_count, rows = ref.shape[1], ref.shape[2]
        for index, (e_mask, d_mask) in enumerate(offsets):
            start = (my_dp ^ d_mask) * (2 * rows) + half * rows
            copies.append(
                pltpu.make_async_copy(
                    ref.at[index // low_count, index % low_count],
                    w_ref.at[my_expert ^ e_mask, pl.ds(pl.multiple_of(start, 16), rows), :],
                    sem,
                )
            )
    for copy in copies:
        copy.start()
    return copies


def dot(left, right, dims=((1,), (0,)), precision=None):
    return lax.dot_general(
        left, right, (dims, ((), ())), precision=precision, preferred_element_type=FULL
    )


NT = ((1,), (1,))
TN = ((0,), (0,))


def grid_of(rows):
    sub = lax.broadcasted_iota(jnp.int32, (rows, 128), 0)
    lane = lax.broadcasted_iota(jnp.int32, (rows, 128), 1)
    return sub, lane


def row_to_column(row, rows, shift=0):
    sub, lane = grid_of(rows)
    column = jnp.sum(jnp.where(lane == sub + shift, row, 0.0), axis=1, keepdims=True)
    return jnp.broadcast_to(column, (rows, 128))


def column_to_row(column, shift=0):
    sub, lane = grid_of(column.shape[0])
    return jnp.sum(jnp.where(lane == sub + shift, column, 0.0), axis=0, keepdims=True)


def turn(value, shift):
    return pltpu.roll(value, shift % value.shape[1], 1)


def slide(value, direction):
    sub = lax.broadcasted_iota(jnp.int32, value.shape, 0)
    for bit in (1, 2, 4):
        value = jnp.where((sub & bit) != 0, turn(value, direction * bit), value)
    return value


def slid_rows(row, count):
    value = slide(jnp.broadcast_to(row, (8, row.shape[1])), 1)
    while value.shape[0] < count:
        value = jnp.concatenate([value, turn(value, value.shape[0])], axis=0)
    return value


def slid_sum(value):
    while value.shape[0] > 8:
        half = value.shape[0] // 2
        value = value[:half] + turn(value[half:], -half)
    return jnp.sum(slide(value, -1), axis=0, keepdims=True)


def early_kernel(
    ranks, local_experts, capacity, slab, tokens_ref, routes_ref, gain_ref, d_out_ref, table_ref,
    onehot_ref, normed_ref, hits_ref, mask_ref, mask_t_ref, bias_ref, up_ref
):
    length = tokens_ref.shape[0]
    normed, _ = normalize(tokens_ref[...].astype(FULL), gain_ref[0:1, :])
    normed_ref[...] = normed.astype(LOW)
    experts = hits_ref.shape[1]
    routes = jnp.broadcast_to(routes_ref[...].astype(FULL), (length, length)).T
    route = routes[:, :1].astype(jnp.int32)
    lanes = lax.broadcasted_iota(jnp.int32, (length, experts), 1)
    hits = (lanes == route).astype(FULL)
    hits_ref[...] = hits
    row = lax.broadcasted_iota(jnp.int32, (length, length), 0)
    col = lax.broadcasted_iota(jnp.int32, (length, length), 1)
    before = dot((col < row).astype(FULL).astype(LOW), hits.astype(LOW))
    placed = jnp.sum(before * hits, axis=1, keepdims=True).astype(jnp.int32)
    rank = jnp.zeros_like(route)
    for r in range(1, ranks):
        rank = rank + (route >= r * local_experts).astype(jnp.int32)
    spot = rank * slab + (route - rank * local_experts) * capacity + placed
    spot = jnp.where(placed < capacity, spot, -1)
    places = lax.broadcasted_iota(jnp.int32, (length, ranks * slab), 1)
    mask = (places == spot).astype(FULL)
    mask_ref[...] = mask.astype(LOW)
    mask_t = mask.T.astype(LOW)
    mask_t_ref[...] = mask_t
    slabs = dot(mask_t, d_out_ref[...])
    for r in range(ranks):
        up_ref[r] = slabs[r * slab : (r + 1) * slab].astype(LOW)
    values = dot(table_ref[...], onehot_ref[...])
    for h in range(bias_ref.shape[0]):
        bias_ref[h] = slid_rows(values[h : h + 1], length)[:, length:]


def forward_kernel(
    places, slab, rank_slots, tokens_ref, normed_ref, seg_ref, bias_ref, gain_ref,
    router_t_ref, hits_ref, mask_t_ref, *rest
):
    count = len(places)
    piece_refs, rest = rest[:count], rest[count:]
    heads_ref, weights_ref, attended_ref, hidden_ref, chance_ref = rest[:5]
    slabs_ref = rest[5]
    w_ref, qkv_ref, att_t_ref, sem = rest[-4:]
    copies = place_weights(places, piece_refs, w_ref, sem)
    ranks, width, columns = w_ref.shape
    cols = columns // 4
    head_count = weights_ref.shape[0]
    head = width // head_count
    length = tokens_ref.shape[0]
    segments = jnp.broadcast_to(seg_ref[...].astype(FULL), (length, length))
    same_doc = segments == segments.T
    normed = normed_ref[...]
    for copy in copies:
        copy.wait()
    for e in range(ranks):
        turned = dot(normed, w_ref[e]).T
        for m in range(3):
            qkv_ref[m, e * cols : (e + 1) * cols, :] = turned[m * cols : (m + 1) * cols]
    heads_ref[...] = qkv_ref[...].astype(LOW)
    for h in range(head_count):
        rows = slice(h * head, (h + 1) * head)
        scores = dot(heads_ref[0, rows, :], heads_ref[1, rows, :], TN) * head ** (-0.5)
        scores = jnp.where(same_doc, scores + bias_ref[h], MASKED)
        grown = jnp.exp(scores - jnp.max(scores, axis=1, keepdims=True))
        weights = grown / jnp.sum(grown, axis=1, keepdims=True)
        weights_ref[h] = weights
        att_t_ref[rows, :] = dot(heads_ref[2, rows, :], weights.astype(LOW), NT)
    attended = att_t_ref[...].T.astype(LOW)
    attended_ref[...] = attended
    low_lane = 3 * cols // 128 * 128
    for e in range(ranks):
        turned = dot(attended, w_ref[e, :, low_lane:]).T
        att_t_ref[e * cols : (e + 1) * cols, :] = turned[3 * cols - low_lane :]
    hidden = tokens_ref[...].astype(FULL) + att_t_ref[...].T
    hidden_ref[...] = hidden
    normed_two, _ = normalize(hidden, gain_ref[1:2, :])
    logits = dot(normed_two, router_t_ref[...].astype(FULL), NT, HIGHEST)
    grown = jnp.exp(logits - jnp.max(logits, axis=1, keepdims=True))
    chance = grown / jnp.sum(grown, axis=1, keepdims=True)
    chance_ref[...] = chance
    gate = jnp.sum(chance * hits_ref[...], axis=1, keepdims=True)
    mask_t = mask_t_ref[...]
    slots = dot(mask_t, normed_two.astype(LOW))
    gates = dot(mask_t.astype(FULL), jnp.broadcast_to(gate, (length, 128)), precision=HIGHEST)
    sub, _ = grid_of(slab)
    for r in range(ranks):
        mine = gates[r * slab : (r + 1) * slab]
        high = mine.astype(LOW).astype(FULL)
        row = column_to_row(high) + column_to_row(mine - high, 64)
        rows = slots[r * slab : (r + 1) * slab]
        start = rows[:, :128] + jnp.where(sub == rank_slots, row, 0.0)
        slabs_ref[r, :, :128] = start.astype(LOW)
        slabs_ref[r, :, 128:] = rows[:, 128:].astype(LOW)


def upstream_kernel(pack_ref, w_out_ref, *rest):
    piece_refs, (rows_ref, act_ref) = rest[:-2], rest[-2:]
    local_experts = w_out_ref.shape[0]
    chunk = pack_ref.shape[0] // local_experts
    for p, piece in enumerate(piece_refs):
        packed = dot(pack_ref[...], piece[...]).astype(LOW)
        for e in range(local_experts):
            rows_ref[e, p * chunk : (p + 1) * chunk, :] = packed[e * chunk : (e + 1) * chunk]
    for e in range(local_experts):
        act_ref[e] = dot(rows_ref[e], w_out_ref[e], NT)


def unpack(pack_t, rows_ref, p, chunk):
    rows = [rows_ref[e, p * chunk : (p + 1) * chunk, :] for e in range(rows_ref.shape[0])]
    return dot(pack_t, jnp.concatenate(rows, axis=0))


def expert_kernel(
    count, slab, rank_slots, pack_ref, pack_t_ref, w_in_ref, up_act_ref, *rest
):
    piece_refs, rest = rest[:count], rest[count:]
    back_refs, rest = rest[:count], rest[count:]
    rows_ref, act_ref, pre_grad_ref, gates_ref, pre_ref, back_ref, part_ref = rest
    local_experts = w_in_ref.shape[0]
    chunk = pack_ref.shape[0] // local_experts
    ranks = pack_ref.shape[1] // slab
    pack, pack_t = pack_ref[...], pack_t_ref[...]
    for p, piece in enumerate(piece_refs):
        packed = dot(pack, piece[...]).astype(LOW)
        tile = piece[:, :128].astype(FULL)
        spread = []
        for shift in (0, 64):
            columns = [
                row_to_column(tile[r * slab + rank_slots : r * slab + rank_slots + 1], slab, shift)
                for r in range(ranks)
            ]
            spread.append(dot(pack, jnp.concatenate(columns, axis=0).astype(LOW)))
        gates = spread[0] + spread[1]
        for e in range(local_experts):
            rows_ref[e, p * chunk : (p + 1) * chunk, :] = packed[e * chunk : (e + 1) * chunk]
            gates_ref[e, p * chunk : (p + 1) * chunk, :] = gates[e * chunk : (e + 1) * chunk]
    root = np.float32(np.sqrt(2.0 / np.pi))
    step = 16
    for e in range(local_experts):
        pre_ref[...] = dot(rows_ref[e], w_in_ref[e])

        def body(index, carry):
            span = pl.ds(pl.multiple_of(index * step, step), step)
            pre = pre_ref[span, :]
            up = up_act_ref[e, span, :]
            square = pre * pre
            curve = jnp.tanh(root * pre * (1.0 + 0.044715 * square))
            rise = 0.5 + 0.5 * curve
            act = (pre * rise).astype(LOW)
            act_ref[e, span, :] = act
            slope = rise + pre * (rise * (1.0 - curve)) * (root + 3 * 0.044715 * root * square)
            gate = gates_ref[e, span, :][:, :1]
            pre_grad_ref[e, span, :] = (slope * (up * gate)).astype(LOW)
            part = jnp.sum(act.astype(FULL) * up, axis=1, keepdims=True)
            part_ref[e, span, :] = jnp.broadcast_to(part, (step, 128)).astype(LOW)
            return carry

        lax.fori_loop(0, pre_ref.shape[0] // step, body, 0, unroll=2)
        back_ref[e] = dot(pre_grad_ref[e], w_in_ref[e], NT).astype(LOW)
    sub, _ = grid_of(slab)
    for p in range(count):
        rows = unpack(pack_t, back_ref, p, chunk)
        parts = unpack(pack_t, part_ref, p, chunk)
        pieces = []
        for r in range(ranks):
            span = slice(r * slab, (r + 1) * slab)
            row = column_to_row(parts[span])
            pieces.append(rows[span, :128] + jnp.where(sub == rank_slots, row, 0.0))
        back_refs[p][:, :128] = jnp.concatenate(pieces, axis=0).astype(LOW)
        back_refs[p][:, 128:] = rows[:, 128:].astype(LOW)


def expert_out_kernel(pack_t_ref, w_out_ref, act_ref, *rest):
    out_refs, returned_ref = rest[:-1], rest[-1]
    chunk = act_ref.shape[1] // len(out_refs)
    for e in range(w_out_ref.shape[0]):
        returned_ref[e] = dot(act_ref[e], w_out_ref[e]).astype(LOW)
    for p, ref in enumerate(out_refs):
        ref[...] = unpack(pack_t_ref[...], returned_ref, p, chunk).astype(LOW)


def expert_grad_kernel(
    rows_ref, act_ref, pre_grad_ref, gates_ref, up_rows_ref, g_in_ref, g_out_ref, token_ref
):
    for e in range(rows_ref.shape[0]):
        g_in_ref[e] = dot(rows_ref[e], pre_grad_ref[e], TN)
        slot_grad = (up_rows_ref[e].astype(FULL) * gates_ref[e][:, :1]).astype(LOW)
        g_out_ref[e] = dot(act_ref[e], slot_grad, TN)
    token_ref[...] = jnp.zeros(token_ref.shape, FULL)


def joined(ref):
    ranks, slab, width = ref.shape
    return ref[...].astype(FULL).reshape(ranks * slab, width).astype(LOW)


def backward_kernel(
    places, rank_slots, tokens_ref, gain_ref, router_t_ref, hits_ref, mask_ref,
    up_ref, hidden_ref, chance_ref, heads_ref, weights_ref, onehot_ref, *rest
):
    count = len(places)
    piece_refs, rest = rest[:count], rest[count:]
    (back_ref, d_input_ref, small_ref, factors_ref,
     w_ref, turned_ref, grads_ref, bias_ref, sem) = rest
    ranks, width, columns = w_ref.shape
    copies = place_weights(places, piece_refs, w_ref, sem)
    cols = columns // 4
    head_count = weights_ref.shape[0]
    head = width // head_count
    factor = head ** (-0.5)
    length = tokens_ref.shape[0]
    slab = back_ref.shape[1]
    hidden = hidden_ref[...]
    gain_two = gain_ref[1:2, :]
    normed_two, scale_two = normalize(hidden, gain_two)
    mask = mask_ref[...]
    chance, hits = chance_ref[...], hits_ref[...]
    gate = jnp.sum(chance * hits, axis=1, keepdims=True)
    spread = [
        row_to_column(back_ref[r, :, :128].astype(FULL)[rank_slots : rank_slots + 1], slab)
        for r in range(ranks)
    ]
    gate_grad = dot(mask, jnp.concatenate(spread, axis=0).astype(LOW))[:, :1]
    logit_grad = chance * (hits - gate) * gate_grad
    experts = hits.shape[1]
    small_ref[:experts, :] = dot(logit_grad, normed_two, TN, HIGHEST)
    router_t = router_t_ref[...].astype(FULL)
    normed_two_grad = dot(logit_grad, router_t, precision=HIGHEST) + dot(mask, joined(back_ref))
    hidden_part, ffn_gain_grad = norm_back(hidden, scale_two, gain_two, normed_two_grad)
    hidden_grad = up_ref[...].astype(FULL) + hidden_part
    turned_ref[...] = hidden_grad.astype(LOW).astype(FULL).T
    for copy in copies:
        copy.wait()
    low_lane = 3 * cols // 128 * 128
    att_grad = None
    for e in range(ranks):
        own = turned_ref[e * cols : (e + 1) * cols, :]
        if 3 * cols > low_lane:
            own = jnp.concatenate([jnp.zeros((3 * cols - low_lane, 128), FULL), own], axis=0)
        part = dot(w_ref[e, :, low_lane:], own.astype(LOW))
        att_grad = part if att_grad is None else att_grad + part
    att_grad = att_grad.astype(LOW)
    for h in range(head_count):
        rows = slice(h * head, (h + 1) * head)
        own = att_grad[rows]
        weights = weights_ref[h]
        grads_ref[2, rows, :] = dot(own, weights.astype(LOW))
        prob_grad = dot(own, heads_ref[2, rows, :], TN)
        score_grad = weights * (prob_grad - jnp.sum(prob_grad * weights, axis=1, keepdims=True))
        score_grad = score_grad.astype(LOW)
        grads_ref[0, rows, :] = dot(heads_ref[1, rows, :], score_grad, NT) * factor
        grads_ref[1, rows, :] = dot(heads_ref[0, rows, :], score_grad) * factor
        wide = [jnp.zeros((length, length), FULL), score_grad.astype(FULL)]
        bias_ref[h : h + 1, :] = slid_sum(jnp.concatenate(wide, axis=1))
    total = None
    for e in range(ranks):
        span = slice(e * cols, (e + 1) * cols)
        held = [grads_ref[m, span, :] for m in range(3)] + [jnp.zeros((cols, 128), FULL)]
        part = dot(w_ref[e], jnp.concatenate(held, axis=0).astype(LOW))
        total = part if total is None else total + part
        sent = [grads_ref[m, span, :] for m in range(3)] + [turned_ref[span, :]]
        sent = jnp.concatenate(sent, axis=0).astype(LOW)
        factors_ref[e % (ranks // 2), e // (ranks // 2)] = sent
    inputs = tokens_ref[...].astype(FULL)
    gain_one = gain_ref[0:1, :]
    _, scale_one = normalize(inputs, gain_one)
    norm_part, attn_gain_grad = norm_back(inputs, scale_one, gain_one, total.T)
    d_input_ref[...] = hidden_grad + norm_part
    sums = dot(bias_ref[...], onehot_ref[...], NT, HIGHEST)
    small_ref[experts : experts + 1, :] = ffn_gain_grad
    small_ref[experts + 1 : experts + 2, :] = attn_gain_grad
    small_ref[experts + 2 :, :] = jnp.zeros((small_ref.shape[0] - experts - 2, width), FULL)
    for h in range(head_count):
        line, place = experts + 2 + h // 6, 128 * (h % 6)
        small_ref[line : line + 1, place : place + sums.shape[1]] = sums[h : h + 1]


def product_kernel(normed_ref, attended_ref, factors_ref, token_ref, *rest):
    piece_refs, total_ref = rest[:-1], rest[-1]
    count, _, columns, length = factors_ref.shape
    cols = columns // 4
    rows = total_ref.shape[2]
    for side in range(2):
        first, second = None, None
        for e in range(count):
            held = factors_ref[e, side].astype(FULL)
            part = dot(held[: 3 * cols].astype(LOW), normed_ref[e])
            first = part if first is None else first + part
            part = dot(held[3 * cols :].astype(LOW), attended_ref[e])
            second = part if second is None else second + part
        total = jnp.concatenate([first, second], axis=0).T
        for j in range(len(piece_refs)):
            total_ref[side, j] = total[j * rows : (j + 1) * rows]
    own = (lax.axis_index("expert") >= count).astype(jnp.int32)
    for j, ref in enumerate(piece_refs):
        place = lax.axis_index("dp") ^ j
        ref[0] = total_ref[own, place].astype(LOW)
        ref[1] = total_ref[1 - own, place].astype(LOW)


def output_kernel(hidden_ref, chance_ref, hits_ref, mask_ref, returned_ref, output_ref):
    gate = jnp.sum(chance_ref[...] * hits_ref[...], axis=1, keepdims=True)
    fetched = dot(mask_ref[...], joined(returned_ref))
    output_ref[...] = (hidden_ref[...] + gate * fetched).astype(LOW)


VMEM = pl.BlockSpec(memory_space=pltpu.VMEM)
ANY = pl.BlockSpec(memory_space=pl.ANY)
LIMIT = 60 * 1024 * 1024


def shaped(dtype, *shape):
    return jax.ShapeDtypeStruct(shape, dtype)


def call(kernel, name, micros, out_shape, args, pieces=(), scratch=(), more=()):
    return pl.pallas_call(
        kernel,
        out_shape=tuple(out_shape),
        in_specs=[VMEM] * len(args) + [ANY] * len(pieces) + [VMEM] * len(more),
        out_specs=(VMEM,) * len(out_shape),
        scratch_shapes=list(scratch),
        compiler_params=pltpu.CompilerParams(vmem_limit_bytes=LIMIT),
        cost_estimate=pl.CostEstimate(
            flops=0, bytes_accessed=micros * 3_600_000, transcendentals=0
        ),
        name=name,
    )(*args, *pieces, *more)


def per_device(
    tokens,
    seg_ids,
    routes,
    attn_gain,
    w_query,
    w_key,
    w_value,
    w_output,
    rel_bias,
    ffn_gain,
    w_router,
    w_in,
    w_out,
    d_out,
):
    length, model_width = tokens.shape
    bucket_count, head_count = rel_bias.shape
    experts_total = w_router.shape[1]
    local_experts, _, hidden_here = w_in.shape
    ranks, dps = lax.axis_size("expert"), lax.axis_size("dp")
    capacity = length * 5 // (4 * experts_total)
    rank_slots = local_experts * capacity
    slab = -(-(rank_slots + 1) // 8) * 8
    rows_here, columns_here = w_query.shape
    inner_width = dps * rows_here
    packed_rows = dps * ranks * capacity
    gains = jnp.stack([attn_gain, ffn_gain]).astype(FULL)
    slabs_shape = shaped(LOW, ranks, slab, model_width)
    router_t = w_router.T
    pack = packing(local_experts, ranks, capacity, slab)
    pack, pack_t = jnp.asarray(pack, LOW), jnp.asarray(pack.T, LOW)

    normed_low, hits, mask, mask_t, bias_full, up_slabs = call(
        functools.partial(early_kernel, ranks, local_experts, capacity, slab),
        "early",
        3,
        [
            shaped(LOW, length, model_width),
            shaped(FULL, length, experts_total),
            shaped(LOW, length, ranks * slab),
            shaped(LOW, ranks * slab, length),
            shaped(FULL, head_count, length, length),
            slabs_shape,
        ],
        [
            tokens,
            routes.reshape(1, length),
            gains,
            d_out,
            rel_bias.T,
            jnp.asarray(bucket_onehot(bucket_count, length), LOW),
        ],
    )

    payload = jnp.concatenate([w_query, w_key, w_value, w_output], axis=1)
    early = (normed_low, hits, mask, mask_t, bias_full)
    pieces, places, early = gather_pieces(payload, early)
    normed_low, hits, mask, mask_t, bias_full = early
    pieces, up_slabs = together(pieces, up_slabs)
    up_arrived = exchange(up_slabs).reshape(ranks * slab, model_width)

    w_shape = (ranks, inner_width, 4 * columns_here)
    heads, weights, attended, hidden, chance, slabs = call(
        functools.partial(forward_kernel, places, slab, rank_slots),
        "attention_forward",
        10,
        [
            shaped(LOW, 3, inner_width, length),
            shaped(FULL, head_count, length, length),
            shaped(LOW, length, inner_width),
            shaped(FULL, length, model_width),
            shaped(FULL, length, experts_total),
            slabs_shape,
        ],
        [tokens, normed_low, seg_ids, bias_full, gains, router_t, hits, mask_t],
        pieces,
        [
            pltpu.VMEM(w_shape, LOW),
            pltpu.VMEM((3, inner_width, length), FULL),
            pltpu.VMEM((inner_width, length), FULL),
            pltpu.SemaphoreType.DMA,
        ],
    )

    slabs, up_arrived = together(slabs, up_arrived)
    arrived = exchange(slabs).reshape(ranks * slab, model_width)
    up_pieces = gather_near(gather_far(up_arrived))
    arrived, up_pieces, normed_own, attended = together(
        arrived, up_pieces, normed_low, attended
    )
    row_far = gather_far(arrived)
    normed_half = lax.all_gather(normed_own, "expert", axis=0, axis_index_groups=halves())
    attended_half = lax.all_gather(attended, "expert", axis=0, axis_index_groups=halves())
    by_expert = (local_experts, packed_rows)
    up_rows, up_act = call(
        upstream_kernel,
        "upstream_rows",
        5,
        [shaped(LOW, *by_expert, model_width), shaped(FULL, *by_expert, hidden_here)],
        [pack, w_out, *up_pieces],
    )
    row_far, up_act = together(row_far, up_act)
    row_pieces = gather_near(row_far)

    *back, slot_rows, activated, pre_grad, gates = call(
        functools.partial(expert_kernel, dps, slab, rank_slots),
        "experts",
        10,
        [shaped(LOW, ranks * slab, model_width)] * dps
        + [
            shaped(LOW, *by_expert, model_width),
            shaped(LOW, *by_expert, hidden_here),
            shaped(LOW, *by_expert, hidden_here),
            shaped(FULL, *by_expert, 128),
        ],
        [pack, pack_t, w_in, up_act, *row_pieces],
        scratch=[
            pltpu.VMEM((packed_rows, hidden_here), FULL),
            pltpu.VMEM((*by_expert, model_width), LOW),
            pltpu.VMEM((*by_expert, 128), LOW),
        ],
    )
    kept, got = scatter_terms(back)
    first_grad, second_grad, token = call(
        expert_grad_kernel,
        "expert_gradients",
        8,
        [shaped(FULL, *w_in.shape), shaped(FULL, *w_out.shape), shaped(FULL, 8, 128)],
        [slot_rows, activated, pre_grad, gates, up_rows],
    )
    got, token = together(got, token)
    back = add(kept, got).reshape(ranks, slab, model_width)
    back, activated = together(back, activated)
    back = exchange(back)
    returned = call(
        expert_out_kernel,
        "expert_outputs",
        12,
        [shaped(LOW, ranks * slab, model_width)] * dps,
        [pack_t, w_out, activated],
        scratch=[pltpu.VMEM((*by_expert, model_width), LOW)],
    )
    returned = scatter_near(returned)
    back, returned = together(back, returned)
    returned = add(*scatter_far(returned)).reshape(ranks, slab, model_width)

    bias_rows = -(-head_count // 6)
    small_rows = -(-(experts_total + 2 + bias_rows) // 8) * 8
    d_input, small, factors = call(
        functools.partial(backward_kernel, places, rank_slots),
        "attention_backward",
        12,
        [
            shaped(FULL, length, model_width),
            shaped(FULL, small_rows, model_width),
            shaped(LOW, ranks // 2, 2, 4 * columns_here, length),
        ],
        [
            tokens,
            gains,
            router_t,
            hits,
            mask,
            d_out,
            hidden,
            chance,
            heads,
            weights,
            jnp.asarray(bucket_onehot(bucket_count, length), FULL),
        ],
        pieces,
        [
            pltpu.VMEM(w_shape, LOW),
            pltpu.VMEM((inner_width, length), FULL),
            pltpu.VMEM((3, inner_width, length), FULL),
            pltpu.VMEM((head_count, 2 * length), FULL),
            pltpu.SemaphoreType.DMA,
        ],
        [back],
    )

    factors, small, returned = together(factors, small, returned)
    factors = lax.all_to_all(
        factors, "expert", split_axis=0, concat_axis=0, tiled=True, axis_index_groups=halves()
    )
    first, *steps, one_but_last, last = sum_steps()
    small = small + swap(small, *first)
    small, returned = together(small, returned)
    returned = exchange(returned)
    for axis, bit in steps:
        small = small + swap(small, axis, bit)
    factors, small = together(factors, small)
    small = small + swap(small, *one_but_last)
    grads = call(
        product_kernel,
        "weight_gradients",
        5,
        [shaped(LOW, 2, rows_here, 4 * columns_here)] * dps,
        [normed_half, attended_half, factors, token],
        scratch=[pltpu.VMEM((2, dps, rows_here, 4 * columns_here), FULL)],
    )
    grads, small = together(scatter_near(grads), small)
    small = small + swap(small, *last)
    (output,) = call(
        output_kernel,
        "output_rows",
        2,
        [shaped(LOW, length, model_width)],
        [hidden, chance, hits, mask, returned],
    )
    kept, got = scatter_far(grads)
    got, output = together(got, output)
    other = swap(add(kept[1], got[1]), "expert", ranks // 2)
    grads = kept[0].astype(FULL) + got[0].astype(FULL) + other.astype(FULL)
    g_query, g_key, g_value, g_output = (
        grads[:, i * columns_here : (i + 1) * columns_here] for i in range(4)
    )
    g_router = small[:experts_total].T
    g_ffn_gain, g_attn_gain = small[experts_total], small[experts_total + 1]
    g_rel_bias = small[experts_total + 2 : experts_total + 2 + bias_rows].reshape(-1, 128)
    g_rel_bias = g_rel_bias[:head_count, :bucket_count].T
    return (
        output,
        d_input,
        g_attn_gain,
        g_query,
        g_key,
        g_value,
        g_output,
        g_rel_bias,
        g_ffn_gain,
        g_router,
        first_grad,
        second_grad,
    )


def solution(mesh):
    return jax.shard_map(
        per_device,
        mesh=mesh,
        in_specs=(
            P(("dp", "expert"), None),
            P(("dp", "expert"), None),
            P(("dp", "expert"), None),
            P(),
            P("dp", "expert"),
            P("dp", "expert"),
            P("dp", "expert"),
            P("dp", "expert"),
            P(),
            P(),
            P(),
            P("expert", None, "dp"),
            P("expert", "dp", None),
            P(("dp", "expert"), None),
        ),
        out_specs=(
            P(("dp", "expert"), None),
            P(("dp", "expert"), None),
            P(),
            P("dp", "expert"),
            P("dp", "expert"),
            P("dp", "expert"),
            P("dp", "expert"),
            P(),
            P(),
            P(),
            P("expert", None, "dp"),
            P("expert", "dp", None),
        ),
        check_vma=False,
    )
```

```python
import functools

import jax
import jax.numpy as jnp
import numpy as np
from jax import lax
from jax.experimental import pallas as pl
from jax.experimental.pallas import tpu as pltpu
from jax.sharding import PartitionSpec as P

EPSILON = 1e-06
LIMITS = (12, 16, 23, 32, 46, 64, 91)
MASKED = -1000000000.0
HIGHEST = lax.Precision.HIGHEST
LOW = jnp.bfloat16
FULL = jnp.float32


def bucket_onehot(buckets, length):
    delta = np.arange(2 * length) - length
    magnitude = np.abs(delta)
    distant = 8 + sum((magnitude >= threshold).astype(np.int32) for threshold in LIMITS)
    ids = np.where(delta > 0, 16, 0) + np.where(magnitude < 8, magnitude, distant)
    return (ids[None, :] == np.arange(buckets)[:, None]).astype(np.float32)


def packing(local_experts, ranks, capacity, slab):
    table = np.zeros((local_experts, ranks, capacity, ranks, slab), np.float32)
    for e in range(local_experts):
        for r in range(ranks):
            for c in range(capacity):
                table[e, r, c, r, e * capacity + c] = 1.0
    return table.reshape(local_experts * ranks * capacity, ranks * slab)


def normalize(matrix, gain_vec):
    scale = lax.rsqrt(jnp.mean(matrix * matrix, axis=-1, keepdims=True) + EPSILON)
    return (matrix * scale * gain_vec, scale)


def norm_back(matrix, scale, gain_vec, incoming):
    weighted = incoming * gain_vec
    average = jnp.mean(matrix * weighted, axis=-1, keepdims=True)
    return (
        scale * weighted - matrix * (scale * scale * scale) * average,
        jnp.sum(incoming * matrix * scale, axis=0, keepdims=True),
    )


def swap(value, axis, mask):
    count = lax.axis_size(axis)
    return lax.ppermute(value, axis, [(i, i ^ mask) for i in range(count)])


def gather_bits(value, axis, masks):
    return jnp.concatenate([value] + [swap(value, axis, mask) for mask in masks], axis=0)


def exchange(value):
    return lax.all_to_all(value, "expert", split_axis=0, concat_axis=0, tiled=True)


def halves():
    half = lax.axis_size("expert") // 2
    return [list(range(half)), list(range(half, 2 * half))]


def gather_far(value):
    found = {0: value}
    bit = lax.axis_size("dp") // 2
    while bit > 1:
        found.update({index ^ bit: swap(item, "dp", bit) for index, item in found.items()})
        bit = bit // 2
    return found


def gather_near(found):
    found = {**found, **{index ^ 1: swap(item, "dp", 1) for index, item in found.items()}}
    return [found[index] for index in range(len(found))]


def add(left, right, dtype=LOW):
    return (left.astype(FULL) + right.astype(FULL)).astype(dtype)


def scatter_near(items):
    taken = [swap(item, "dp", 1) for item in items[1::2]]
    return [add(kept, got) for kept, got in zip(items[0::2], taken)]


def scatter_far(items):
    bit = 2
    while len(items) > 2:
        taken = [swap(item, "dp", bit) for item in items[1::2]]
        items = [add(kept, got) for kept, got in zip(items[0::2], taken)]
        bit = bit * 2
    return items[0], swap(items[1], "dp", bit)


def scatter_terms(items):
    return scatter_far(scatter_near(items))


def sum_steps():
    steps = []
    for axis in ("dp", "expert"):
        bit = 1
        while bit < lax.axis_size(axis):
            steps.append((axis, bit))
            bit = bit * 2
    return steps


def together(*values):
    return lax.optimization_barrier(values)


def gather_pieces(payload, early):
    ranks, dps = lax.axis_size("expert"), lax.axis_size("dp")
    half = payload.shape[0] // 2
    far = list(range(0, ranks, 2))
    sides = {"x": ("expert", [0, 1]), "y": ("dp", list(range(0, dps, 2)))}
    value, early = together(gather_bits(payload[None], "expert", far[1:]), early)
    values = (value[:, :half], value[:, half:])
    firsts = []
    for value, letter in zip(values, "xy"):
        axis, masks = sides[letter]
        firsts.append(gather_bits(value[None], axis, masks[1:]))
    seconds = []
    for value, letter in zip(firsts, "yx"):
        axis, masks = sides[letter]
        seconds.append([swap(value, axis, mask) for mask in masks[1:]])
    others = [swap(value, "dp", 1) for value in firsts]
    pieces, places = [], []
    for index, order in enumerate(("xy", "yx")):
        masks, other_masks = sides[order[0]][1], sides[order[1]][1]
        found = [(firsts[index], 0, 0), (others[index], 0, 1)]
        for value, mask in zip(seconds[index], other_masks[1:]):
            found += [(value, mask, 0), (swap(value, "dp", 1), mask, 1)]
        for piece, mask, core in found:
            offsets = []
            for first in masks:
                for low in far:
                    x_mask, y_mask = (first, mask) if order == "xy" else (mask, first)
                    offsets.append((low ^ x_mask, y_mask ^ core))
            pieces.append(piece)
            places.append((index, offsets))
    return pieces, places, early


def place_weights(places, piece_refs, w_ref, sem):
    my_expert, my_dp = lax.axis_index("expert"), lax.axis_index("dp")
    copies = []
    for ref, (half, offsets) in zip(piece_refs, places):
        low_count, rows = ref.shape[1], ref.shape[2]
        for index, (e_mask, d_mask) in enumerate(offsets):
            start = (my_dp ^ d_mask) * (2 * rows) + half * rows
            copies.append(
                pltpu.make_async_copy(
                    ref.at[index // low_count, index % low_count],
                    w_ref.at[my_expert ^ e_mask, pl.ds(pl.multiple_of(start, 16), rows), :],
                    sem,
                )
            )
    for copy in copies:
        copy.start()
    return copies


def dot(left, right, dims=((1,), (0,)), precision=None):
    return lax.dot_general(
        left, right, (dims, ((), ())), precision=precision, preferred_element_type=FULL
    )


NT = ((1,), (1,))
TN = ((0,), (0,))


def grid_of(rows):
    sub = lax.broadcasted_iota(jnp.int32, (rows, 128), 0)
    lane = lax.broadcasted_iota(jnp.int32, (rows, 128), 1)
    return sub, lane


def row_to_column(row, rows, shift=0):
    sub, lane = grid_of(rows)
    column = jnp.sum(jnp.where(lane == sub + shift, row, 0.0), axis=1, keepdims=True)
    return jnp.broadcast_to(column, (rows, 128))


def column_to_row(column, shift=0):
    sub, lane = grid_of(column.shape[0])
    return jnp.sum(jnp.where(lane == sub + shift, column, 0.0), axis=0, keepdims=True)


def turn(value, shift):
    return pltpu.roll(value, shift % value.shape[1], 1)


def slide(value, direction):
    sub = lax.broadcasted_iota(jnp.int32, value.shape, 0)
    for bit in (1, 2, 4):
        value = jnp.where((sub & bit) != 0, turn(value, direction * bit), value)
    return value


def slid_rows(row, count):
    value = slide(jnp.broadcast_to(row, (8, row.shape[1])), 1)
    while value.shape[0] < count:
        value = jnp.concatenate([value, turn(value, value.shape[0])], axis=0)
    return value


def slid_sum(value):
    while value.shape[0] > 8:
        half = value.shape[0] // 2
        value = value[:half] + turn(value[half:], -half)
    return jnp.sum(slide(value, -1), axis=0, keepdims=True)


def early_kernel(
    ranks, local_experts, capacity, slab, tokens_ref, routes_ref, gain_ref, d_out_ref, table_ref,
    onehot_ref, normed_ref, hits_ref, mask_ref, mask_t_ref, bias_ref, up_ref
):
    length = tokens_ref.shape[0]
    normed, _ = normalize(tokens_ref[...].astype(FULL), gain_ref[0:1, :])
    normed_ref[...] = normed.astype(LOW)
    experts = hits_ref.shape[1]
    routes = jnp.broadcast_to(routes_ref[...].astype(FULL), (length, length)).T
    route = routes[:, :1].astype(jnp.int32)
    lanes = lax.broadcasted_iota(jnp.int32, (length, experts), 1)
    hits = (lanes == route).astype(FULL)
    hits_ref[...] = hits
    row = lax.broadcasted_iota(jnp.int32, (length, length), 0)
    col = lax.broadcasted_iota(jnp.int32, (length, length), 1)
    before = dot((col < row).astype(FULL).astype(LOW), hits.astype(LOW))
    placed = jnp.sum(before * hits, axis=1, keepdims=True).astype(jnp.int32)
    rank = jnp.zeros_like(route)
    for r in range(1, ranks):
        rank = rank + (route >= r * local_experts).astype(jnp.int32)
    spot = rank * slab + (route - rank * local_experts) * capacity + placed
    spot = jnp.where(placed < capacity, spot, -1)
    places = lax.broadcasted_iota(jnp.int32, (length, ranks * slab), 1)
    mask = (places == spot).astype(FULL)
    mask_ref[...] = mask.astype(LOW)
    mask_t = mask.T.astype(LOW)
    mask_t_ref[...] = mask_t
    slabs = dot(mask_t, d_out_ref[...])
    for r in range(ranks):
        up_ref[r] = slabs[r * slab : (r + 1) * slab].astype(LOW)
    values = dot(table_ref[...], onehot_ref[...])
    for h in range(bias_ref.shape[0]):
        bias_ref[h] = slid_rows(values[h : h + 1], length)[:, length:]


def forward_kernel(
    places, slab, rank_slots, tokens_ref, normed_ref, seg_ref, bias_ref, gain_ref,
    router_t_ref, hits_ref, mask_t_ref, *rest
):
    count = len(places)
    piece_refs, rest = rest[:count], rest[count:]
    heads_ref, weights_ref, rows_ref, hidden_ref, chance_ref = rest[:5]
    slabs_ref = rest[5]
    w_ref, qkv_ref, att_t_ref, sem = rest[-4:]
    copies = place_weights(places, piece_refs, w_ref, sem)
    ranks, width, columns = w_ref.shape
    cols = columns // 4
    head_count = weights_ref.shape[0]
    head = width // head_count
    length = tokens_ref.shape[0]
    segments = jnp.broadcast_to(seg_ref[...].astype(FULL), (length, length))
    same_doc = segments == segments.T
    normed = normed_ref[...]
    for copy in copies:
        copy.wait()
    for e in range(ranks):
        turned = dot(normed, w_ref[e]).T
        for m in range(3):
            qkv_ref[m, e * cols : (e + 1) * cols, :] = turned[m * cols : (m + 1) * cols]
    heads_ref[...] = qkv_ref[...].astype(LOW)
    for h in range(head_count):
        rows = slice(h * head, (h + 1) * head)
        scores = dot(heads_ref[0, rows, :], heads_ref[1, rows, :], TN) * head ** (-0.5)
        scores = jnp.where(same_doc, scores + bias_ref[h], MASKED)
        grown = jnp.exp(scores - jnp.max(scores, axis=1, keepdims=True))
        weights = grown / jnp.sum(grown, axis=1, keepdims=True)
        weights_ref[h] = weights
        att_t_ref[rows, :] = dot(heads_ref[2, rows, :], weights.astype(LOW), NT)
    attended = att_t_ref[...].T.astype(LOW)
    rows_ref[0] = normed
    rows_ref[1] = attended
    low_lane = 3 * cols // 128 * 128
    for e in range(ranks):
        turned = dot(attended, w_ref[e, :, low_lane:]).T
        att_t_ref[e * cols : (e + 1) * cols, :] = turned[3 * cols - low_lane :]
    hidden = tokens_ref[...].astype(FULL) + att_t_ref[...].T
    hidden_ref[...] = hidden
    normed_two, _ = normalize(hidden, gain_ref[1:2, :])
    logits = dot(normed_two, router_t_ref[...].astype(FULL), NT, HIGHEST)
    grown = jnp.exp(logits - jnp.max(logits, axis=1, keepdims=True))
    chance = grown / jnp.sum(grown, axis=1, keepdims=True)
    chance_ref[...] = chance
    gate = jnp.sum(chance * hits_ref[...], axis=1, keepdims=True)
    mask_t = mask_t_ref[...]
    slots = dot(mask_t, normed_two.astype(LOW))
    gates = dot(mask_t.astype(FULL), jnp.broadcast_to(gate, (length, 128)), precision=HIGHEST)
    sub, _ = grid_of(slab)
    for r in range(ranks):
        mine = gates[r * slab : (r + 1) * slab]
        high = mine.astype(LOW).astype(FULL)
        row = column_to_row(high) + column_to_row(mine - high, 64)
        rows = slots[r * slab : (r + 1) * slab]
        start = rows[:, :128] + jnp.where(sub == rank_slots, row, 0.0)
        slabs_ref[r, :, :128] = start.astype(LOW)
        slabs_ref[r, :, 128:] = rows[:, 128:].astype(LOW)


def upstream_kernel(pack_ref, w_out_ref, *rest):
    piece_refs, (rows_ref, act_ref) = rest[:-2], rest[-2:]
    local_experts = w_out_ref.shape[0]
    chunk = pack_ref.shape[0] // local_experts
    for p, piece in enumerate(piece_refs):
        packed = dot(pack_ref[...], piece[...]).astype(LOW)
        for e in range(local_experts):
            rows_ref[e, p * chunk : (p + 1) * chunk, :] = packed[e * chunk : (e + 1) * chunk]
    for e in range(local_experts):
        act_ref[e] = dot(rows_ref[e], w_out_ref[e], NT)


def unpack(pack_t, rows_ref, p, chunk):
    rows = [rows_ref[e, p * chunk : (p + 1) * chunk, :] for e in range(rows_ref.shape[0])]
    return dot(pack_t, jnp.concatenate(rows, axis=0))


def expert_kernel(
    count, slab, rank_slots, pack_ref, pack_t_ref, w_in_ref, up_act_ref, *rest
):
    piece_refs, rest = rest[:count], rest[count:]
    back_refs, rest = rest[:count], rest[count:]
    rows_ref, act_ref, pre_grad_ref, gates_ref, pre_ref, back_ref, part_ref = rest
    local_experts = w_in_ref.shape[0]
    chunk = pack_ref.shape[0] // local_experts
    ranks = pack_ref.shape[1] // slab
    pack, pack_t = pack_ref[...], pack_t_ref[...]
    for p, piece in enumerate(piece_refs):
        packed = dot(pack, piece[...]).astype(LOW)
        tile = piece[:, :128].astype(FULL)
        spread = []
        for shift in (0, 64):
            columns = [
                row_to_column(tile[r * slab + rank_slots : r * slab + rank_slots + 1], slab, shift)
                for r in range(ranks)
            ]
            spread.append(dot(pack, jnp.concatenate(columns, axis=0).astype(LOW)))
        gates = spread[0] + spread[1]
        for e in range(local_experts):
            rows_ref[e, p * chunk : (p + 1) * chunk, :] = packed[e * chunk : (e + 1) * chunk]
            gates_ref[e, p * chunk : (p + 1) * chunk, :] = gates[e * chunk : (e + 1) * chunk]
    root = np.float32(np.sqrt(2.0 / np.pi))
    step = 16
    for e in range(local_experts):
        pre_ref[...] = dot(rows_ref[e], w_in_ref[e])

        def body(index, carry):
            span = pl.ds(pl.multiple_of(index * step, step), step)
            pre = pre_ref[span, :]
            up = up_act_ref[e, span, :]
            square = pre * pre
            curve = jnp.tanh(root * pre * (1.0 + 0.044715 * square))
            rise = 0.5 + 0.5 * curve
            act = (pre * rise).astype(LOW)
            act_ref[e, span, :] = act
            slope = rise + pre * (rise * (1.0 - curve)) * (root + 3 * 0.044715 * root * square)
            gate = gates_ref[e, span, :][:, :1]
            pre_grad_ref[e, span, :] = (slope * (up * gate)).astype(LOW)
            part = jnp.sum(act.astype(FULL) * up, axis=1, keepdims=True)
            part_ref[e, span, :] = jnp.broadcast_to(part, (step, 128)).astype(LOW)
            return carry

        lax.fori_loop(0, pre_ref.shape[0] // step, body, 0, unroll=2)
        back_ref[e] = dot(pre_grad_ref[e], w_in_ref[e], NT).astype(LOW)
    sub, _ = grid_of(slab)
    for p in range(count):
        rows = unpack(pack_t, back_ref, p, chunk)
        parts = unpack(pack_t, part_ref, p, chunk)
        pieces = []
        for r in range(ranks):
            span = slice(r * slab, (r + 1) * slab)
            row = column_to_row(parts[span])
            pieces.append(rows[span, :128] + jnp.where(sub == rank_slots, row, 0.0))
        back_refs[p][:, :128] = jnp.concatenate(pieces, axis=0).astype(LOW)
        back_refs[p][:, 128:] = rows[:, 128:].astype(LOW)


def expert_out_kernel(pack_t_ref, w_out_ref, act_ref, *rest):
    out_refs, returned_ref = rest[:-1], rest[-1]
    chunk = act_ref.shape[1] // len(out_refs)
    for e in range(w_out_ref.shape[0]):
        returned_ref[e] = dot(act_ref[e], w_out_ref[e]).astype(LOW)
    for p, ref in enumerate(out_refs):
        ref[...] = unpack(pack_t_ref[...], returned_ref, p, chunk).astype(LOW)


def expert_grad_kernel(
    rows_ref, act_ref, pre_grad_ref, gates_ref, up_rows_ref, g_in_ref, g_out_ref, token_ref
):
    for e in range(rows_ref.shape[0]):
        g_in_ref[e] = dot(rows_ref[e], pre_grad_ref[e], TN)
        slot_grad = (up_rows_ref[e].astype(FULL) * gates_ref[e][:, :1]).astype(LOW)
        g_out_ref[e] = dot(act_ref[e], slot_grad, TN)
    token_ref[...] = jnp.zeros(token_ref.shape, FULL)


def joined(ref):
    ranks, slab, width = ref.shape
    return ref[...].astype(FULL).reshape(ranks * slab, width).astype(LOW)


def backward_kernel(
    places, rank_slots, tokens_ref, gain_ref, router_t_ref, hits_ref, mask_ref,
    up_ref, hidden_ref, chance_ref, heads_ref, weights_ref, onehot_ref, *rest
):
    count = len(places)
    piece_refs, rest = rest[:count], rest[count:]
    (back_ref, d_input_ref, small_ref, factors_ref,
     w_ref, turned_ref, grads_ref, bias_ref, sem) = rest
    ranks, width, columns = w_ref.shape
    copies = place_weights(places, piece_refs, w_ref, sem)
    cols = columns // 4
    head_count = weights_ref.shape[0]
    head = width // head_count
    factor = head ** (-0.5)
    length = tokens_ref.shape[0]
    slab = back_ref.shape[1]
    hidden = hidden_ref[...]
    gain_two = gain_ref[1:2, :]
    normed_two, scale_two = normalize(hidden, gain_two)
    mask = mask_ref[...]
    chance, hits = chance_ref[...], hits_ref[...]
    gate = jnp.sum(chance * hits, axis=1, keepdims=True)
    spread = [
        row_to_column(back_ref[r, :, :128].astype(FULL)[rank_slots : rank_slots + 1], slab)
        for r in range(ranks)
    ]
    gate_grad = dot(mask, jnp.concatenate(spread, axis=0).astype(LOW))[:, :1]
    logit_grad = chance * (hits - gate) * gate_grad
    experts = hits.shape[1]
    small_ref[:experts, :] = dot(logit_grad, normed_two, TN, HIGHEST)
    router_t = router_t_ref[...].astype(FULL)
    normed_two_grad = dot(logit_grad, router_t, precision=HIGHEST) + dot(mask, joined(back_ref))
    hidden_part, ffn_gain_grad = norm_back(hidden, scale_two, gain_two, normed_two_grad)
    hidden_grad = up_ref[...].astype(FULL) + hidden_part
    turned_ref[...] = hidden_grad.astype(LOW).astype(FULL).T
    for copy in copies:
        copy.wait()
    low_lane = 3 * cols // 128 * 128
    att_grad = None
    for e in range(ranks):
        own = turned_ref[e * cols : (e + 1) * cols, :]
        if 3 * cols > low_lane:
            own = jnp.concatenate([jnp.zeros((3 * cols - low_lane, 128), FULL), own], axis=0)
        part = dot(w_ref[e, :, low_lane:], own.astype(LOW))
        att_grad = part if att_grad is None else att_grad + part
    att_grad = att_grad.astype(LOW)
    for h in range(head_count):
        rows = slice(h * head, (h + 1) * head)
        own = att_grad[rows]
        weights = weights_ref[h]
        grads_ref[2, rows, :] = dot(own, weights.astype(LOW))
        prob_grad = dot(own, heads_ref[2, rows, :], TN)
        score_grad = weights * (prob_grad - jnp.sum(prob_grad * weights, axis=1, keepdims=True))
        score_grad = score_grad.astype(LOW)
        grads_ref[0, rows, :] = dot(heads_ref[1, rows, :], score_grad, NT) * factor
        grads_ref[1, rows, :] = dot(heads_ref[0, rows, :], score_grad) * factor
        wide = [jnp.zeros((length, length), FULL), score_grad.astype(FULL)]
        bias_ref[h : h + 1, :] = slid_sum(jnp.concatenate(wide, axis=1))
    total = None
    for e in range(ranks):
        span = slice(e * cols, (e + 1) * cols)
        held = [grads_ref[m, span, :] for m in range(3)] + [jnp.zeros((cols, 128), FULL)]
        part = dot(w_ref[e], jnp.concatenate(held, axis=0).astype(LOW))
        total = part if total is None else total + part
        sent = [grads_ref[m, span, :] for m in range(3)] + [turned_ref[span, :]]
        sent = jnp.concatenate(sent, axis=0).astype(LOW)
        factors_ref[e % (ranks // 2), e // (ranks // 2)] = sent
    inputs = tokens_ref[...].astype(FULL)
    gain_one = gain_ref[0:1, :]
    _, scale_one = normalize(inputs, gain_one)
    norm_part, attn_gain_grad = norm_back(inputs, scale_one, gain_one, total.T)
    d_input_ref[...] = hidden_grad + norm_part
    sums = dot(bias_ref[...], onehot_ref[...], NT, HIGHEST)
    small_ref[experts : experts + 1, :] = ffn_gain_grad
    small_ref[experts + 1 : experts + 2, :] = attn_gain_grad
    small_ref[experts + 2 :, :] = jnp.zeros((small_ref.shape[0] - experts - 2, width), FULL)
    for h in range(head_count):
        line, place = experts + 2 + h // 6, 128 * (h % 6)
        small_ref[line : line + 1, place : place + sums.shape[1]] = sums[h : h + 1]


def product_kernel(factors_ref, token_ref, *rest):
    count, _, columns, length = factors_ref.shape
    row_refs, piece_refs, total_ref = rest[:count], rest[count:-1], rest[-1]
    cols = columns // 4
    rows = total_ref.shape[2]
    mine = lax.rem(lax.axis_index("expert"), count)
    for side in range(2):
        first, second = None, None
        for j, ref in enumerate(row_refs):
            held = factors_ref[mine ^ j, side].astype(FULL)
            part = dot(held[: 3 * cols].astype(LOW), ref[0])
            first = part if first is None else first + part
            part = dot(held[3 * cols :].astype(LOW), ref[1])
            second = part if second is None else second + part
        total = jnp.concatenate([first, second], axis=0).T
        for j in range(len(piece_refs)):
            total_ref[side, j] = total[j * rows : (j + 1) * rows]
    own = (lax.axis_index("expert") >= count).astype(jnp.int32)
    for j, ref in enumerate(piece_refs):
        place = lax.axis_index("dp") ^ j
        ref[0] = total_ref[own, place].astype(LOW)
        ref[1] = total_ref[1 - own, place].astype(LOW)


def output_kernel(hidden_ref, chance_ref, hits_ref, mask_ref, returned_ref, output_ref):
    gate = jnp.sum(chance_ref[...] * hits_ref[...], axis=1, keepdims=True)
    fetched = dot(mask_ref[...], joined(returned_ref))
    output_ref[...] = (hidden_ref[...] + gate * fetched).astype(LOW)


VMEM = pl.BlockSpec(memory_space=pltpu.VMEM)
ANY = pl.BlockSpec(memory_space=pl.ANY)
LIMIT = 60 * 1024 * 1024


def shaped(dtype, *shape):
    return jax.ShapeDtypeStruct(shape, dtype)


def call(kernel, name, micros, out_shape, args, pieces=(), scratch=(), more=()):
    return pl.pallas_call(
        kernel,
        out_shape=tuple(out_shape),
        in_specs=[VMEM] * len(args) + [ANY] * len(pieces) + [VMEM] * len(more),
        out_specs=(VMEM,) * len(out_shape),
        scratch_shapes=list(scratch),
        compiler_params=pltpu.CompilerParams(vmem_limit_bytes=LIMIT),
        cost_estimate=pl.CostEstimate(
            flops=0, bytes_accessed=micros * 3_600_000, transcendentals=0
        ),
        name=name,
    )(*args, *pieces, *more)


def per_device(
    tokens,
    seg_ids,
    routes,
    attn_gain,
    w_query,
    w_key,
    w_value,
    w_output,
    rel_bias,
    ffn_gain,
    w_router,
    w_in,
    w_out,
    d_out,
):
    length, model_width = tokens.shape
    bucket_count, head_count = rel_bias.shape
    experts_total = w_router.shape[1]
    local_experts, _, hidden_here = w_in.shape
    ranks, dps = lax.axis_size("expert"), lax.axis_size("dp")
    capacity = length * 5 // (4 * experts_total)
    rank_slots = local_experts * capacity
    slab = -(-(rank_slots + 1) // 8) * 8
    rows_here, columns_here = w_query.shape
    inner_width = dps * rows_here
    packed_rows = dps * ranks * capacity
    gains = jnp.stack([attn_gain, ffn_gain]).astype(FULL)
    slabs_shape = shaped(LOW, ranks, slab, model_width)
    router_t = w_router.T
    pack = packing(local_experts, ranks, capacity, slab)
    pack, pack_t = jnp.asarray(pack, LOW), jnp.asarray(pack.T, LOW)

    normed_low, hits, mask, mask_t, bias_full, up_slabs = call(
        functools.partial(early_kernel, ranks, local_experts, capacity, slab),
        "early",
        3,
        [
            shaped(LOW, length, model_width),
            shaped(FULL, length, experts_total),
            shaped(LOW, length, ranks * slab),
            shaped(LOW, ranks * slab, length),
            shaped(FULL, head_count, length, length),
            slabs_shape,
        ],
        [
            tokens,
            routes.reshape(1, length),
            gains,
            d_out,
            rel_bias.T,
            jnp.asarray(bucket_onehot(bucket_count, length), LOW),
        ],
    )

    payload = jnp.concatenate([w_query, w_key, w_value, w_output], axis=1)
    early = (normed_low, hits, mask, mask_t, bias_full)
    pieces, places, early = gather_pieces(payload, early)
    normed_low, hits, mask, mask_t, bias_full = early
    pieces, up_slabs = together(pieces, up_slabs)
    up_arrived = exchange(up_slabs).reshape(ranks * slab, model_width)

    w_shape = (ranks, inner_width, 4 * columns_here)
    heads, weights, rows, hidden, chance, slabs = call(
        functools.partial(forward_kernel, places, slab, rank_slots),
        "attention_forward",
        10,
        [
            shaped(LOW, 3, inner_width, length),
            shaped(FULL, head_count, length, length),
            shaped(LOW, 2, length, inner_width),
            shaped(FULL, length, model_width),
            shaped(FULL, length, experts_total),
            slabs_shape,
        ],
        [tokens, normed_low, seg_ids, bias_full, gains, router_t, hits, mask_t],
        pieces,
        [
            pltpu.VMEM(w_shape, LOW),
            pltpu.VMEM((3, inner_width, length), FULL),
            pltpu.VMEM((inner_width, length), FULL),
            pltpu.SemaphoreType.DMA,
        ],
    )

    slabs, up_arrived = together(slabs, up_arrived)
    arrived = exchange(slabs).reshape(ranks * slab, model_width)
    up_pieces = gather_near(gather_far(up_arrived))
    arrived, up_pieces, rows = together(arrived, up_pieces, rows)
    row_far = gather_far(arrived)
    half = ranks // 2
    near_rows = [swap(rows, "expert", j) for j in range(1, half)]
    by_expert = (local_experts, packed_rows)
    up_rows, up_act = call(
        upstream_kernel,
        "upstream_rows",
        5,
        [shaped(LOW, *by_expert, model_width), shaped(FULL, *by_expert, hidden_here)],
        [pack, w_out, *up_pieces],
    )
    row_far, up_act = together(row_far, up_act)
    row_pieces = gather_near(row_far)

    *back, slot_rows, activated, pre_grad, gates = call(
        functools.partial(expert_kernel, dps, slab, rank_slots),
        "experts",
        10,
        [shaped(LOW, ranks * slab, model_width)] * dps
        + [
            shaped(LOW, *by_expert, model_width),
            shaped(LOW, *by_expert, hidden_here),
            shaped(LOW, *by_expert, hidden_here),
            shaped(FULL, *by_expert, 128),
        ],
        [pack, pack_t, w_in, up_act, *row_pieces],
        scratch=[
            pltpu.VMEM((packed_rows, hidden_here), FULL),
            pltpu.VMEM((*by_expert, model_width), LOW),
            pltpu.VMEM((*by_expert, 128), LOW),
        ],
    )
    kept, got = scatter_terms(back)
    first_grad, second_grad, token = call(
        expert_grad_kernel,
        "expert_gradients",
        8,
        [shaped(FULL, *w_in.shape), shaped(FULL, *w_out.shape), shaped(FULL, 8, 128)],
        [slot_rows, activated, pre_grad, gates, up_rows],
    )
    got, token, near_rows = together(got, token, near_rows)
    back = add(kept, got).reshape(ranks, slab, model_width)
    back, activated = together(back, activated)
    back = exchange(back)
    returned = call(
        expert_out_kernel,
        "expert_outputs",
        12,
        [shaped(LOW, ranks * slab, model_width)] * dps,
        [pack_t, w_out, activated],
        scratch=[pltpu.VMEM((*by_expert, model_width), LOW)],
    )
    returned = scatter_near(returned)
    back, returned = together(back, returned)
    returned = add(*scatter_far(returned)).reshape(ranks, slab, model_width)

    bias_rows = -(-head_count // 6)
    small_rows = -(-(experts_total + 2 + bias_rows) // 8) * 8
    d_input, small, factors = call(
        functools.partial(backward_kernel, places, rank_slots),
        "attention_backward",
        12,
        [
            shaped(FULL, length, model_width),
            shaped(FULL, small_rows, model_width),
            shaped(LOW, ranks // 2, 2, 4 * columns_here, length),
        ],
        [
            tokens,
            gains,
            router_t,
            hits,
            mask,
            d_out,
            hidden,
            chance,
            heads,
            weights,
            jnp.asarray(bucket_onehot(bucket_count, length), FULL),
        ],
        pieces,
        [
            pltpu.VMEM(w_shape, LOW),
            pltpu.VMEM((inner_width, length), FULL),
            pltpu.VMEM((3, inner_width, length), FULL),
            pltpu.VMEM((head_count, 2 * length), FULL),
            pltpu.SemaphoreType.DMA,
        ],
        [back],
    )

    factors, small, returned = together(factors, small, returned)
    factors = lax.all_to_all(
        factors, "expert", split_axis=0, concat_axis=0, tiled=True, axis_index_groups=halves()
    )
    first, *steps, one_but_last, last = sum_steps()
    small = small + swap(small, *first)
    small, returned = together(small, returned)
    returned = exchange(returned)
    for axis, bit in steps:
        small = small + swap(small, axis, bit)
    factors, small, returned = together(factors, small, returned)
    small = small + swap(small, *one_but_last)
    grads = call(
        product_kernel,
        "weight_gradients",
        5,
        [shaped(LOW, 2, rows_here, 4 * columns_here)] * dps,
        [factors, token, rows, *near_rows],
        scratch=[pltpu.VMEM((2, dps, rows_here, 4 * columns_here), FULL)],
    )
    grads, small = together(scatter_near(grads), small)
    small = small + swap(small, *last)
    (output,) = call(
        output_kernel,
        "output_rows",
        2,
        [shaped(LOW, length, model_width)],
        [hidden, chance, hits, mask, returned],
    )
    kept, got = scatter_far(grads)
    got, output = together(got, output)
    other = swap(add(kept[1], got[1]), "expert", ranks // 2)
    grads = kept[0].astype(FULL) + got[0].astype(FULL) + other.astype(FULL)
    g_query, g_key, g_value, g_output = (
        grads[:, i * columns_here : (i + 1) * columns_here] for i in range(4)
    )
    g_router = small[:experts_total].T
    g_ffn_gain, g_attn_gain = small[experts_total], small[experts_total + 1]
    g_rel_bias = small[experts_total + 2 : experts_total + 2 + bias_rows].reshape(-1, 128)
    g_rel_bias = g_rel_bias[:head_count, :bucket_count].T
    return (
        output,
        d_input,
        g_attn_gain,
        g_query,
        g_key,
        g_value,
        g_output,
        g_rel_bias,
        g_ffn_gain,
        g_router,
        first_grad,
        second_grad,
    )


def solution(mesh):
    return jax.shard_map(
        per_device,
        mesh=mesh,
        in_specs=(
            P(("dp", "expert"), None),
            P(("dp", "expert"), None),
            P(("dp", "expert"), None),
            P(),
            P("dp", "expert"),
            P("dp", "expert"),
            P("dp", "expert"),
            P("dp", "expert"),
            P(),
            P(),
            P(),
            P("expert", None, "dp"),
            P("expert", "dp", None),
            P(("dp", "expert"), None),
        ),
        out_specs=(
            P(("dp", "expert"), None),
            P(("dp", "expert"), None),
            P(),
            P("dp", "expert"),
            P("dp", "expert"),
            P("dp", "expert"),
            P("dp", "expert"),
            P(),
            P(),
            P(),
            P("expert", None, "dp"),
            P("expert", "dp", None),
        ),
        check_vma=False,
    )
```

```python
import functools

import jax
import jax.numpy as jnp
import numpy as np
from jax import lax
from jax.experimental import pallas as pl
from jax.experimental.pallas import tpu as pltpu
from jax.sharding import PartitionSpec as P

EPSILON = 1e-06
LIMITS = (12, 16, 23, 32, 46, 64, 91)
MASKED = -1000000000.0
HIGHEST = lax.Precision.HIGHEST
LOW = jnp.bfloat16
FULL = jnp.float32


def bucket_onehot(buckets, length):
    delta = np.arange(2 * length) - length
    magnitude = np.abs(delta)
    distant = 8 + sum((magnitude >= threshold).astype(np.int32) for threshold in LIMITS)
    ids = np.where(delta > 0, 16, 0) + np.where(magnitude < 8, magnitude, distant)
    return (ids[None, :] == np.arange(buckets)[:, None]).astype(np.float32)


def packing(local_experts, ranks, capacity, slab):
    table = np.zeros((local_experts, ranks, capacity, ranks, slab), np.float32)
    for e in range(local_experts):
        for r in range(ranks):
            for c in range(capacity):
                table[e, r, c, r, e * capacity + c] = 1.0
    return table.reshape(local_experts * ranks * capacity, ranks * slab)


def normalize(matrix, gain_vec):
    scale = lax.rsqrt(jnp.mean(matrix * matrix, axis=-1, keepdims=True) + EPSILON)
    return (matrix * scale * gain_vec, scale)


def norm_back(matrix, scale, gain_vec, incoming):
    weighted = incoming * gain_vec
    average = jnp.mean(matrix * weighted, axis=-1, keepdims=True)
    return (
        scale * weighted - matrix * (scale * scale * scale) * average,
        jnp.sum(incoming * matrix * scale, axis=0, keepdims=True),
    )


def swap(value, axis, mask):
    count = lax.axis_size(axis)
    return lax.ppermute(value, axis, [(i, i ^ mask) for i in range(count)])


def gather_bits(value, axis, masks):
    return jnp.concatenate([value] + [swap(value, axis, mask) for mask in masks], axis=0)


def exchange(value):
    return lax.all_to_all(value, "expert", split_axis=0, concat_axis=0, tiled=True)


def halves():
    half = lax.axis_size("expert") // 2
    return [list(range(half)), list(range(half, 2 * half))]


def gather_far(value):
    found = {0: value}
    bit = lax.axis_size("dp") // 2
    while bit > 1:
        found.update({index ^ bit: swap(item, "dp", bit) for index, item in found.items()})
        bit = bit // 2
    return found


def gather_near(found):
    found = {**found, **{index ^ 1: swap(item, "dp", 1) for index, item in found.items()}}
    return [found[index] for index in range(len(found))]


def add(left, right, dtype=LOW):
    return (left.astype(FULL) + right.astype(FULL)).astype(dtype)


def scatter_near(items):
    taken = [swap(item, "dp", 1) for item in items[1::2]]
    return [add(kept, got) for kept, got in zip(items[0::2], taken)]


def scatter_far(items):
    bit = 2
    while len(items) > 2:
        taken = [swap(item, "dp", bit) for item in items[1::2]]
        items = [add(kept, got) for kept, got in zip(items[0::2], taken)]
        bit = bit * 2
    return items[0], swap(items[1], "dp", bit)


def scatter_terms(items):
    return scatter_far(scatter_near(items))


def sum_steps():
    steps = []
    for axis in ("dp", "expert"):
        bit = 1
        while bit < lax.axis_size(axis):
            steps.append((axis, bit))
            bit = bit * 2
    return steps


def together(*values):
    return lax.optimization_barrier(values)


def gather_pieces(payload, early):
    ranks, dps = lax.axis_size("expert"), lax.axis_size("dp")
    half = payload.shape[0] // 2
    far = list(range(0, ranks, 2))
    sides = {"x": ("expert", [0, 1]), "y": ("dp", list(range(0, dps, 2)))}
    value, early = together(gather_bits(payload[None], "expert", far[1:]), early)
    values = (value[:, :half], value[:, half:])
    firsts = []
    for value, letter in zip(values, "xy"):
        axis, masks = sides[letter]
        firsts.append(gather_bits(value[None], axis, masks[1:]))
    seconds = []
    for value, letter in zip(firsts, "yx"):
        axis, masks = sides[letter]
        seconds.append([swap(value, axis, mask) for mask in masks[1:]])
    others = [swap(value, "dp", 1) for value in firsts]
    pieces, places = [], []
    for index, order in enumerate(("xy", "yx")):
        masks, other_masks = sides[order[0]][1], sides[order[1]][1]
        found = [(firsts[index], 0, 0), (others[index], 0, 1)]
        for value, mask in zip(seconds[index], other_masks[1:]):
            found += [(value, mask, 0), (swap(value, "dp", 1), mask, 1)]
        for piece, mask, core in found:
            offsets = []
            for first in masks:
                for low in far:
                    x_mask, y_mask = (first, mask) if order == "xy" else (mask, first)
                    offsets.append((low ^ x_mask, y_mask ^ core))
            pieces.append(piece)
            places.append((index, offsets))
    return pieces, places, early


def place_weights(places, piece_refs, w_ref, sem):
    my_expert, my_dp = lax.axis_index("expert"), lax.axis_index("dp")
    copies = []
    for ref, (half, offsets) in zip(piece_refs, places):
        low_count, rows = ref.shape[1], ref.shape[2]
        for index, (e_mask, d_mask) in enumerate(offsets):
            start = (my_dp ^ d_mask) * (2 * rows) + half * rows
            copies.append(
                pltpu.make_async_copy(
                    ref.at[index // low_count, index % low_count],
                    w_ref.at[my_expert ^ e_mask, pl.ds(pl.multiple_of(start, 16), rows), :],
                    sem,
                )
            )
    for copy in copies:
        copy.start()
    return copies


def dot(left, right, dims=((1,), (0,)), precision=None):
    return lax.dot_general(
        left, right, (dims, ((), ())), precision=precision, preferred_element_type=FULL
    )


NT = ((1,), (1,))
TN = ((0,), (0,))


def grid_of(rows):
    sub = lax.broadcasted_iota(jnp.int32, (rows, 128), 0)
    lane = lax.broadcasted_iota(jnp.int32, (rows, 128), 1)
    return sub, lane


def row_to_column(row, rows, shift=0):
    sub, lane = grid_of(rows)
    column = jnp.sum(jnp.where(lane == sub + shift, row, 0.0), axis=1, keepdims=True)
    return jnp.broadcast_to(column, (rows, 128))


def column_to_row(column, shift=0):
    sub, lane = grid_of(column.shape[0])
    return jnp.sum(jnp.where(lane == sub + shift, column, 0.0), axis=0, keepdims=True)


def turn(value, shift):
    return pltpu.roll(value, shift % value.shape[1], 1)


def slide(value, direction):
    sub = lax.broadcasted_iota(jnp.int32, value.shape, 0)
    for bit in (1, 2, 4):
        value = jnp.where((sub & bit) != 0, turn(value, direction * bit), value)
    return value


def slid_rows(row, count):
    value = slide(jnp.broadcast_to(row, (8, row.shape[1])), 1)
    while value.shape[0] < count:
        value = jnp.concatenate([value, turn(value, value.shape[0])], axis=0)
    return value


def slid_sum(value):
    while value.shape[0] > 8:
        half = value.shape[0] // 2
        value = value[:half] + turn(value[half:], -half)
    return jnp.sum(slide(value, -1), axis=0, keepdims=True)


def early_kernel(
    ranks, local_experts, capacity, slab, tokens_ref, routes_ref, gain_ref, d_out_ref, table_ref,
    onehot_ref, normed_ref, hits_ref, mask_ref, mask_t_ref, bias_ref, up_ref
):
    length = tokens_ref.shape[0]
    normed, _ = normalize(tokens_ref[...].astype(FULL), gain_ref[0:1, :])
    normed_ref[...] = normed.astype(LOW)
    experts = hits_ref.shape[1]
    routes = jnp.broadcast_to(routes_ref[...].astype(FULL), (length, length)).T
    route = routes[:, :1].astype(jnp.int32)
    lanes = lax.broadcasted_iota(jnp.int32, (length, experts), 1)
    hits = (lanes == route).astype(FULL)
    hits_ref[...] = hits
    row = lax.broadcasted_iota(jnp.int32, (length, length), 0)
    col = lax.broadcasted_iota(jnp.int32, (length, length), 1)
    before = dot((col < row).astype(FULL).astype(LOW), hits.astype(LOW))
    placed = jnp.sum(before * hits, axis=1, keepdims=True).astype(jnp.int32)
    rank = jnp.zeros_like(route)
    for r in range(1, ranks):
        rank = rank + (route >= r * local_experts).astype(jnp.int32)
    spot = rank * slab + (route - rank * local_experts) * capacity + placed
    spot = jnp.where(placed < capacity, spot, -1)
    places = lax.broadcasted_iota(jnp.int32, (length, ranks * slab), 1)
    mask = (places == spot).astype(FULL)
    mask_ref[...] = mask.astype(LOW)
    mask_t = mask.T.astype(LOW)
    mask_t_ref[...] = mask_t
    slabs = dot(mask_t, d_out_ref[...])
    for r in range(ranks):
        up_ref[r] = slabs[r * slab : (r + 1) * slab].astype(LOW)
    values = dot(table_ref[...], onehot_ref[...])
    for h in range(bias_ref.shape[0]):
        bias_ref[h] = slid_rows(values[h : h + 1], length)[:, length:]


def forward_kernel(
    places, slab, rank_slots, tokens_ref, normed_ref, seg_ref, bias_ref, gain_ref,
    router_t_ref, hits_ref, mask_t_ref, *rest
):
    count = len(places)
    piece_refs, rest = rest[:count], rest[count:]
    heads_ref, weights_ref, rows_ref, hidden_ref, chance_ref = rest[:5]
    slabs_ref = rest[5]
    w_ref, qkv_ref, att_t_ref, sem = rest[-4:]
    copies = place_weights(places, piece_refs, w_ref, sem)
    ranks, width, columns = w_ref.shape
    cols = columns // 4
    head_count = weights_ref.shape[0]
    head = width // head_count
    length = tokens_ref.shape[0]
    segments = jnp.broadcast_to(seg_ref[...].astype(FULL), (length, length))
    same_doc = segments == segments.T
    normed = normed_ref[...]
    for copy in copies:
        copy.wait()
    for e in range(ranks):
        turned = dot(normed, w_ref[e]).T
        for m in range(3):
            qkv_ref[m, e * cols : (e + 1) * cols, :] = turned[m * cols : (m + 1) * cols]
    heads_ref[...] = qkv_ref[...].astype(LOW)
    for h in range(head_count):
        rows = slice(h * head, (h + 1) * head)
        scores = dot(heads_ref[0, rows, :], heads_ref[1, rows, :], TN) * head ** (-0.5)
        scores = jnp.where(same_doc, scores + bias_ref[h], MASKED)
        grown = jnp.exp(scores - jnp.max(scores, axis=1, keepdims=True))
        weights = grown / jnp.sum(grown, axis=1, keepdims=True)
        weights_ref[h] = weights
        att_t_ref[rows, :] = dot(heads_ref[2, rows, :], weights.astype(LOW), NT)
    attended = att_t_ref[...].T.astype(LOW)
    rows_ref[0] = normed
    rows_ref[1] = attended
    low_lane = 3 * cols // 128 * 128
    for e in range(ranks):
        turned = dot(attended, w_ref[e, :, low_lane:]).T
        att_t_ref[e * cols : (e + 1) * cols, :] = turned[3 * cols - low_lane :]
    hidden = tokens_ref[...].astype(FULL) + att_t_ref[...].T
    hidden_ref[...] = hidden
    normed_two, _ = normalize(hidden, gain_ref[1:2, :])
    logits = dot(normed_two, router_t_ref[...].astype(FULL), NT, HIGHEST)
    grown = jnp.exp(logits - jnp.max(logits, axis=1, keepdims=True))
    chance = grown / jnp.sum(grown, axis=1, keepdims=True)
    chance_ref[...] = chance
    gate = jnp.sum(chance * hits_ref[...], axis=1, keepdims=True)
    mask_t = mask_t_ref[...]
    slots = dot(mask_t, normed_two.astype(LOW))
    gates = dot(mask_t.astype(FULL), jnp.broadcast_to(gate, (length, 128)), precision=HIGHEST)
    sub, _ = grid_of(slab)
    for r in range(ranks):
        mine = gates[r * slab : (r + 1) * slab]
        high = mine.astype(LOW).astype(FULL)
        row = column_to_row(high) + column_to_row(mine - high, 64)
        rows = slots[r * slab : (r + 1) * slab]
        start = rows[:, :128] + jnp.where(sub == rank_slots, row, 0.0)
        slabs_ref[r, :, :128] = start.astype(LOW)
        slabs_ref[r, :, 128:] = rows[:, 128:].astype(LOW)


def upstream_kernel(pack_ref, w_out_ref, *rest):
    piece_refs, (rows_ref, act_ref) = rest[:-2], rest[-2:]
    local_experts = w_out_ref.shape[0]
    chunk = pack_ref.shape[0] // local_experts
    for p, piece in enumerate(piece_refs):
        packed = dot(pack_ref[...], piece[...]).astype(LOW)
        for e in range(local_experts):
            rows_ref[e, p * chunk : (p + 1) * chunk, :] = packed[e * chunk : (e + 1) * chunk]
    for e in range(local_experts):
        act_ref[e] = dot(rows_ref[e], w_out_ref[e], NT)


def unpack(pack_t, rows_ref, p, chunk):
    rows = [rows_ref[e, p * chunk : (p + 1) * chunk, :] for e in range(rows_ref.shape[0])]
    return dot(pack_t, jnp.concatenate(rows, axis=0))


def expert_kernel(
    count, slab, rank_slots, pack_ref, pack_t_ref, w_in_ref, up_act_ref, *rest
):
    piece_refs, rest = rest[:count], rest[count:]
    back_refs, rest = rest[:count], rest[count:]
    rows_ref, act_ref, pre_grad_ref, gates_ref, pre_ref, back_ref, part_ref = rest
    local_experts = w_in_ref.shape[0]
    chunk = pack_ref.shape[0] // local_experts
    ranks = pack_ref.shape[1] // slab
    pack, pack_t = pack_ref[...], pack_t_ref[...]
    for p, piece in enumerate(piece_refs):
        packed = dot(pack, piece[...]).astype(LOW)
        tile = piece[:, :128].astype(FULL)
        spread = []
        for shift in (0, 64):
            columns = [
                row_to_column(tile[r * slab + rank_slots : r * slab + rank_slots + 1], slab, shift)
                for r in range(ranks)
            ]
            spread.append(dot(pack, jnp.concatenate(columns, axis=0).astype(LOW)))
        gates = spread[0] + spread[1]
        for e in range(local_experts):
            rows_ref[e, p * chunk : (p + 1) * chunk, :] = packed[e * chunk : (e + 1) * chunk]
            gates_ref[e, p * chunk : (p + 1) * chunk, :] = gates[e * chunk : (e + 1) * chunk]
    root = np.float32(np.sqrt(2.0 / np.pi))
    step = 16
    for e in range(local_experts):
        pre_ref[...] = dot(rows_ref[e], w_in_ref[e])

        def body(index, carry):
            span = pl.ds(pl.multiple_of(index * step, step), step)
            pre = pre_ref[span, :]
            up = up_act_ref[e, span, :]
            square = pre * pre
            curve = jnp.tanh(root * pre * (1.0 + 0.044715 * square))
            rise = 0.5 + 0.5 * curve
            act = (pre * rise).astype(LOW)
            act_ref[e, span, :] = act
            slope = rise + pre * (rise * (1.0 - curve)) * (root + 3 * 0.044715 * root * square)
            gate = gates_ref[e, span, :][:, :1]
            pre_grad_ref[e, span, :] = (slope * (up * gate)).astype(LOW)
            part = jnp.sum(act.astype(FULL) * up, axis=1, keepdims=True)
            part_ref[e, span, :] = jnp.broadcast_to(part, (step, 128)).astype(LOW)
            return carry

        lax.fori_loop(0, pre_ref.shape[0] // step, body, 0, unroll=2)
        back_ref[e] = dot(pre_grad_ref[e], w_in_ref[e], NT).astype(LOW)
    sub, _ = grid_of(slab)
    for p in range(count):
        rows = unpack(pack_t, back_ref, p, chunk)
        parts = unpack(pack_t, part_ref, p, chunk)
        pieces = []
        for r in range(ranks):
            span = slice(r * slab, (r + 1) * slab)
            row = column_to_row(parts[span])
            pieces.append(rows[span, :128] + jnp.where(sub == rank_slots, row, 0.0))
        back_refs[p][:, :128] = jnp.concatenate(pieces, axis=0).astype(LOW)
        back_refs[p][:, 128:] = rows[:, 128:].astype(LOW)


def expert_out_kernel(pack_t_ref, w_out_ref, act_ref, *rest):
    out_refs, returned_ref = rest[:-1], rest[-1]
    chunk = act_ref.shape[1] // len(out_refs)
    for e in range(w_out_ref.shape[0]):
        returned_ref[e] = dot(act_ref[e], w_out_ref[e]).astype(LOW)
    for p, ref in enumerate(out_refs):
        ref[...] = unpack(pack_t_ref[...], returned_ref, p, chunk).astype(LOW)


def expert_grad_kernel(
    rows_ref, act_ref, pre_grad_ref, gates_ref, up_rows_ref, g_in_ref, g_out_ref, token_ref
):
    for e in range(rows_ref.shape[0]):
        g_in_ref[e] = dot(rows_ref[e], pre_grad_ref[e], TN)
        slot_grad = (up_rows_ref[e].astype(FULL) * gates_ref[e][:, :1]).astype(LOW)
        g_out_ref[e] = dot(act_ref[e], slot_grad, TN)
    token_ref[...] = jnp.zeros(token_ref.shape, FULL)


def joined(ref):
    ranks, slab, width = ref.shape
    return ref[...].astype(FULL).reshape(ranks * slab, width).astype(LOW)


def backward_kernel(
    places, rank_slots, tokens_ref, gain_ref, router_t_ref, hits_ref, mask_ref,
    up_ref, hidden_ref, chance_ref, heads_ref, weights_ref, onehot_ref, *rest
):
    count = len(places)
    piece_refs, rest = rest[:count], rest[count:]
    (back_ref, d_input_ref, small_ref, factors_ref,
     w_ref, turned_ref, grads_ref, bias_ref, sem) = rest
    ranks, width, columns = w_ref.shape
    copies = place_weights(places, piece_refs, w_ref, sem)
    cols = columns // 4
    head_count = weights_ref.shape[0]
    head = width // head_count
    factor = head ** (-0.5)
    length = tokens_ref.shape[0]
    slab = back_ref.shape[1]
    hidden = hidden_ref[...]
    gain_two = gain_ref[1:2, :]
    normed_two, scale_two = normalize(hidden, gain_two)
    mask = mask_ref[...]
    chance, hits = chance_ref[...], hits_ref[...]
    gate = jnp.sum(chance * hits, axis=1, keepdims=True)
    spread = [
        row_to_column(back_ref[r, :, :128].astype(FULL)[rank_slots : rank_slots + 1], slab)
        for r in range(ranks)
    ]
    gate_grad = dot(mask, jnp.concatenate(spread, axis=0).astype(LOW))[:, :1]
    logit_grad = chance * (hits - gate) * gate_grad
    experts = hits.shape[1]
    small_ref[:experts, :] = dot(logit_grad, normed_two, TN, HIGHEST)
    router_t = router_t_ref[...].astype(FULL)
    normed_two_grad = dot(logit_grad, router_t, precision=HIGHEST) + dot(mask, joined(back_ref))
    hidden_part, ffn_gain_grad = norm_back(hidden, scale_two, gain_two, normed_two_grad)
    hidden_grad = up_ref[...].astype(FULL) + hidden_part
    turned_ref[...] = hidden_grad.astype(LOW).astype(FULL).T
    for copy in copies:
        copy.wait()
    low_lane = 3 * cols // 128 * 128
    att_grad = None
    for e in range(ranks):
        own = turned_ref[e * cols : (e + 1) * cols, :]
        if 3 * cols > low_lane:
            own = jnp.concatenate([jnp.zeros((3 * cols - low_lane, 128), FULL), own], axis=0)
        part = dot(w_ref[e, :, low_lane:], own.astype(LOW))
        att_grad = part if att_grad is None else att_grad + part
    att_grad = att_grad.astype(LOW)
    for h in range(head_count):
        rows = slice(h * head, (h + 1) * head)
        own = att_grad[rows]
        weights = weights_ref[h]
        grads_ref[2, rows, :] = dot(own, weights.astype(LOW))
        prob_grad = dot(own, heads_ref[2, rows, :], TN)
        score_grad = weights * (prob_grad - jnp.sum(prob_grad * weights, axis=1, keepdims=True))
        score_grad = score_grad.astype(LOW)
        grads_ref[0, rows, :] = dot(heads_ref[1, rows, :], score_grad, NT) * factor
        grads_ref[1, rows, :] = dot(heads_ref[0, rows, :], score_grad) * factor
        wide = [jnp.zeros((length, length), FULL), score_grad.astype(FULL)]
        bias_ref[h : h + 1, :] = slid_sum(jnp.concatenate(wide, axis=1))
    total = None
    for e in range(ranks):
        span = slice(e * cols, (e + 1) * cols)
        held = [grads_ref[m, span, :] for m in range(3)] + [jnp.zeros((cols, 128), FULL)]
        part = dot(w_ref[e], jnp.concatenate(held, axis=0).astype(LOW))
        total = part if total is None else total + part
        sent = [grads_ref[m, span, :] for m in range(3)] + [turned_ref[span, :]]
        sent = jnp.concatenate(sent, axis=0).astype(LOW)
        factors_ref[e % (ranks // 2), e // (ranks // 2)] = sent
    inputs = tokens_ref[...].astype(FULL)
    gain_one = gain_ref[0:1, :]
    _, scale_one = normalize(inputs, gain_one)
    norm_part, attn_gain_grad = norm_back(inputs, scale_one, gain_one, total.T)
    d_input_ref[...] = hidden_grad + norm_part
    sums = dot(bias_ref[...], onehot_ref[...], NT, HIGHEST)
    small_ref[experts : experts + 1, :] = ffn_gain_grad
    small_ref[experts + 1 : experts + 2, :] = attn_gain_grad
    small_ref[experts + 2 :, :] = jnp.zeros((small_ref.shape[0] - experts - 2, width), FULL)
    for h in range(head_count):
        line, place = experts + 2 + h // 6, 128 * (h % 6)
        small_ref[line : line + 1, place : place + sums.shape[1]] = sums[h : h + 1]


def product_kernel(factors_ref, token_ref, *rest):
    count, _, columns, length = factors_ref.shape
    row_refs, piece_refs, total_ref = rest[:count], rest[count:-1], rest[-1]
    cols = columns // 4
    rows = total_ref.shape[2]
    mine = lax.rem(lax.axis_index("expert"), count)
    for side in range(2):
        first, second = None, None
        for j, ref in enumerate(row_refs):
            held = factors_ref[mine ^ j, side].astype(FULL)
            part = dot(held[: 3 * cols].astype(LOW), ref[0])
            first = part if first is None else first + part
            part = dot(held[3 * cols :].astype(LOW), ref[1])
            second = part if second is None else second + part
        total = jnp.concatenate([first, second], axis=0).T
        for j in range(len(piece_refs)):
            total_ref[side, j] = total[j * rows : (j + 1) * rows]
    own = (lax.axis_index("expert") >= count).astype(jnp.int32)
    for j, ref in enumerate(piece_refs):
        place = lax.axis_index("dp") ^ j
        ref[0] = total_ref[own, place].astype(LOW)
        ref[1] = total_ref[1 - own, place].astype(LOW)


def output_kernel(hidden_ref, chance_ref, hits_ref, mask_ref, returned_ref, output_ref):
    gate = jnp.sum(chance_ref[...] * hits_ref[...], axis=1, keepdims=True)
    fetched = dot(mask_ref[...], joined(returned_ref))
    output_ref[...] = (hidden_ref[...] + gate * fetched).astype(LOW)


VMEM = pl.BlockSpec(memory_space=pltpu.VMEM)
ANY = pl.BlockSpec(memory_space=pl.ANY)
LIMIT = 60 * 1024 * 1024


def shaped(dtype, *shape):
    return jax.ShapeDtypeStruct(shape, dtype)


def call(kernel, name, micros, out_shape, args, pieces=(), scratch=(), more=()):
    return pl.pallas_call(
        kernel,
        out_shape=tuple(out_shape),
        in_specs=[VMEM] * len(args) + [ANY] * len(pieces) + [VMEM] * len(more),
        out_specs=(VMEM,) * len(out_shape),
        scratch_shapes=list(scratch),
        compiler_params=pltpu.CompilerParams(vmem_limit_bytes=LIMIT),
        cost_estimate=pl.CostEstimate(
            flops=0, bytes_accessed=micros * 3_600_000, transcendentals=0
        ),
        name=name,
    )(*args, *pieces, *more)


def per_device(
    tokens,
    seg_ids,
    routes,
    attn_gain,
    w_query,
    w_key,
    w_value,
    w_output,
    rel_bias,
    ffn_gain,
    w_router,
    w_in,
    w_out,
    d_out,
):
    length, model_width = tokens.shape
    bucket_count, head_count = rel_bias.shape
    experts_total = w_router.shape[1]
    local_experts, _, hidden_here = w_in.shape
    ranks, dps = lax.axis_size("expert"), lax.axis_size("dp")
    capacity = length * 5 // (4 * experts_total)
    rank_slots = local_experts * capacity
    slab = -(-(rank_slots + 1) // 8) * 8
    rows_here, columns_here = w_query.shape
    inner_width = dps * rows_here
    packed_rows = dps * ranks * capacity
    gains = jnp.stack([attn_gain, ffn_gain]).astype(FULL)
    slabs_shape = shaped(LOW, ranks, slab, model_width)
    router_t = w_router.T
    pack = packing(local_experts, ranks, capacity, slab)
    pack, pack_t = jnp.asarray(pack, LOW), jnp.asarray(pack.T, LOW)

    normed_low, hits, mask, mask_t, bias_full, up_slabs = call(
        functools.partial(early_kernel, ranks, local_experts, capacity, slab),
        "early",
        3,
        [
            shaped(LOW, length, model_width),
            shaped(FULL, length, experts_total),
            shaped(LOW, length, ranks * slab),
            shaped(LOW, ranks * slab, length),
            shaped(FULL, head_count, length, length),
            slabs_shape,
        ],
        [
            tokens,
            routes.reshape(1, length),
            gains,
            d_out,
            rel_bias.T,
            jnp.asarray(bucket_onehot(bucket_count, length), LOW),
        ],
    )

    payload = jnp.concatenate([w_query, w_key, w_value, w_output], axis=1)
    early = (normed_low, hits, mask, mask_t, bias_full)
    pieces, places, early = gather_pieces(payload, early)
    normed_low, hits, mask, mask_t, bias_full = early
    pieces, up_slabs = together(pieces, up_slabs)
    up_arrived = exchange(up_slabs).reshape(ranks * slab, model_width)

    w_shape = (ranks, inner_width, 4 * columns_here)
    heads, weights, rows, hidden, chance, slabs = call(
        functools.partial(forward_kernel, places, slab, rank_slots),
        "attention_forward",
        10,
        [
            shaped(LOW, 3, inner_width, length),
            shaped(FULL, head_count, length, length),
            shaped(LOW, 2, length, inner_width),
            shaped(FULL, length, model_width),
            shaped(FULL, length, experts_total),
            slabs_shape,
        ],
        [tokens, normed_low, seg_ids, bias_full, gains, router_t, hits, mask_t],
        pieces,
        [
            pltpu.VMEM(w_shape, LOW),
            pltpu.VMEM((3, inner_width, length), FULL),
            pltpu.VMEM((inner_width, length), FULL),
            pltpu.SemaphoreType.DMA,
        ],
    )

    slabs, up_arrived = together(slabs, up_arrived)
    arrived = exchange(slabs).reshape(ranks * slab, model_width)
    up_pieces = gather_near(gather_far(up_arrived))
    arrived, up_pieces, rows = together(arrived, up_pieces, rows)
    row_far = gather_far(arrived)
    half = ranks // 2
    near_rows = [swap(rows, "expert", j) for j in range(1, half)]
    by_expert = (local_experts, packed_rows)
    up_rows, up_act = call(
        upstream_kernel,
        "upstream_rows",
        5,
        [shaped(LOW, *by_expert, model_width), shaped(FULL, *by_expert, hidden_here)],
        [pack, w_out, *up_pieces],
    )
    row_far, up_act = together(row_far, up_act)
    row_pieces = gather_near(row_far)

    *back, slot_rows, activated, pre_grad, gates = call(
        functools.partial(expert_kernel, dps, slab, rank_slots),
        "experts",
        10,
        [shaped(LOW, ranks * slab, model_width)] * dps
        + [
            shaped(LOW, *by_expert, model_width),
            shaped(LOW, *by_expert, hidden_here),
            shaped(LOW, *by_expert, hidden_here),
            shaped(FULL, *by_expert, 128),
        ],
        [pack, pack_t, w_in, up_act, *row_pieces],
        scratch=[
            pltpu.VMEM((packed_rows, hidden_here), FULL),
            pltpu.VMEM((*by_expert, model_width), LOW),
            pltpu.VMEM((*by_expert, 128), LOW),
        ],
    )
    kept, got = scatter_terms(back)
    first_grad, second_grad, token = call(
        expert_grad_kernel,
        "expert_gradients",
        1,
        [shaped(FULL, *w_in.shape), shaped(FULL, *w_out.shape), shaped(FULL, 8, 128)],
        [slot_rows, activated, pre_grad, gates, up_rows],
    )
    got, token, near_rows = together(got, token, near_rows)
    back = add(kept, got).reshape(ranks, slab, model_width)
    back, activated = together(back, activated)
    back = exchange(back)
    returned = call(
        expert_out_kernel,
        "expert_outputs",
        12,
        [shaped(LOW, ranks * slab, model_width)] * dps,
        [pack_t, w_out, activated],
        scratch=[pltpu.VMEM((*by_expert, model_width), LOW)],
    )
    returned = add(*scatter_terms(returned)).reshape(ranks, slab, model_width)
    back, returned = together(back, returned)
    returned = exchange(returned)

    bias_rows = -(-head_count // 6)
    small_rows = -(-(experts_total + 2 + bias_rows) // 8) * 8
    d_input, small, factors = call(
        functools.partial(backward_kernel, places, rank_slots),
        "attention_backward",
        12,
        [
            shaped(FULL, length, model_width),
            shaped(FULL, small_rows, model_width),
            shaped(LOW, ranks // 2, 2, 4 * columns_here, length),
        ],
        [
            tokens,
            gains,
            router_t,
            hits,
            mask,
            d_out,
            hidden,
            chance,
            heads,
            weights,
            jnp.asarray(bucket_onehot(bucket_count, length), FULL),
        ],
        pieces,
        [
            pltpu.VMEM(w_shape, LOW),
            pltpu.VMEM((inner_width, length), FULL),
            pltpu.VMEM((3, inner_width, length), FULL),
            pltpu.VMEM((head_count, 2 * length), FULL),
            pltpu.SemaphoreType.DMA,
        ],
        [back],
    )

    factors, small, returned = together(factors, small, returned)
    factors = lax.all_to_all(
        factors, "expert", split_axis=0, concat_axis=0, tiled=True, axis_index_groups=halves()
    )
    first, *steps, one_but_last, last = sum_steps()
    small = small + swap(small, *first)
    for axis, bit in steps:
        small = small + swap(small, axis, bit)
    factors, small = together(factors, small)
    small = small + swap(small, *one_but_last)
    grads = call(
        product_kernel,
        "weight_gradients",
        5,
        [shaped(LOW, 2, rows_here, 4 * columns_here)] * dps,
        [factors, token, rows, *near_rows],
        scratch=[pltpu.VMEM((2, dps, rows_here, 4 * columns_here), FULL)],
    )
    grads, small = together(scatter_near(grads), small)
    small = small + swap(small, *last)
    (output,) = call(
        output_kernel,
        "output_rows",
        2,
        [shaped(LOW, length, model_width)],
        [hidden, chance, hits, mask, returned],
    )
    kept, got = scatter_far(grads)
    got, output = together(got, output)
    other = swap(add(kept[1], got[1]), "expert", ranks // 2)
    grads = kept[0].astype(FULL) + got[0].astype(FULL) + other.astype(FULL)
    g_query, g_key, g_value, g_output = (
        grads[:, i * columns_here : (i + 1) * columns_here] for i in range(4)
    )
    g_router = small[:experts_total].T
    g_ffn_gain, g_attn_gain = small[experts_total], small[experts_total + 1]
    g_rel_bias = small[experts_total + 2 : experts_total + 2 + bias_rows].reshape(-1, 128)
    g_rel_bias = g_rel_bias[:head_count, :bucket_count].T
    return (
        output,
        d_input,
        g_attn_gain,
        g_query,
        g_key,
        g_value,
        g_output,
        g_rel_bias,
        g_ffn_gain,
        g_router,
        first_grad,
        second_grad,
    )


def solution(mesh):
    return jax.shard_map(
        per_device,
        mesh=mesh,
        in_specs=(
            P(("dp", "expert"), None),
            P(("dp", "expert"), None),
            P(("dp", "expert"), None),
            P(),
            P("dp", "expert"),
            P("dp", "expert"),
            P("dp", "expert"),
            P("dp", "expert"),
            P(),
            P(),
            P(),
            P("expert", None, "dp"),
            P("expert", "dp", None),
            P(("dp", "expert"), None),
        ),
        out_specs=(
            P(("dp", "expert"), None),
            P(("dp", "expert"), None),
            P(),
            P("dp", "expert"),
            P("dp", "expert"),
            P("dp", "expert"),
            P("dp", "expert"),
            P(),
            P(),
            P(),
            P("expert", None, "dp"),
            P("expert", "dp", None),
        ),
        check_vma=False,
    )
```

```python
import functools

import jax
import jax.numpy as jnp
import numpy as np
from jax import lax
from jax.experimental import pallas as pl
from jax.experimental.pallas import tpu as pltpu
from jax.sharding import PartitionSpec as P

EPSILON = 1e-06
LIMITS = (12, 16, 23, 32, 46, 64, 91)
MASKED = -1000000000.0
HIGHEST = lax.Precision.HIGHEST
LOW = jnp.bfloat16
FULL = jnp.float32


def bucket_onehot(buckets, length):
    delta = np.arange(2 * length) - length
    magnitude = np.abs(delta)
    distant = 8 + sum((magnitude >= threshold).astype(np.int32) for threshold in LIMITS)
    ids = np.where(delta > 0, 16, 0) + np.where(magnitude < 8, magnitude, distant)
    return (ids[None, :] == np.arange(buckets)[:, None]).astype(np.float32)


def packing(local_experts, ranks, capacity, slab):
    table = np.zeros((local_experts, ranks, capacity, ranks, slab), np.float32)
    for e in range(local_experts):
        for r in range(ranks):
            for c in range(capacity):
                table[e, r, c, r, e * capacity + c] = 1.0
    return table.reshape(local_experts * ranks * capacity, ranks * slab)


def normalize(matrix, gain_vec):
    scale = lax.rsqrt(jnp.mean(matrix * matrix, axis=-1, keepdims=True) + EPSILON)
    return (matrix * scale * gain_vec, scale)


def norm_back(matrix, scale, gain_vec, incoming):
    weighted = incoming * gain_vec
    average = jnp.mean(matrix * weighted, axis=-1, keepdims=True)
    return (
        scale * weighted - matrix * (scale * scale * scale) * average,
        jnp.sum(incoming * matrix * scale, axis=0, keepdims=True),
    )


def swap(value, axis, mask):
    count = lax.axis_size(axis)
    return lax.ppermute(value, axis, [(i, i ^ mask) for i in range(count)])


def gather_bits(value, axis, masks):
    return jnp.concatenate([value] + [swap(value, axis, mask) for mask in masks], axis=0)


def exchange(value):
    return lax.all_to_all(value, "expert", split_axis=0, concat_axis=0, tiled=True)


def half_ranks(value):
    return [value] + [swap(value, "expert", j) for j in range(1, lax.axis_size("expert") // 2)]


def halves():
    half = lax.axis_size("expert") // 2
    return [list(range(half)), list(range(half, 2 * half))]


def gather_far(value):
    found = {0: value}
    bit = lax.axis_size("dp") // 2
    while bit > 1:
        found.update({index ^ bit: swap(item, "dp", bit) for index, item in found.items()})
        bit = bit // 2
    return found


def gather_near(found):
    found = {**found, **{index ^ 1: swap(item, "dp", 1) for index, item in found.items()}}
    return [found[index] for index in range(len(found))]


def add(left, right, dtype=LOW):
    return (left.astype(FULL) + right.astype(FULL)).astype(dtype)


def scatter_near(items):
    taken = [swap(item, "dp", 1) for item in items[1::2]]
    return [add(kept, got) for kept, got in zip(items[0::2], taken)]


def scatter_far(items):
    bit = 2
    while len(items) > 2:
        taken = [swap(item, "dp", bit) for item in items[1::2]]
        items = [add(kept, got) for kept, got in zip(items[0::2], taken)]
        bit = bit * 2
    return items[0], swap(items[1], "dp", bit)


def scatter_terms(items):
    return scatter_far(scatter_near(items))


def sum_steps():
    steps = []
    for axis in ("dp", "expert"):
        bit = 1
        while bit < lax.axis_size(axis):
            steps.append((axis, bit))
            bit = bit * 2
    return steps


def together(*values):
    return lax.optimization_barrier(values)


def gather_pieces(payload, early):
    ranks, dps = lax.axis_size("expert"), lax.axis_size("dp")
    half = payload.shape[0] // 2
    far = list(range(0, ranks, 2))
    sides = {"x": ("expert", [0, 1]), "y": ("dp", list(range(0, dps, 2)))}
    value, early = together(gather_bits(payload[None], "expert", far[1:]), early)
    values = (value[:, :half], value[:, half:])
    firsts = []
    for value, letter in zip(values, "xy"):
        axis, masks = sides[letter]
        firsts.append(gather_bits(value[None], axis, masks[1:]))
    seconds = []
    for value, letter in zip(firsts, "yx"):
        axis, masks = sides[letter]
        seconds.append([swap(value, axis, mask) for mask in masks[1:]])
    others = [swap(value, "dp", 1) for value in firsts]
    pieces, places = [], []
    for index, order in enumerate(("xy", "yx")):
        masks, other_masks = sides[order[0]][1], sides[order[1]][1]
        found = [(firsts[index], 0, 0), (others[index], 0, 1)]
        for value, mask in zip(seconds[index], other_masks[1:]):
            found += [(value, mask, 0), (swap(value, "dp", 1), mask, 1)]
        for piece, mask, core in found:
            offsets = []
            for first in masks:
                for low in far:
                    x_mask, y_mask = (first, mask) if order == "xy" else (mask, first)
                    offsets.append((low ^ x_mask, y_mask ^ core))
            pieces.append(piece)
            places.append((index, offsets))
    return pieces, places, early


def place_weights(places, piece_refs, w_ref, sem):
    my_expert, my_dp = lax.axis_index("expert"), lax.axis_index("dp")
    copies = []
    for ref, (half, offsets) in zip(piece_refs, places):
        low_count, rows = ref.shape[1], ref.shape[2]
        for index, (e_mask, d_mask) in enumerate(offsets):
            start = (my_dp ^ d_mask) * (2 * rows) + half * rows
            copies.append(
                pltpu.make_async_copy(
                    ref.at[index // low_count, index % low_count],
                    w_ref.at[my_expert ^ e_mask, pl.ds(pl.multiple_of(start, 16), rows), :],
                    sem,
                )
            )
    for copy in copies:
        copy.start()
    return copies


def dot(left, right, dims=((1,), (0,)), precision=None):
    return lax.dot_general(
        left, right, (dims, ((), ())), precision=precision, preferred_element_type=FULL
    )


NT = ((1,), (1,))
TN = ((0,), (0,))


def grid_of(rows):
    sub = lax.broadcasted_iota(jnp.int32, (rows, 128), 0)
    lane = lax.broadcasted_iota(jnp.int32, (rows, 128), 1)
    return sub, lane


def row_to_column(row, rows, shift=0):
    sub, lane = grid_of(rows)
    column = jnp.sum(jnp.where(lane == sub + shift, row, 0.0), axis=1, keepdims=True)
    return jnp.broadcast_to(column, (rows, 128))


def column_to_row(column, shift=0):
    sub, lane = grid_of(column.shape[0])
    return jnp.sum(jnp.where(lane == sub + shift, column, 0.0), axis=0, keepdims=True)


def turn(value, shift):
    return pltpu.roll(value, shift % value.shape[1], 1)


def slide(value, direction):
    sub = lax.broadcasted_iota(jnp.int32, value.shape, 0)
    for bit in (1, 2, 4):
        value = jnp.where((sub & bit) != 0, turn(value, direction * bit), value)
    return value


def slid_rows(row, count):
    value = slide(jnp.broadcast_to(row, (8, row.shape[1])), 1)
    while value.shape[0] < count:
        value = jnp.concatenate([value, turn(value, value.shape[0])], axis=0)
    return value


def slid_sum(value):
    while value.shape[0] > 8:
        half = value.shape[0] // 2
        value = value[:half] + turn(value[half:], -half)
    return jnp.sum(slide(value, -1), axis=0, keepdims=True)


def early_kernel(
    ranks, local_experts, capacity, slab, tokens_ref, routes_ref, gain_ref, d_out_ref, table_ref,
    onehot_ref, normed_ref, hits_ref, mask_ref, mask_t_ref, bias_ref, up_ref
):
    length = tokens_ref.shape[0]
    normed, _ = normalize(tokens_ref[...].astype(FULL), gain_ref[0:1, :])
    normed_ref[...] = normed.astype(LOW)
    experts = hits_ref.shape[1]
    routes = jnp.broadcast_to(routes_ref[...].astype(FULL), (length, length)).T
    route = routes[:, :1].astype(jnp.int32)
    lanes = lax.broadcasted_iota(jnp.int32, (length, experts), 1)
    hits = (lanes == route).astype(FULL)
    hits_ref[...] = hits
    row = lax.broadcasted_iota(jnp.int32, (length, length), 0)
    col = lax.broadcasted_iota(jnp.int32, (length, length), 1)
    before = dot((col < row).astype(FULL).astype(LOW), hits.astype(LOW))
    placed = jnp.sum(before * hits, axis=1, keepdims=True).astype(jnp.int32)
    rank = jnp.zeros_like(route)
    for r in range(1, ranks):
        rank = rank + (route >= r * local_experts).astype(jnp.int32)
    spot = rank * slab + (route - rank * local_experts) * capacity + placed
    spot = jnp.where(placed < capacity, spot, -1)
    places = lax.broadcasted_iota(jnp.int32, (length, ranks * slab), 1)
    mask = (places == spot).astype(FULL)
    mask_ref[...] = mask.astype(LOW)
    mask_t = mask.T.astype(LOW)
    mask_t_ref[...] = mask_t
    slabs = dot(mask_t, d_out_ref[...])
    for r in range(ranks):
        up_ref[r] = slabs[r * slab : (r + 1) * slab].astype(LOW)
    values = dot(table_ref[...], onehot_ref[...])
    for h in range(bias_ref.shape[0]):
        bias_ref[h] = slid_rows(values[h : h + 1], length)[:, length:]


def forward_kernel(
    places, slab, rank_slots, tokens_ref, normed_ref, seg_ref, bias_ref, gain_ref,
    router_t_ref, hits_ref, mask_t_ref, *rest
):
    count = len(places)
    piece_refs, rest = rest[:count], rest[count:]
    heads_ref, weights_ref, rows_ref, hidden_ref, chance_ref = rest[:5]
    slabs_ref = rest[5]
    w_ref, qkv_ref, att_t_ref, sem = rest[-4:]
    copies = place_weights(places, piece_refs, w_ref, sem)
    ranks, width, columns = w_ref.shape
    cols = columns // 4
    head_count = weights_ref.shape[0]
    head = width // head_count
    length = tokens_ref.shape[0]
    segments = jnp.broadcast_to(seg_ref[...].astype(FULL), (length, length))
    same_doc = segments == segments.T
    normed = normed_ref[...]
    for copy in copies:
        copy.wait()
    for e in range(ranks):
        turned = dot(normed, w_ref[e]).T
        for m in range(3):
            qkv_ref[m, e * cols : (e + 1) * cols, :] = turned[m * cols : (m + 1) * cols]
    heads_ref[...] = qkv_ref[...].astype(LOW)
    for h in range(head_count):
        rows = slice(h * head, (h + 1) * head)
        scores = dot(heads_ref[0, rows, :], heads_ref[1, rows, :], TN) * head ** (-0.5)
        scores = jnp.where(same_doc, scores + bias_ref[h], MASKED)
        grown = jnp.exp(scores - jnp.max(scores, axis=1, keepdims=True))
        weights = grown / jnp.sum(grown, axis=1, keepdims=True)
        weights_ref[h] = weights
        att_t_ref[rows, :] = dot(heads_ref[2, rows, :], weights.astype(LOW), NT)
    attended = att_t_ref[...].T.astype(LOW)
    rows_ref[...] = attended
    low_lane = 3 * cols // 128 * 128
    for e in range(ranks):
        turned = dot(attended, w_ref[e, :, low_lane:]).T
        att_t_ref[e * cols : (e + 1) * cols, :] = turned[3 * cols - low_lane :]
    hidden = tokens_ref[...].astype(FULL) + att_t_ref[...].T
    hidden_ref[...] = hidden
    normed_two, _ = normalize(hidden, gain_ref[1:2, :])
    logits = dot(normed_two, router_t_ref[...].astype(FULL), NT, HIGHEST)
    grown = jnp.exp(logits - jnp.max(logits, axis=1, keepdims=True))
    chance = grown / jnp.sum(grown, axis=1, keepdims=True)
    chance_ref[...] = chance
    gate = jnp.sum(chance * hits_ref[...], axis=1, keepdims=True)
    mask_t = mask_t_ref[...]
    slots = dot(mask_t, normed_two.astype(LOW))
    gates = dot(mask_t.astype(FULL), jnp.broadcast_to(gate, (length, 128)), precision=HIGHEST)
    sub, _ = grid_of(slab)
    for r in range(ranks):
        mine = gates[r * slab : (r + 1) * slab]
        high = mine.astype(LOW).astype(FULL)
        row = column_to_row(high) + column_to_row(mine - high, 64)
        rows = slots[r * slab : (r + 1) * slab]
        start = rows[:, :128] + jnp.where(sub == rank_slots, row, 0.0)
        slabs_ref[r, :, :128] = start.astype(LOW)
        slabs_ref[r, :, 128:] = rows[:, 128:].astype(LOW)


def upstream_kernel(pack_ref, w_out_ref, *rest):
    piece_refs, (rows_ref, act_ref) = rest[:-2], rest[-2:]
    local_experts = w_out_ref.shape[0]
    chunk = pack_ref.shape[0] // local_experts
    for p, piece in enumerate(piece_refs):
        packed = dot(pack_ref[...], piece[...]).astype(LOW)
        for e in range(local_experts):
            rows_ref[e, p * chunk : (p + 1) * chunk, :] = packed[e * chunk : (e + 1) * chunk]
    for e in range(local_experts):
        act_ref[e] = dot(rows_ref[e], w_out_ref[e], NT)


def unpack(pack_t, rows_ref, p, chunk):
    rows = [rows_ref[e, p * chunk : (p + 1) * chunk, :] for e in range(rows_ref.shape[0])]
    return dot(pack_t, jnp.concatenate(rows, axis=0))


def expert_kernel(
    count, slab, rank_slots, pack_ref, pack_t_ref, w_in_ref, up_act_ref, *rest
):
    piece_refs, rest = rest[:count], rest[count:]
    back_refs, rest = rest[:count], rest[count:]
    rows_ref, act_ref, pre_grad_ref, gates_ref, pre_ref, back_ref, part_ref = rest
    local_experts = w_in_ref.shape[0]
    chunk = pack_ref.shape[0] // local_experts
    ranks = pack_ref.shape[1] // slab
    pack, pack_t = pack_ref[...], pack_t_ref[...]
    for p, piece in enumerate(piece_refs):
        packed = dot(pack, piece[...]).astype(LOW)
        tile = piece[:, :128].astype(FULL)
        spread = []
        for shift in (0, 64):
            columns = [
                row_to_column(tile[r * slab + rank_slots : r * slab + rank_slots + 1], slab, shift)
                for r in range(ranks)
            ]
            spread.append(dot(pack, jnp.concatenate(columns, axis=0).astype(LOW)))
        gates = spread[0] + spread[1]
        for e in range(local_experts):
            rows_ref[e, p * chunk : (p + 1) * chunk, :] = packed[e * chunk : (e + 1) * chunk]
            gates_ref[e, p * chunk : (p + 1) * chunk, :] = gates[e * chunk : (e + 1) * chunk]
    root = np.float32(np.sqrt(2.0 / np.pi))
    step = 16
    for e in range(local_experts):
        pre_ref[...] = dot(rows_ref[e], w_in_ref[e])

        def body(index, carry):
            span = pl.ds(pl.multiple_of(index * step, step), step)
            pre = pre_ref[span, :]
            up = up_act_ref[e, span, :]
            square = pre * pre
            curve = jnp.tanh(root * pre * (1.0 + 0.044715 * square))
            rise = 0.5 + 0.5 * curve
            act = (pre * rise).astype(LOW)
            act_ref[e, span, :] = act
            slope = rise + pre * (rise * (1.0 - curve)) * (root + 3 * 0.044715 * root * square)
            gate = gates_ref[e, span, :][:, :1]
            pre_grad_ref[e, span, :] = (slope * (up * gate)).astype(LOW)
            part = jnp.sum(act.astype(FULL) * up, axis=1, keepdims=True)
            part_ref[e, span, :] = jnp.broadcast_to(part, (step, 128)).astype(LOW)
            return carry

        lax.fori_loop(0, pre_ref.shape[0] // step, body, 0, unroll=2)
        back_ref[e] = dot(pre_grad_ref[e], w_in_ref[e], NT).astype(LOW)
    sub, _ = grid_of(slab)
    for p in range(count):
        rows = unpack(pack_t, back_ref, p, chunk)
        parts = unpack(pack_t, part_ref, p, chunk)
        pieces = []
        for r in range(ranks):
            span = slice(r * slab, (r + 1) * slab)
            row = column_to_row(parts[span])
            pieces.append(rows[span, :128] + jnp.where(sub == rank_slots, row, 0.0))
        back_refs[p][:, :128] = jnp.concatenate(pieces, axis=0).astype(LOW)
        back_refs[p][:, 128:] = rows[:, 128:].astype(LOW)


def expert_out_kernel(pack_t_ref, w_out_ref, act_ref, *rest):
    out_refs, returned_ref = rest[:-1], rest[-1]
    chunk = act_ref.shape[1] // len(out_refs)
    for e in range(w_out_ref.shape[0]):
        returned_ref[e] = dot(act_ref[e], w_out_ref[e]).astype(LOW)
    for p, ref in enumerate(out_refs):
        ref[...] = unpack(pack_t_ref[...], returned_ref, p, chunk).astype(LOW)


def expert_grad_kernel(
    rows_ref, act_ref, pre_grad_ref, gates_ref, up_rows_ref, g_in_ref, g_out_ref, token_ref
):
    for e in range(rows_ref.shape[0]):
        g_in_ref[e] = dot(rows_ref[e], pre_grad_ref[e], TN)
        slot_grad = (up_rows_ref[e].astype(FULL) * gates_ref[e][:, :1]).astype(LOW)
        g_out_ref[e] = dot(act_ref[e], slot_grad, TN)
    token_ref[...] = jnp.zeros(token_ref.shape, LOW)


def joined(ref):
    ranks, slab, width = ref.shape
    return ref[...].astype(FULL).reshape(ranks * slab, width).astype(LOW)


def backward_kernel(
    places, rank_slots, tokens_ref, gain_ref, router_t_ref, hits_ref, mask_ref,
    up_ref, hidden_ref, chance_ref, heads_ref, weights_ref, onehot_ref, *rest
):
    count = len(places)
    piece_refs, rest = rest[:count], rest[count:]
    (back_ref, d_input_ref, small_ref, factors_ref,
     w_ref, turned_ref, grads_ref, bias_ref, sem) = rest
    ranks, width, columns = w_ref.shape
    copies = place_weights(places, piece_refs, w_ref, sem)
    cols = columns // 4
    head_count = weights_ref.shape[0]
    head = width // head_count
    factor = head ** (-0.5)
    length = tokens_ref.shape[0]
    slab = back_ref.shape[1]
    hidden = hidden_ref[...]
    gain_two = gain_ref[1:2, :]
    normed_two, scale_two = normalize(hidden, gain_two)
    mask = mask_ref[...]
    chance, hits = chance_ref[...], hits_ref[...]
    gate = jnp.sum(chance * hits, axis=1, keepdims=True)
    spread = [
        row_to_column(back_ref[r, :, :128].astype(FULL)[rank_slots : rank_slots + 1], slab)
        for r in range(ranks)
    ]
    gate_grad = dot(mask, jnp.concatenate(spread, axis=0).astype(LOW))[:, :1]
    logit_grad = chance * (hits - gate) * gate_grad
    experts = hits.shape[1]
    small_ref[:experts, :] = dot(logit_grad, normed_two, TN, HIGHEST)
    router_t = router_t_ref[...].astype(FULL)
    normed_two_grad = dot(logit_grad, router_t, precision=HIGHEST) + dot(mask, joined(back_ref))
    hidden_part, ffn_gain_grad = norm_back(hidden, scale_two, gain_two, normed_two_grad)
    hidden_grad = up_ref[...].astype(FULL) + hidden_part
    turned_ref[...] = hidden_grad.astype(LOW).astype(FULL).T
    for copy in copies:
        copy.wait()
    low_lane = 3 * cols // 128 * 128
    att_grad = None
    for e in range(ranks):
        own = turned_ref[e * cols : (e + 1) * cols, :]
        if 3 * cols > low_lane:
            own = jnp.concatenate([jnp.zeros((3 * cols - low_lane, 128), FULL), own], axis=0)
        part = dot(w_ref[e, :, low_lane:], own.astype(LOW))
        att_grad = part if att_grad is None else att_grad + part
    att_grad = att_grad.astype(LOW)
    for h in range(head_count):
        rows = slice(h * head, (h + 1) * head)
        own = att_grad[rows]
        weights = weights_ref[h]
        grads_ref[2, rows, :] = dot(own, weights.astype(LOW))
        prob_grad = dot(own, heads_ref[2, rows, :], TN)
        score_grad = weights * (prob_grad - jnp.sum(prob_grad * weights, axis=1, keepdims=True))
        score_grad = score_grad.astype(LOW)
        grads_ref[0, rows, :] = dot(heads_ref[1, rows, :], score_grad, NT) * factor
        grads_ref[1, rows, :] = dot(heads_ref[0, rows, :], score_grad) * factor
        wide = [jnp.zeros((length, length), FULL), score_grad.astype(FULL)]
        bias_ref[h : h + 1, :] = slid_sum(jnp.concatenate(wide, axis=1))
    total = None
    for e in range(ranks):
        span = slice(e * cols, (e + 1) * cols)
        held = [grads_ref[m, span, :] for m in range(3)] + [jnp.zeros((cols, 128), FULL)]
        part = dot(w_ref[e], jnp.concatenate(held, axis=0).astype(LOW))
        total = part if total is None else total + part
        sent = [grads_ref[m, span, :] for m in range(3)] + [turned_ref[span, :]]
        sent = jnp.concatenate(sent, axis=0).astype(LOW)
        factors_ref[e % (ranks // 2), e // (ranks // 2)] = sent
    inputs = tokens_ref[...].astype(FULL)
    gain_one = gain_ref[0:1, :]
    _, scale_one = normalize(inputs, gain_one)
    norm_part, attn_gain_grad = norm_back(inputs, scale_one, gain_one, total.T)
    d_input_ref[...] = hidden_grad + norm_part
    sums = dot(bias_ref[...], onehot_ref[...], NT, HIGHEST)
    small_ref[experts : experts + 1, :] = ffn_gain_grad
    small_ref[experts + 1 : experts + 2, :] = attn_gain_grad
    small_ref[experts + 2 :, :] = jnp.zeros((small_ref.shape[0] - experts - 2, width), FULL)
    for h in range(head_count):
        line, place = experts + 2 + h // 6, 128 * (h % 6)
        small_ref[line : line + 1, place : place + sums.shape[1]] = sums[h : h + 1]


def product_kernel(factors_ref, *rest):
    count, _, columns, length = factors_ref.shape
    normed_refs, attended_refs = rest[:count], rest[count : 2 * count]
    piece_refs, total_ref = rest[2 * count : -1], rest[-1]
    cols = columns // 4
    rows = total_ref.shape[2]
    mine = lax.rem(lax.axis_index("expert"), count)
    for side in range(2):
        first, second = None, None
        for j in range(count):
            held = factors_ref[mine ^ j, side].astype(FULL)
            part = dot(held[: 3 * cols].astype(LOW), normed_refs[j][...])
            first = part if first is None else first + part
            part = dot(held[3 * cols :].astype(LOW), attended_refs[j][...])
            second = part if second is None else second + part
        total = jnp.concatenate([first, second], axis=0).T
        for j in range(len(piece_refs)):
            total_ref[side, j] = total[j * rows : (j + 1) * rows]
    own = (lax.axis_index("expert") >= count).astype(jnp.int32)
    for j, ref in enumerate(piece_refs):
        place = lax.axis_index("dp") ^ j
        ref[0] = total_ref[own, place].astype(LOW)
        ref[1] = total_ref[1 - own, place].astype(LOW)


def output_kernel(hidden_ref, chance_ref, hits_ref, mask_ref, returned_ref, output_ref):
    gate = jnp.sum(chance_ref[...] * hits_ref[...], axis=1, keepdims=True)
    fetched = dot(mask_ref[...], joined(returned_ref))
    output_ref[...] = (hidden_ref[...] + gate * fetched).astype(LOW)


VMEM = pl.BlockSpec(memory_space=pltpu.VMEM)
ANY = pl.BlockSpec(memory_space=pl.ANY)
LIMIT = 60 * 1024 * 1024


def shaped(dtype, *shape):
    return jax.ShapeDtypeStruct(shape, dtype)


def call(kernel, name, micros, out_shape, args, pieces=(), scratch=(), more=()):
    return pl.pallas_call(
        kernel,
        out_shape=tuple(out_shape),
        in_specs=[VMEM] * len(args) + [ANY] * len(pieces) + [VMEM] * len(more),
        out_specs=(VMEM,) * len(out_shape),
        scratch_shapes=list(scratch),
        compiler_params=pltpu.CompilerParams(vmem_limit_bytes=LIMIT),
        cost_estimate=pl.CostEstimate(
            flops=0, bytes_accessed=micros * 3_600_000, transcendentals=0
        ),
        name=name,
    )(*args, *pieces, *more)


def per_device(
    tokens,
    seg_ids,
    routes,
    attn_gain,
    w_query,
    w_key,
    w_value,
    w_output,
    rel_bias,
    ffn_gain,
    w_router,
    w_in,
    w_out,
    d_out,
):
    length, model_width = tokens.shape
    bucket_count, head_count = rel_bias.shape
    experts_total = w_router.shape[1]
    local_experts, _, hidden_here = w_in.shape
    ranks, dps = lax.axis_size("expert"), lax.axis_size("dp")
    capacity = length * 5 // (4 * experts_total)
    rank_slots = local_experts * capacity
    slab = -(-(rank_slots + 1) // 8) * 8
    rows_here, columns_here = w_query.shape
    inner_width = dps * rows_here
    packed_rows = dps * ranks * capacity
    gains = jnp.stack([attn_gain, ffn_gain]).astype(FULL)
    slabs_shape = shaped(LOW, ranks, slab, model_width)
    router_t = w_router.T
    pack = packing(local_experts, ranks, capacity, slab)
    pack, pack_t = jnp.asarray(pack, LOW), jnp.asarray(pack.T, LOW)

    normed_low, hits, mask, mask_t, bias_full, up_slabs = call(
        functools.partial(early_kernel, ranks, local_experts, capacity, slab),
        "early",
        3,
        [
            shaped(LOW, length, model_width),
            shaped(FULL, length, experts_total),
            shaped(LOW, length, ranks * slab),
            shaped(LOW, ranks * slab, length),
            shaped(FULL, head_count, length, length),
            slabs_shape,
        ],
        [
            tokens,
            routes.reshape(1, length),
            gains,
            d_out,
            rel_bias.T,
            jnp.asarray(bucket_onehot(bucket_count, length), LOW),
        ],
    )

    payload = jnp.concatenate([w_query, w_key, w_value, w_output], axis=1)
    early = (normed_low, hits, mask, mask_t, bias_full)
    pieces, places, early = gather_pieces(payload, early)
    normed_low, hits, mask, mask_t, bias_full = early
    pieces, up_slabs = together(pieces, up_slabs)
    up_arrived = exchange(up_slabs).reshape(ranks * slab, model_width)

    w_shape = (ranks, inner_width, 4 * columns_here)
    heads, weights, attended, hidden, chance, slabs = call(
        functools.partial(forward_kernel, places, slab, rank_slots),
        "attention_forward",
        10,
        [
            shaped(LOW, 3, inner_width, length),
            shaped(FULL, head_count, length, length),
            shaped(LOW, length, inner_width),
            shaped(FULL, length, model_width),
            shaped(FULL, length, experts_total),
            slabs_shape,
        ],
        [tokens, normed_low, seg_ids, bias_full, gains, router_t, hits, mask_t],
        pieces,
        [
            pltpu.VMEM(w_shape, LOW),
            pltpu.VMEM((3, inner_width, length), FULL),
            pltpu.VMEM((inner_width, length), FULL),
            pltpu.SemaphoreType.DMA,
        ],
    )

    slabs, up_arrived = together(slabs, up_arrived)
    arrived = exchange(slabs).reshape(ranks * slab, model_width)
    up_pieces = gather_near(gather_far(up_arrived))
    arrived, up_pieces, normed_own = together(arrived, up_pieces, normed_low)
    row_far = gather_far(arrived)
    near_normed = half_ranks(normed_own)
    by_expert = (local_experts, packed_rows)
    up_rows, up_act = call(
        upstream_kernel,
        "upstream_rows",
        5,
        [shaped(LOW, *by_expert, model_width), shaped(FULL, *by_expert, hidden_here)],
        [pack, w_out, *up_pieces],
    )
    row_far, up_act, near_normed = together(row_far, up_act, near_normed)
    row_pieces = gather_near(row_far)

    *back, slot_rows, activated, pre_grad, gates = call(
        functools.partial(expert_kernel, dps, slab, rank_slots),
        "experts",
        10,
        [shaped(LOW, ranks * slab, model_width)] * dps
        + [
            shaped(LOW, *by_expert, model_width),
            shaped(LOW, *by_expert, hidden_here),
            shaped(LOW, *by_expert, hidden_here),
            shaped(FULL, *by_expert, 128),
        ],
        [pack, pack_t, w_in, up_act, *row_pieces],
        scratch=[
            pltpu.VMEM((packed_rows, hidden_here), FULL),
            pltpu.VMEM((*by_expert, model_width), LOW),
            pltpu.VMEM((*by_expert, 128), LOW),
        ],
    )
    near, attended_own = together(scatter_near(back), attended)
    kept, got = scatter_far(near)
    near_attended = half_ranks(attended_own)
    near, late_activated = together(near, activated)
    returned = call(
        expert_out_kernel,
        "expert_outputs",
        3,
        [shaped(LOW, ranks * slab, model_width)] * dps,
        [pack_t, w_out, late_activated],
        scratch=[pltpu.VMEM((*by_expert, model_width), LOW)],
    )
    got, returned, near_attended = together(got, returned, near_attended)
    back = add(kept, got).reshape(ranks, slab, model_width)
    back, returned = together(back, returned)
    back = exchange(back)
    returned = add(*scatter_terms(returned)).reshape(ranks, slab, model_width)
    back, returned = together(back, returned)
    returned = exchange(returned)

    bias_rows = -(-head_count // 6)
    small_rows = -(-(experts_total + 2 + bias_rows) // 8) * 8
    d_input, small, factors = call(
        functools.partial(backward_kernel, places, rank_slots),
        "attention_backward",
        12,
        [
            shaped(FULL, length, model_width),
            shaped(FULL, small_rows, model_width),
            shaped(LOW, ranks // 2, 2, 4 * columns_here, length),
        ],
        [
            tokens,
            gains,
            router_t,
            hits,
            mask,
            d_out,
            hidden,
            chance,
            heads,
            weights,
            jnp.asarray(bucket_onehot(bucket_count, length), FULL),
        ],
        pieces,
        [
            pltpu.VMEM(w_shape, LOW),
            pltpu.VMEM((inner_width, length), FULL),
            pltpu.VMEM((3, inner_width, length), FULL),
            pltpu.VMEM((head_count, 2 * length), FULL),
            pltpu.SemaphoreType.DMA,
        ],
        [back],
    )

    factors, small, returned = together(factors, small, returned)
    factors = lax.all_to_all(
        factors, "expert", split_axis=0, concat_axis=0, tiled=True, axis_index_groups=halves()
    )
    first, *steps, one_but_last, last = sum_steps()
    small = small + swap(small, *first)
    for axis, bit in steps:
        small = small + swap(small, axis, bit)
    factors, small = together(factors, small)
    small = small + swap(small, *one_but_last)
    grads = call(
        product_kernel,
        "weight_gradients",
        5,
        [shaped(LOW, 2, rows_here, 4 * columns_here)] * dps,
        [factors, *near_normed, *near_attended],
        scratch=[pltpu.VMEM((2, dps, rows_here, 4 * columns_here), FULL)],
    )
    grads, small = together(scatter_near(grads), small)
    small = small + swap(small, *last)
    (output,) = call(
        output_kernel,
        "output_rows",
        2,
        [shaped(LOW, length, model_width)],
        [hidden, chance, hits, mask, returned],
    )
    kept, got = scatter_far(grads)
    got, output = together(got, output)
    other, activated = together(add(kept[1], got[1]), activated)
    other = swap(other, "expert", ranks // 2)
    first_grad, second_grad, token = call(
        expert_grad_kernel,
        "expert_gradients",
        8,
        [shaped(FULL, *w_in.shape), shaped(FULL, *w_out.shape), shaped(LOW, 16, 128)],
        [slot_rows, activated, pre_grad, gates, up_rows],
    )
    other, token = together(other, token)
    other = other + jnp.sum(token)
    grads = kept[0].astype(FULL) + got[0].astype(FULL) + other.astype(FULL)
    g_query, g_key, g_value, g_output = (
        grads[:, i * columns_here : (i + 1) * columns_here] for i in range(4)
    )
    g_router = small[:experts_total].T
    g_ffn_gain, g_attn_gain = small[experts_total], small[experts_total + 1]
    g_rel_bias = small[experts_total + 2 : experts_total + 2 + bias_rows].reshape(-1, 128)
    g_rel_bias = g_rel_bias[:head_count, :bucket_count].T
    return (
        output,
        d_input,
        g_attn_gain,
        g_query,
        g_key,
        g_value,
        g_output,
        g_rel_bias,
        g_ffn_gain,
        g_router,
        first_grad,
        second_grad,
    )


def solution(mesh):
    return jax.shard_map(
        per_device,
        mesh=mesh,
        in_specs=(
            P(("dp", "expert"), None),
            P(("dp", "expert"), None),
            P(("dp", "expert"), None),
            P(),
            P("dp", "expert"),
            P("dp", "expert"),
            P("dp", "expert"),
            P("dp", "expert"),
            P(),
            P(),
            P(),
            P("expert", None, "dp"),
            P("expert", "dp", None),
            P(("dp", "expert"), None),
        ),
        out_specs=(
            P(("dp", "expert"), None),
            P(("dp", "expert"), None),
            P(),
            P("dp", "expert"),
            P("dp", "expert"),
            P("dp", "expert"),
            P("dp", "expert"),
            P(),
            P(),
            P(),
            P("expert", None, "dp"),
            P("expert", "dp", None),
        ),
        check_vma=False,
    )
```

```python
import functools

import jax
import jax.numpy as jnp
import numpy as np
from jax import lax
from jax.experimental import pallas as pl
from jax.experimental.pallas import tpu as pltpu
from jax.sharding import PartitionSpec as P

EPSILON = 1e-06
LIMITS = (12, 16, 23, 32, 46, 64, 91)
MASKED = -1000000000.0
HIGHEST = lax.Precision.HIGHEST
LOW = jnp.bfloat16
FULL = jnp.float32


def bucket_onehot(buckets, length):
    delta = np.arange(2 * length) - length
    magnitude = np.abs(delta)
    distant = 8 + sum((magnitude >= threshold).astype(np.int32) for threshold in LIMITS)
    ids = np.where(delta > 0, 16, 0) + np.where(magnitude < 8, magnitude, distant)
    return (ids[None, :] == np.arange(buckets)[:, None]).astype(np.float32)


def packing(local_experts, ranks, capacity, slab):
    table = np.zeros((local_experts, ranks, capacity, ranks, slab), np.float32)
    for e in range(local_experts):
        for r in range(ranks):
            for c in range(capacity):
                table[e, r, c, r, e * capacity + c] = 1.0
    return table.reshape(local_experts * ranks * capacity, ranks * slab)


def normalize(matrix, gain_vec):
    scale = lax.rsqrt(jnp.mean(matrix * matrix, axis=-1, keepdims=True) + EPSILON)
    return (matrix * scale * gain_vec, scale)


def norm_back(matrix, scale, gain_vec, incoming):
    weighted = incoming * gain_vec
    average = jnp.mean(matrix * weighted, axis=-1, keepdims=True)
    return (
        scale * weighted - matrix * (scale * scale * scale) * average,
        jnp.sum(incoming * matrix * scale, axis=0, keepdims=True),
    )


def swap(value, axis, mask):
    count = lax.axis_size(axis)
    return lax.ppermute(value, axis, [(i, i ^ mask) for i in range(count)])


def gather_bits(value, axis, masks):
    return jnp.concatenate([value] + [swap(value, axis, mask) for mask in masks], axis=0)


def exchange(value):
    return lax.all_to_all(value, "expert", split_axis=0, concat_axis=0, tiled=True)


def half_ranks(value):
    return [value] + [swap(value, "expert", j) for j in range(1, lax.axis_size("expert") // 2)]


def halves():
    half = lax.axis_size("expert") // 2
    return [list(range(half)), list(range(half, 2 * half))]


def gather_far(value):
    found = {0: value}
    bit = lax.axis_size("dp") // 2
    while bit > 1:
        found.update({index ^ bit: swap(item, "dp", bit) for index, item in found.items()})
        bit = bit // 2
    return found


def gather_near(found):
    found = {**found, **{index ^ 1: swap(item, "dp", 1) for index, item in found.items()}}
    return [found[index] for index in range(len(found))]


def add(left, right, dtype=LOW):
    return (left.astype(FULL) + right.astype(FULL)).astype(dtype)


def scatter_near(items):
    taken = [swap(item, "dp", 1) for item in items[1::2]]
    return [add(kept, got) for kept, got in zip(items[0::2], taken)]


def scatter_far(items):
    bit = 2
    while len(items) > 2:
        taken = [swap(item, "dp", bit) for item in items[1::2]]
        items = [add(kept, got) for kept, got in zip(items[0::2], taken)]
        bit = bit * 2
    return items[0], swap(items[1], "dp", bit)


def scatter_terms(items):
    return scatter_far(scatter_near(items))


def sum_steps():
    steps = []
    for axis in ("dp", "expert"):
        bit = 1
        while bit < lax.axis_size(axis):
            steps.append((axis, bit))
            bit = bit * 2
    return steps


def together(*values):
    return lax.optimization_barrier(values)


def gather_pieces(payload, early):
    ranks, dps = lax.axis_size("expert"), lax.axis_size("dp")
    half = payload.shape[0] // 2
    far = list(range(0, ranks, 2))
    sides = {"x": ("expert", [0, 1]), "y": ("dp", list(range(0, dps, 2)))}
    value, early = together(gather_bits(payload[None], "expert", far[1:]), early)
    values = (value[:, :half], value[:, half:])
    firsts = []
    for value, letter in zip(values, "xy"):
        axis, masks = sides[letter]
        firsts.append(gather_bits(value[None], axis, masks[1:]))
    seconds = []
    for value, letter in zip(firsts, "yx"):
        axis, masks = sides[letter]
        seconds.append([swap(value, axis, mask) for mask in masks[1:]])
    others = [swap(value, "dp", 1) for value in firsts]
    pieces, places = [], []
    for index, order in enumerate(("xy", "yx")):
        masks, other_masks = sides[order[0]][1], sides[order[1]][1]
        found = [(firsts[index], 0, 0), (others[index], 0, 1)]
        for value, mask in zip(seconds[index], other_masks[1:]):
            found += [(value, mask, 0), (swap(value, "dp", 1), mask, 1)]
        for piece, mask, core in found:
            offsets = []
            for first in masks:
                for low in far:
                    x_mask, y_mask = (first, mask) if order == "xy" else (mask, first)
                    offsets.append((low ^ x_mask, y_mask ^ core))
            pieces.append(piece)
            places.append((index, offsets))
    return pieces, places, early


def place_weights(places, piece_refs, w_ref, sem):
    my_expert, my_dp = lax.axis_index("expert"), lax.axis_index("dp")
    copies, masks = [], []
    for ref, (half, offsets) in zip(piece_refs, places):
        low_count, rows = ref.shape[1], ref.shape[2]
        for index, (e_mask, d_mask) in enumerate(offsets):
            start = (my_dp ^ d_mask) * (2 * rows) + half * rows
            copies.append(
                pltpu.make_async_copy(
                    ref.at[index // low_count, index % low_count],
                    w_ref.at[my_expert ^ e_mask, pl.ds(pl.multiple_of(start, 16), rows), :],
                    sem.at[e_mask],
                )
            )
            masks.append(e_mask)
    groups = [[] for _ in range(w_ref.shape[0])]
    for copy, e_mask in zip(copies, masks):
        groups[e_mask].append(copy)
    for group in groups:
        for copy in group:
            copy.start()
    return groups


def dot(left, right, dims=((1,), (0,)), precision=None):
    return lax.dot_general(
        left, right, (dims, ((), ())), precision=precision, preferred_element_type=FULL
    )


NT = ((1,), (1,))
TN = ((0,), (0,))


def grid_of(rows):
    sub = lax.broadcasted_iota(jnp.int32, (rows, 128), 0)
    lane = lax.broadcasted_iota(jnp.int32, (rows, 128), 1)
    return sub, lane


def row_to_column(row, rows, shift=0):
    sub, lane = grid_of(rows)
    column = jnp.sum(jnp.where(lane == sub + shift, row, 0.0), axis=1, keepdims=True)
    return jnp.broadcast_to(column, (rows, 128))


def column_to_row(column, shift=0):
    sub, lane = grid_of(column.shape[0])
    return jnp.sum(jnp.where(lane == sub + shift, column, 0.0), axis=0, keepdims=True)


def turn(value, shift):
    return pltpu.roll(value, shift % value.shape[1], 1)


def slide(value, direction):
    sub = lax.broadcasted_iota(jnp.int32, value.shape, 0)
    for bit in (1, 2, 4):
        value = jnp.where((sub & bit) != 0, turn(value, direction * bit), value)
    return value


def slid_rows(row, count):
    value = slide(jnp.broadcast_to(row, (8, row.shape[1])), 1)
    while value.shape[0] < count:
        value = jnp.concatenate([value, turn(value, value.shape[0])], axis=0)
    return value


def slid_sum(value):
    while value.shape[0] > 8:
        half = value.shape[0] // 2
        value = value[:half] + turn(value[half:], -half)
    return jnp.sum(slide(value, -1), axis=0, keepdims=True)


def early_kernel(
    ranks, local_experts, capacity, slab, tokens_ref, routes_ref, gain_ref, d_out_ref, table_ref,
    onehot_ref, normed_ref, hits_ref, mask_ref, mask_t_ref, bias_ref, up_ref
):
    length = tokens_ref.shape[0]
    normed, _ = normalize(tokens_ref[...].astype(FULL), gain_ref[0:1, :])
    normed_ref[...] = normed.astype(LOW)
    experts = hits_ref.shape[1]
    routes = jnp.broadcast_to(routes_ref[...].astype(FULL), (length, length)).T
    route = routes[:, :1].astype(jnp.int32)
    lanes = lax.broadcasted_iota(jnp.int32, (length, experts), 1)
    hits = (lanes == route).astype(FULL)
    hits_ref[...] = hits
    row = lax.broadcasted_iota(jnp.int32, (length, length), 0)
    col = lax.broadcasted_iota(jnp.int32, (length, length), 1)
    before = dot((col < row).astype(FULL).astype(LOW), hits.astype(LOW))
    placed = jnp.sum(before * hits, axis=1, keepdims=True).astype(jnp.int32)
    rank = jnp.zeros_like(route)
    for r in range(1, ranks):
        rank = rank + (route >= r * local_experts).astype(jnp.int32)
    spot = rank * slab + (route - rank * local_experts) * capacity + placed
    spot = jnp.where(placed < capacity, spot, -1)
    places = lax.broadcasted_iota(jnp.int32, (length, ranks * slab), 1)
    mask = (places == spot).astype(FULL)
    mask_ref[...] = mask.astype(LOW)
    mask_t = mask.T.astype(LOW)
    mask_t_ref[...] = mask_t
    slabs = dot(mask_t, d_out_ref[...])
    for r in range(ranks):
        up_ref[r] = slabs[r * slab : (r + 1) * slab].astype(LOW)
    values = dot(table_ref[...], onehot_ref[...])
    for h in range(bias_ref.shape[0]):
        bias_ref[h] = slid_rows(values[h : h + 1], length)[:, length:]


def forward_kernel(
    places, slab, rank_slots, tokens_ref, normed_ref, seg_ref, bias_ref, gain_ref,
    router_t_ref, hits_ref, mask_t_ref, *rest
):
    count = len(places)
    piece_refs, rest = rest[:count], rest[count:]
    heads_ref, weights_ref, rows_ref, hidden_ref, chance_ref = rest[:5]
    slabs_ref = rest[5]
    w_ref, qkv_ref, att_t_ref, sem = rest[-4:]
    copies = place_weights(places, piece_refs, w_ref, sem)
    ranks, width, columns = w_ref.shape
    cols = columns // 4
    head_count = weights_ref.shape[0]
    head = width // head_count
    length = tokens_ref.shape[0]
    segments = jnp.broadcast_to(seg_ref[...].astype(FULL), (length, length))
    same_doc = segments == segments.T
    normed = normed_ref[...]
    for j, group in enumerate(copies):
        for copy in group:
            copy.wait()
        e = lax.axis_index("expert") ^ j
        turned = dot(normed, w_ref[e]).T
        for m in range(3):
            qkv_ref[m, e] = turned[m * cols : (m + 1) * cols]
    heads_ref[...] = qkv_ref[...].reshape(3, width, length).astype(LOW)
    for h in range(head_count):
        rows = slice(h * head, (h + 1) * head)
        scores = dot(heads_ref[0, rows, :], heads_ref[1, rows, :], TN) * head ** (-0.5)
        scores = jnp.where(same_doc, scores + bias_ref[h], MASKED)
        grown = jnp.exp(scores - jnp.max(scores, axis=1, keepdims=True))
        weights = grown / jnp.sum(grown, axis=1, keepdims=True)
        weights_ref[h] = weights
        att_t_ref[rows, :] = dot(heads_ref[2, rows, :], weights.astype(LOW), NT)
    attended = att_t_ref[...].T.astype(LOW)
    rows_ref[...] = attended
    low_lane = 3 * cols // 128 * 128
    for e in range(ranks):
        turned = dot(attended, w_ref[e, :, low_lane:]).T
        att_t_ref[e * cols : (e + 1) * cols, :] = turned[3 * cols - low_lane :]
    hidden = tokens_ref[...].astype(FULL) + att_t_ref[...].T
    hidden_ref[...] = hidden
    normed_two, _ = normalize(hidden, gain_ref[1:2, :])
    logits = dot(normed_two, router_t_ref[...].astype(FULL), NT, HIGHEST)
    grown = jnp.exp(logits - jnp.max(logits, axis=1, keepdims=True))
    chance = grown / jnp.sum(grown, axis=1, keepdims=True)
    chance_ref[...] = chance
    gate = jnp.sum(chance * hits_ref[...], axis=1, keepdims=True)
    mask_t = mask_t_ref[...]
    slots = dot(mask_t, normed_two.astype(LOW))
    gates = dot(mask_t.astype(FULL), jnp.broadcast_to(gate, (length, 128)), precision=HIGHEST)
    sub, _ = grid_of(slab)
    for r in range(ranks):
        mine = gates[r * slab : (r + 1) * slab]
        high = mine.astype(LOW).astype(FULL)
        row = column_to_row(high) + column_to_row(mine - high, 64)
        rows = slots[r * slab : (r + 1) * slab]
        start = rows[:, :128] + jnp.where(sub == rank_slots, row, 0.0)
        slabs_ref[r, :, :128] = start.astype(LOW)
        slabs_ref[r, :, 128:] = rows[:, 128:].astype(LOW)


def upstream_kernel(pack_ref, w_out_ref, *rest):
    piece_refs, (rows_ref, act_ref) = rest[:-2], rest[-2:]
    local_experts = w_out_ref.shape[0]
    chunk = pack_ref.shape[0] // local_experts
    for p, piece in enumerate(piece_refs):
        packed = dot(pack_ref[...], piece[...]).astype(LOW)
        for e in range(local_experts):
            rows_ref[e, p * chunk : (p + 1) * chunk, :] = packed[e * chunk : (e + 1) * chunk]
    for e in range(local_experts):
        act_ref[e] = dot(rows_ref[e], w_out_ref[e], NT)


def unpack(pack_t, rows_ref, p, chunk):
    rows = [rows_ref[e, p * chunk : (p + 1) * chunk, :] for e in range(rows_ref.shape[0])]
    return dot(pack_t, jnp.concatenate(rows, axis=0))


def expert_kernel(
    count, slab, rank_slots, pack_ref, pack_t_ref, w_in_ref, up_act_ref, *rest
):
    piece_refs, rest = rest[:count], rest[count:]
    back_refs, rest = rest[:count], rest[count:]
    rows_ref, act_ref, pre_grad_ref, gates_ref, pre_ref, back_ref, part_ref = rest
    local_experts = w_in_ref.shape[0]
    chunk = pack_ref.shape[0] // local_experts
    ranks = pack_ref.shape[1] // slab
    pack, pack_t = pack_ref[...], pack_t_ref[...]
    for p, piece in enumerate(piece_refs):
        packed = dot(pack, piece[...]).astype(LOW)
        tile = piece[:, :128].astype(FULL)
        spread = []
        for shift in (0, 64):
            columns = [
                row_to_column(tile[r * slab + rank_slots : r * slab + rank_slots + 1], slab, shift)
                for r in range(ranks)
            ]
            spread.append(dot(pack, jnp.concatenate(columns, axis=0).astype(LOW)))
        gates = spread[0] + spread[1]
        for e in range(local_experts):
            rows_ref[e, p * chunk : (p + 1) * chunk, :] = packed[e * chunk : (e + 1) * chunk]
            gates_ref[e, p * chunk : (p + 1) * chunk, :] = gates[e * chunk : (e + 1) * chunk]
    root = np.float32(np.sqrt(2.0 / np.pi))
    step = 16
    for e in range(local_experts):
        pre_ref[...] = dot(rows_ref[e], w_in_ref[e])

        def body(index, carry):
            span = pl.ds(pl.multiple_of(index * step, step), step)
            pre = pre_ref[span, :]
            up = up_act_ref[e, span, :]
            square = pre * pre
            curve = jnp.tanh(root * pre * (1.0 + 0.044715 * square))
            rise = 0.5 + 0.5 * curve
            act = (pre * rise).astype(LOW)
            act_ref[e, span, :] = act
            slope = rise + pre * (rise * (1.0 - curve)) * (root + 3 * 0.044715 * root * square)
            gate = gates_ref[e, span, :][:, :1]
            pre_grad_ref[e, span, :] = (slope * (up * gate)).astype(LOW)
            part = jnp.sum(act.astype(FULL) * up, axis=1, keepdims=True)
            part_ref[e, span, :] = jnp.broadcast_to(part, (step, 128)).astype(LOW)
            return carry

        lax.fori_loop(0, pre_ref.shape[0] // step, body, 0, unroll=2)
        back_ref[e] = dot(pre_grad_ref[e], w_in_ref[e], NT).astype(LOW)
    sub, _ = grid_of(slab)
    for p in range(count):
        rows = unpack(pack_t, back_ref, p, chunk)
        parts = unpack(pack_t, part_ref, p, chunk)
        pieces = []
        for r in range(ranks):
            span = slice(r * slab, (r + 1) * slab)
            row = column_to_row(parts[span])
            pieces.append(rows[span, :128] + jnp.where(sub == rank_slots, row, 0.0))
        back_refs[p][:, :128] = jnp.concatenate(pieces, axis=0).astype(LOW)
        back_refs[p][:, 128:] = rows[:, 128:].astype(LOW)


def expert_out_kernel(pack_t_ref, w_out_ref, act_ref, *rest):
    out_refs, returned_ref = rest[:-1], rest[-1]
    chunk = act_ref.shape[1] // len(out_refs)
    for e in range(w_out_ref.shape[0]):
        returned_ref[e] = dot(act_ref[e], w_out_ref[e]).astype(LOW)
    for p, ref in enumerate(out_refs):
        ref[...] = unpack(pack_t_ref[...], returned_ref, p, chunk).astype(LOW)


def expert_grad_kernel(
    rows_ref, act_ref, pre_grad_ref, gates_ref, up_rows_ref, g_in_ref, g_out_ref
):
    g_in_ref[0] = dot(rows_ref[0], pre_grad_ref[0], TN)
    slot_grad = (up_rows_ref[0].astype(FULL) * gates_ref[0][:, :1]).astype(LOW)
    g_out_ref[0] = dot(act_ref[0], slot_grad, TN)


def expert_gradients(shapes, args):
    def block(item):
        return pl.BlockSpec((1,) + item.shape[1:], lambda e: (e, 0, 0))

    return pl.pallas_call(
        expert_grad_kernel,
        grid=(shapes[0].shape[0],),
        out_shape=tuple(shapes),
        in_specs=[block(item) for item in args],
        out_specs=tuple(block(item) for item in shapes),
        compiler_params=pltpu.CompilerParams(vmem_limit_bytes=LIMIT),
        cost_estimate=pl.CostEstimate(flops=0, bytes_accessed=28_800_000, transcendentals=0),
        name="expert_gradients",
    )(*args)


def joined(ref):
    ranks, slab, width = ref.shape
    return ref[...].astype(FULL).reshape(ranks * slab, width).astype(LOW)


def backward_kernel(
    places, rank_slots, tokens_ref, gain_ref, router_t_ref, hits_ref, mask_ref,
    up_ref, hidden_ref, chance_ref, heads_ref, weights_ref, onehot_ref, *rest
):
    count = len(places)
    piece_refs, rest = rest[:count], rest[count:]
    (back_ref, d_input_ref, small_ref, factors_ref,
     w_ref, turned_ref, grads_ref, bias_ref, sem) = rest
    ranks, width, columns = w_ref.shape
    copies = place_weights(places, piece_refs, w_ref, sem)
    cols = columns // 4
    head_count = weights_ref.shape[0]
    head = width // head_count
    factor = head ** (-0.5)
    length = tokens_ref.shape[0]
    slab = back_ref.shape[1]
    hidden = hidden_ref[...]
    gain_two = gain_ref[1:2, :]
    normed_two, scale_two = normalize(hidden, gain_two)
    mask = mask_ref[...]
    chance, hits = chance_ref[...], hits_ref[...]
    gate = jnp.sum(chance * hits, axis=1, keepdims=True)
    spread = [
        row_to_column(back_ref[r, :, :128].astype(FULL)[rank_slots : rank_slots + 1], slab)
        for r in range(ranks)
    ]
    gate_grad = dot(mask, jnp.concatenate(spread, axis=0).astype(LOW))[:, :1]
    logit_grad = chance * (hits - gate) * gate_grad
    experts = hits.shape[1]
    small_ref[:experts, :] = dot(logit_grad, normed_two, TN, HIGHEST)
    router_t = router_t_ref[...].astype(FULL)
    normed_two_grad = dot(logit_grad, router_t, precision=HIGHEST) + dot(mask, joined(back_ref))
    hidden_part, ffn_gain_grad = norm_back(hidden, scale_two, gain_two, normed_two_grad)
    hidden_grad = up_ref[...].astype(FULL) + hidden_part
    turned_ref[...] = hidden_grad.astype(LOW).astype(FULL).T
    for group in copies:
        for copy in group:
            copy.wait()
    low_lane = 3 * cols // 128 * 128
    att_grad = None
    for e in range(ranks):
        own = turned_ref[e * cols : (e + 1) * cols, :]
        if 3 * cols > low_lane:
            own = jnp.concatenate([jnp.zeros((3 * cols - low_lane, 128), FULL), own], axis=0)
        part = dot(w_ref[e, :, low_lane:], own.astype(LOW))
        att_grad = part if att_grad is None else att_grad + part
    att_grad = att_grad.astype(LOW)
    for h in range(head_count):
        rows = slice(h * head, (h + 1) * head)
        own = att_grad[rows]
        weights = weights_ref[h]
        grads_ref[2, rows, :] = dot(own, weights.astype(LOW))
        prob_grad = dot(own, heads_ref[2, rows, :], TN)
        score_grad = weights * (prob_grad - jnp.sum(prob_grad * weights, axis=1, keepdims=True))
        score_grad = score_grad.astype(LOW)
        grads_ref[0, rows, :] = dot(heads_ref[1, rows, :], score_grad, NT) * factor
        grads_ref[1, rows, :] = dot(heads_ref[0, rows, :], score_grad) * factor
        wide = [jnp.zeros((length, length), FULL), score_grad.astype(FULL)]
        bias_ref[h : h + 1, :] = slid_sum(jnp.concatenate(wide, axis=1))
    total = None
    for e in range(ranks):
        span = slice(e * cols, (e + 1) * cols)
        held = [grads_ref[m, span, :] for m in range(3)] + [jnp.zeros((cols, 128), FULL)]
        part = dot(w_ref[e], jnp.concatenate(held, axis=0).astype(LOW))
        total = part if total is None else total + part
        sent = [grads_ref[m, span, :] for m in range(3)] + [turned_ref[span, :]]
        sent = jnp.concatenate(sent, axis=0).astype(LOW)
        factors_ref[e % (ranks // 2), e // (ranks // 2)] = sent
    inputs = tokens_ref[...].astype(FULL)
    gain_one = gain_ref[0:1, :]
    _, scale_one = normalize(inputs, gain_one)
    norm_part, attn_gain_grad = norm_back(inputs, scale_one, gain_one, total.T)
    d_input_ref[...] = hidden_grad + norm_part
    sums = dot(bias_ref[...], onehot_ref[...], NT, HIGHEST)
    small_ref[experts : experts + 1, :] = ffn_gain_grad
    small_ref[experts + 1 : experts + 2, :] = attn_gain_grad
    small_ref[experts + 2 :, :] = jnp.zeros((small_ref.shape[0] - experts - 2, width), FULL)
    for h in range(head_count):
        line, place = experts + 2 + h // 6, 128 * (h % 6)
        small_ref[line : line + 1, place : place + sums.shape[1]] = sums[h : h + 1]


def product_kernel(factors_ref, *rest):
    count, _, columns, length = factors_ref.shape
    normed_refs, attended_refs = rest[:count], rest[count : 2 * count]
    piece_refs, total_ref = rest[2 * count : -1], rest[-1]
    cols = columns // 4
    rows = total_ref.shape[2]
    mine = lax.rem(lax.axis_index("expert"), count)
    for side in range(2):
        first, second = None, None
        for j in range(count):
            held = factors_ref[mine ^ j, side].astype(FULL)
            part = dot(held[: 3 * cols].astype(LOW), normed_refs[j][...])
            first = part if first is None else first + part
            part = dot(held[3 * cols :].astype(LOW), attended_refs[j][...])
            second = part if second is None else second + part
        total = jnp.concatenate([first, second], axis=0).T
        for j in range(len(piece_refs)):
            total_ref[side, j] = total[j * rows : (j + 1) * rows]
    own = (lax.axis_index("expert") >= count).astype(jnp.int32)
    for j, ref in enumerate(piece_refs):
        place = lax.axis_index("dp") ^ j
        ref[0] = total_ref[own, place].astype(LOW)
        ref[1] = total_ref[1 - own, place].astype(LOW)


def output_kernel(hidden_ref, chance_ref, hits_ref, mask_ref, returned_ref, output_ref):
    gate = jnp.sum(chance_ref[...] * hits_ref[...], axis=1, keepdims=True)
    fetched = dot(mask_ref[...], joined(returned_ref))
    output_ref[...] = (hidden_ref[...] + gate * fetched).astype(LOW)


VMEM = pl.BlockSpec(memory_space=pltpu.VMEM)
ANY = pl.BlockSpec(memory_space=pl.ANY)
LIMIT = 60 * 1024 * 1024


def shaped(dtype, *shape):
    return jax.ShapeDtypeStruct(shape, dtype)


def call(kernel, name, micros, out_shape, args, pieces=(), scratch=(), more=()):
    return pl.pallas_call(
        kernel,
        out_shape=tuple(out_shape),
        in_specs=[VMEM] * len(args) + [ANY] * len(pieces) + [VMEM] * len(more),
        out_specs=(VMEM,) * len(out_shape),
        scratch_shapes=list(scratch),
        compiler_params=pltpu.CompilerParams(vmem_limit_bytes=LIMIT),
        cost_estimate=pl.CostEstimate(
            flops=0, bytes_accessed=micros * 3_600_000, transcendentals=0
        ),
        name=name,
    )(*args, *pieces, *more)


def per_device(
    tokens,
    seg_ids,
    routes,
    attn_gain,
    w_query,
    w_key,
    w_value,
    w_output,
    rel_bias,
    ffn_gain,
    w_router,
    w_in,
    w_out,
    d_out,
):
    length, model_width = tokens.shape
    bucket_count, head_count = rel_bias.shape
    experts_total = w_router.shape[1]
    local_experts, _, hidden_here = w_in.shape
    ranks, dps = lax.axis_size("expert"), lax.axis_size("dp")
    capacity = length * 5 // (4 * experts_total)
    rank_slots = local_experts * capacity
    slab = -(-(rank_slots + 1) // 8) * 8
    rows_here, columns_here = w_query.shape
    inner_width = dps * rows_here
    packed_rows = dps * ranks * capacity
    gains = jnp.stack([attn_gain, ffn_gain]).astype(FULL)
    slabs_shape = shaped(LOW, ranks, slab, model_width)
    router_t = w_router.T
    pack = packing(local_experts, ranks, capacity, slab)
    pack, pack_t = jnp.asarray(pack, LOW), jnp.asarray(pack.T, LOW)

    normed_low, hits, mask, mask_t, bias_full, up_slabs = call(
        functools.partial(early_kernel, ranks, local_experts, capacity, slab),
        "early",
        3,
        [
            shaped(LOW, length, model_width),
            shaped(FULL, length, experts_total),
            shaped(LOW, length, ranks * slab),
            shaped(LOW, ranks * slab, length),
            shaped(FULL, head_count, length, length),
            slabs_shape,
        ],
        [
            tokens,
            routes.reshape(1, length),
            gains,
            d_out,
            rel_bias.T,
            jnp.asarray(bucket_onehot(bucket_count, length), LOW),
        ],
    )

    payload = jnp.concatenate([w_query, w_key, w_value, w_output], axis=1)
    early = (normed_low, hits, mask, mask_t, bias_full)
    pieces, places, early = gather_pieces(payload, early)
    normed_low, hits, mask, mask_t, bias_full = early
    pieces, up_slabs = together(pieces, up_slabs)
    up_arrived = exchange(up_slabs).reshape(ranks * slab, model_width)

    w_shape = (ranks, inner_width, 4 * columns_here)
    heads, weights, attended, hidden, chance, slabs = call(
        functools.partial(forward_kernel, places, slab, rank_slots),
        "attention_forward",
        10,
        [
            shaped(LOW, 3, inner_width, length),
            shaped(FULL, head_count, length, length),
            shaped(LOW, length, inner_width),
            shaped(FULL, length, model_width),
            shaped(FULL, length, experts_total),
            slabs_shape,
        ],
        [tokens, normed_low, seg_ids, bias_full, gains, router_t, hits, mask_t],
        pieces,
        [
            pltpu.VMEM(w_shape, LOW),
            pltpu.VMEM((3, ranks, columns_here, length), FULL),
            pltpu.VMEM((inner_width, length), FULL),
            pltpu.SemaphoreType.DMA((ranks,)),
        ],
    )

    slabs, up_arrived = together(slabs, up_arrived)
    arrived = exchange(slabs).reshape(ranks * slab, model_width)
    up_pieces = gather_near(gather_far(up_arrived))
    arrived, up_pieces, normed_own = together(arrived, up_pieces, normed_low)
    row_far = gather_far(arrived)
    near_normed = half_ranks(normed_own)
    by_expert = (local_experts, packed_rows)
    up_rows, up_act = call(
        upstream_kernel,
        "upstream_rows",
        5,
        [shaped(LOW, *by_expert, model_width), shaped(FULL, *by_expert, hidden_here)],
        [pack, w_out, *up_pieces],
    )
    row_far, up_act, near_normed = together(row_far, up_act, near_normed)
    row_pieces = gather_near(row_far)

    *back, slot_rows, activated, pre_grad, gates = call(
        functools.partial(expert_kernel, dps, slab, rank_slots),
        "experts",
        10,
        [shaped(LOW, ranks * slab, model_width)] * dps
        + [
            shaped(LOW, *by_expert, model_width),
            shaped(LOW, *by_expert, hidden_here),
            shaped(LOW, *by_expert, hidden_here),
            shaped(FULL, *by_expert, 128),
        ],
        [pack, pack_t, w_in, up_act, *row_pieces],
        scratch=[
            pltpu.VMEM((packed_rows, hidden_here), FULL),
            pltpu.VMEM((*by_expert, model_width), LOW),
            pltpu.VMEM((*by_expert, 128), LOW),
        ],
    )
    near, attended_own = together(scatter_near(back), attended)
    kept, got = scatter_far(near)
    near_attended = half_ranks(attended_own)
    near, late_activated = together(near, activated)
    returned = call(
        expert_out_kernel,
        "expert_outputs",
        3,
        [shaped(LOW, ranks * slab, model_width)] * dps,
        [pack_t, w_out, late_activated],
        scratch=[pltpu.VMEM((*by_expert, model_width), LOW)],
    )
    got, returned, near_attended = together(got, returned, near_attended)
    back = add(kept, got).reshape(ranks, slab, model_width)
    back, returned = together(back, returned)
    back = exchange(back)
    returned = add(*scatter_terms(returned)).reshape(ranks, slab, model_width)
    back, returned = together(back, returned)
    returned = exchange(returned)

    bias_rows = -(-head_count // 6)
    small_rows = -(-(experts_total + 2 + bias_rows) // 8) * 8
    d_input, small, factors = call(
        functools.partial(backward_kernel, places, rank_slots),
        "attention_backward",
        12,
        [
            shaped(FULL, length, model_width),
            shaped(FULL, small_rows, model_width),
            shaped(LOW, ranks // 2, 2, 4 * columns_here, length),
        ],
        [
            tokens,
            gains,
            router_t,
            hits,
            mask,
            d_out,
            hidden,
            chance,
            heads,
            weights,
            jnp.asarray(bucket_onehot(bucket_count, length), FULL),
        ],
        pieces,
        [
            pltpu.VMEM(w_shape, LOW),
            pltpu.VMEM((inner_width, length), FULL),
            pltpu.VMEM((3, inner_width, length), FULL),
            pltpu.VMEM((head_count, 2 * length), FULL),
            pltpu.SemaphoreType.DMA((ranks,)),
        ],
        [back],
    )

    factors, small, returned = together(factors, small, returned)
    factors = lax.all_to_all(
        factors, "expert", split_axis=0, concat_axis=0, tiled=True, axis_index_groups=halves()
    )
    first, *steps, one_but_last, last = sum_steps()
    small = small + swap(small, *first)
    for axis, bit in steps:
        small = small + swap(small, axis, bit)
    factors, small = together(factors, small)
    small = small + swap(small, *one_but_last)
    grads = call(
        product_kernel,
        "weight_gradients",
        5,
        [shaped(LOW, 2, rows_here, 4 * columns_here)] * dps,
        [factors, *near_normed, *near_attended],
        scratch=[pltpu.VMEM((2, dps, rows_here, 4 * columns_here), FULL)],
    )
    grads, small = together(scatter_near(grads), small)
    small = small + swap(small, *last)
    (output,) = call(
        output_kernel,
        "output_rows",
        2,
        [shaped(LOW, length, model_width)],
        [hidden, chance, hits, mask, returned],
    )
    kept, got = scatter_far(grads)
    got, output = together(got, output)
    other, activated = together(add(kept[1], got[1]), activated)
    other = swap(other, "expert", ranks // 2)
    first_grad, second_grad = expert_gradients(
        [shaped(FULL, *w_in.shape), shaped(FULL, *w_out.shape)],
        [slot_rows, activated, pre_grad, gates, up_rows],
    )
    other, first_grad = together(other, first_grad)
    grads = kept[0].astype(FULL) + got[0].astype(FULL) + other.astype(FULL)
    g_query, g_key, g_value, g_output = (
        grads[:, i * columns_here : (i + 1) * columns_here] for i in range(4)
    )
    g_router = small[:experts_total].T
    g_ffn_gain, g_attn_gain = small[experts_total], small[experts_total + 1]
    g_rel_bias = small[experts_total + 2 : experts_total + 2 + bias_rows].reshape(-1, 128)
    g_rel_bias = g_rel_bias[:head_count, :bucket_count].T
    return (
        output,
        d_input,
        g_attn_gain,
        g_query,
        g_key,
        g_value,
        g_output,
        g_rel_bias,
        g_ffn_gain,
        g_router,
        first_grad,
        second_grad,
    )


def solution(mesh):
    return jax.shard_map(
        per_device,
        mesh=mesh,
        in_specs=(
            P(("dp", "expert"), None),
            P(("dp", "expert"), None),
            P(("dp", "expert"), None),
            P(),
            P("dp", "expert"),
            P("dp", "expert"),
            P("dp", "expert"),
            P("dp", "expert"),
            P(),
            P(),
            P(),
            P("expert", None, "dp"),
            P("expert", "dp", None),
            P(("dp", "expert"), None),
        ),
        out_specs=(
            P(("dp", "expert"), None),
            P(("dp", "expert"), None),
            P(),
            P("dp", "expert"),
            P("dp", "expert"),
            P("dp", "expert"),
            P("dp", "expert"),
            P(),
            P(),
            P(),
            P("expert", None, "dp"),
            P("expert", "dp", None),
        ),
        check_vma=False,
    )
```

```python
import functools

import jax
import jax.numpy as jnp
import numpy as np
from jax import lax
from jax.experimental import pallas as pl
from jax.experimental.pallas import tpu as pltpu
from jax.sharding import PartitionSpec as P

EPSILON = 1e-06
LIMITS = (12, 16, 23, 32, 46, 64, 91)
MASKED = -1000000000.0
HIGHEST = lax.Precision.HIGHEST
LOW = jnp.bfloat16
FULL = jnp.float32


def bucket_onehot(buckets, length):
    delta = np.arange(2 * length) - length
    magnitude = np.abs(delta)
    distant = 8 + sum((magnitude >= threshold).astype(np.int32) for threshold in LIMITS)
    ids = np.where(delta > 0, 16, 0) + np.where(magnitude < 8, magnitude, distant)
    return (ids[None, :] == np.arange(buckets)[:, None]).astype(np.float32)


def packing(local_experts, ranks, capacity, slab):
    table = np.zeros((local_experts, ranks, capacity, ranks, slab), np.float32)
    for e in range(local_experts):
        for r in range(ranks):
            for c in range(capacity):
                table[e, r, c, r, e * capacity + c] = 1.0
    return table.reshape(local_experts * ranks * capacity, ranks * slab)


def normalize(matrix, gain_vec):
    scale = lax.rsqrt(jnp.mean(matrix * matrix, axis=-1, keepdims=True) + EPSILON)
    return (matrix * scale * gain_vec, scale)


def norm_back(matrix, scale, gain_vec, incoming):
    weighted = incoming * gain_vec
    average = jnp.mean(matrix * weighted, axis=-1, keepdims=True)
    return (
        scale * weighted - matrix * (scale * scale * scale) * average,
        jnp.sum(incoming * matrix * scale, axis=0, keepdims=True),
    )


def swap(value, axis, mask):
    count = lax.axis_size(axis)
    return lax.ppermute(value, axis, [(i, i ^ mask) for i in range(count)])


def gather_bits(value, axis, masks):
    return jnp.concatenate([value] + [swap(value, axis, mask) for mask in masks], axis=0)


def exchange(value):
    return lax.all_to_all(value, "expert", split_axis=0, concat_axis=0, tiled=True)


def half_ranks(value):
    return [value] + [swap(value, "expert", j) for j in range(1, lax.axis_size("expert") // 2)]


def halves():
    half = lax.axis_size("expert") // 2
    return [list(range(half)), list(range(half, 2 * half))]


def gather_far(value):
    found = {0: value}
    bit = lax.axis_size("dp") // 2
    while bit > 1:
        found.update({index ^ bit: swap(item, "dp", bit) for index, item in found.items()})
        bit = bit // 2
    return found


def gather_near(found):
    found = {**found, **{index ^ 1: swap(item, "dp", 1) for index, item in found.items()}}
    return [found[index] for index in range(len(found))]


def add(left, right, dtype=LOW):
    return (left.astype(FULL) + right.astype(FULL)).astype(dtype)


def scatter_near(items):
    taken = [swap(item, "dp", 1) for item in items[1::2]]
    return [add(kept, got) for kept, got in zip(items[0::2], taken)]


def scatter_far(items):
    bit = 2
    while len(items) > 2:
        taken = [swap(item, "dp", bit) for item in items[1::2]]
        items = [add(kept, got) for kept, got in zip(items[0::2], taken)]
        bit = bit * 2
    return items[0], swap(items[1], "dp", bit)


def scatter_terms(items):
    return scatter_far(scatter_near(items))


def sum_steps():
    steps = []
    for axis in ("dp", "expert"):
        bit = 1
        while bit < lax.axis_size(axis):
            steps.append((axis, bit))
            bit = bit * 2
    return steps


def together(*values):
    return lax.optimization_barrier(values)


def gather_pieces(payload, early):
    ranks, dps = lax.axis_size("expert"), lax.axis_size("dp")
    half = payload.shape[0] // 2
    far = list(range(0, ranks, 2))
    sides = {"x": ("expert", [0, 1]), "y": ("dp", list(range(0, dps, 2)))}
    value, early = together(gather_bits(payload[None], "expert", far[1:]), early)
    values = (value[:, :half], value[:, half:])
    firsts = []
    for value, letter in zip(values, "xy"):
        axis, masks = sides[letter]
        firsts.append(gather_bits(value[None], axis, masks[1:]))
    seconds = []
    for value, letter in zip(firsts, "yx"):
        axis, masks = sides[letter]
        seconds.append([swap(value, axis, mask) for mask in masks[1:]])
    others = [swap(value, "dp", 1) for value in firsts]
    pieces, places = [], []
    for index, order in enumerate(("xy", "yx")):
        masks, other_masks = sides[order[0]][1], sides[order[1]][1]
        found = [(firsts[index], 0, 0), (others[index], 0, 1)]
        for value, mask in zip(seconds[index], other_masks[1:]):
            found += [(value, mask, 0), (swap(value, "dp", 1), mask, 1)]
        for piece, mask, core in found:
            offsets = []
            for first in masks:
                for low in far:
                    x_mask, y_mask = (first, mask) if order == "xy" else (mask, first)
                    offsets.append((low ^ x_mask, y_mask ^ core))
            pieces.append(piece)
            places.append((index, offsets))
    return pieces, places, early


def place_weights(places, piece_refs, w_ref, sem):
    my_expert, my_dp = lax.axis_index("expert"), lax.axis_index("dp")
    copies, masks = [], []
    for ref, (half, offsets) in zip(piece_refs, places):
        low_count, rows = ref.shape[1], ref.shape[2]
        for index, (e_mask, d_mask) in enumerate(offsets):
            start = (my_dp ^ d_mask) * (2 * rows) + half * rows
            copies.append(
                pltpu.make_async_copy(
                    ref.at[index // low_count, index % low_count],
                    w_ref.at[my_expert ^ e_mask, pl.ds(pl.multiple_of(start, 16), rows), :],
                    sem.at[e_mask],
                )
            )
            masks.append(e_mask)
    groups = [[] for _ in range(w_ref.shape[0])]
    for copy, e_mask in zip(copies, masks):
        groups[e_mask].append(copy)
    for group in groups:
        for copy in group:
            copy.start()
    return groups


def dot(left, right, dims=((1,), (0,)), precision=None):
    return lax.dot_general(
        left, right, (dims, ((), ())), precision=precision, preferred_element_type=FULL
    )


NT = ((1,), (1,))
TN = ((0,), (0,))


def grid_of(rows):
    sub = lax.broadcasted_iota(jnp.int32, (rows, 128), 0)
    lane = lax.broadcasted_iota(jnp.int32, (rows, 128), 1)
    return sub, lane


def row_to_column(row, rows, shift=0):
    sub, lane = grid_of(rows)
    column = jnp.sum(jnp.where(lane == sub + shift, row, 0.0), axis=1, keepdims=True)
    return jnp.broadcast_to(column, (rows, 128))


def column_to_row(column, shift=0):
    sub, lane = grid_of(column.shape[0])
    return jnp.sum(jnp.where(lane == sub + shift, column, 0.0), axis=0, keepdims=True)


def turn(value, shift):
    return pltpu.roll(value, shift % value.shape[1], 1)


def slide(value, direction):
    sub = lax.broadcasted_iota(jnp.int32, value.shape, 0)
    for bit in (1, 2, 4):
        value = jnp.where((sub & bit) != 0, turn(value, direction * bit), value)
    return value


def slid_rows(row, count):
    value = slide(jnp.broadcast_to(row, (8, row.shape[1])), 1)
    while value.shape[0] < count:
        value = jnp.concatenate([value, turn(value, value.shape[0])], axis=0)
    return value


def slid_sum(value):
    while value.shape[0] > 8:
        half = value.shape[0] // 2
        value = value[:half] + turn(value[half:], -half)
    return jnp.sum(slide(value, -1), axis=0, keepdims=True)


def early_kernel(
    ranks, local_experts, capacity, slab, tokens_ref, routes_ref, gain_ref, d_out_ref, table_ref,
    onehot_ref, normed_ref, hits_ref, mask_ref, mask_t_ref, bias_ref, up_ref
):
    length = tokens_ref.shape[0]
    normed, _ = normalize(tokens_ref[...].astype(FULL), gain_ref[0:1, :])
    normed_ref[...] = normed.astype(LOW)
    experts = hits_ref.shape[1]
    routes = jnp.broadcast_to(routes_ref[...].astype(FULL), (length, length)).T
    route = routes[:, :1].astype(jnp.int32)
    lanes = lax.broadcasted_iota(jnp.int32, (length, experts), 1)
    hits = (lanes == route).astype(FULL)
    hits_ref[...] = hits
    row = lax.broadcasted_iota(jnp.int32, (length, length), 0)
    col = lax.broadcasted_iota(jnp.int32, (length, length), 1)
    before = dot((col < row).astype(FULL).astype(LOW), hits.astype(LOW))
    placed = jnp.sum(before * hits, axis=1, keepdims=True).astype(jnp.int32)
    rank = jnp.zeros_like(route)
    for r in range(1, ranks):
        rank = rank + (route >= r * local_experts).astype(jnp.int32)
    spot = rank * slab + (route - rank * local_experts) * capacity + placed
    spot = jnp.where(placed < capacity, spot, -1)
    places = lax.broadcasted_iota(jnp.int32, (length, ranks * slab), 1)
    mask = (places == spot).astype(FULL)
    mask_ref[...] = mask.astype(LOW)
    mask_t = mask.T.astype(LOW)
    mask_t_ref[...] = mask_t
    slabs = dot(mask_t, d_out_ref[...])
    for r in range(ranks):
        up_ref[r] = slabs[r * slab : (r + 1) * slab].astype(LOW)
    values = dot(table_ref[...], onehot_ref[...])
    for h in range(bias_ref.shape[0]):
        bias_ref[h] = slid_rows(values[h : h + 1], length)[:, length:]


def forward_kernel(
    places, slab, rank_slots, tokens_ref, normed_ref, seg_ref, bias_ref, gain_ref,
    router_t_ref, hits_ref, mask_t_ref, *rest
):
    count = len(places)
    piece_refs, rest = rest[:count], rest[count:]
    heads_ref, weights_ref, rows_ref, hidden_ref, chance_ref = rest[:5]
    slabs_ref = rest[5]
    w_ref, qkv_ref, att_t_ref, sem = rest[-4:]
    copies = place_weights(places, piece_refs, w_ref, sem)
    ranks, width, columns = w_ref.shape
    cols = columns // 4
    head_count = weights_ref.shape[0]
    head = width // head_count
    length = tokens_ref.shape[0]
    segments = jnp.broadcast_to(seg_ref[...].astype(FULL), (length, length))
    same_doc = segments == segments.T
    normed = normed_ref[...]
    for j, group in enumerate(copies):
        for copy in group:
            copy.wait()
        e = lax.axis_index("expert") ^ j
        turned = dot(normed, w_ref[e]).T
        for m in range(3):
            qkv_ref[m, e] = turned[m * cols : (m + 1) * cols]
    heads_ref[...] = qkv_ref[...].reshape(3, width, length).astype(LOW)
    for h in range(head_count):
        rows = slice(h * head, (h + 1) * head)
        scores = dot(heads_ref[0, rows, :], heads_ref[1, rows, :], TN) * head ** (-0.5)
        scores = jnp.where(same_doc, scores + bias_ref[h], MASKED)
        grown = jnp.exp(scores - jnp.max(scores, axis=1, keepdims=True))
        weights = grown / jnp.sum(grown, axis=1, keepdims=True)
        weights_ref[h] = weights
        att_t_ref[rows, :] = dot(heads_ref[2, rows, :], weights.astype(LOW), NT)
    attended = att_t_ref[...].T.astype(LOW)
    rows_ref[...] = attended
    low_lane = 3 * cols // 128 * 128
    for e in range(ranks):
        turned = dot(attended, w_ref[e, :, low_lane:]).T
        att_t_ref[e * cols : (e + 1) * cols, :] = turned[3 * cols - low_lane :]
    hidden = tokens_ref[...].astype(FULL) + att_t_ref[...].T
    hidden_ref[...] = hidden
    normed_two, _ = normalize(hidden, gain_ref[1:2, :])
    logits = dot(normed_two, router_t_ref[...].astype(FULL), NT, HIGHEST)
    grown = jnp.exp(logits - jnp.max(logits, axis=1, keepdims=True))
    chance = grown / jnp.sum(grown, axis=1, keepdims=True)
    chance_ref[...] = chance
    gate = jnp.sum(chance * hits_ref[...], axis=1, keepdims=True)
    mask_t = mask_t_ref[...]
    slots = dot(mask_t, normed_two.astype(LOW))
    gates = dot(mask_t.astype(FULL), jnp.broadcast_to(gate, (length, 128)), precision=HIGHEST)
    sub, _ = grid_of(slab)
    for r in range(ranks):
        mine = gates[r * slab : (r + 1) * slab]
        high = mine.astype(LOW).astype(FULL)
        row = column_to_row(high) + column_to_row(mine - high, 64)
        rows = slots[r * slab : (r + 1) * slab]
        start = rows[:, :128] + jnp.where(sub == rank_slots, row, 0.0)
        slabs_ref[r, :, :128] = start.astype(LOW)
        slabs_ref[r, :, 128:] = rows[:, 128:].astype(LOW)


def upstream_kernel(pack_ref, w_out_ref, *rest):
    piece_refs, (rows_ref, act_ref) = rest[:-2], rest[-2:]
    local_experts = w_out_ref.shape[0]
    chunk = pack_ref.shape[0] // local_experts
    for p, piece in enumerate(piece_refs):
        packed = dot(pack_ref[...], piece[...]).astype(LOW)
        for e in range(local_experts):
            rows_ref[e, p * chunk : (p + 1) * chunk, :] = packed[e * chunk : (e + 1) * chunk]
    for e in range(local_experts):
        act_ref[e] = dot(rows_ref[e], w_out_ref[e], NT)


def unpack(pack_t, rows_ref, p, chunk):
    rows = [rows_ref[e, p * chunk : (p + 1) * chunk, :] for e in range(rows_ref.shape[0])]
    return dot(pack_t, jnp.concatenate(rows, axis=0))


def expert_kernel(
    count, slab, rank_slots, pack_ref, pack_t_ref, w_in_ref, up_act_ref, *rest
):
    piece_refs, rest = rest[:count], rest[count:]
    back_refs, rest = rest[:count], rest[count:]
    rows_ref, act_ref, pre_grad_ref, gates_ref, pre_ref, back_ref, part_ref = rest
    local_experts = w_in_ref.shape[0]
    chunk = pack_ref.shape[0] // local_experts
    ranks = pack_ref.shape[1] // slab
    pack, pack_t = pack_ref[...], pack_t_ref[...]
    for p, piece in enumerate(piece_refs):
        packed = dot(pack, piece[...]).astype(LOW)
        tile = piece[:, :128].astype(FULL)
        spread = []
        for shift in (0, 64):
            columns = [
                row_to_column(tile[r * slab + rank_slots : r * slab + rank_slots + 1], slab, shift)
                for r in range(ranks)
            ]
            spread.append(dot(pack, jnp.concatenate(columns, axis=0).astype(LOW)))
        gates = spread[0] + spread[1]
        for e in range(local_experts):
            rows_ref[e, p * chunk : (p + 1) * chunk, :] = packed[e * chunk : (e + 1) * chunk]
            gates_ref[e, p * chunk : (p + 1) * chunk, :] = gates[e * chunk : (e + 1) * chunk]
    root = np.float32(np.sqrt(2.0 / np.pi))
    step = 16
    for e in range(local_experts):
        pre_ref[...] = dot(rows_ref[e], w_in_ref[e])

        def body(index, carry):
            span = pl.ds(pl.multiple_of(index * step, step), step)
            pre = pre_ref[span, :]
            up = up_act_ref[e, span, :]
            square = pre * pre
            curve = jnp.tanh(root * pre * (1.0 + 0.044715 * square))
            rise = 0.5 + 0.5 * curve
            act = (pre * rise).astype(LOW)
            act_ref[e, span, :] = act
            slope = rise + pre * (rise * (1.0 - curve)) * (root + 3 * 0.044715 * root * square)
            gate = gates_ref[e, span, :][:, :1]
            pre_grad_ref[e, span, :] = (slope * (up * gate)).astype(LOW)
            part = jnp.sum(act.astype(FULL) * up, axis=1, keepdims=True)
            part_ref[e, span, :] = jnp.broadcast_to(part, (step, 128)).astype(LOW)
            return carry

        lax.fori_loop(0, pre_ref.shape[0] // step, body, 0, unroll=2)
        back_ref[e] = dot(pre_grad_ref[e], w_in_ref[e], NT).astype(LOW)
    sub, _ = grid_of(slab)
    for p in range(count):
        rows = unpack(pack_t, back_ref, p, chunk)
        parts = unpack(pack_t, part_ref, p, chunk)
        pieces = []
        for r in range(ranks):
            span = slice(r * slab, (r + 1) * slab)
            row = column_to_row(parts[span])
            pieces.append(rows[span, :128] + jnp.where(sub == rank_slots, row, 0.0))
        back_refs[p][:, :128] = jnp.concatenate(pieces, axis=0).astype(LOW)
        back_refs[p][:, 128:] = rows[:, 128:].astype(LOW)


def expert_out_kernel(pack_t_ref, w_out_ref, act_ref, *rest):
    out_refs, returned_ref = rest[:-1], rest[-1]
    chunk = act_ref.shape[1] // len(out_refs)
    for e in range(w_out_ref.shape[0]):
        returned_ref[e] = dot(act_ref[e], w_out_ref[e]).astype(LOW)
    for p, ref in enumerate(out_refs):
        ref[...] = unpack(pack_t_ref[...], returned_ref, p, chunk).astype(LOW)


def expert_grad_kernel(
    rows_ref, act_ref, pre_grad_ref, gates_ref, up_rows_ref, g_in_ref, g_out_ref
):
    g_in_ref[0] = dot(rows_ref[0], pre_grad_ref[0], TN)
    slot_grad = (up_rows_ref[0].astype(FULL) * gates_ref[0][:, :1]).astype(LOW)
    g_out_ref[0] = dot(act_ref[0], slot_grad, TN)


def expert_gradients(shapes, args):
    def block(item):
        return pl.BlockSpec((1,) + item.shape[1:], lambda e: (e, 0, 0))

    return pl.pallas_call(
        expert_grad_kernel,
        grid=(shapes[0].shape[0],),
        out_shape=tuple(shapes),
        in_specs=[block(item) for item in args],
        out_specs=tuple(block(item) for item in shapes),
        compiler_params=pltpu.CompilerParams(vmem_limit_bytes=LIMIT),
        cost_estimate=pl.CostEstimate(flops=0, bytes_accessed=28_800_000, transcendentals=0),
        name="expert_gradients",
    )(*args)


def joined(ref):
    ranks, slab, width = ref.shape
    return ref[...].astype(FULL).reshape(ranks * slab, width).astype(LOW)


def backward_kernel(
    places, rank_slots, tokens_ref, gain_ref, router_t_ref, hits_ref, mask_ref,
    up_ref, hidden_ref, chance_ref, heads_ref, weights_ref, onehot_ref, *rest
):
    count = len(places)
    piece_refs, rest = rest[:count], rest[count:]
    (back_ref, d_input_ref, small_ref, factors_ref,
     w_ref, turned_ref, grads_ref, bias_ref, sem) = rest
    ranks, width, columns = w_ref.shape
    copies = place_weights(places, piece_refs, w_ref, sem)
    cols = columns // 4
    head_count = weights_ref.shape[0]
    head = width // head_count
    factor = head ** (-0.5)
    length = tokens_ref.shape[0]
    slab = back_ref.shape[1]
    hidden = hidden_ref[...]
    gain_two = gain_ref[1:2, :]
    normed_two, scale_two = normalize(hidden, gain_two)
    mask = mask_ref[...]
    chance, hits = chance_ref[...], hits_ref[...]
    gate = jnp.sum(chance * hits, axis=1, keepdims=True)
    spread = [
        row_to_column(back_ref[r, :, :128].astype(FULL)[rank_slots : rank_slots + 1], slab)
        for r in range(ranks)
    ]
    gate_grad = dot(mask, jnp.concatenate(spread, axis=0).astype(LOW))[:, :1]
    logit_grad = chance * (hits - gate) * gate_grad
    experts = hits.shape[1]
    small_ref[:experts, :] = dot(logit_grad, normed_two, TN, HIGHEST)
    router_t = router_t_ref[...].astype(FULL)
    normed_two_grad = dot(logit_grad, router_t, precision=HIGHEST) + dot(mask, joined(back_ref))
    hidden_part, ffn_gain_grad = norm_back(hidden, scale_two, gain_two, normed_two_grad)
    hidden_grad = up_ref[...].astype(FULL) + hidden_part
    turned_ref[...] = hidden_grad.astype(LOW).astype(FULL).T
    for group in copies:
        for copy in group:
            copy.wait()
    low_lane = 3 * cols // 128 * 128
    att_grad = None
    for e in range(ranks):
        own = turned_ref[e * cols : (e + 1) * cols, :]
        if 3 * cols > low_lane:
            own = jnp.concatenate([jnp.zeros((3 * cols - low_lane, 128), FULL), own], axis=0)
        part = dot(w_ref[e, :, low_lane:], own.astype(LOW))
        att_grad = part if att_grad is None else att_grad + part
    att_grad = att_grad.astype(LOW)
    for h in range(head_count):
        rows = slice(h * head, (h + 1) * head)
        own = att_grad[rows]
        weights = weights_ref[h]
        grads_ref[2, rows, :] = dot(own, weights.astype(LOW))
        prob_grad = dot(own, heads_ref[2, rows, :], TN)
        score_grad = weights * (prob_grad - jnp.sum(prob_grad * weights, axis=1, keepdims=True))
        score_grad = score_grad.astype(LOW)
        grads_ref[0, rows, :] = dot(heads_ref[1, rows, :], score_grad, NT) * factor
        grads_ref[1, rows, :] = dot(heads_ref[0, rows, :], score_grad) * factor
        wide = [jnp.zeros((length, length), FULL), score_grad.astype(FULL)]
        bias_ref[h : h + 1, :] = slid_sum(jnp.concatenate(wide, axis=1))
    total = None
    for e in range(ranks):
        span = slice(e * cols, (e + 1) * cols)
        held = [grads_ref[m, span, :] for m in range(3)] + [jnp.zeros((cols, 128), FULL)]
        part = dot(w_ref[e], jnp.concatenate(held, axis=0).astype(LOW))
        total = part if total is None else total + part
        sent = [grads_ref[m, span, :] for m in range(3)] + [turned_ref[span, :]]
        sent = jnp.concatenate(sent, axis=0).astype(LOW)
        factors_ref[e % (ranks // 2), e // (ranks // 2)] = sent
    inputs = tokens_ref[...].astype(FULL)
    gain_one = gain_ref[0:1, :]
    _, scale_one = normalize(inputs, gain_one)
    norm_part, attn_gain_grad = norm_back(inputs, scale_one, gain_one, total.T)
    d_input_ref[...] = hidden_grad + norm_part
    sums = dot(bias_ref[...], onehot_ref[...], NT, HIGHEST)
    small_ref[experts : experts + 1, :] = ffn_gain_grad
    small_ref[experts + 1 : experts + 2, :] = attn_gain_grad
    small_ref[experts + 2 :, :] = jnp.zeros((small_ref.shape[0] - experts - 2, width), FULL)
    for h in range(head_count):
        line, place = experts + 2 + h // 6, 128 * (h % 6)
        small_ref[line : line + 1, place : place + sums.shape[1]] = sums[h : h + 1]


def product_kernel(factors_ref, *rest):
    count, _, columns, length = factors_ref.shape
    normed_refs, attended_refs = rest[:count], rest[count : 2 * count]
    piece_refs, total_ref = rest[2 * count : -1], rest[-1]
    cols = columns // 4
    rows = total_ref.shape[2]
    mine = lax.rem(lax.axis_index("expert"), count)
    for side in range(2):
        first, second = None, None
        for j in range(count):
            held = factors_ref[mine ^ j, side].astype(FULL)
            part = dot(held[: 3 * cols].astype(LOW), normed_refs[j][...])
            first = part if first is None else first + part
            part = dot(held[3 * cols :].astype(LOW), attended_refs[j][...])
            second = part if second is None else second + part
        total = jnp.concatenate([first, second], axis=0).T
        for j in range(len(piece_refs)):
            total_ref[side, j] = total[j * rows : (j + 1) * rows]
    own = (lax.axis_index("expert") >= count).astype(jnp.int32)
    for j, ref in enumerate(piece_refs):
        place = lax.axis_index("dp") ^ j
        ref[0] = total_ref[own, place].astype(LOW)
        ref[1] = total_ref[1 - own, place].astype(LOW)


def output_kernel(hidden_ref, chance_ref, hits_ref, mask_ref, returned_ref, output_ref):
    gate = jnp.sum(chance_ref[...] * hits_ref[...], axis=1, keepdims=True)
    fetched = dot(mask_ref[...], joined(returned_ref))
    output_ref[...] = (hidden_ref[...] + gate * fetched).astype(LOW)


VMEM = pl.BlockSpec(memory_space=pltpu.VMEM)
ANY = pl.BlockSpec(memory_space=pl.ANY)
LIMIT = 60 * 1024 * 1024


def shaped(dtype, *shape):
    return jax.ShapeDtypeStruct(shape, dtype)


def call(kernel, name, micros, out_shape, args, pieces=(), scratch=(), more=()):
    return pl.pallas_call(
        kernel,
        out_shape=tuple(out_shape),
        in_specs=[VMEM] * len(args) + [ANY] * len(pieces) + [VMEM] * len(more),
        out_specs=(VMEM,) * len(out_shape),
        scratch_shapes=list(scratch),
        compiler_params=pltpu.CompilerParams(vmem_limit_bytes=LIMIT),
        cost_estimate=pl.CostEstimate(
            flops=0, bytes_accessed=micros * 3_600_000, transcendentals=0
        ),
        name=name,
    )(*args, *pieces, *more)


def per_device(
    tokens,
    seg_ids,
    routes,
    attn_gain,
    w_query,
    w_key,
    w_value,
    w_output,
    rel_bias,
    ffn_gain,
    w_router,
    w_in,
    w_out,
    d_out,
):
    length, model_width = tokens.shape
    bucket_count, head_count = rel_bias.shape
    experts_total = w_router.shape[1]
    local_experts, _, hidden_here = w_in.shape
    ranks, dps = lax.axis_size("expert"), lax.axis_size("dp")
    capacity = length * 5 // (4 * experts_total)
    rank_slots = local_experts * capacity
    slab = -(-(rank_slots + 1) // 8) * 8
    rows_here, columns_here = w_query.shape
    inner_width = dps * rows_here
    packed_rows = dps * ranks * capacity
    gains = jnp.stack([attn_gain, ffn_gain]).astype(FULL)
    slabs_shape = shaped(LOW, ranks, slab, model_width)
    router_t = w_router.T
    pack = packing(local_experts, ranks, capacity, slab)
    pack, pack_t = jnp.asarray(pack, LOW), jnp.asarray(pack.T, LOW)

    normed_low, hits, mask, mask_t, bias_full, up_slabs = call(
        functools.partial(early_kernel, ranks, local_experts, capacity, slab),
        "early",
        3,
        [
            shaped(LOW, length, model_width),
            shaped(FULL, length, experts_total),
            shaped(LOW, length, ranks * slab),
            shaped(LOW, ranks * slab, length),
            shaped(FULL, head_count, length, length),
            slabs_shape,
        ],
        [
            tokens,
            routes.reshape(1, length),
            gains,
            d_out,
            rel_bias.T,
            jnp.asarray(bucket_onehot(bucket_count, length), LOW),
        ],
    )

    payload = jnp.concatenate([w_query, w_key, w_value, w_output], axis=1)
    early = (normed_low, hits, mask, mask_t, bias_full)
    pieces, places, early = gather_pieces(payload, early)
    normed_low, hits, mask, mask_t, bias_full = early
    pieces, up_slabs = together(pieces, up_slabs)
    up_arrived = exchange(up_slabs).reshape(ranks * slab, model_width)

    w_shape = (ranks, inner_width, 4 * columns_here)
    heads, weights, attended, hidden, chance, slabs = call(
        functools.partial(forward_kernel, places, slab, rank_slots),
        "attention_forward",
        10,
        [
            shaped(LOW, 3, inner_width, length),
            shaped(FULL, head_count, length, length),
            shaped(LOW, length, inner_width),
            shaped(FULL, length, model_width),
            shaped(FULL, length, experts_total),
            slabs_shape,
        ],
        [tokens, normed_low, seg_ids, bias_full, gains, router_t, hits, mask_t],
        pieces,
        [
            pltpu.VMEM(w_shape, LOW),
            pltpu.VMEM((3, ranks, columns_here, length), FULL),
            pltpu.VMEM((inner_width, length), FULL),
            pltpu.SemaphoreType.DMA((ranks,)),
        ],
    )

    slabs, up_arrived = together(slabs, up_arrived)
    arrived = exchange(slabs).reshape(ranks * slab, model_width)
    up_pieces = gather_near(gather_far(up_arrived))
    by_expert = (local_experts, packed_rows)
    up_rows, up_act = call(
        upstream_kernel,
        "upstream_rows",
        1,
        [shaped(LOW, *by_expert, model_width), shaped(FULL, *by_expert, hidden_here)],
        [pack, w_out, *up_pieces],
    )
    arrived, up_act, attended_own = together(arrived, up_act, attended)
    row_far = gather_far(arrived)
    row_far, near_attended = together(row_far, half_ranks(attended_own))
    row_pieces = gather_near(row_far)

    *back, slot_rows, activated, pre_grad, gates = call(
        functools.partial(expert_kernel, dps, slab, rank_slots),
        "experts",
        10,
        [shaped(LOW, ranks * slab, model_width)] * dps
        + [
            shaped(LOW, *by_expert, model_width),
            shaped(LOW, *by_expert, hidden_here),
            shaped(LOW, *by_expert, hidden_here),
            shaped(FULL, *by_expert, 128),
        ],
        [pack, pack_t, w_in, up_act, *row_pieces],
        scratch=[
            pltpu.VMEM((packed_rows, hidden_here), FULL),
            pltpu.VMEM((*by_expert, model_width), LOW),
            pltpu.VMEM((*by_expert, 128), LOW),
        ],
    )
    near, late_activated = together(scatter_near(back), activated)
    kept, got = scatter_far(near)
    returned = call(
        expert_out_kernel,
        "expert_outputs",
        3,
        [shaped(LOW, ranks * slab, model_width)] * dps,
        [pack_t, w_out, late_activated],
        scratch=[pltpu.VMEM((*by_expert, model_width), LOW)],
    )
    got, returned = together(got, returned)
    back = add(kept, got).reshape(ranks, slab, model_width)
    back, returned = together(back, returned)
    back = exchange(back)
    returned = add(*scatter_terms(returned)).reshape(ranks, slab, model_width)
    back, returned, normed_own = together(back, returned, normed_low)
    returned = exchange(returned)
    near_normed = half_ranks(normed_own)

    bias_rows = -(-head_count // 6)
    small_rows = -(-(experts_total + 2 + bias_rows) // 8) * 8
    d_input, small, factors = call(
        functools.partial(backward_kernel, places, rank_slots),
        "attention_backward",
        12,
        [
            shaped(FULL, length, model_width),
            shaped(FULL, small_rows, model_width),
            shaped(LOW, ranks // 2, 2, 4 * columns_here, length),
        ],
        [
            tokens,
            gains,
            router_t,
            hits,
            mask,
            d_out,
            hidden,
            chance,
            heads,
            weights,
            jnp.asarray(bucket_onehot(bucket_count, length), FULL),
        ],
        pieces,
        [
            pltpu.VMEM(w_shape, LOW),
            pltpu.VMEM((inner_width, length), FULL),
            pltpu.VMEM((3, inner_width, length), FULL),
            pltpu.VMEM((head_count, 2 * length), FULL),
            pltpu.SemaphoreType.DMA((ranks,)),
        ],
        [back],
    )

    factors, small, returned, near_normed = together(factors, small, returned, near_normed)
    factors = lax.all_to_all(
        factors, "expert", split_axis=0, concat_axis=0, tiled=True, axis_index_groups=halves()
    )
    first, *steps, one_but_last, last = sum_steps()
    small = small + swap(small, *first)
    for axis, bit in steps:
        small = small + swap(small, axis, bit)
    factors, small = together(factors, small)
    small = small + swap(small, *one_but_last)
    grads = call(
        product_kernel,
        "weight_gradients",
        5,
        [shaped(LOW, 2, rows_here, 4 * columns_here)] * dps,
        [factors, *near_normed, *near_attended],
        scratch=[pltpu.VMEM((2, dps, rows_here, 4 * columns_here), FULL)],
    )
    grads, small = together(scatter_near(grads), small)
    small = small + swap(small, *last)
    (output,) = call(
        output_kernel,
        "output_rows",
        2,
        [shaped(LOW, length, model_width)],
        [hidden, chance, hits, mask, returned],
    )
    kept, got = scatter_far(grads)
    got, output = together(got, output)
    other, activated = together(add(kept[1], got[1]), activated)
    other = swap(other, "expert", ranks // 2)
    first_grad, second_grad = expert_gradients(
        [shaped(FULL, *w_in.shape), shaped(FULL, *w_out.shape)],
        [slot_rows, activated, pre_grad, gates, up_rows],
    )
    other, first_grad = together(other, first_grad)
    grads = kept[0].astype(FULL) + got[0].astype(FULL) + other.astype(FULL)
    g_query, g_key, g_value, g_output = (
        grads[:, i * columns_here : (i + 1) * columns_here] for i in range(4)
    )
    g_router = small[:experts_total].T
    g_ffn_gain, g_attn_gain = small[experts_total], small[experts_total + 1]
    g_rel_bias = small[experts_total + 2 : experts_total + 2 + bias_rows].reshape(-1, 128)
    g_rel_bias = g_rel_bias[:head_count, :bucket_count].T
    return (
        output,
        d_input,
        g_attn_gain,
        g_query,
        g_key,
        g_value,
        g_output,
        g_rel_bias,
        g_ffn_gain,
        g_router,
        first_grad,
        second_grad,
    )


def solution(mesh):
    return jax.shard_map(
        per_device,
        mesh=mesh,
        in_specs=(
            P(("dp", "expert"), None),
            P(("dp", "expert"), None),
            P(("dp", "expert"), None),
            P(),
            P("dp", "expert"),
            P("dp", "expert"),
            P("dp", "expert"),
            P("dp", "expert"),
            P(),
            P(),
            P(),
            P("expert", None, "dp"),
            P("expert", "dp", None),
            P(("dp", "expert"), None),
        ),
        out_specs=(
            P(("dp", "expert"), None),
            P(("dp", "expert"), None),
            P(),
            P("dp", "expert"),
            P("dp", "expert"),
            P("dp", "expert"),
            P("dp", "expert"),
            P(),
            P(),
            P(),
            P("expert", None, "dp"),
            P("expert", "dp", None),
        ),
        check_vma=False,
    )
```

```python
import functools

import jax
import jax.numpy as jnp
import numpy as np
from jax import lax
from jax.experimental import pallas as pl
from jax.experimental.pallas import tpu as pltpu
from jax.sharding import PartitionSpec as P

EPSILON = 1e-06
LIMITS = (12, 16, 23, 32, 46, 64, 91)
MASKED = -1000000000.0
HIGHEST = lax.Precision.HIGHEST
LOW = jnp.bfloat16
FULL = jnp.float32


def bucket_onehot(buckets, length):
    delta = np.arange(2 * length) - length
    magnitude = np.abs(delta)
    distant = 8 + sum((magnitude >= threshold).astype(np.int32) for threshold in LIMITS)
    ids = np.where(delta > 0, 16, 0) + np.where(magnitude < 8, magnitude, distant)
    return (ids[None, :] == np.arange(buckets)[:, None]).astype(np.float32)


def packing(local_experts, ranks, capacity, slab):
    table = np.zeros((local_experts, ranks, capacity, ranks, slab), np.float32)
    for e in range(local_experts):
        for r in range(ranks):
            for c in range(capacity):
                table[e, r, c, r, e * capacity + c] = 1.0
    return table.reshape(local_experts * ranks * capacity, ranks * slab)


def normalize(matrix, gain_vec):
    scale = lax.rsqrt(jnp.mean(matrix * matrix, axis=-1, keepdims=True) + EPSILON)
    return (matrix * scale * gain_vec, scale)


def norm_back(matrix, scale, gain_vec, incoming):
    weighted = incoming * gain_vec
    average = jnp.mean(matrix * weighted, axis=-1, keepdims=True)
    return (
        scale * weighted - matrix * (scale * scale * scale) * average,
        jnp.sum(incoming * matrix * scale, axis=0, keepdims=True),
    )


def swap(value, axis, mask):
    count = lax.axis_size(axis)
    return lax.ppermute(value, axis, [(i, i ^ mask) for i in range(count)])


def gather_bits(value, axis, masks):
    return jnp.concatenate([value] + [swap(value, axis, mask) for mask in masks], axis=0)


def exchange(value):
    return lax.all_to_all(value, "expert", split_axis=0, concat_axis=0, tiled=True)


def half_ranks(value):
    return [value] + [swap(value, "expert", j) for j in range(1, lax.axis_size("expert") // 2)]


def halves():
    half = lax.axis_size("expert") // 2
    return [list(range(half)), list(range(half, 2 * half))]


def gather_far(value):
    found = {0: value}
    bit = lax.axis_size("dp") // 2
    while bit > 1:
        found.update({index ^ bit: swap(item, "dp", bit) for index, item in found.items()})
        bit = bit // 2
    return found


def gather_near(found):
    found = {**found, **{index ^ 1: swap(item, "dp", 1) for index, item in found.items()}}
    return [found[index] for index in range(len(found))]


def add(left, right, dtype=LOW):
    return (left.astype(FULL) + right.astype(FULL)).astype(dtype)


def scatter_near(items):
    taken = [swap(item, "dp", 1) for item in items[1::2]]
    return [add(kept, got) for kept, got in zip(items[0::2], taken)]


def scatter_far(items):
    bit = 2
    while len(items) > 2:
        taken = [swap(item, "dp", bit) for item in items[1::2]]
        items = [add(kept, got) for kept, got in zip(items[0::2], taken)]
        bit = bit * 2
    return items[0], swap(items[1], "dp", bit)


def scatter_terms(items):
    return scatter_far(scatter_near(items))


def sum_steps():
    steps = []
    for axis in ("dp", "expert"):
        bit = 1
        while bit < lax.axis_size(axis):
            steps.append((axis, bit))
            bit = bit * 2
    return steps


def together(*values):
    return lax.optimization_barrier(values)


def gather_pieces(payload, early):
    ranks, dps = lax.axis_size("expert"), lax.axis_size("dp")
    half = payload.shape[0] // 2
    far = list(range(0, ranks, 2))
    sides = {"x": ("expert", [0, 1]), "y": ("dp", list(range(0, dps, 2)))}
    value, early = together(gather_bits(payload[None], "expert", far[1:]), early)
    values = (value[:, :half], value[:, half:])
    firsts = []
    for value, letter in zip(values, "xy"):
        axis, masks = sides[letter]
        firsts.append(gather_bits(value[None], axis, masks[1:]))
    seconds = []
    for value, letter in zip(firsts, "yx"):
        axis, masks = sides[letter]
        seconds.append([swap(value, axis, mask) for mask in masks[1:]])
    others = [swap(value, "dp", 1) for value in firsts]
    pieces, places = [], []
    for index, order in enumerate(("xy", "yx")):
        masks, other_masks = sides[order[0]][1], sides[order[1]][1]
        found = [(firsts[index], 0, 0), (others[index], 0, 1)]
        for value, mask in zip(seconds[index], other_masks[1:]):
            found += [(value, mask, 0), (swap(value, "dp", 1), mask, 1)]
        for piece, mask, core in found:
            offsets = []
            for first in masks:
                for low in far:
                    x_mask, y_mask = (first, mask) if order == "xy" else (mask, first)
                    offsets.append((low ^ x_mask, y_mask ^ core))
            pieces.append(piece)
            places.append((index, offsets))
    return pieces, places, early


def place_weights(places, piece_refs, w_ref, sem):
    my_expert, my_dp = lax.axis_index("expert"), lax.axis_index("dp")
    copies, masks = [], []
    for ref, (half, offsets) in zip(piece_refs, places):
        low_count, rows = ref.shape[1], ref.shape[2]
        for index, (e_mask, d_mask) in enumerate(offsets):
            start = (my_dp ^ d_mask) * (2 * rows) + half * rows
            copies.append(
                pltpu.make_async_copy(
                    ref.at[index // low_count, index % low_count],
                    w_ref.at[my_expert ^ e_mask, pl.ds(pl.multiple_of(start, 16), rows), :],
                    sem.at[e_mask],
                )
            )
            masks.append(e_mask)
    groups = [[] for _ in range(w_ref.shape[0])]
    for copy, e_mask in zip(copies, masks):
        groups[e_mask].append(copy)
    for group in groups:
        for copy in group:
            copy.start()
    return groups


def dot(left, right, dims=((1,), (0,)), precision=None):
    return lax.dot_general(
        left, right, (dims, ((), ())), precision=precision, preferred_element_type=FULL
    )


NT = ((1,), (1,))
TN = ((0,), (0,))


def grid_of(rows):
    sub = lax.broadcasted_iota(jnp.int32, (rows, 128), 0)
    lane = lax.broadcasted_iota(jnp.int32, (rows, 128), 1)
    return sub, lane


def row_to_column(row, rows, shift=0):
    sub, lane = grid_of(rows)
    column = jnp.sum(jnp.where(lane == sub + shift, row, 0.0), axis=1, keepdims=True)
    return jnp.broadcast_to(column, (rows, 128))


def column_to_row(column, shift=0):
    sub, lane = grid_of(column.shape[0])
    return jnp.sum(jnp.where(lane == sub + shift, column, 0.0), axis=0, keepdims=True)


def turn(value, shift):
    return pltpu.roll(value, shift % value.shape[1], 1)


def slide(value, direction):
    sub = lax.broadcasted_iota(jnp.int32, value.shape, 0)
    for bit in (1, 2, 4):
        value = jnp.where((sub & bit) != 0, turn(value, direction * bit), value)
    return value


def slid_rows(row, count):
    value = slide(jnp.broadcast_to(row, (8, row.shape[1])), 1)
    while value.shape[0] < count:
        value = jnp.concatenate([value, turn(value, value.shape[0])], axis=0)
    return value


def slid_sum(value):
    while value.shape[0] > 8:
        half = value.shape[0] // 2
        value = value[:half] + turn(value[half:], -half)
    return jnp.sum(slide(value, -1), axis=0, keepdims=True)


def early_kernel(
    ranks, local_experts, capacity, slab, tokens_ref, routes_ref, gain_ref, d_out_ref, table_ref,
    onehot_ref, normed_ref, hits_ref, mask_ref, mask_t_ref, bias_ref, up_ref
):
    length = tokens_ref.shape[0]
    normed, _ = normalize(tokens_ref[...].astype(FULL), gain_ref[0:1, :])
    normed_ref[...] = normed.astype(LOW)
    experts = hits_ref.shape[1]
    routes = jnp.broadcast_to(routes_ref[...].astype(FULL), (length, length)).T
    route = routes[:, :1].astype(jnp.int32)
    lanes = lax.broadcasted_iota(jnp.int32, (length, experts), 1)
    hits = (lanes == route).astype(FULL)
    hits_ref[...] = hits
    row = lax.broadcasted_iota(jnp.int32, (length, length), 0)
    col = lax.broadcasted_iota(jnp.int32, (length, length), 1)
    before = dot((col < row).astype(FULL).astype(LOW), hits.astype(LOW))
    placed = jnp.sum(before * hits, axis=1, keepdims=True).astype(jnp.int32)
    rank = jnp.zeros_like(route)
    for r in range(1, ranks):
        rank = rank + (route >= r * local_experts).astype(jnp.int32)
    spot = rank * slab + (route - rank * local_experts) * capacity + placed
    spot = jnp.where(placed < capacity, spot, -1)
    places = lax.broadcasted_iota(jnp.int32, (length, ranks * slab), 1)
    mask = (places == spot).astype(FULL)
    mask_ref[...] = mask.astype(LOW)
    mask_t = mask.T.astype(LOW)
    mask_t_ref[...] = mask_t
    slabs = dot(mask_t, d_out_ref[...])
    for r in range(ranks):
        up_ref[r] = slabs[r * slab : (r + 1) * slab].astype(LOW)
    values = dot(table_ref[...], onehot_ref[...])
    for h in range(bias_ref.shape[0]):
        bias_ref[h] = slid_rows(values[h : h + 1], length)[:, length:]


def forward_kernel(
    places, slab, rank_slots, tokens_ref, normed_ref, seg_ref, bias_ref, gain_ref,
    router_t_ref, hits_ref, mask_t_ref, *rest
):
    count = len(places)
    piece_refs, rest = rest[:count], rest[count:]
    heads_ref, weights_ref, rows_ref, hidden_ref, chance_ref = rest[:5]
    slabs_ref = rest[5]
    w_ref, qkv_ref, att_t_ref, sem = rest[-4:]
    copies = place_weights(places, piece_refs, w_ref, sem)
    ranks, width, columns = w_ref.shape
    cols = columns // 4
    head_count = weights_ref.shape[0]
    head = width // head_count
    length = tokens_ref.shape[0]
    segments = jnp.broadcast_to(seg_ref[...].astype(FULL), (length, length))
    same_doc = segments == segments.T
    normed = normed_ref[...]
    for j, group in enumerate(copies):
        for copy in group:
            copy.wait()
        e = lax.axis_index("expert") ^ j
        turned = dot(normed, w_ref[e]).T
        for m in range(3):
            qkv_ref[m, e] = turned[m * cols : (m + 1) * cols]
    heads_ref[...] = qkv_ref[...].reshape(3, width, length).astype(LOW)
    for h in range(head_count):
        rows = slice(h * head, (h + 1) * head)
        scores = dot(heads_ref[0, rows, :], heads_ref[1, rows, :], TN) * head ** (-0.5)
        scores = jnp.where(same_doc, scores + bias_ref[h], MASKED)
        grown = jnp.exp(scores - jnp.max(scores, axis=1, keepdims=True))
        weights = grown / jnp.sum(grown, axis=1, keepdims=True)
        weights_ref[h] = weights
        att_t_ref[rows, :] = dot(heads_ref[2, rows, :], weights.astype(LOW), NT)
    attended = att_t_ref[...].T.astype(LOW)
    rows_ref[...] = attended
    low_lane = 3 * cols // 128 * 128
    for e in range(ranks):
        turned = dot(attended, w_ref[e, :, low_lane:]).T
        att_t_ref[e * cols : (e + 1) * cols, :] = turned[3 * cols - low_lane :]
    hidden = tokens_ref[...].astype(FULL) + att_t_ref[...].T
    hidden_ref[...] = hidden
    normed_two, _ = normalize(hidden, gain_ref[1:2, :])
    logits = dot(normed_two, router_t_ref[...].astype(FULL), NT, HIGHEST)
    grown = jnp.exp(logits - jnp.max(logits, axis=1, keepdims=True))
    chance = grown / jnp.sum(grown, axis=1, keepdims=True)
    chance_ref[...] = chance
    gate = jnp.sum(chance * hits_ref[...], axis=1, keepdims=True)
    mask_t = mask_t_ref[...]
    slots = dot(mask_t, normed_two.astype(LOW))
    gates = dot(mask_t.astype(FULL), jnp.broadcast_to(gate, (length, 128)), precision=HIGHEST)
    sub, _ = grid_of(slab)
    for r in range(ranks):
        mine = gates[r * slab : (r + 1) * slab]
        high = mine.astype(LOW).astype(FULL)
        row = column_to_row(high) + column_to_row(mine - high, 64)
        rows = slots[r * slab : (r + 1) * slab]
        start = rows[:, :128] + jnp.where(sub == rank_slots, row, 0.0)
        slabs_ref[r, :, :128] = start.astype(LOW)
        slabs_ref[r, :, 128:] = rows[:, 128:].astype(LOW)


def upstream_kernel(pack_ref, w_out_ref, *rest):
    piece_refs, (rows_ref, act_ref) = rest[:-2], rest[-2:]
    local_experts = w_out_ref.shape[0]
    chunk = pack_ref.shape[0] // local_experts
    for p, piece in enumerate(piece_refs):
        packed = dot(pack_ref[...], piece[...]).astype(LOW)
        for e in range(local_experts):
            rows_ref[e, p * chunk : (p + 1) * chunk, :] = packed[e * chunk : (e + 1) * chunk]
    for e in range(local_experts):
        act_ref[e] = dot(rows_ref[e], w_out_ref[e], NT)


def unpack(pack_t, rows_ref, p, chunk):
    rows = [rows_ref[e, p * chunk : (p + 1) * chunk, :] for e in range(rows_ref.shape[0])]
    return dot(pack_t, jnp.concatenate(rows, axis=0))


def expert_kernel(
    count, slab, rank_slots, pack_ref, pack_t_ref, w_in_ref, up_act_ref, *rest
):
    piece_refs, rest = rest[:count], rest[count:]
    back_refs, rest = rest[:count], rest[count:]
    rows_ref, act_ref, pre_grad_ref, gates_ref, pre_ref, back_ref, part_ref = rest
    local_experts = w_in_ref.shape[0]
    chunk = pack_ref.shape[0] // local_experts
    ranks = pack_ref.shape[1] // slab
    pack, pack_t = pack_ref[...], pack_t_ref[...]
    for p, piece in enumerate(piece_refs):
        packed = dot(pack, piece[...]).astype(LOW)
        tile = piece[:, :128].astype(FULL)
        spread = []
        for shift in (0, 64):
            columns = [
                row_to_column(tile[r * slab + rank_slots : r * slab + rank_slots + 1], slab, shift)
                for r in range(ranks)
            ]
            spread.append(dot(pack, jnp.concatenate(columns, axis=0).astype(LOW)))
        gates = spread[0] + spread[1]
        for e in range(local_experts):
            rows_ref[e, p * chunk : (p + 1) * chunk, :] = packed[e * chunk : (e + 1) * chunk]
            gates_ref[e, p * chunk : (p + 1) * chunk, :] = gates[e * chunk : (e + 1) * chunk]
    root = np.float32(np.sqrt(2.0 / np.pi))
    step = 16
    for e in range(local_experts):
        pre_ref[...] = dot(rows_ref[e], w_in_ref[e])

        def body(index, carry):
            span = pl.ds(pl.multiple_of(index * step, step), step)
            pre = pre_ref[span, :]
            up = up_act_ref[e, span, :]
            square = pre * pre
            curve = jnp.tanh(root * pre * (1.0 + 0.044715 * square))
            rise = 0.5 + 0.5 * curve
            act = (pre * rise).astype(LOW)
            act_ref[e, span, :] = act
            slope = rise + pre * (rise * (1.0 - curve)) * (root + 3 * 0.044715 * root * square)
            gate = gates_ref[e, span, :][:, :1]
            pre_grad_ref[e, span, :] = (slope * (up * gate)).astype(LOW)
            part = jnp.sum(act.astype(FULL) * up, axis=1, keepdims=True)
            part_ref[e, span, :] = jnp.broadcast_to(part, (step, 128)).astype(LOW)
            return carry

        lax.fori_loop(0, pre_ref.shape[0] // step, body, 0, unroll=2)
        back_ref[e] = dot(pre_grad_ref[e], w_in_ref[e], NT).astype(LOW)
    sub, _ = grid_of(slab)
    for p in range(count):
        rows = unpack(pack_t, back_ref, p, chunk)
        parts = unpack(pack_t, part_ref, p, chunk)
        pieces = []
        for r in range(ranks):
            span = slice(r * slab, (r + 1) * slab)
            row = column_to_row(parts[span])
            pieces.append(rows[span, :128] + jnp.where(sub == rank_slots, row, 0.0))
        back_refs[p][:, :128] = jnp.concatenate(pieces, axis=0).astype(LOW)
        back_refs[p][:, 128:] = rows[:, 128:].astype(LOW)


def expert_out_kernel(pack_t_ref, w_out_ref, act_ref, *rest):
    out_refs, returned_ref = rest[:-1], rest[-1]
    chunk = act_ref.shape[1] // len(out_refs)
    for e in range(w_out_ref.shape[0]):
        returned_ref[e] = dot(act_ref[e], w_out_ref[e]).astype(LOW)
    for p, ref in enumerate(out_refs):
        ref[...] = unpack(pack_t_ref[...], returned_ref, p, chunk).astype(LOW)


def expert_grad_kernel(
    rows_ref, act_ref, pre_grad_ref, gates_ref, up_rows_ref, g_in_ref, g_out_ref
):
    g_in_ref[0] = dot(rows_ref[0], pre_grad_ref[0], TN)
    slot_grad = (up_rows_ref[0].astype(FULL) * gates_ref[0][:, :1]).astype(LOW)
    g_out_ref[0] = dot(act_ref[0], slot_grad, TN)


def expert_gradients(shapes, args):
    def block(item):
        return pl.BlockSpec((1,) + item.shape[1:], lambda e: (e, 0, 0))

    return pl.pallas_call(
        expert_grad_kernel,
        grid=(shapes[0].shape[0],),
        out_shape=tuple(shapes),
        in_specs=[block(item) for item in args],
        out_specs=tuple(block(item) for item in shapes),
        compiler_params=pltpu.CompilerParams(vmem_limit_bytes=LIMIT),
        cost_estimate=pl.CostEstimate(flops=0, bytes_accessed=28_800_000, transcendentals=0),
        name="expert_gradients",
    )(*args)


def joined(ref):
    ranks, slab, width = ref.shape
    return ref[...].astype(FULL).reshape(ranks * slab, width).astype(LOW)


def backward_kernel(
    places, rank_slots, tokens_ref, gain_ref, router_t_ref, hits_ref, mask_ref,
    up_ref, hidden_ref, chance_ref, heads_ref, weights_ref, onehot_ref, *rest
):
    count = len(places)
    piece_refs, rest = rest[:count], rest[count:]
    (back_ref, d_input_ref, small_ref, factors_ref,
     w_ref, turned_ref, grads_ref, bias_ref, sem) = rest
    ranks, width, columns = w_ref.shape
    copies = place_weights(places, piece_refs, w_ref, sem)
    cols = columns // 4
    head_count = weights_ref.shape[0]
    head = width // head_count
    factor = head ** (-0.5)
    length = tokens_ref.shape[0]
    slab = back_ref.shape[1]
    hidden = hidden_ref[...]
    gain_two = gain_ref[1:2, :]
    normed_two, scale_two = normalize(hidden, gain_two)
    mask = mask_ref[...]
    chance, hits = chance_ref[...], hits_ref[...]
    gate = jnp.sum(chance * hits, axis=1, keepdims=True)
    spread = [
        row_to_column(back_ref[r, :, :128].astype(FULL)[rank_slots : rank_slots + 1], slab)
        for r in range(ranks)
    ]
    gate_grad = dot(mask, jnp.concatenate(spread, axis=0).astype(LOW))[:, :1]
    logit_grad = chance * (hits - gate) * gate_grad
    experts = hits.shape[1]
    small_ref[:experts, :] = dot(logit_grad, normed_two, TN, HIGHEST)
    router_t = router_t_ref[...].astype(FULL)
    normed_two_grad = dot(logit_grad, router_t, precision=HIGHEST) + dot(mask, joined(back_ref))
    hidden_part, ffn_gain_grad = norm_back(hidden, scale_two, gain_two, normed_two_grad)
    hidden_grad = up_ref[...].astype(FULL) + hidden_part
    turned_ref[...] = hidden_grad.astype(LOW).astype(FULL).T
    for group in copies:
        for copy in group:
            copy.wait()
    low_lane = 3 * cols // 128 * 128
    att_grad = None
    for e in range(ranks):
        own = turned_ref[e * cols : (e + 1) * cols, :]
        if 3 * cols > low_lane:
            own = jnp.concatenate([jnp.zeros((3 * cols - low_lane, 128), FULL), own], axis=0)
        part = dot(w_ref[e, :, low_lane:], own.astype(LOW))
        att_grad = part if att_grad is None else att_grad + part
    att_grad = att_grad.astype(LOW)
    for h in range(head_count):
        rows = slice(h * head, (h + 1) * head)
        own = att_grad[rows]
        weights = weights_ref[h]
        grads_ref[2, rows, :] = dot(own, weights.astype(LOW))
        prob_grad = dot(own, heads_ref[2, rows, :], TN)
        score_grad = weights * (prob_grad - jnp.sum(prob_grad * weights, axis=1, keepdims=True))
        score_grad = score_grad.astype(LOW)
        grads_ref[0, rows, :] = dot(heads_ref[1, rows, :], score_grad, NT) * factor
        grads_ref[1, rows, :] = dot(heads_ref[0, rows, :], score_grad) * factor
        wide = [jnp.zeros((length, length), FULL), score_grad.astype(FULL)]
        bias_ref[h : h + 1, :] = slid_sum(jnp.concatenate(wide, axis=1))
    total = None
    for e in range(ranks):
        span = slice(e * cols, (e + 1) * cols)
        held = [grads_ref[m, span, :] for m in range(3)] + [jnp.zeros((cols, 128), FULL)]
        part = dot(w_ref[e], jnp.concatenate(held, axis=0).astype(LOW))
        total = part if total is None else total + part
        sent = [grads_ref[m, span, :] for m in range(3)] + [turned_ref[span, :]]
        sent = jnp.concatenate(sent, axis=0).astype(LOW)
        factors_ref[e % (ranks // 2), e // (ranks // 2)] = sent
    inputs = tokens_ref[...].astype(FULL)
    gain_one = gain_ref[0:1, :]
    _, scale_one = normalize(inputs, gain_one)
    norm_part, attn_gain_grad = norm_back(inputs, scale_one, gain_one, total.T)
    d_input_ref[...] = hidden_grad + norm_part
    sums = dot(bias_ref[...], onehot_ref[...], NT, HIGHEST)
    small_ref[experts : experts + 1, :] = ffn_gain_grad
    small_ref[experts + 1 : experts + 2, :] = attn_gain_grad
    small_ref[experts + 2 :, :] = jnp.zeros((small_ref.shape[0] - experts - 2, width), FULL)
    for h in range(head_count):
        line, place = experts + 2 + h // 6, 128 * (h % 6)
        small_ref[line : line + 1, place : place + sums.shape[1]] = sums[h : h + 1]


def product_kernel(factors_ref, *rest):
    count, _, columns, length = factors_ref.shape
    normed_refs, attended_refs = rest[:count], rest[count : 2 * count]
    piece_refs, total_ref = rest[2 * count : -1], rest[-1]
    cols = columns // 4
    rows = total_ref.shape[2]
    mine = lax.rem(lax.axis_index("expert"), count)
    for side in range(2):
        first, second = None, None
        for j in range(count):
            held = factors_ref[mine ^ j, side].astype(FULL)
            part = dot(held[: 3 * cols].astype(LOW), normed_refs[j][...])
            first = part if first is None else first + part
            part = dot(held[3 * cols :].astype(LOW), attended_refs[j][...])
            second = part if second is None else second + part
        total = jnp.concatenate([first, second], axis=0).T
        for j in range(len(piece_refs)):
            total_ref[side, j] = total[j * rows : (j + 1) * rows]
    own = (lax.axis_index("expert") >= count).astype(jnp.int32)
    for j, ref in enumerate(piece_refs):
        place = lax.axis_index("dp") ^ j
        ref[0] = total_ref[own, place].astype(LOW)
        ref[1] = total_ref[1 - own, place].astype(LOW)


def output_kernel(hidden_ref, chance_ref, hits_ref, mask_ref, returned_ref, output_ref):
    gate = jnp.sum(chance_ref[...] * hits_ref[...], axis=1, keepdims=True)
    fetched = dot(mask_ref[...], joined(returned_ref))
    output_ref[...] = (hidden_ref[...] + gate * fetched).astype(LOW)


VMEM = pl.BlockSpec(memory_space=pltpu.VMEM)
ANY = pl.BlockSpec(memory_space=pl.ANY)
LIMIT = 60 * 1024 * 1024


def shaped(dtype, *shape):
    return jax.ShapeDtypeStruct(shape, dtype)


def call(kernel, name, micros, out_shape, args, pieces=(), scratch=(), more=()):
    return pl.pallas_call(
        kernel,
        out_shape=tuple(out_shape),
        in_specs=[VMEM] * len(args) + [ANY] * len(pieces) + [VMEM] * len(more),
        out_specs=(VMEM,) * len(out_shape),
        scratch_shapes=list(scratch),
        compiler_params=pltpu.CompilerParams(vmem_limit_bytes=LIMIT),
        cost_estimate=pl.CostEstimate(
            flops=0, bytes_accessed=micros * 3_600_000, transcendentals=0
        ),
        name=name,
    )(*args, *pieces, *more)


def per_device(
    tokens,
    seg_ids,
    routes,
    attn_gain,
    w_query,
    w_key,
    w_value,
    w_output,
    rel_bias,
    ffn_gain,
    w_router,
    w_in,
    w_out,
    d_out,
):
    length, model_width = tokens.shape
    bucket_count, head_count = rel_bias.shape
    experts_total = w_router.shape[1]
    local_experts, _, hidden_here = w_in.shape
    ranks, dps = lax.axis_size("expert"), lax.axis_size("dp")
    capacity = length * 5 // (4 * experts_total)
    rank_slots = local_experts * capacity
    slab = -(-(rank_slots + 1) // 8) * 8
    rows_here, columns_here = w_query.shape
    inner_width = dps * rows_here
    packed_rows = dps * ranks * capacity
    gains = jnp.stack([attn_gain, ffn_gain]).astype(FULL)
    slabs_shape = shaped(LOW, ranks, slab, model_width)
    router_t = w_router.T
    pack = packing(local_experts, ranks, capacity, slab)
    pack, pack_t = jnp.asarray(pack, LOW), jnp.asarray(pack.T, LOW)

    normed_low, hits, mask, mask_t, bias_full, up_slabs = call(
        functools.partial(early_kernel, ranks, local_experts, capacity, slab),
        "early",
        3,
        [
            shaped(LOW, length, model_width),
            shaped(FULL, length, experts_total),
            shaped(LOW, length, ranks * slab),
            shaped(LOW, ranks * slab, length),
            shaped(FULL, head_count, length, length),
            slabs_shape,
        ],
        [
            tokens,
            routes.reshape(1, length),
            gains,
            d_out,
            rel_bias.T,
            jnp.asarray(bucket_onehot(bucket_count, length), LOW),
        ],
    )

    payload = jnp.concatenate([w_query, w_key, w_value, w_output], axis=1)
    early = (normed_low, hits, mask, mask_t, bias_full)
    pieces, places, early = gather_pieces(payload, early)
    normed_low, hits, mask, mask_t, bias_full = early
    pieces, up_slabs = together(pieces, up_slabs)
    up_arrived = exchange(up_slabs).reshape(ranks * slab, model_width)

    w_shape = (ranks, inner_width, 4 * columns_here)
    heads, weights, attended, hidden, chance, slabs = call(
        functools.partial(forward_kernel, places, slab, rank_slots),
        "attention_forward",
        10,
        [
            shaped(LOW, 3, inner_width, length),
            shaped(FULL, head_count, length, length),
            shaped(LOW, length, inner_width),
            shaped(FULL, length, model_width),
            shaped(FULL, length, experts_total),
            slabs_shape,
        ],
        [tokens, normed_low, seg_ids, bias_full, gains, router_t, hits, mask_t],
        pieces,
        [
            pltpu.VMEM(w_shape, LOW),
            pltpu.VMEM((3, ranks, columns_here, length), FULL),
            pltpu.VMEM((inner_width, length), FULL),
            pltpu.SemaphoreType.DMA((ranks,)),
        ],
    )

    slabs, up_arrived = together(slabs, up_arrived)
    arrived = exchange(slabs).reshape(ranks * slab, model_width)
    up_pieces = gather_near(gather_far(up_arrived))
    by_expert = (local_experts, packed_rows)
    up_rows, up_act = call(
        upstream_kernel,
        "upstream_rows",
        1,
        [shaped(LOW, *by_expert, model_width), shaped(FULL, *by_expert, hidden_here)],
        [pack, w_out, *up_pieces],
    )
    arrived, up_act, attended_own = together(arrived, up_act, attended)
    row_far = gather_far(arrived)
    near_attended = half_ranks(attended_own)
    row_pieces = gather_near(row_far)

    *back, slot_rows, activated, pre_grad, gates = call(
        functools.partial(expert_kernel, dps, slab, rank_slots),
        "experts",
        10,
        [shaped(LOW, ranks * slab, model_width)] * dps
        + [
            shaped(LOW, *by_expert, model_width),
            shaped(LOW, *by_expert, hidden_here),
            shaped(LOW, *by_expert, hidden_here),
            shaped(FULL, *by_expert, 128),
        ],
        [pack, pack_t, w_in, up_act, *row_pieces],
        scratch=[
            pltpu.VMEM((packed_rows, hidden_here), FULL),
            pltpu.VMEM((*by_expert, model_width), LOW),
            pltpu.VMEM((*by_expert, 128), LOW),
        ],
    )
    back, near_attended = together(back, near_attended)
    near, late_activated = together(scatter_near(back), activated)
    kept, got = scatter_far(near)
    returned = call(
        expert_out_kernel,
        "expert_outputs",
        3,
        [shaped(LOW, ranks * slab, model_width)] * dps,
        [pack_t, w_out, late_activated],
        scratch=[pltpu.VMEM((*by_expert, model_width), LOW)],
    )
    got, returned = together(got, returned)
    back = add(kept, got).reshape(ranks, slab, model_width)
    back, returned = together(back, returned)
    back = exchange(back)
    returned = add(*scatter_terms(returned)).reshape(ranks, slab, model_width)
    back, returned, normed_own = together(back, returned, normed_low)
    returned = exchange(returned)
    near_normed = half_ranks(normed_own)

    bias_rows = -(-head_count // 6)
    small_rows = -(-(experts_total + 2 + bias_rows) // 8) * 8
    d_input, small, factors = call(
        functools.partial(backward_kernel, places, rank_slots),
        "attention_backward",
        12,
        [
            shaped(FULL, length, model_width),
            shaped(FULL, small_rows, model_width),
            shaped(LOW, ranks // 2, 2, 4 * columns_here, length),
        ],
        [
            tokens,
            gains,
            router_t,
            hits,
            mask,
            d_out,
            hidden,
            chance,
            heads,
            weights,
            jnp.asarray(bucket_onehot(bucket_count, length), FULL),
        ],
        pieces,
        [
            pltpu.VMEM(w_shape, LOW),
            pltpu.VMEM((inner_width, length), FULL),
            pltpu.VMEM((3, inner_width, length), FULL),
            pltpu.VMEM((head_count, 2 * length), FULL),
            pltpu.SemaphoreType.DMA((ranks,)),
        ],
        [back],
    )

    factors, small, returned, near_normed = together(factors, small, returned, near_normed)
    factors = lax.all_to_all(
        factors, "expert", split_axis=0, concat_axis=0, tiled=True, axis_index_groups=halves()
    )
    first, *steps, one_but_last, last = sum_steps()
    small = small + swap(small, *first)
    for axis, bit in steps:
        small = small + swap(small, axis, bit)
    factors, small = together(factors, small)
    small = small + swap(small, *one_but_last)
    grads = call(
        product_kernel,
        "weight_gradients",
        5,
        [shaped(LOW, 2, rows_here, 4 * columns_here)] * dps,
        [factors, *near_normed, *near_attended],
        scratch=[pltpu.VMEM((2, dps, rows_here, 4 * columns_here), FULL)],
    )
    grads, small = together(scatter_near(grads), small)
    small = small + swap(small, *last)
    (output,) = call(
        output_kernel,
        "output_rows",
        2,
        [shaped(LOW, length, model_width)],
        [hidden, chance, hits, mask, returned],
    )
    kept, got = scatter_far(grads)
    got, output = together(got, output)
    other, activated = together(add(kept[1], got[1]), activated)
    other = swap(other, "expert", ranks // 2)
    first_grad, second_grad = expert_gradients(
        [shaped(FULL, *w_in.shape), shaped(FULL, *w_out.shape)],
        [slot_rows, activated, pre_grad, gates, up_rows],
    )
    other, first_grad = together(other, first_grad)
    grads = kept[0].astype(FULL) + got[0].astype(FULL) + other.astype(FULL)
    g_query, g_key, g_value, g_output = (
        grads[:, i * columns_here : (i + 1) * columns_here] for i in range(4)
    )
    g_router = small[:experts_total].T
    g_ffn_gain, g_attn_gain = small[experts_total], small[experts_total + 1]
    g_rel_bias = small[experts_total + 2 : experts_total + 2 + bias_rows].reshape(-1, 128)
    g_rel_bias = g_rel_bias[:head_count, :bucket_count].T
    return (
        output,
        d_input,
        g_attn_gain,
        g_query,
        g_key,
        g_value,
        g_output,
        g_rel_bias,
        g_ffn_gain,
        g_router,
        first_grad,
        second_grad,
    )


def solution(mesh):
    return jax.shard_map(
        per_device,
        mesh=mesh,
        in_specs=(
            P(("dp", "expert"), None),
            P(("dp", "expert"), None),
            P(("dp", "expert"), None),
            P(),
            P("dp", "expert"),
            P("dp", "expert"),
            P("dp", "expert"),
            P("dp", "expert"),
            P(),
            P(),
            P(),
            P("expert", None, "dp"),
            P("expert", "dp", None),
            P(("dp", "expert"), None),
        ),
        out_specs=(
            P(("dp", "expert"), None),
            P(("dp", "expert"), None),
            P(),
            P("dp", "expert"),
            P("dp", "expert"),
            P("dp", "expert"),
            P("dp", "expert"),
            P(),
            P(),
            P(),
            P("expert", None, "dp"),
            P("expert", "dp", None),
        ),
        check_vma=False,
    )
```
